32 devices in a mesh: section: 2 (over x), batch: 16 (over z, y, core).
Axes of the slice: x: 2, y: 2, z: 4, core: 2. Of those that a mesh axis runs over, the one named last changes fastest.
Arguments:
- inputs: bfloat16 [2, 16, 256, 768], P(None, 'batch'), may hold values from -6 to 6
- cotangent: bfloat16 [2, 16, 256, 768], P(None, 'batch'), may hold values from -6 to 6
- lengths: int32 [2, 16, 4], P(None, 'batch'), may hold values from 1 to 128, 256 in all within a row
- qkv_weight: bfloat16 [2, 768, 2304], P('section', 'batch'), may hold values from -0.21875 to 0.21875
- out_weight: bfloat16 [2, 768, 768], P('section', 'batch'), may hold values from -0.875 to 0.875
- up_weight: bfloat16 [2, 768, 3072], P('section', 'batch'), may hold values from -0.21875 to 0.21875
- down_weight: bfloat16 [2, 3072, 768], P('section', 'batch'), may hold values from -0.109375 to 0.109375
- biases: bfloat16 [2, 6144], P('section', 'batch'), may hold values from -3 to 3
- norm_gains: bfloat16 [2, 2, 768], P('section', None, 'batch'), may hold values from 0.099609375 to 1.8984375
- norm_shifts: bfloat16 [2, 2, 768], P('section', None, 'batch'), may hold values from -3 to 3
Outputs:
- activations: bfloat16 [2, 2, 16, 256, 768], P('section', None, 'batch')
- input_grads: bfloat16 [2, 2, 16, 256, 768], P('section', None, 'batch')
- qkv_grad: float32 [2, 768, 2304], P('section', 'batch')
- out_grad: float32 [2, 768, 768], P('section', 'batch')
- up_grad: float32 [2, 768, 3072], P('section', 'batch')
- down_grad: float32 [2, 3072, 768], P('section', 'batch')
- bias_grad: float32 [2, 6144], P('section', 'batch')
- gain_grad: float32 [2, 2, 768], P('section', None, 'batch')
- shift_grad: float32 [2, 2, 768], P('section', None, 'batch')
The draws below stay inside these ranges and needn't reach their ends.
Inputs may be any that keep to these rules, and one draw needn't show every extreme that they name: In each packed row the 4 lengths sum to 256, and one of them equals 128.
All inputs are finite; a program needn't handle non-finite values.
Results may differ from the reference program's by a relative error of at most 0.025.
Values may be sent and summed in bfloat16 or wider, within the bound.
No kernel may reach another device: no remote copies, remote signals or barrier semaphores. Data moves between devices by JAX's collectives and lax.ppermute only.
A program may use at most 192 MiB of HBM per device.

```python
import math
import jax
import jax.numpy as jnp
import numpy as np
from jax import lax

D = 768
HEADS = 12
FF = 3072
HEAD_DIM = 64
ROW = 256
LONGEST = 128
SEGS = 4
MICRO = 2
ROWS = 16
BIAS = 6144
N_SECTION = 2


def spiked(values, rng, source, target, parts, factor):
    def block_of(axis_at):
        return (jnp.arange(values.shape[axis_at]) // (values.shape[axis_at] // parts)).reshape((-1,) + (1,) * (values.ndim - 1 - axis_at))

    one_side = jax.random.permutation(rng, parts)[block_of(target)]
    second = (block_of(target) + parts // 2) % parts
    return jnp.where((block_of(source) == one_side) | (block_of(source) == second), factor * values, values)


def block_scale(rng, dims, shards, least, largest):
    loudness = 1.0
    for axis_at, shards_of in shards:
        steps = jax.random.uniform(jax.random.fold_in(jax.random.fold_in(rng, 6), axis_at), (shards_of,), jnp.float32, least / len(shards), largest / len(shards))
        loudness = loudness * jnp.repeat(jnp.exp(steps), dims[axis_at] // shards_of).reshape((-1,) + (1,) * (len(dims) - 1 - axis_at))
    return loudness


def split_up(amount, total, bound, lean):
    loads = [(1 << 20) // math.isqrt(grade ** lean) + 1 for grade in range(2, amount + 1)]
    spare, given = total - bound - (amount - 1), [1] * (amount - 1)
    while spare > 0:
        candidates = [i for i in range(amount - 1) if given[i] < bound]
        mass, remaining = sum([loads[i] for i in candidates]), spare
        for i in candidates:
            addition = min(bound - given[i], max(1, remaining * loads[i] // mass), spare)
            given[i] = given[i] + addition
            spare = spare - addition
    return np.array([bound] + given)


def uneven(own_key, number_of, total, most, lean):
    if number_of == 2:
        one = jax.random.randint(own_key, (), max(1, total - most), min(most, total - 1) + 1)
        return jnp.stack([one, total - one])
    sizes = jnp.asarray(split_up(number_of, total, most, lean), jnp.int32)
    twos = (number_of - 1) // 2
    donor, sink = sizes[1:1 + 2 * twos:2], sizes[2:2 + 2 * twos:2]
    margin = jnp.minimum(donor - 1, most - sink)
    shifted = jax.random.randint(jax.random.fold_in(own_key, 1), (twos,), 0, 1 << 20) % (margin + 1)
    sizes = sizes.at[1:1 + 2 * twos:2].set(donor - shifted).at[2:2 + 2 * twos:2].set(sink + shifted)
    return sizes[jax.random.permutation(jax.random.fold_in(own_key, 2), number_of)]


def gaussian(key, shape, deviation, bound, cuts=(), kind=jnp.bfloat16):
    loudness = block_scale(key, shape, cuts, -0.22, 0.18) if cuts else 1.0
    entries = jax.random.normal(key, shape, jnp.float32) * deviation * loudness
    return jnp.minimum(jnp.maximum(entries, -bound), bound).astype(kind)


def noise_with(own_key, shape, width, limit, shards, heavy, held_as=jnp.bfloat16):
    result = width * jax.random.normal(own_key, shape, jnp.float32)
    if shards:
        result = result * block_scale(own_key, shape, shards, -0.22, 0.18)
    return jnp.clip(spiked(result, jax.random.fold_in(own_key, 3), *heavy), -limit, limit).astype(held_as)


def setup_inputs(seed: int = 0) -> dict:
    seeds = jax.random.split(jax.random.key(seed), 11)
    return {
        "inputs": noise_with(seeds[0], (MICRO, ROWS, ROW, D), 1.0, 6.0, ((1, 16),), (1, 3, 16, 2.0)),
        "cotangent": gaussian(seeds[1], (MICRO, ROWS, ROW, D), 1.0, 6.0, ((1, 16),)),
        "lengths": jax.vmap(lambda own: uneven(own, SEGS, ROW, LONGEST, 2))(jax.random.split(seeds[2], MICRO * ROWS)).reshape((MICRO, ROWS, SEGS)).astype(jnp.int32),
        "qkv_weight": gaussian(seeds[3], (N_SECTION, D, 3 * D), D ** -0.5, 0.21875, ((0, 2), (1, 16))),
        "out_weight": gaussian(seeds[4], (N_SECTION, D, D), (D // 16) ** -0.5, 0.875, ((0, 2), (1, 16))),
        "up_weight": gaussian(seeds[5], (N_SECTION, D, FF), D ** -0.5, 0.21875, ((0, 2), (1, 16))),
        "down_weight": gaussian(seeds[6], (N_SECTION, FF, D), FF ** -0.5, 0.109375, ((0, 2), (1, 16))),
        "biases": gaussian(seeds[7], (N_SECTION, BIAS), 0.3, 3.0, ((0, 2), (1, 16))),
        "norm_gains": jnp.clip(1.0 + 0.18 * jax.random.normal(seeds[8], (N_SECTION, 2, D), jnp.float32), 0.099609375, 1.8984375).astype(jnp.bfloat16),
        "norm_shifts": gaussian(seeds[9], (N_SECTION, 2, D), 0.3, 3.0, ((0, 2), (2, 16))),
    }


@jax.custom_vjp
def low(v):
    return lax.optimization_barrier(v.astype(jnp.bfloat16)).astype(jnp.float32)

@jax.custom_vjp
def low_back(v):
    return v

def low_keep(v):
    return (low(v), None)

def low_pass(kept, grad):
    return (grad,)

def back_keep(v):
    return (v, None)

def back_low(kept, grad):
    return (low(grad),)
low.defvjp(low_keep, low_pass)
low_back.defvjp(back_keep, back_low)
epsilon = 1e-12
masked_value = -1e+30
highest = lax.Precision.HIGHEST

def layer_norm(values, gain_vec, shift_vec):
    average = lax.optimization_barrier(jnp.mean(values, axis=-1, keepdims=True))
    centred = values - average
    spread = lax.optimization_barrier(jnp.mean(centred * centred, axis=-1, keepdims=True))
    return centred * lax.rsqrt(spread + epsilon) * gain_vec + shift_vec

def segment_mask(row_lengths):
    bounds = jnp.cumsum(row_lengths)
    places = jnp.arange(ROW, dtype=jnp.int32)
    segment = lax.optimization_barrier(jnp.sum((places[:, None] >= bounds[None, :]).astype(jnp.int32), axis=1))
    return segment[:, None] == segment[None, :]

def layer_forward(tokens, qkv_w, out_w, up_w, down_w, bias_row, gain_pair, shift_pair, row_mask):
    joined_proj = jnp.dot(tokens, qkv_w, precision=highest)
    queries = low_back(low(joined_proj[:, :D] + bias_row[:D]))
    key_rows = low_back(low(joined_proj[:, D:2 * D]))
    value_rows = low_back(low(joined_proj[:, 2 * D:] + bias_row[D:2 * D]))
    shaped = (ROW, HEADS, HEAD_DIM)
    raw_scores = jnp.einsum('qhd,khd->hqk', queries.reshape(shaped), key_rows.reshape(shaped), precision=highest)
    raw_scores = low_back(raw_scores) * HEAD_DIM ** (-0.5)
    raw_scores = jnp.where(row_mask[None], raw_scores, masked_value)
    attn_probs = jax.nn.softmax(raw_scores, axis=-1)
    context = jnp.einsum('hqk,khd->qhd', low(attn_probs), value_rows.reshape(shaped), precision=highest)
    context = low_back(low(context.reshape(ROW, D)))
    attended = low_back(jnp.dot(context, out_w, precision=highest) + bias_row[2 * D:3 * D])
    normed = layer_norm(tokens + attended, gain_pair[0], shift_pair[0])
    inner_pre = low_back(jnp.dot(low(normed), up_w, precision=highest) + bias_row[3 * D:3 * D + FF])
    active = low(jax.nn.gelu(inner_pre, approximate=False))
    branch = low_back(jnp.dot(active, down_w, precision=highest) + bias_row[3 * D + FF:])
    return layer_norm(normed + branch, gain_pair[1], shift_pair[1])

def two_layers(tokens, middle_zero, params, row_mask):
    qkv_w, out_w, up_w, down_w, bias_all, gain_all, shift_all = params
    first_out = low(layer_forward(tokens, qkv_w[0], out_w[0], up_w[0], down_w[0], bias_all[0], gain_all[0], shift_all[0], row_mask))
    second_in = low_back(first_out) + middle_zero
    second_out = layer_forward(second_in, qkv_w[1], out_w[1], up_w[1], down_w[1], bias_all[1], gain_all[1], shift_all[1], row_mask)
    return (first_out, low(second_out))

def reference(inputs, cotangent, lengths, qkv_weight, out_weight, up_weight, down_weight, biases, norm_gains, norm_shifts):
    params = tuple((member.astype(jnp.float32) for member in (qkv_weight, out_weight, up_weight, down_weight, biases, norm_gains, norm_shifts)))
    flat_in = inputs.reshape(-1, ROW, D)
    flat_co = cotangent.reshape(-1, ROW, D)
    flat_len = lengths.reshape(-1, lengths.shape[-1])

    def one_row(totals, pieces):
        row_in, row_co, row_len = pieces
        row_mask = segment_mask(row_len)

        def forward(tokens, middle, weights):
            return two_layers(tokens, middle, weights, row_mask)
        zero_mid = jnp.zeros((ROW, D), jnp.float32)
        outputs, pullback = jax.vjp(forward, row_in.astype(jnp.float32), zero_mid, params)
        first_low, second_low = outputs
        grad_in, grad_mid, grad_params = pullback((jnp.zeros_like(first_low), row_co.astype(jnp.float32)))
        totals = jax.tree.map(jnp.add, totals, grad_params)
        return (totals, (first_low.astype(jnp.bfloat16), second_low.astype(jnp.bfloat16), grad_in.astype(jnp.bfloat16), grad_mid.astype(jnp.bfloat16)))
    start = tuple((jnp.zeros_like(member) for member in params))
    totals, rows_out = lax.scan(one_row, start, (flat_in, flat_co, flat_len))
    first_low, second_low, grad_in, grad_mid = rows_out
    activations = jnp.stack([first_low, second_low]).reshape((2,) + inputs.shape)
    input_grads = jnp.stack([grad_in, grad_mid]).reshape((2,) + inputs.shape)
    return (activations, input_grads, totals[0], totals[1], totals[2], totals[3], totals[4], totals[5], totals[6])
```

```python
from functools import partial

import jax
import jax.numpy as jnp
from jax import lax
from jax.experimental import pallas as pl
from jax.experimental.pallas import tpu as pltpu
from jax.sharding import PartitionSpec as P

D = 768
HEADS = 12
FF = 3072
HEAD_DIM = 64
ROW = 256
PAIRS = HEADS // 2
PAIR = 2 * HEAD_DIM
FFC = FF // D
BIAS = 6144
VMEM_LIMIT = 56 * 1024 * 1024

BF = jnp.bfloat16
F32 = jnp.float32
epsilon = 1e-12
masked_value = -1e30
inv_sqrt2 = 0.7071067811865476
inv_sqrt2pi = 0.3989422804014327


def nn(a, b):
    return jnp.dot(a, b, preferred_element_type=F32)


def nt(a, b):
    return lax.dot_general(a, b, (((1,), (1,)), ((), ())), preferred_element_type=F32)


def tn(a, b):
    return lax.dot_general(a, b, (((0,), (0,)), ((), ())), preferred_element_type=F32)


def head_masks():
    lane = lax.broadcasted_iota(jnp.int32, (1, PAIR), 1)
    low = (lane < HEAD_DIM).astype(F32)
    return (low.astype(BF), (1.0 - low).astype(BF))


def segment_penalty(lengths_ref, micro):
    first = lengths_ref[micro, 0]
    second = first + lengths_ref[micro, 1]
    third = second + lengths_ref[micro, 2]

    def number(axis):
        place = lax.broadcasted_iota(jnp.int32, (ROW, ROW), axis)
        one = jnp.where(place >= first, 1, 0)
        two = jnp.where(place >= second, 1, 0)
        return one + two + jnp.where(place >= third, 1, 0)

    return jnp.where(number(0) == number(1), 0.0, masked_value)


def standardize(values):
    centred = values - jnp.mean(values, axis=-1, keepdims=True)
    spread = jnp.mean(centred * centred, axis=-1, keepdims=True)
    scale = lax.rsqrt(spread + epsilon)
    return centred * scale, scale


def norm_back(grad, unit, scale, gain):
    scaled = grad * gain
    mean_one = jnp.mean(scaled, axis=-1, keepdims=True)
    mean_two = jnp.mean(scaled * unit, axis=-1, keepdims=True)
    return scale * (scaled - mean_one - unit * mean_two)


class Copies:
    def __init__(self, sems):
        self.sems = sems
        self.used = 0

    def start(self, src, dst):
        copy = pltpu.make_async_copy(src, dst, self.sems.at[self.used])
        self.used += 1
        copy.start()
        return copy


def chunk(index):
    return slice(index * D, (index + 1) * D)


STATE = (
    ("qkv", (ROW, 3 * D), BF),
    ("probs", (HEADS, ROW, ROW), BF),
    ("context", (ROW, D), BF),
    ("hidden", (ROW, D), BF),
    ("active", (ROW, FF), BF),
    ("slope", (ROW, FF), BF),
    ("unit1", (ROW, D), F32),
    ("unit2", (ROW, D), F32),
    ("scales", (2, ROW, 128), F32),
)
STATE_AT = {entry[0]: place for place, entry in enumerate(STATE)}


def forward_kernel(step, last, *refs):
    info, lengths, biases, gains, shifts, inputs, received = refs[:7]
    qkv_w, out_w, up_w, down_w = refs[7:11]
    result = refs[11]
    outs = refs[12 : 12 + len(STATE)]
    rest = refs[12 + len(STATE) :]
    tokens_v, result_v = rest[:2]
    kept = rest[2 : 2 + len(STATE)]
    qkv_v, out_v, up_v, down_v, first_sum, second_sum, sems = rest[2 + len(STATE) :]
    section = info[0]
    name = {entry[0]: (kept[place], outs[place]) for place, entry in enumerate(STATE)}

    def work():
        copies = Copies(sems)
        if step == 0:
            tokens_in = copies.start(inputs.at[0, 0], tokens_v)
        elif step == last:
            tokens_in = copies.start(received, tokens_v)
        else:
            tokens_in = pltpu.make_async_copy(received, tokens_v, sems.at[copies.used])
            copies.used += 1

            @pl.when(section == 0)
            def _():
                pltpu.make_async_copy(inputs.at[step, 0], tokens_v, tokens_in_sem).start()

            @pl.when(section != 0)
            def _():
                tokens_in.start()

        qkv_in = [copies.start(qkv_w.at[:, chunk(j)], qkv_v.at[:, chunk(j)]) for j in range(3)]
        out_in = copies.start(out_w, out_v)
        up_in = [copies.start(up_w.at[:, chunk(j)], up_v.at[:, chunk(j)]) for j in range(FFC)]
        down_in = [copies.start(down_w.at[chunk(j)], down_v.at[chunk(j)]) for j in range(FFC)]
        leaving = []

        def leave(key, part=None):
            src, dst = name[key]
            if part is not None:
                src, dst = src.at[part], dst.at[part]
            leaving.append(copies.start(src, dst))

        bias = lambda start, size: biases[:, start : start + size].astype(F32)
        penalty = segment_penalty(lengths, jnp.where(section == 0, step, step - 1))
        qkv = name["qkv"][0]
        probs = name["probs"][0]
        tokens_in.wait()
        tokens = tokens_v[...]
        for j in range(3):
            qkv_in[j].wait()
            part = nn(tokens, qkv_v[:, chunk(j)])
            if j != 1:
                part = part + bias(0 if j == 0 else D, D)
            qkv[:, chunk(j)] = part.astype(BF)
        leave("qkv")
        masks = head_masks()
        context = name["context"][0]
        for pair in range(PAIRS):
            at = pair * PAIR
            queries = qkv[:, at : at + PAIR]
            keys = qkv[:, D + at : D + at + PAIR]
            values = qkv[:, 2 * D + at : 2 * D + at + PAIR]
            total = None
            for half in range(2):
                scores = nt(queries * masks[half], keys) * HEAD_DIM ** (-0.5) + penalty
                raised = jnp.exp(scores - jnp.max(scores, axis=-1, keepdims=True))
                share = (raised * (1.0 / jnp.sum(raised, axis=-1, keepdims=True))).astype(BF)
                probs[2 * pair + half] = share
                term = nn(share, values * masks[half])
                total = term if total is None else total + term
            context[:, at : at + PAIR] = total.astype(BF)
            leave("probs", slice(2 * pair, 2 * pair + 2))
        leave("context")
        out_in.wait()
        attended = nn(context[...], out_v[...]) + bias(2 * D, D)
        unit, scale = standardize(tokens.astype(F32) + attended)
        name["unit1"][0][...] = unit
        name["scales"][0][0] = jnp.broadcast_to(scale, (ROW, 128))
        leave("unit1")
        normed = unit * gains[0:1, :] + shifts[0:1, :]
        hidden = name["hidden"][0]
        hidden[...] = normed.astype(BF)
        leave("hidden")
        second_sum[...] = normed + bias(3 * D + FF, D)
        active, slope = name["active"][0], name["slope"][0]
        for j in range(FFC):
            up_in[j].wait()
            inner = nn(hidden[...], up_v[:, chunk(j)]) + bias(3 * D + j * D, D)
            phi = 0.5 * (1.0 + lax.erf(inner * inv_sqrt2))
            active[:, chunk(j)] = (inner * phi).astype(BF)
            bell = jnp.exp(inner * inner * -0.5) * inv_sqrt2pi
            slope[:, chunk(j)] = (phi + inner * bell).astype(BF)
            down_in[j].wait()
            second_sum[...] += nn(active[:, chunk(j)], down_v[chunk(j)])
        leave("active")
        leave("slope")
        unit, scale = standardize(second_sum[...])
        result_v[...] = (unit * gains[1:2, :] + shifts[1:2, :]).astype(BF)
        leaving.append(copies.start(result_v, result))
        name["unit2"][0][...] = unit
        name["scales"][0][1] = jnp.broadcast_to(scale, (ROW, 128))
        leave("unit2")
        leave("scales")
        for copy in leaving:
            copy.wait()

    tokens_in_sem = sems.at[0]
    if step == 0:
        pl.when(section == 0)(work)
    elif step == last:
        pl.when(section != 0)(work)
    else:
        work()


ANY = pl.BlockSpec(memory_space=pl.ANY)
SMEM = pl.BlockSpec(memory_space=pltpu.SMEM)
VMEM = pl.BlockSpec(memory_space=pltpu.VMEM)


def forward(step, last, section, lengths, small, inputs, received, weights):
    biases, gains, shifts = small
    scratch = [pltpu.VMEM((ROW, D), BF), pltpu.VMEM((ROW, D), BF)]
    scratch += [pltpu.VMEM(shape, kind) for _, shape, kind in STATE]
    scratch += [
        pltpu.VMEM((D, 3 * D), BF),
        pltpu.VMEM((D, D), BF),
        pltpu.VMEM((D, FF), BF),
        pltpu.VMEM((FF, D), BF),
        pltpu.VMEM((8, 128), F32),
        pltpu.VMEM((ROW, D), F32),
        pltpu.SemaphoreType.DMA((40,)),
    ]
    outs = pl.pallas_call(
        partial(forward_kernel, step, last),
        out_shape=[jax.ShapeDtypeStruct((ROW, D), BF)]
        + [jax.ShapeDtypeStruct(shape, kind) for _, shape, kind in STATE],
        in_specs=[SMEM, SMEM, VMEM, VMEM, VMEM] + [ANY] * 6,
        out_specs=[ANY] * (1 + len(STATE)),
        scratch_shapes=scratch,
        name="layer_forward",
        compiler_params=pltpu.CompilerParams(vmem_limit_bytes=VMEM_LIMIT),
        cost_estimate=pl.CostEstimate(
            flops=2 * ROW * (12 * D * D), bytes_accessed=24 << 20, transcendentals=ROW * FF
        ),
    )(section, lengths, biases, gains, shifts, inputs, received, *weights)
    return outs[0], outs[1:]


BACK = (
    ("down_side", (ROW, D), BF),
    ("inner", (ROW, FF), BF),
    ("attended", (ROW, D), BF),
    ("joined", (ROW, 3 * D), BF),
    ("norms", (8, D), F32),
)


def backward_kernel(step, last, *refs):
    info, biases, gains, cotangent, received = refs[:5]
    qkv_w, out_w, up_w, down_w = refs[5:9]
    state = refs[9 : 9 + len(STATE)]
    refs = refs[9 + len(STATE) :]
    result = refs[0]
    outs = refs[1 : 1 + len(BACK)]
    refs = refs[1 + len(BACK) :]
    grad_v, result_v, sum_v = refs[:3]
    refs = refs[3:]
    kept = refs[: len(BACK)]
    refs = refs[len(BACK) :]
    qkv_s, probs_s, slope_s, unit1_s, unit2_s, scales_s = refs[:6]
    qkv_v, out_v, up_v, down_v, sems = refs[6:]
    section = info[0]
    name = {entry[0]: (kept[place], outs[place]) for place, entry in enumerate(BACK)}
    held = lambda key: state[STATE_AT[key]]

    def work():
        copies = Copies(sems)
        if step == 0:
            grad_in = copies.start(cotangent.at[last - 1, 0], grad_v)
        elif step == last:
            grad_in = copies.start(received, grad_v)
        else:
            grad_in = pltpu.make_async_copy(received, grad_v, sems.at[0])
            copies.used += 1

            @pl.when(section != 0)
            def _():
                pltpu.make_async_copy(cotangent.at[last - 1 - step, 0], grad_v, sems.at[0]).start()

            @pl.when(section == 0)
            def _():
                grad_in.start()

        unit2_in = copies.start(held("unit2"), unit2_s)
        scales_in = copies.start(held("scales"), scales_s)
        down_in, slope_in, up_in = [], [], []
        for j in range(FFC):
            down_in.append(copies.start(down_w.at[chunk(j)], down_v.at[chunk(j)]))
            slope_in.append(copies.start(held("slope").at[:, chunk(j)], slope_s.at[:, chunk(j)]))
            up_in.append(copies.start(up_w.at[:, chunk(j)], up_v.at[:, chunk(j)]))
        unit1_in = copies.start(held("unit1"), unit1_s)
        out_in = copies.start(out_w, out_v)
        state_in = copies.start(held("qkv"), qkv_s)
        probs_in = copies.start(held("probs"), probs_s)
        qkv_in = copies.start(qkv_w, qkv_v)
        leaving = []

        def leave(key):
            leaving.append(copies.start(*name[key]))

        norms = name["norms"][0]
        grad_in.wait()
        unit2_in.wait()
        scales_in.wait()
        grad = grad_v[...].astype(F32)
        unit = unit2_s[...]
        norms[1:2, :] = jnp.sum(grad * unit, axis=0, keepdims=True)
        norms[3:4, :] = jnp.sum(grad, axis=0, keepdims=True)
        grad = norm_back(grad, unit, scales_s[1, :, 0:1], gains[1:2, :])
        down_side = name["down_side"][0]
        down_side[...] = grad.astype(BF)
        leave("down_side")
        sum_v[...] = grad
        inner = name["inner"][0]
        for j in range(FFC):
            down_in[j].wait()
            through = nt(down_side[...], down_v[chunk(j)])
            slope_in[j].wait()
            inner[:, chunk(j)] = (through * slope_s[:, chunk(j)].astype(F32)).astype(BF)
            up_in[j].wait()
            sum_v[...] += nt(inner[:, chunk(j)], up_v[:, chunk(j)])
        leave("inner")
        grad = sum_v[...]
        unit1_in.wait()
        unit = unit1_s[...]
        norms[0:1, :] = jnp.sum(grad * unit, axis=0, keepdims=True)
        norms[2:3, :] = jnp.sum(grad, axis=0, keepdims=True)
        norms[4:8, :] = jnp.zeros((4, D), F32)
        leave("norms")
        grad = norm_back(grad, unit, scales_s[0, :, 0:1], gains[0:1, :])
        sum_v[...] = grad
        attended = name["attended"][0]
        attended[...] = grad.astype(BF)
        leave("attended")
        out_in.wait()
        context_grad = nt(attended[...], out_v[...]).astype(BF)
        state_in.wait()
        probs_in.wait()
        masks = head_masks()
        joined = name["joined"][0]
        for pair in range(PAIRS):
            at = pair * PAIR
            queries = qkv_s[:, at : at + PAIR]
            keys = qkv_s[:, D + at : D + at + PAIR]
            values = qkv_s[:, 2 * D + at : 2 * D + at + PAIR]
            pair_grad = context_grad[:, at : at + PAIR]
            totals = [None, None, None]
            for half in range(2):
                mask = masks[half]
                share = probs_s[2 * pair + half]
                own_grad = pair_grad * mask
                prob_grad = nt(own_grad, values)
                wide = share.astype(F32)
                weighted = wide * prob_grad
                inner_sum = jnp.sum(weighted, axis=-1, keepdims=True)
                score_grad = ((weighted - wide * inner_sum) * HEAD_DIM ** (-0.5)).astype(BF)
                terms = (
                    nn(score_grad, keys * mask),
                    tn(score_grad, queries * mask),
                    tn(share, own_grad),
                )
                totals = [t if s is None else s + t for s, t in zip(totals, terms)]
            for which in range(3):
                joined[:, which * D + at : which * D + at + PAIR] = totals[which].astype(BF)
        leave("joined")
        qkv_in.wait()
        result_v[...] = (sum_v[...] + nt(joined[...], qkv_v[...])).astype(BF)
        leaving.append(copies.start(result_v, result))
        for copy in leaving:
            copy.wait()

    if step == 0:
        pl.when(section != 0)(work)
    elif step == last:
        pl.when(section == 0)(work)
    else:
        work()


def backward(step, last, section, small, cotangent, received, weights, state):
    biases, gains, shifts = small
    scratch = [pltpu.VMEM((ROW, D), BF), pltpu.VMEM((ROW, D), BF), pltpu.VMEM((ROW, D), F32)]
    scratch += [pltpu.VMEM(shape, kind) for _, shape, kind in BACK]
    scratch += [
        pltpu.VMEM(STATE[STATE_AT[key]][1], STATE[STATE_AT[key]][2])
        for key in ("qkv", "probs", "slope", "unit1", "unit2", "scales")
    ]
    scratch += [
        pltpu.VMEM((D, 3 * D), BF),
        pltpu.VMEM((D, D), BF),
        pltpu.VMEM((D, FF), BF),
        pltpu.VMEM((FF, D), BF),
        pltpu.SemaphoreType.DMA((40,)),
    ]
    outs = pl.pallas_call(
        partial(backward_kernel, step, last),
        out_shape=[jax.ShapeDtypeStruct((ROW, D), BF)]
        + [jax.ShapeDtypeStruct(shape, kind) for _, shape, kind in BACK],
        in_specs=[SMEM, VMEM, VMEM] + [ANY] * (6 + len(STATE)),
        out_specs=[ANY] * (1 + len(BACK)),
        scratch_shapes=scratch,
        name="layer_backward",
        compiler_params=pltpu.CompilerParams(vmem_limit_bytes=VMEM_LIMIT),
        cost_estimate=pl.CostEstimate(
            flops=2 * ROW * (12 * D * D), bytes_accessed=24 << 20, transcendentals=0
        ),
    )(section, biases, gains, cotangent, received, *weights, *state)
    return outs[0], outs[1:]


def two_rows(section, pieces, scratch, copies):
    shared, alone_first, alone_second = pieces
    one = copies.start(shared, scratch.at[0])
    two = pltpu.make_async_copy(alone_first, scratch.at[1], copies.sems.at[copies.used])
    copies.used += 1

    @pl.when(section == 0)
    def _():
        two.start()

    @pl.when(section != 0)
    def _():
        pltpu.make_async_copy(alone_second, scratch.at[1], two_sem(copies)).start()

    return (one, two)


def two_sem(copies):
    return copies.sems.at[copies.used - 1]


def both(ref, columns=slice(None)):
    wide = ref[:, :, columns]
    return wide.reshape(2 * ROW, wide.shape[-1])


def column_sums(values):
    return nn(jnp.ones((8, 2 * ROW), BF), values)[0:1, :]


def ffn_weight_kernel(*refs):
    info = refs[0]
    hidden, active, inner, down_side = (refs[1 + 3 * k : 4 + 3 * k] for k in range(4))
    up_o, down_o, bias_o = refs[13:16]
    hidden_v, active_v, inner_v, down_side_v, up_v, down_v, bias_v, sems = refs[16:]
    section = info[0]
    copies = Copies(sems)
    down_in = two_rows(section, down_side, down_side_v, copies)
    active_in = two_rows(section, active, active_v, copies)
    hidden_in = two_rows(section, hidden, hidden_v, copies)
    inner_in = two_rows(section, inner, inner_v, copies)
    leaving = []
    for copy in down_in + active_in:
        copy.wait()
    down_side_all = both(down_side_v)
    bias_v[:, FF:] = column_sums(down_side_all)
    for j in range(FFC):
        down_v[chunk(j)] = tn(both(active_v, chunk(j)), down_side_all).astype(BF)
        leaving.append(copies.start(down_v.at[chunk(j)], down_o.at[chunk(j)]))
    for copy in hidden_in + inner_in:
        copy.wait()
    hidden_all = both(hidden_v)
    for j in range(FFC):
        inner_part = both(inner_v, chunk(j))
        bias_v[:, chunk(j)] = column_sums(inner_part)
        up_v[:, chunk(j)] = tn(hidden_all, inner_part).astype(BF)
        leaving.append(copies.start(up_v.at[:, chunk(j)], up_o.at[:, chunk(j)]))
    leaving.append(copies.start(bias_v, bias_o))
    for copy in leaving:
        copy.wait()


def ffn_weight(section, hidden, active, inner, down_side):
    return pl.pallas_call(
        ffn_weight_kernel,
        out_shape=[
            jax.ShapeDtypeStruct((D, FF), BF),
            jax.ShapeDtypeStruct((FF, D), BF),
            jax.ShapeDtypeStruct((1, FF + D), F32),
        ],
        in_specs=[SMEM] + [ANY] * 12,
        out_specs=[ANY] * 3,
        scratch_shapes=[
            pltpu.VMEM((2, ROW, D), BF),
            pltpu.VMEM((2, ROW, FF), BF),
            pltpu.VMEM((2, ROW, FF), BF),
            pltpu.VMEM((2, ROW, D), BF),
            pltpu.VMEM((D, FF), BF),
            pltpu.VMEM((FF, D), BF),
            pltpu.VMEM((1, FF + D), F32),
            pltpu.SemaphoreType.DMA((24,)),
        ],
        name="ffn_weights",
        compiler_params=pltpu.CompilerParams(vmem_limit_bytes=VMEM_LIMIT),
        cost_estimate=pl.CostEstimate(
            flops=4 * ROW * (8 * D * D), bytes_accessed=24 << 20, transcendentals=0
        ),
    )(section, *hidden, *active, *inner, *down_side)


def attention_weight_kernel(*refs):
    info = refs[0]
    context, joined, attended, norms = (refs[1 + 3 * k : 4 + 3 * k] for k in range(4))
    inputs, received_one, received_two = refs[13:16]
    qkv_o, out_o, bias_o, norms_o = refs[16:20]
    tokens_v, context_v, joined_v, attended_v, norms_v, qkv_v, out_v, bias_v, sums_v, sems = refs[20:]
    section = info[0]
    copies = Copies(sems)
    attended_in = two_rows(section, attended, attended_v, copies)
    context_in = two_rows(section, context, context_v, copies)
    tokens_sems = [sems.at[copies.used], sems.at[copies.used + 1]]
    copies.used += 2

    @pl.when(section == 0)
    def _():
        pltpu.make_async_copy(inputs.at[1, 0], tokens_v.at[0], tokens_sems[0]).start()
        pltpu.make_async_copy(inputs.at[0, 0], tokens_v.at[1], tokens_sems[1]).start()

    @pl.when(section != 0)
    def _():
        pltpu.make_async_copy(received_one, tokens_v.at[0], tokens_sems[0]).start()
        pltpu.make_async_copy(received_two, tokens_v.at[1], tokens_sems[1]).start()

    tokens_in = (
        pltpu.make_async_copy(received_one, tokens_v.at[0], tokens_sems[0]),
        pltpu.make_async_copy(received_two, tokens_v.at[1], tokens_sems[1]),
    )
    joined_in = two_rows(section, joined, joined_v, copies)
    norms_in = two_rows(section, norms, norms_v, copies)
    leaving = []
    for copy in attended_in + context_in:
        copy.wait()
    attended_all = both(attended_v)
    bias_v[:, 2 * D :] = column_sums(attended_all)
    out_v[...] = tn(both(context_v), attended_all).astype(BF)
    leaving.append(copies.start(out_v, out_o))
    for copy in tokens_in + joined_in:
        copy.wait()
    tokens_all = both(tokens_v)
    for j in range(3):
        joined_part = both(joined_v, chunk(j))
        if j != 1:
            bias_v[:, chunk(j // 2)] = column_sums(joined_part)
        qkv_v[:, chunk(j)] = tn(tokens_all, joined_part).astype(BF)
        leaving.append(copies.start(qkv_v.at[:, chunk(j)], qkv_o.at[:, chunk(j)]))
    leaving.append(copies.start(bias_v, bias_o))
    for copy in norms_in:
        copy.wait()
    sums_v[...] = norms_v[0] + norms_v[1]
    leaving.append(copies.start(sums_v, norms_o))
    for copy in leaving:
        copy.wait()


def attention_weight(section, context, joined, attended, norms, tokens):
    return pl.pallas_call(
        attention_weight_kernel,
        out_shape=[
            jax.ShapeDtypeStruct((D, 3 * D), BF),
            jax.ShapeDtypeStruct((D, D), BF),
            jax.ShapeDtypeStruct((1, 3 * D), F32),
            jax.ShapeDtypeStruct((8, D), F32),
        ],
        in_specs=[SMEM] + [ANY] * 15,
        out_specs=[ANY] * 4,
        scratch_shapes=[
            pltpu.VMEM((2, ROW, D), BF),
            pltpu.VMEM((2, ROW, D), BF),
            pltpu.VMEM((2, ROW, 3 * D), BF),
            pltpu.VMEM((2, ROW, D), BF),
            pltpu.VMEM((2, 8, D), F32),
            pltpu.VMEM((D, 3 * D), BF),
            pltpu.VMEM((D, D), BF),
            pltpu.VMEM((1, 3 * D), F32),
            pltpu.VMEM((8, D), F32),
            pltpu.SemaphoreType.DMA((24,)),
        ],
        name="attention_weights",
        compiler_params=pltpu.CompilerParams(vmem_limit_bytes=VMEM_LIMIT),
        cost_estimate=pl.CostEstimate(
            flops=4 * ROW * (4 * D * D), bytes_accessed=16 << 20, transcendentals=0
        ),
    )(section, *context, *joined, *attended, *norms, *tokens)


def relay(value, steps):
    count = lax.axis_size("section")
    first, last = (max(0, -steps), min(count, count - steps))
    return lax.ppermute(
        value, "section", [(source, source + steps) for source in range(first, last)]
    )


def body(
    inputs,
    cotangent,
    lengths,
    qkv_weight,
    out_weight,
    up_weight,
    down_weight,
    biases,
    norm_gains,
    norm_shifts,
):
    shards = lax.axis_size("batch")
    width = D // shards
    bias_width = BIAS // shards
    place = lax.axis_index("section")
    section = place.astype(jnp.int32).reshape(1)
    first_section = place == 0
    gather = lambda value: lax.all_gather(value, "batch", axis=0, tiled=True)
    packed = jnp.concatenate([biases[0], norm_gains[0].reshape(-1), norm_shifts[0].reshape(-1)])
    small_all = gather(packed[None])
    weights = (
        gather(qkv_weight[0]),
        gather(out_weight[0]),
        gather(up_weight[0]),
        gather(down_weight[0]),
    )
    unpack = lambda start: (
        small_all[:, start : start + 2 * width]
        .reshape(shards, 2, width)
        .transpose(1, 0, 2)
        .reshape(2, D)
        .astype(F32)
    )
    small = (
        small_all[:, :bias_width].reshape(1, BIAS),
        unpack(bias_width),
        unpack(bias_width + 2 * width),
    )
    lengths = lengths[:, 0]
    micro_count = inputs.shape[0]
    last = micro_count
    received = inputs[0, 0]
    results, states, arrivals = [], [], []
    for step in range(last + 1):
        result, state = forward(
            step, last, section, lengths, small, inputs, received, weights
        )
        results.append(result)
        states.append(state)
        arrivals.append(received)
        if step < last:
            received = relay(result, 1)
    received = cotangent[0, 0]
    grads, backs = [], []
    for step in range(last + 1):
        grad, back = backward(
            step, last, section, small, cotangent, received, weights, states[last - step]
        )
        grads.append(grad)
        backs.append(back)
        if step < last:
            received = relay(grad, -1)
    rows = lambda key: (states[1][STATE_AT[key]], states[0][STATE_AT[key]], states[2][STATE_AT[key]])
    turns = lambda at: (backs[1][at], backs[2][at], backs[0][at])
    up_mat, down_mat, ffn_bias = ffn_weight(
        section, rows("hidden"), rows("active"), turns(1), turns(0)
    )
    qkv_mat, out_mat, attn_bias, norms = attention_weight(
        section,
        rows("context"),
        turns(3),
        turns(2),
        turns(4),
        (inputs, arrivals[1], arrivals[2]),
    )
    scatter = lambda value: lax.psum_scatter(value, "batch", scatter_dimension=0, tiled=True)
    bias_total = jnp.concatenate([attn_bias[0], ffn_bias[0]]).reshape(shards, bias_width)
    norm_total = norms[:4].reshape(4, shards, width).transpose(1, 0, 2).reshape(shards, 4 * width)
    small_total = jnp.concatenate([bias_total, norm_total], axis=1)
    up_sum = scatter(up_mat).astype(F32)[None]
    down_sum = scatter(down_mat).astype(F32)[None]
    qkv_sum = scatter(qkv_mat).astype(F32)[None]
    out_sum = scatter(out_mat).astype(F32)[None]
    small_sum = scatter(small_total)
    norm_sum = small_sum[:, bias_width:].reshape(1, 4, width)
    activations = jnp.stack(
        [jnp.where(first_section, results[m], results[m + 1]) for m in range(micro_count)]
    )[None, :, None]
    input_grads = jnp.stack(
        [
            jnp.where(first_section, grads[micro_count - m], grads[micro_count - 1 - m])
            for m in range(micro_count)
        ]
    )[None, :, None]
    return (
        activations,
        input_grads,
        qkv_sum,
        out_sum,
        up_sum,
        down_sum,
        small_sum[:, :bias_width],
        norm_sum[:, :2],
        norm_sum[:, 2:],
    )


def solution(mesh):
    in_specs = (
        P(None, "batch", None, None),
        P(None, "batch", None, None),
        P(None, "batch", None),
        P("section", "batch", None),
        P("section", "batch", None),
        P("section", "batch", None),
        P("section", "batch", None),
        P("section", "batch"),
        P("section", None, "batch"),
        P("section", None, "batch"),
    )
    out_specs = (
        P("section", None, "batch", None, None),
        P("section", None, "batch", None, None),
        P("section", "batch", None),
        P("section", "batch", None),
        P("section", "batch", None),
        P("section", "batch", None),
        P("section", "batch"),
        P("section", None, "batch"),
        P("section", None, "batch"),
    )
    return jax.shard_map(body, mesh=mesh, in_specs=in_specs, out_specs=out_specs, check_vma=False)
```

```python
from functools import partial

import jax
import jax.numpy as jnp
from jax import lax
from jax.experimental import pallas as pl
from jax.experimental.pallas import tpu as pltpu
from jax.sharding import PartitionSpec as P

D = 768
HEADS = 12
FF = 3072
HEAD_DIM = 64
ROW = 256
PAIRS = HEADS // 2
PAIR = 2 * HEAD_DIM
FFC = FF // D
BIAS = 6144
VMEM_LIMIT = 56 * 1024 * 1024

BF = jnp.bfloat16
F32 = jnp.float32
epsilon = 1e-12
masked_value = -1e30
inv_sqrt2 = 0.7071067811865476
inv_sqrt2pi = 0.3989422804014327


def nn(a, b):
    return jnp.dot(a, b, preferred_element_type=F32)


def nt(a, b):
    return lax.dot_general(a, b, (((1,), (1,)), ((), ())), preferred_element_type=F32)


def tn(a, b):
    return lax.dot_general(a, b, (((0,), (0,)), ((), ())), preferred_element_type=F32)


def head_masks():
    lane = lax.broadcasted_iota(jnp.int32, (1, PAIR), 1)
    low = (lane < HEAD_DIM).astype(F32)
    return (low.astype(BF), (1.0 - low).astype(BF))


def segment_penalty(lengths_ref, micro):
    first = lengths_ref[micro, 0]
    second = first + lengths_ref[micro, 1]
    third = second + lengths_ref[micro, 2]

    def number(axis):
        place = lax.broadcasted_iota(jnp.int32, (ROW, ROW), axis)
        one = jnp.where(place >= first, 1, 0)
        two = jnp.where(place >= second, 1, 0)
        return one + two + jnp.where(place >= third, 1, 0)

    return jnp.where(number(0) == number(1), 0.0, masked_value)


def standardize(values):
    centred = values - jnp.mean(values, axis=-1, keepdims=True)
    spread = jnp.mean(centred * centred, axis=-1, keepdims=True)
    scale = lax.rsqrt(spread + epsilon)
    return centred * scale, scale


def norm_back(grad, unit, scale, gain):
    scaled = grad * gain
    mean_one = jnp.mean(scaled, axis=-1, keepdims=True)
    mean_two = jnp.mean(scaled * unit, axis=-1, keepdims=True)
    return scale * (scaled - mean_one - unit * mean_two)


class Copies:
    def __init__(self, sems):
        self.sems = sems
        self.used = 0

    def start(self, src, dst):
        copy = pltpu.make_async_copy(src, dst, self.sems.at[self.used])
        self.used += 1
        copy.start()
        return copy


def chunk(index):
    return slice(index * D, (index + 1) * D)

ANY = pl.BlockSpec(memory_space=pl.ANY)
SMEM = pl.BlockSpec(memory_space=pltpu.SMEM)
VMEM = pl.BlockSpec(memory_space=pltpu.VMEM)
FIRST_WIDTH = 4 * D + 128
SMALL = 4 * D

SHAPES = {
    "qkv": ((ROW, 3 * D), BF),
    "probs": ((HEADS, ROW, ROW), BF),
    "context": ((ROW, D), BF),
    "hidden": ((ROW, D), BF),
    "unit1": ((ROW, D), F32),
    "scale1": ((ROW, 128), F32),
    "active": ((ROW, FF), BF),
    "slope": ((ROW, FF), BF),
    "result": ((ROW, D), BF),
    "unit2": ((ROW, D), F32),
    "scale2": ((ROW, 128), F32),
    "down_side": ((ROW, D), BF),
    "inner": ((ROW, FF), BF),
    "attended": ((ROW, D), BF),
    "sum1": ((ROW, D), F32),
    "ffn_sums": ((16, D), F32),
    "joined": ((ROW, 3 * D), BF),
    "attn_sums": ((8, D), F32),
    "grad": ((ROW, D), BF),
}
PIECES = {"first": (D, FIRST_WIDTH), "up": (D, FF), "down": (FF, D)}
PART_PIECE = {"attn": "first", "up": "up", "down": "down"}
MAKES = {
    "attn": ("qkv", "probs", "context", "unit1", "scale1", "hidden"),
    "up": ("active", "slope"),
    "down": ("result", "unit2", "scale2"),
}
TAKES = {"attn": (), "up": ("hidden",), "down": ("unit1", "active")}
BACK_MAKES = {
    "ffn": ("down_side", "inner", "attended", "sum1", "ffn_sums"),
    "attn": ("joined", "attn_sums", "grad"),
}
BACK_TAKES = {
    "ffn": ("unit2", "scale2", "slope", "unit1", "scale1"),
    "attn": ("qkv", "probs", "attended", "sum1"),
}
BACK_PIECES = {"ffn": ("down", "up"), "attn": ("first",)}


def struct(key):
    return jax.ShapeDtypeStruct(*SHAPES[key])


def buffer(key):
    return pltpu.VMEM(*SHAPES[key])


def flops_of(microseconds):
    return pl.CostEstimate(
        flops=int(microseconds * 1.1e9), bytes_accessed=1 << 20, transcendentals=0
    )


def call(kernel, outs, operands, specs, scratch, name, time):
    return pl.pallas_call(
        kernel,
        out_shape=outs,
        in_specs=specs,
        out_specs=[ANY] * len(outs),
        scratch_shapes=scratch,
        name=name,
        compiler_params=pltpu.CompilerParams(vmem_limit_bytes=VMEM_LIMIT),
        cost_estimate=flops_of(time),
    )(*operands)


class Reader:
    def __init__(self, refs):
        self.refs = list(refs)

    def take(self, count=None):
        if count is None:
            return self.refs.pop(0)
        taken, self.refs = self.refs[:count], self.refs[count:]
        return taken


def from_either(section, first, second, target, sem):
    if second is None or first is None:
        copy = pltpu.make_async_copy(second if first is None else first, target, sem)
        copy.start()
        return copy
    copy = pltpu.make_async_copy(first, target, sem)

    @pl.when(section == 0)
    def _():
        copy.start()

    @pl.when(section != 0)
    def _():
        pltpu.make_async_copy(second, target, sem).start()

    return copy


def column_parts(shape):
    return [(slice(None), chunk(j)) for j in range(shape[1] // D)]


def row_parts(shape):
    return [(chunk(j), slice(None)) for j in range(shape[0] // D)]


def forward_kernel(step, last, parts, groups, *refs):
    raw = groups > 0
    reader = Reader(refs)
    info, table, lengths, biases, gains, shifts = reader.take(6)
    inputs, received = (reader.take(2)) if "attn" in parts else (None, None)
    made = [key for part in parts for key in MAKES[part]]
    taken = [key for part in parts for key in TAKES[part] if key not in made]
    sources = dict(zip(taken, reader.take(len(taken))))
    pieces = [PART_PIECE[part] for part in parts]
    weight_in = {key: reader.take(2 * groups if raw else 1) for key in pieces}
    outs = dict(zip(made, reader.take(len(made))))
    weight_out = {key: reader.take() for key in pieces} if raw else {}
    kept = {key: reader.take() for key in made + taken}
    held = {key: reader.take() for key in pieces}
    tokens_v = reader.take() if "attn" in parts else None
    sum_v = reader.take() if "down" in parts else None
    sems, weight_sems = reader.take(2)
    section = info[0]
    copies = Copies(sems)
    weight_copies = Copies(weight_sems)
    weight_parts = {}
    whole_leaving = []
    if raw:
        for key in pieces:
            rows = PIECES[key][0] // (2 * groups)
            arriving = []
            for place, ref in enumerate(weight_in[key]):
                at = table[place // groups, place % groups] * rows
                target = held[key].at[pl.ds(pl.multiple_of(at, rows), rows)]
                arriving.append(weight_copies.start(ref, target))
            for copy in arriving:
                copy.wait()
            whole_leaving.append(weight_copies.start(held[key], weight_out[key]))

    def work():
        arriving = {key: copies.start(sources[key], kept[key]) for key in taken}
        if "attn" in parts:
            own = inputs.at[step, 0] if step < last else None
            other = received if step > 0 else None
            tokens_in = from_either(section, own, other, tokens_v, sems.at[copies.used])
            copies.used += 1
        for key in pieces:
            shape = PIECES[key]
            split = row_parts(shape) if key == "down" else column_parts(shape)
            weight_parts[key] = [
                None if raw else weight_copies.start(weight_in[key][0].at[part], held[key].at[part])
                for part in split
            ]

        def ready(key, j):
            if not raw:
                weight_parts[key][j].wait()

        def arrived(key):
            if key in arriving:
                arriving[key].wait()

        leaving = []

        def leave(key, part=None):
            src, dst = kept[key], outs[key]
            if part is not None:
                src, dst = src.at[part], dst.at[part]
            leaving.append(copies.start(src, dst))

        bias = lambda start, size: biases[:, start : start + size].astype(F32)
        if "attn" in parts:
            qkv, probs, context = kept["qkv"], kept["probs"], kept["context"]
            weight = held["first"]
            penalty = segment_penalty(lengths, jnp.where(section == 0, step, step - 1))
            tokens_in.wait()
            tokens = tokens_v[...]
            for j in range(3):
                ready("first", j)
                part = nn(tokens, weight[:, chunk(j)])
                if j != 1:
                    part = part + bias(0 if j == 0 else D, D)
                qkv[:, chunk(j)] = part.astype(BF)
            leave("qkv")
            masks = head_masks()
            for pair in range(PAIRS):
                at = pair * PAIR
                queries = qkv[:, at : at + PAIR]
                keys = qkv[:, D + at : D + at + PAIR]
                values = qkv[:, 2 * D + at : 2 * D + at + PAIR]
                total = None
                for half in range(2):
                    scores = nt(queries * masks[half], keys) * HEAD_DIM ** (-0.5) + penalty
                    raised = jnp.exp(scores - jnp.max(scores, axis=-1, keepdims=True))
                    share = raised * (1.0 / jnp.sum(raised, axis=-1, keepdims=True))
                    share = share.astype(BF)
                    probs[2 * pair + half] = share
                    term = nn(share, values * masks[half])
                    total = term if total is None else total + term
                context[:, at : at + PAIR] = total.astype(BF)
                leave("probs", slice(2 * pair, 2 * pair + 2))
            leave("context")
            ready("first", 3)
            attended = nn(context[...], weight[:, chunk(3)]) + bias(2 * D, D)
            unit, scale = standardize(tokens.astype(F32) + attended)
            kept["unit1"][...] = unit
            kept["scale1"][...] = jnp.broadcast_to(scale, (ROW, 128))
            leave("unit1")
            leave("scale1")
            kept["hidden"][...] = (unit * gains[0:1, :] + shifts[0:1, :]).astype(BF)
            leave("hidden")
        if "down" in parts:
            arrived("unit1")
            normed = kept["unit1"][...] * gains[0:1, :] + shifts[0:1, :]
            sum_v[...] = normed + bias(3 * D + FF, D)
        if "up" in parts:
            arrived("hidden")
        if "up" not in parts and "down" in parts:
            arrived("active")
        for j in range(FFC):
            if "up" in parts:
                ready("up", j)
                inner = nn(kept["hidden"][...], held["up"][:, chunk(j)])
                inner = inner + bias(3 * D + j * D, D)
                phi = 0.5 * (1.0 + lax.erf(inner * inv_sqrt2))
                kept["active"][:, chunk(j)] = (inner * phi).astype(BF)
                bell = jnp.exp(inner * inner * -0.5) * inv_sqrt2pi
                kept["slope"][:, chunk(j)] = (phi + inner * bell).astype(BF)
            if "down" in parts:
                ready("down", j)
                sum_v[...] += nn(kept["active"][:, chunk(j)], held["down"][chunk(j)])
        if "up" in parts:
            leave("active")
            leave("slope")
        if "down" in parts:
            unit, scale = standardize(sum_v[...])
            kept["result"][...] = (unit * gains[1:2, :] + shifts[1:2, :]).astype(BF)
            leave("result")
            kept["unit2"][...] = unit
            kept["scale2"][...] = jnp.broadcast_to(scale, (ROW, 128))
            leave("unit2")
            leave("scale2")
        for copy in leaving:
            copy.wait()

    if step == 0:
        pl.when(section == 0)(work)
    elif step == last:
        pl.when(section != 0)(work)
    else:
        work()
    for copy in whole_leaving:
        copy.wait()


def forward(step, last, parts, common, inputs, received, state, weights, groups=0):
    made = [key for part in parts for key in MAKES[part]]
    taken = [key for part in parts for key in TAKES[part] if key not in made]
    pieces = [PART_PIECE[part] for part in parts]
    outs = [struct(key) for key in made]
    if groups:
        outs += [jax.ShapeDtypeStruct(PIECES[key], BF) for key in pieces]
    scratch = [buffer(key) for key in made + taken]
    scratch += [pltpu.VMEM(PIECES[key], BF) for key in pieces]
    operands, specs = list(common), [SMEM, SMEM, SMEM, VMEM, VMEM, VMEM]
    if "attn" in parts:
        scratch.append(pltpu.VMEM((ROW, D), BF))
        operands += [inputs, received]
        specs += [ANY] * 2
    if "down" in parts:
        scratch.append(pltpu.VMEM((ROW, D), F32))
    scratch += [pltpu.SemaphoreType.DMA((32,)), pltpu.SemaphoreType.DMA((64,))]
    operands += [state[key] for key in taken]
    for key in pieces:
        operands += weights[key] if groups else [weights[key]]
    specs += [ANY] * (len(operands) - len(specs))
    found = call(
        partial(forward_kernel, step, last, parts, groups),
        outs,
        operands,
        specs,
        scratch,
        "forward_" + "_".join(parts),
        5 * len(parts),
    )
    state.update(zip(made, found))
    if groups:
        weights.update(zip(pieces, found[len(made) :]))
    return state


def backward_kernel(step, last, parts, *refs):
    reader = Reader(refs)
    info, gains = reader.take(2)
    cotangent, received = reader.take(2) if "ffn" in parts else (None, None)
    made = [key for part in parts for key in BACK_MAKES[part]]
    taken = [key for part in parts for key in BACK_TAKES[part] if key not in made]
    pieces = [key for part in parts for key in BACK_PIECES[part]]
    sources = dict(zip(taken, reader.take(len(taken))))
    weights = dict(zip(pieces, reader.take(len(pieces))))
    outs = dict(zip(made, reader.take(len(made))))
    kept = {key: reader.take() for key in made + taken}
    held = {key: reader.take() for key in pieces}
    grad_v, sum_v = reader.take(2) if "ffn" in parts else (None, None)
    (sems,) = reader.take(1)
    section = info[0]

    def work():
        copies = Copies(sems)
        if "ffn" in parts:
            own = received if step > 0 else None
            other = cotangent.at[last - 1 - step, 0] if step < last else None
            grad_in = from_either(section, own, other, grad_v, sems.at[0])
            copies.used += 1
        arriving = {}
        for part in parts:
            if part == "ffn":
                for key in ("unit2", "scale2"):
                    arriving[key] = copies.start(sources[key], kept[key])
                for j in range(FFC):
                    at = chunk(j)
                    arriving["down", j] = copies.start(weights["down"].at[at], held["down"].at[at])
                    arriving["slope", j] = copies.start(
                        sources["slope"].at[:, at], kept["slope"].at[:, at]
                    )
                    arriving["up", j] = copies.start(
                        weights["up"].at[:, at], held["up"].at[:, at]
                    )
                for key in ("unit1", "scale1"):
                    arriving[key] = copies.start(sources[key], kept[key])
            else:
                for key in ("attended", "sum1"):
                    if key in taken:
                        arriving[key] = copies.start(sources[key], kept[key])
                arriving["out"] = copies.start(
                    weights["first"].at[:, chunk(3)], held["first"].at[:, chunk(3)]
                )
                for key in ("qkv", "probs"):
                    arriving[key] = copies.start(sources[key], kept[key])
                joined_part = (slice(None), slice(0, 3 * D))
                arriving["first"] = copies.start(
                    weights["first"].at[joined_part], held["first"].at[joined_part]
                )

        def arrived(*key):
            key = key if len(key) > 1 else key[0]
            if key in arriving:
                arriving[key].wait()

        leaving = []

        def leave(key):
            leaving.append(copies.start(kept[key], outs[key]))

        if "ffn" in parts:
            sums = kept["ffn_sums"]
            grad_in.wait()
            arrived("unit2")
            arrived("scale2")
            grad = grad_v[...].astype(F32)
            unit = kept["unit2"][...]
            sums[1:2, :] = jnp.sum(grad * unit, axis=0, keepdims=True)
            sums[3:4, :] = jnp.sum(grad, axis=0, keepdims=True)
            grad = norm_back(grad, unit, kept["scale2"][:, 0:1], gains[1:2, :])
            sums[9:10, :] = jnp.sum(grad, axis=0, keepdims=True)
            kept["down_side"][...] = grad.astype(BF)
            leave("down_side")
            sum_v[...] = grad
            inner = kept["inner"]
            for j in range(FFC):
                arrived("down", j)
                through = nt(kept["down_side"][...], held["down"][chunk(j)])
                arrived("slope", j)
                through = through * kept["slope"][:, chunk(j)].astype(F32)
                sums[5 + j : 6 + j, :] = jnp.sum(through, axis=0, keepdims=True)
                inner[:, chunk(j)] = through.astype(BF)
                arrived("up", j)
                sum_v[...] += nt(inner[:, chunk(j)], held["up"][:, chunk(j)])
            leave("inner")
            grad = sum_v[...]
            arrived("unit1")
            arrived("scale1")
            unit = kept["unit1"][...]
            sums[0:1, :] = jnp.sum(grad * unit, axis=0, keepdims=True)
            sums[2:3, :] = jnp.sum(grad, axis=0, keepdims=True)
            grad = norm_back(grad, unit, kept["scale1"][:, 0:1], gains[0:1, :])
            sums[4:5, :] = jnp.sum(grad, axis=0, keepdims=True)
            sums[10:16, :] = jnp.zeros((6, D), F32)
            leave("ffn_sums")
            kept["sum1"][...] = grad
            kept["attended"][...] = grad.astype(BF)
            leave("attended")
            leave("sum1")
        if "attn" in parts:
            arrived("attended")
            arrived("out")
            context_grad = nt(kept["attended"][...], held["first"][:, chunk(3)]).astype(BF)
            arrived("qkv")
            arrived("probs")
            masks = head_masks()
            qkv, joined, sums = kept["qkv"], kept["joined"], kept["attn_sums"]
            sums[2:8, :] = jnp.zeros((6, D), F32)
            for pair in range(PAIRS):
                at = pair * PAIR
                queries = qkv[:, at : at + PAIR]
                keys = qkv[:, D + at : D + at + PAIR]
                values = qkv[:, 2 * D + at : 2 * D + at + PAIR]
                pair_grad = context_grad[:, at : at + PAIR]
                totals = [None, None, None]
                for half in range(2):
                    mask = masks[half]
                    share = kept["probs"][2 * pair + half]
                    own_grad = pair_grad * mask
                    prob_grad = nt(own_grad, values)
                    wide = share.astype(F32)
                    weighted = wide * prob_grad
                    inner_sum = jnp.sum(weighted, axis=-1, keepdims=True)
                    score_grad = (weighted - wide * inner_sum) * HEAD_DIM ** (-0.5)
                    score_grad = score_grad.astype(BF)
                    terms = (
                        nn(score_grad, keys * mask),
                        tn(score_grad, queries * mask),
                        tn(share, own_grad),
                    )
                    totals = [t if s is None else s + t for s, t in zip(totals, terms)]
                for which in range(3):
                    joined[:, which * D + at : which * D + at + PAIR] = totals[which].astype(BF)
                    if which != 1:
                        row = which // 2
                        sums[row : row + 1, at : at + PAIR] = jnp.sum(
                            totals[which], axis=0, keepdims=True
                        )
            leave("joined")
            leave("attn_sums")
            arrived("first")
            arrived("sum1")
            through = nt(joined[...], held["first"][:, : 3 * D])
            kept["grad"][...] = (kept["sum1"][...] + through).astype(BF)
            leave("grad")
        for copy in leaving:
            copy.wait()

    if step == 0:
        pl.when(section != 0)(work)
    elif step == last:
        pl.when(section == 0)(work)
    else:
        work()


def backward(step, last, parts, section, gains, cotangent, received, state, weights):
    made = [key for part in parts for key in BACK_MAKES[part]]
    taken = [key for part in parts for key in BACK_TAKES[part] if key not in made]
    pieces = [key for part in parts for key in BACK_PIECES[part]]
    scratch = [buffer(key) for key in made + taken]
    scratch += [pltpu.VMEM(PIECES[key], BF) for key in pieces]
    operands, specs = [section, gains], [SMEM, VMEM]
    if "ffn" in parts:
        operands += [cotangent, received]
        scratch += [pltpu.VMEM((ROW, D), BF), pltpu.VMEM((ROW, D), F32)]
    scratch.append(pltpu.SemaphoreType.DMA((40,)))
    operands += [state[key] for key in taken] + [weights[key] for key in pieces]
    specs += [ANY] * (len(operands) - len(specs))
    found = call(
        partial(backward_kernel, step, last, parts),
        [struct(key) for key in made],
        operands,
        specs,
        scratch,
        "backward_" + "_".join(parts),
        7 * len(parts),
    )
    state = dict(state)
    state.update(zip(made, found))
    return state


def both(ref, columns=slice(None)):
    wide = ref[:, :, columns]
    return wide.reshape(2 * ROW, wide.shape[-1])


def send_rows(copies, table, groups, whole, own, other):
    rows = whole.shape[0] // (2 * groups)
    leaving = []
    for side, target in enumerate((own, other)):
        for place in range(groups):
            at = pl.multiple_of(table[side, place] * rows, rows)
            leaving.append(copies.start(whole.at[pl.ds(at, rows)], target.at[place]))
    return leaving


def weight_kernel(piece, groups, *refs):
    reader = Reader(refs)
    info, table = reader.take(2)
    section = info[0]
    names = WEIGHT_TAKES[piece]
    sources = {key: reader.take(3) for key in names}
    if piece == "first":
        small, inputs, received_one, received_two = reader.take(4)
    own, other = reader.take(2)
    kept = {key: reader.take() for key in names}
    tokens_v = reader.take() if piece == "first" else None
    whole, sems = reader.take(2)
    copies = Copies(sems)
    arriving = {}
    if piece == "first":
        tokens_in = []
        for place, received in enumerate((received_one, received_two)):
            sem = sems.at[copies.used]
            copies.used += 1
            own_tokens = inputs.at[1 - place, 0]
            tokens_in.append(from_either(section, own_tokens, received, tokens_v.at[place], sem))
    for key in names:
        shared, first, second = sources[key]
        one = copies.start(shared, kept[key].at[0])
        sem = sems.at[copies.used]
        copies.used += 1
        arriving[key] = (one, from_either(section, first, second, kept[key].at[1], sem))
    for key in names:
        for copy in arriving[key]:
            copy.wait()
    if piece == "down":
        right = both(kept["down_side"])
        for j in range(FFC):
            whole[chunk(j)] = tn(both(kept["active"], chunk(j)), right).astype(BF)
    elif piece == "up":
        left = both(kept["hidden"])
        for j in range(FFC):
            whole[:, chunk(j)] = tn(left, both(kept["inner"], chunk(j))).astype(BF)
    else:
        whole[:, SMALL:] = small[...]
        whole[:, chunk(3)] = tn(both(kept["context"]), both(kept["attended"])).astype(BF)
        for copy in tokens_in:
            copy.wait()
        left = both(tokens_v)
        for j in range(3):
            whole[:, chunk(j)] = tn(left, both(kept["joined"], chunk(j))).astype(BF)
    for copy in send_rows(copies, table, groups, whole, own, other):
        copy.wait()


WEIGHT_TAKES = {
    "down": ("down_side", "active"),
    "up": ("hidden", "inner"),
    "first": ("attended", "context", "joined"),
}


def weight_grad(piece, groups, section, table, states, extra=()):
    names = WEIGHT_TAKES[piece]
    operands = [section, table] + [state[key] for key in names for state in states] + list(extra)
    specs = [SMEM, SMEM] + [ANY] * (3 * len(names))
    if extra:
        specs += [VMEM] + [ANY] * 3
    rows, columns = PIECES[piece]
    part = jax.ShapeDtypeStruct((groups, rows // (2 * groups), columns), BF)
    scratch = [pltpu.VMEM((2,) + SHAPES[key][0], SHAPES[key][1]) for key in names]
    if extra:
        scratch.append(pltpu.VMEM((2, ROW, D), BF))
    scratch += [pltpu.VMEM((rows, columns), BF), pltpu.SemaphoreType.DMA((32,))]
    return call(
        partial(weight_kernel, piece, groups),
        [part, part],
        operands,
        specs,
        scratch,
        "weight_" + piece,
        5,
    )


CORES = 2
RING = (0, -1, 1, -2, 2, -3, 3, 4)


def ring_device(place, core):
    place = place % len(RING)
    z, y = (place, 0) if place < 4 else (7 - place, 1)
    return (z * 2 + y) * 2 + core


def ring_places():
    return [(place, core) for place in range(len(RING)) for core in range(CORES)]


def ring_table():
    rows = {}
    for place, core in ring_places():
        rows[ring_device(place, core)] = [
            [ring_device(place + ahead, core ^ side) for ahead in RING] for side in range(CORES)
        ]
    return jnp.array([rows[device] for device in range(len(rows))], jnp.int32)


def around(value, steps):
    pairs = [(ring_device(p, c), ring_device(p + steps, c)) for p, c in ring_places()]
    return lax.ppermute(value, "batch", pairs)


def to_other_core(value):
    pairs = [(ring_device(p, c), ring_device(p, 1 - c)) for p, c in ring_places()]
    return lax.ppermute(value, "batch", pairs)


def after(value, *earlier):
    return lax.optimization_barrier((value,) + earlier)[0]


def ring_gather(first, up, down):
    one, two, three = {0: first}, {0: up}, {0: down}

    def step(held, index, forwards=True, backwards=True):
        if forwards:
            held[-index] = around(held[1 - index], 1)
        if backwards:
            held[index] = around(held[index - 1], -1)

    step(one, 1)
    step(two, 1)
    step(one, 2)
    step(two, 2)
    step(one, 3)
    three[0] = after(down, one[-2], one[2])
    step(two, 3)
    one[4] = around(one[-3], 1)
    step(three, 1)
    step(two, 4, forwards=False)
    step(three, 2)
    step(three, 3)
    half = down.shape[0] // 2
    three[4] = jnp.concatenate(
        [around(three[-3][:half], 1), around(three[3][half:], -1)], axis=0
    )
    found = []
    for held in (one, two, three):
        own = [held[ahead] for ahead in RING]
        found.append(own + [to_other_core(shard) for shard in own])
    return found


def add(*values):
    total = values[0].astype(F32)
    for value in values[1:]:
        total = total + value.astype(F32)
    return total


def ring_scatter(own, other, far):
    total = add(own, to_other_core(other)).astype(BF)
    part = lambda ahead: total[RING.index(ahead)]
    half = own.shape[1] // 2
    arrived = {}
    for way in (1, -1):
        if far == way:
            value = around(part(4), way)
        elif far == 0:
            value = around(part(4)[:half] if way == 1 else part(4)[half:], way)
        else:
            value = None
        for ahead in (3, 2, 1):
            mine = part(way * ahead)
            if value is None:
                value = mine
            elif value.shape == mine.shape:
                value = add(mine, value).astype(BF)
            elif way == 1:
                value = jnp.concatenate([add(mine[:half], value).astype(BF), mine[half:]], axis=0)
            else:
                value = jnp.concatenate([mine[:half], add(mine[half:], value).astype(BF)], axis=0)
            value = around(value, way)
        arrived[way] = value
    return add(part(0), arrived[1], arrived[-1])


def relay(value, steps):
    count = lax.axis_size("section")
    first, last = (max(0, -steps), min(count, count - steps))
    return lax.ppermute(
        value, "section", [(source, source + steps) for source in range(first, last)]
    )


def body(
    inputs,
    cotangent,
    lengths,
    qkv_weight,
    out_weight,
    up_weight,
    down_weight,
    biases,
    norm_gains,
    norm_shifts,
):
    shards = lax.axis_size("batch")
    ring = shards == CORES * len(RING)
    groups = len(RING) if ring else 1
    width = D // shards
    place = lax.axis_index("section")
    section = place.astype(jnp.int32).reshape(1)
    first_section = place == 0
    packed = [biases[0].reshape(width, 8), norm_gains[0].T, norm_shifts[0].T]
    packed = jnp.pad(jnp.concatenate(packed, axis=1), ((0, 0), (0, 128 - 12)))
    first = jnp.concatenate([qkv_weight[0], out_weight[0], packed], axis=1)
    if ring:
        table = ring_table()[lax.axis_index("batch")]
        gathered = ring_gather(first, up_weight[0], down_weight[0])
        weights = dict(zip(PIECES, gathered))
        rows = lambda shard: shard[:, SMALL : SMALL + 12]
        by_device = jnp.stack([rows(shard) for shard in weights["first"]])
        order = jnp.argsort(table.reshape(-1))
        small_all = by_device[order].reshape(D, 12)
    else:
        table = jnp.arange(CORES, dtype=jnp.int32).reshape(CORES, 1)
        weights = {}
        for key, value in zip(PIECES, (first, up_weight[0], down_weight[0])):
            whole = lax.all_gather(value, "batch", axis=0, tiled=True)
            weights[key] = jnp.split(whole, CORES, axis=0)
        small_all = jnp.concatenate([half[:, SMALL : SMALL + 12] for half in weights["first"]])
    bias_row = small_all[:, :8].reshape(1, BIAS)
    gains = small_all[:, 8:10].T.astype(F32)
    shifts = small_all[:, 10:12].T.astype(F32)
    common = (section, table, lengths[:, 0], bias_row, gains, shifts)
    micro_count = inputs.shape[0]
    last = micro_count
    received = inputs[0, 0]
    states, arrivals = [], []
    parts = ("attn", "up", "down")
    for step in range(last + 1):
        state = {}
        if step == 0:
            for part in parts:
                forward(step, last, (part,), common, inputs, received, state, weights, groups)
        else:
            forward(step, last, parts, common, inputs, received, state, weights)
        states.append(state)
        arrivals.append(received)
        if step < last:
            received = relay(state["result"], 1)
    received = cotangent[0, 0]
    backs = []
    for step in range(last + 1):
        state = states[last - step]
        for parts in (("ffn",), ("attn",)) if step == last else (("ffn", "attn"),):
            state = backward(
                step, last, parts, section, gains, cotangent, received, state, weights
            )
        backs.append(state)
        if step < last:
            received = relay(state["grad"], -1)
    turns = (backs[1], backs[2], backs[0])
    down_parts = weight_grad("down", groups, section, table, turns)
    up_parts = weight_grad("up", groups, section, table, turns)
    alone = lambda key: jnp.where(first_section, backs[2][key], backs[0][key])
    ffn_sums = backs[1]["ffn_sums"] + alone("ffn_sums")
    attn_sums = backs[1]["attn_sums"] + alone("attn_sums")
    bias_total = jnp.concatenate([attn_sums[:2], ffn_sums[4:10]]).reshape(D, 8)
    small_total = jnp.concatenate([bias_total, ffn_sums[:4].T], axis=1)
    small_total = jnp.pad(small_total, ((0, 0), (0, 128 - 12))).astype(BF)
    extra = (small_total, inputs, arrivals[1], arrivals[2])
    first_parts = weight_grad("first", groups, section, table, turns, extra)
    if ring:
        down_sum = ring_scatter(*down_parts, 0)
        up_sum = ring_scatter(*up_parts, 1)
        first_sum = ring_scatter(*first_parts, -1)
    else:
        scatter = lambda parts: lax.psum_scatter(
            jnp.concatenate([part[0] for part in parts]), "batch", scatter_dimension=0, tiled=True
        ).astype(F32)
        down_sum, up_sum, first_sum = map(scatter, (down_parts, up_parts, first_parts))
    norm_sum = first_sum[:, SMALL + 8 : SMALL + 12].T
    activations = jnp.stack(
        [
            jnp.where(first_section, states[m]["result"], states[m + 1]["result"])
            for m in range(micro_count)
        ]
    )
    input_grads = jnp.stack(
        [
            jnp.where(first_section, backs[last - m]["grad"], backs[last - 1 - m]["grad"])
            for m in range(micro_count)
        ]
    )
    return (
        activations[None, :, None],
        input_grads[None, :, None],
        first_sum[None, :, : 3 * D],
        first_sum[None, :, 3 * D : SMALL],
        up_sum[None],
        down_sum[None],
        first_sum[:, SMALL : SMALL + 8].reshape(1, -1),
        norm_sum[None, :2],
        norm_sum[None, 2:],
    )


def solution(mesh):
    in_specs = (
        P(None, "batch", None, None),
        P(None, "batch", None, None),
        P(None, "batch", None),
        P("section", "batch", None),
        P("section", "batch", None),
        P("section", "batch", None),
        P("section", "batch", None),
        P("section", "batch"),
        P("section", None, "batch"),
        P("section", None, "batch"),
    )
    out_specs = (
        P("section", None, "batch", None, None),
        P("section", None, "batch", None, None),
        P("section", "batch", None),
        P("section", "batch", None),
        P("section", "batch", None),
        P("section", "batch", None),
        P("section", "batch"),
        P("section", None, "batch"),
        P("section", None, "batch"),
    )
    return jax.shard_map(body, mesh=mesh, in_specs=in_specs, out_specs=out_specs, check_vma=False)
```

```python
from functools import partial

import jax
import jax.numpy as jnp
import numpy as np
from jax import lax
from jax.experimental import pallas as pl
from jax.experimental.pallas import tpu as pltpu
from jax.sharding import PartitionSpec as P

D = 768
HEADS = 12
FF = 3072
HEAD_DIM = 64
ROW = 256
PAIRS = HEADS // 2
PAIR = 2 * HEAD_DIM
FFC = FF // D
BIAS = 6144
VMEM_LIMIT = 16 * 1024 * 1024

BF = jnp.bfloat16
F32 = jnp.float32
epsilon = 1e-12
masked_value = -1e30
inv_sqrt2 = 0.7071067811865476
inv_sqrt2pi = 0.3989422804014327


def nn(a, b):
    return jnp.dot(a, b, preferred_element_type=F32)


def nt(a, b):
    return lax.dot_general(a, b, (((1,), (1,)), ((), ())), preferred_element_type=F32)


def tn(a, b):
    return lax.dot_general(a, b, (((0,), (0,)), ((), ())), preferred_element_type=F32)


def head_masks():
    lane = lax.broadcasted_iota(jnp.int32, (1, PAIR), 1)
    low = (lane < HEAD_DIM).astype(F32)
    return (low.astype(BF), (1.0 - low).astype(BF))


def segment_penalty(lengths_ref, micro):
    first = lengths_ref[micro, 0]
    second = first + lengths_ref[micro, 1]
    third = second + lengths_ref[micro, 2]

    def number(axis):
        place = lax.broadcasted_iota(jnp.int32, (ROW, ROW), axis)
        one = jnp.where(place >= first, 1, 0)
        two = jnp.where(place >= second, 1, 0)
        return one + two + jnp.where(place >= third, 1, 0)

    return jnp.where(number(0) == number(1), 0.0, masked_value)


def standardize(values):
    centred = values - jnp.mean(values, axis=-1, keepdims=True)
    spread = jnp.mean(centred * centred, axis=-1, keepdims=True)
    scale = lax.rsqrt(spread + epsilon)
    return centred * scale, scale


def norm_back(grad, unit, scale, gain):
    scaled = grad * gain
    mean_one = jnp.mean(scaled, axis=-1, keepdims=True)
    mean_two = jnp.mean(scaled * unit, axis=-1, keepdims=True)
    return scale * (scaled - mean_one - unit * mean_two)


class Copies:
    def __init__(self, sems):
        self.sems = sems
        self.used = 0

    def start(self, src, dst):
        copy = pltpu.make_async_copy(src, dst, self.sems.at[self.used])
        self.used += 1
        copy.start()
        return copy


class Reader:
    def __init__(self, refs):
        self.refs = list(refs)

    def take(self, count=None):
        if count is None:
            return self.refs.pop(0)
        taken, self.refs = self.refs[:count], self.refs[count:]
        return taken


def chunk(index, size=D):
    return slice(index * size, (index + 1) * size)


HBM = pl.BlockSpec(memory_space=pltpu.HBM)
SMEM = pl.BlockSpec(memory_space=pltpu.SMEM)
VMEM = pl.BlockSpec(memory_space=pltpu.VMEM)
LANES = 128
BLOCKS = 4
SMALL_ROWS = 16
BIAS_ROWS = BIAS // D

SHAPES = {
    "tokens": ((ROW, D), BF),
    "qkv": ((ROW, 3 * D), BF),
    "probs": ((HEADS, ROW, ROW), BF),
    "context": ((ROW, D), BF),
    "hidden": ((ROW, D), BF),
    "unit1": ((ROW, D), F32),
    "scale1": ((ROW, LANES), F32),
    "active": ((ROW, FF), BF),
    "slope": ((ROW, FF), BF),
    "unit2": ((ROW, D), F32),
    "scale2": ((ROW, LANES), F32),
    "down_side": ((ROW, D), BF),
    "inner": ((ROW, FF), BF),
    "attended": ((ROW, D), BF),
    "sum1": ((ROW, D), F32),
    "result": ((ROW, D), BF),
    "grad": ((ROW, D), BF),
    "ffn_sums": ((16, D), F32),
    "joined": ((ROW, 3 * D), BF),
    "attn_sums": ((8, D), F32),
}
PIECES = {"first": (BLOCKS, D, D), "up": (BLOCKS, D, D), "down": (FF, D)}
PART_PIECE = {"attn": "first", "up": "up", "down": "down"}
MAKES = {
    "attn": ("qkv", "probs", "unit1", "scale1"),
    "up": ("slope",),
    "down": ("unit2", "scale2", "result"),
}
STORES = {"attn": ("tokens", "context", "hidden"), "up": ("active",), "down": ()}
PASSES = {"attn": ("hidden",), "up": ("active",), "down": ()}
TAKES = {"attn": (), "up": ("hidden",), "down": ("unit1", "active")}
BACK_MAKES = {"ffn": ("ffn_sums",), "attn": ("attn_sums", "grad")}
BACK_STORES = {"ffn": ("down_side", "inner", "attended"), "attn": ("joined",)}
BACK_PASSES = {"ffn": ("attended", "sum1"), "attn": ()}
BACK_TAKES = {
    "ffn": ("unit2", "scale2", "slope", "unit1", "scale1"),
    "attn": ("qkv", "probs", "attended", "sum1"),
}
BACK_PIECES = {"ffn": ("down", "up"), "attn": ("first",)}


class Call:
    def __init__(self):
        self.operands, self.specs, self.in_names = [], [], []
        self.outs, self.out_specs, self.out_names = [], [], []
        self.scratch, self.scratch_names = [], []
        self.aliases = {}

    def give(self, name, value, spec):
        if spec is not SMEM:
            value = pltpu.with_memory_space_constraint(value, spec.memory_space)
        self.in_names.append(name)
        self.operands.append(value)
        self.specs.append(spec)

    def make(self, name, shape, kind, spec, old=None):
        if old is not None:
            self.aliases[len(self.operands)] = len(self.outs)
            self.give("old_" + name, old, spec)
        self.out_names.append(name)
        self.outs.append((pltpu.VMEM if spec is VMEM else pltpu.HBM)(shape, kind))
        self.out_specs.append(spec)

    def follow(self, values):
        for place, value in enumerate(values):
            self.give(("earlier", place), value, VMEM)

    def of_parts(self, parts, state, takes, makes, stores, passes):
        inside = [key for part in parts for key in passes[part] + makes[part]]
        for part in parts:
            for key in takes[part]:
                if key not in inside:
                    self.give(key, state[key], VMEM)
        for part in parts:
            for key in makes[part]:
                self.make(key, *SHAPES[key], VMEM, state.get(key))
            for key in stores[part]:
                self.make("store_" + key, *SHAPES[key], HBM, state.get("store_" + key))
                if key not in passes[part]:
                    self.hold(key, pltpu.VMEM(*SHAPES[key]))
            for key in passes[part]:
                if part == parts[-1]:
                    self.make(key, *SHAPES[key], VMEM)
                else:
                    self.hold(key, pltpu.VMEM(*SHAPES[key]))

    def hold(self, name, value):
        self.scratch_names.append(name)
        self.scratch.append(value)

    def run(self, kernel, name, time):
        names = self.in_names + self.out_names + self.scratch_names

        def named(*refs):
            kernel(dict(zip(names, refs)))

        found = pl.pallas_call(
            named,
            out_shape=self.outs,
            in_specs=self.specs,
            out_specs=self.out_specs,
            scratch_shapes=self.scratch,
            input_output_aliases=self.aliases,
            name=name,
            compiler_params=pltpu.CompilerParams(vmem_limit_bytes=VMEM_LIMIT),
            cost_estimate=pl.CostEstimate(
                flops=int(time * 1.1e9), bytes_accessed=1 << 20, transcendentals=0
            ),
        )(*self.operands)
        return dict(zip(self.out_names, found))


def rows_of(pieces, start, size):
    for piece in pieces:
        if start < piece.shape[0]:
            return piece.at[pl.ds(start, size)]
        start -= piece.shape[0]


def forward_kernel(origin, row, parts, shards, refs):
    get = refs.__getitem__
    small = get("small")
    bias = lambda index: small[index : index + 1, :]
    gain = lambda index: bias(BIAS_ROWS + index)
    shift = lambda index: bias(BIAS_ROWS + 2 + index)
    copies = Copies(get("sems"))
    section = get("section")[0]
    if shards is not None:
        table, rows = get("table"), D // len(shards)
        arriving = []
        for place, count in enumerate(shards):
            pieces = [get(("shard", place, index)) for index in range(count)]
            goes = table[place]
            for part in parts:
                if part == "down":
                    at = pl.multiple_of(goes * BLOCKS * rows, BLOCKS * rows)
                    source = rows_of(pieces, 0, BLOCKS * rows)
                    target = get("down").at[pl.ds(at, BLOCKS * rows)]
                    arriving.append(copies.start(source, target))
                    continue
                for j in range(BLOCKS):
                    at = pl.multiple_of(goes * rows, rows)
                    source = rows_of(pieces, (j + BLOCKS * (part == "up")) * rows, rows)
                    target = get(PART_PIECE[part]).at[j, pl.ds(at, rows)]
                    arriving.append(copies.start(source, target))
        for copy in arriving:
            copy.wait()

    @pl.when(section == origin)
    def _():
        leaving = []
        store = lambda key: leaving.append(copies.start(get(key), get("store_" + key)))
        if "attn" in parts:
            tokens = get("source")[row, 0] if origin == 0 else get("source")[...]
            get("tokens")[...] = tokens
            store("tokens")
            qkv, probs, context, weight = get("qkv"), get("probs"), get("context"), get("first")
            penalty = segment_penalty(get("lengths"), row)
            for j in range(3):
                part = nn(tokens, weight[j])
                if j != 1:
                    part = part + bias(j // 2)
                qkv[:, chunk(j)] = part.astype(BF)
            masks = head_masks()
            for pair in range(PAIRS):
                at = pair * PAIR
                queries = qkv[:, at : at + PAIR]
                keys = qkv[:, D + at : D + at + PAIR]
                values = qkv[:, 2 * D + at : 2 * D + at + PAIR]
                total = None
                for half in range(2):
                    scores = nt(queries * masks[half], keys) * HEAD_DIM ** (-0.5) + penalty
                    raised = jnp.exp(scores - jnp.max(scores, axis=-1, keepdims=True))
                    share = raised * (1.0 / jnp.sum(raised, axis=-1, keepdims=True))
                    share = share.astype(BF)
                    probs[2 * pair + half] = share
                    term = nn(share, values * masks[half])
                    total = term if total is None else total + term
                context[:, at : at + PAIR] = total.astype(BF)
            store("context")
            attended = nn(context[...], weight[3]) + bias(2)
            unit, scale = standardize(tokens.astype(F32) + attended)
            get("unit1")[...] = unit
            get("scale1")[...] = jnp.broadcast_to(scale, (ROW, LANES))
            get("hidden")[...] = (unit * gain(0) + shift(0)).astype(BF)
            store("hidden")
        if "up" in parts:
            hidden, active, slope = get("hidden"), get("active"), get("slope")
            for j in range(FFC):
                inner = nn(hidden[...], get("up")[j]) + bias(3 + j)
                phi = 0.5 * (1.0 + lax.erf(inner * inv_sqrt2))
                active[:, chunk(j)] = (inner * phi).astype(BF)
                bell = jnp.exp(inner * inner * -0.5) * inv_sqrt2pi
                slope[:, chunk(j)] = (phi + inner * bell).astype(BF)
            store("active")
        if "down" in parts:
            normed = get("unit1")[...] * gain(0) + shift(0)
            total = normed + bias(7) + nn(get("active")[...], get("down")[...])
            unit, scale = standardize(total)
            get("result")[...] = (unit * gain(1) + shift(1)).astype(BF)
            get("unit2")[...] = unit
            get("scale2")[...] = jnp.broadcast_to(scale, (ROW, LANES))
        for copy in leaving:
            copy.wait()

    if "mark" in refs:
        get("mark")[...] = jnp.zeros((8, LANES), F32)


def forward(origin, row, parts, common, small, source, state, weights, shards=None, earlier=()):
    section, table, lengths = common
    call = Call()
    call.follow(earlier)
    call.give("section", section, SMEM)
    call.give("small", small, VMEM)
    if "attn" in parts:
        call.give("lengths", lengths, SMEM)
        call.give("source", source, VMEM)
    for part in parts:
        key = PART_PIECE[part]
        if shards is None:
            call.give(key, weights[key], VMEM)
        else:
            call.make(key, PIECES[key], BF, VMEM)
    if shards is not None:
        call.give("table", table, SMEM)
        for place, shard in enumerate(shards):
            for index, piece in enumerate(shard):
                call.give(("shard", place, index), piece, HBM)
        call.make("mark", (8, LANES), F32, VMEM)
    call.of_parts(parts, state, TAKES, MAKES, STORES, PASSES)
    call.hold("sems", pltpu.SemaphoreType.DMA((80,)))
    found = call.run(
        partial(forward_kernel, origin, row, parts, shards and [len(shard) for shard in shards]),
        "forward_" + "_".join(parts),
        3 * len(parts),
    )
    weights.update((key, found.pop(key)) for key in PIECES if key in found)
    mark = found.pop("mark", None)
    state.update(found)
    return found.get("result"), mark


def backward_kernel(origin, row, parts, refs):
    get = refs.__getitem__
    small = get("small")
    gain = lambda index: small[BIAS_ROWS + index : BIAS_ROWS + index + 1, :]

    copies = Copies(get("sems"))

    @pl.when(get("section")[0] == origin)
    def _():
        leaving = []
        store = lambda key: leaving.append(copies.start(get(key), get("store_" + key)))
        if "ffn" in parts:
            grad = get("source")[row, 0] if origin == 1 else get("source")[...]
            sums, inner = get("ffn_sums"), get("inner")
            grad = grad.astype(F32)
            unit = get("unit2")[...]
            sums[1:2, :] = jnp.sum(grad * unit, axis=0, keepdims=True)
            sums[3:4, :] = jnp.sum(grad, axis=0, keepdims=True)
            grad = norm_back(grad, unit, get("scale2")[:, 0:1], gain(1))
            sums[9:10, :] = jnp.sum(grad, axis=0, keepdims=True)
            side = grad.astype(BF)
            get("down_side")[...] = side
            store("down_side")
            sum_v = get("sum_v")
            sum_v[...] = grad
            for j in range(FFC):
                through = nt(side, get("down")[chunk(j)])
                through = through * get("slope")[:, chunk(j)].astype(F32)
                sums[5 + j : 6 + j, :] = jnp.sum(through, axis=0, keepdims=True)
                inner[:, chunk(j)] = through.astype(BF)
            store("inner")
            grad = sum_v[...]
            for j in range(BLOCKS):
                grad = grad + nt(inner[:, chunk(j)], get("up")[j])
            unit = get("unit1")[...]
            sums[0:1, :] = jnp.sum(grad * unit, axis=0, keepdims=True)
            sums[2:3, :] = jnp.sum(grad, axis=0, keepdims=True)
            grad = norm_back(grad, unit, get("scale1")[:, 0:1], gain(0))
            sums[4:5, :] = jnp.sum(grad, axis=0, keepdims=True)
            sums[10:16, :] = jnp.zeros((6, D), F32)
            get("sum1")[...] = grad
            get("attended")[...] = grad.astype(BF)
            store("attended")
        if "attn" in parts:
            weight = get("first")
            context_grad = nt(get("attended")[...], weight[3]).astype(BF)
            masks = head_masks()
            qkv, joined, sums = get("qkv"), get("joined"), get("attn_sums")
            sums[2:8, :] = jnp.zeros((6, D), F32)
            for pair in range(PAIRS):
                at = pair * PAIR
                queries = qkv[:, at : at + PAIR]
                keys = qkv[:, D + at : D + at + PAIR]
                values = qkv[:, 2 * D + at : 2 * D + at + PAIR]
                pair_grad = context_grad[:, at : at + PAIR]
                totals = [None, None, None]
                for half in range(2):
                    mask = masks[half]
                    share = get("probs")[2 * pair + half]
                    own_grad = pair_grad * mask
                    prob_grad = nt(own_grad, values)
                    wide = share.astype(F32)
                    weighted = wide * prob_grad
                    inner_sum = jnp.sum(weighted, axis=-1, keepdims=True)
                    score_grad = (weighted - wide * inner_sum) * HEAD_DIM ** (-0.5)
                    score_grad = score_grad.astype(BF)
                    terms = (
                        nn(score_grad, keys * mask),
                        tn(score_grad, queries * mask),
                        tn(share, own_grad),
                    )
                    totals = [t if s is None else s + t for s, t in zip(totals, terms)]
                for which in range(3):
                    joined[:, which * D + at : which * D + at + PAIR] = totals[which].astype(BF)
                    if which != 1:
                        line = which // 2
                        sums[line : line + 1, at : at + PAIR] = jnp.sum(
                            totals[which], axis=0, keepdims=True
                        )
            store("joined")
            grad = get("sum1")[...]
            for j in range(3):
                grad = grad + nt(joined[:, chunk(j)], weight[j])
            get("grad")[...] = grad.astype(BF)
        for copy in leaving:
            copy.wait()


def backward(origin, row, parts, section, small, source, state, weights, earlier=()):
    call = Call()
    call.follow(earlier)
    call.give("section", section, SMEM)
    call.give("small", small, VMEM)
    for part in parts:
        for key in BACK_PIECES[part]:
            call.give(key, weights[key], VMEM)
    if "ffn" in parts:
        call.give("source", source, VMEM)
        call.hold("sum_v", pltpu.VMEM((ROW, D), F32))
    call.of_parts(parts, state, BACK_TAKES, BACK_MAKES, BACK_STORES, BACK_PASSES)
    call.hold("sems", pltpu.SemaphoreType.DMA((8,)))
    found = call.run(
        partial(backward_kernel, origin, row, parts), "backward_" + "_".join(parts), 5 * len(parts)
    )
    state.update(found)
    return found.get("grad")


WEIGHT_TAKES = {
    "down": ("active", "down_side"),
    "up": ("hidden", "inner"),
    "first": ("context", "attended", "tokens", "joined"),
}


def weight_kernel(piece, groups, refs):
    get = refs.__getitem__
    copies = Copies(get("sems"))
    table, held = get("table"), get("held")
    targets = (get("own"), get("other"))
    rows = D // (2 * groups)
    arriving = {}
    for key in WEIGHT_TAKES[piece]:
        for j in range(SHAPES[key][0][1] // D):
            arriving[key, j] = [
                copies.start(get((key, row)).at[:, chunk(j)], get(key).at[chunk(row, ROW), chunk(j)])
                for row in range(2)
            ]

    def both(key, j=0):
        for copy in arriving.pop((key, j), ()):
            copy.wait()
        return get(key)[:, chunk(j)]

    places = [(place // groups, place % groups) for place in range(2 * groups)]
    if piece == "down":
        right = both("down_side")
        for j in range(FFC):
            held[chunk(j)] = tn(both("active", j), right).astype(BF)
        for side, place in places:
            at = pl.multiple_of(table[side * groups + place] * BLOCKS * rows, BLOCKS * rows)
            targets[side][place] = held[pl.ds(at, BLOCKS * rows)]
        return
    names = WEIGHT_TAKES[piece]
    jobs = [(names[0], names[1], j, j) for j in range(BLOCKS)]
    if piece == "first":
        sums, row = get("sums"), get("row_sums")
        bias_rows = [get(("attn_sums", 0))[k : k + 1] + get(("attn_sums", 1))[k : k + 1] for k in range(2)]
        ffn = get(("ffn_sums", 0))[...] + get(("ffn_sums", 1))[...]
        bias_rows += [ffn[4 + k : 5 + k] for k in range(6)]
        row[...] = jnp.zeros((SMALL_ROWS, D), F32)
        row[1:5, :] = ffn[:4]
        if groups > 1:
            per_row = 2 * groups // BIAS_ROWS
            width = D // per_row
            for device in range(2 * groups):
                start = device % per_row * width
                row[0:1, :width] = bias_rows[device // per_row][:, start : start + width]
                sums[device] = row[...].astype(BF)
            for side, place in places:
                targets[side][place, BLOCKS * rows :] = sums[table[side * groups + place]]
        jobs = [("context", "attended", 0, 3)] + [("tokens", "joined", j, j) for j in range(3)]
    for left, right, j, block in jobs:
        held[:D] = tn(both(left), both(right, j)).astype(BF)
        for side, place in places:
            at = pl.multiple_of(table[side * groups + place] * rows, rows)
            targets[side][place, chunk(block, rows)] = held[pl.ds(at, rows)]


def weight_grad(piece, groups, table, states, earlier=()):
    call = Call()
    call.follow(earlier)
    call.give("table", table, SMEM)
    for key in WEIGHT_TAKES[piece]:
        for row, state in enumerate(states):
            call.give((key, row), state["store_" + key], HBM)
        shape, kind = SHAPES[key]
        call.hold(key, pltpu.VMEM((2 * ROW, shape[1]), kind))
    rows = BLOCKS * D // (2 * groups)
    if piece == "first":
        rows += SMALL_ROWS
        for key in ("attn_sums", "ffn_sums"):
            for row, state in enumerate(states):
                call.give((key, row), state[key], VMEM)
        call.hold("sums", pltpu.VMEM((2 * groups, SMALL_ROWS, D), BF))
        call.hold("row_sums", pltpu.VMEM((SMALL_ROWS, D), F32))
    for name in ("own", "other"):
        call.make(name, (groups, rows, D), BF, VMEM)
    call.hold("held", pltpu.VMEM((FF if piece == "down" else D, D), BF))
    call.hold("sems", pltpu.SemaphoreType.DMA((16,)))
    found = call.run(partial(weight_kernel, piece, groups), "weight_" + piece, 4)
    return found["own"], found["other"]


CORES = 2
RING = (0, -1, 1, -2, 2, -3, 3, 4)


def ring_device(place, core):
    place = place % len(RING)
    z, y = (place, 0) if place < 4 else (7 - place, 1)
    return (z * 2 + y) * 2 + core


def ring_places():
    return [(place, core) for place in range(len(RING)) for core in range(CORES)]


def ring_table():
    rows = {}
    for place, core in ring_places():
        rows[ring_device(place, core)] = [
            [ring_device(place + ahead, core ^ side) for ahead in RING] for side in range(CORES)
        ]
    return np.array([rows[device] for device in range(len(rows))], np.int32)


def around(value, steps):
    pairs = [(ring_device(p, c), ring_device(p + steps, c)) for p, c in ring_places()]
    return lax.ppermute(value, "batch", pairs)


def to_other_core(value):
    pairs = [(ring_device(p, c), ring_device(p, 1 - c)) for p, c in ring_places()]
    return lax.ppermute(value, "batch", pairs)


def after(value, *earlier):
    return lax.optimization_barrier((value,) + earlier)[0]


def pack_kernel(refs):
    get = refs.__getitem__
    attn, ffn, row = get("attn"), get("ffn"), get("row")
    rows = get("out").shape[0]
    for j in range(3):
        attn[chunk(j, rows)] = get("qkv")[:, chunk(j)]
    attn[chunk(3, rows)] = get("out")[...]
    row[...] = jnp.zeros((SMALL_ROWS, D), F32)
    row[0:1, : get("bias").shape[1]] = get("bias")[...].astype(F32)
    row[1:5, :] = get("norms")[...].astype(F32)
    attn[BLOCKS * rows :] = row[...].astype(BF)
    ffn[: BLOCKS * rows] = get("down")[...]
    for j in range(BLOCKS):
        ffn[(BLOCKS + j) * rows : (BLOCKS + j + 1) * rows] = get("up")[:, chunk(j)]


def pack(qkv, out, up, down, bias, norms):
    call = Call()
    for name, value in zip(
        ("qkv", "out", "up", "down", "bias", "norms"), (qkv, out, up, down, bias, norms)
    ):
        call.give(name, value, VMEM)
    rows = out.shape[0]
    call.make("attn", (BLOCKS * rows + SMALL_ROWS, D), BF, VMEM)
    call.make("ffn", (2 * BLOCKS * rows, D), BF, VMEM)
    call.hold("row", pltpu.VMEM((SMALL_ROWS, D), F32))
    found = call.run(pack_kernel, "pack", 1)
    return found["attn"], found["ffn"]


def ring_gather(own, cut):
    held = {0: own}
    for ahead in (1, 2, 3):
        held[-ahead] = around(held[1 - ahead], 1)
        held[ahead] = around(held[ahead - 1], -1)
    far = (around(held[-3][:cut], 1), around(held[3][cut:], -1))
    return [(held[ahead],) for ahead in RING[:-1]] + [far]


def both_cores(shards):
    return shards + [tuple(to_other_core(piece) for piece in shard) for shard in shards]


def total_kernel(count, cut, refs):
    get = refs.__getitem__
    total = get("total")
    start = 0
    for index in range(count):
        own, other = get(("own", index)), get(("other", index))
        size = own.shape[1]
        part = own[...].astype(F32) + other[...].astype(F32)
        total[:, start : start + size] = part.astype(BF)
        start += size
    far = total[RING.index(4)]
    get(1)[...] = far[:cut]
    get(-1)[...] = far[cut:]


def merge_kernel(ahead, cut, refs):
    get = refs.__getitem__
    for way in (1, -1):
        mine = get("total")[RING.index(way * ahead)].astype(F32)
        came, out = get(("came", way))[...].astype(F32), get(way)
        if ahead < 3:
            out[...] = (mine + came).astype(BF)
        elif way == 1:
            out[:cut] = (mine[:cut] + came).astype(BF)
            out[cut:] = mine[cut:].astype(BF)
        else:
            out[:cut] = mine[:cut].astype(BF)
            out[cut:] = (mine[cut:] + came).astype(BF)


def finish_kernel(piece, refs):
    get = refs.__getitem__
    total = get("total")[0].astype(F32)
    total = total + get(("came", 1))[...].astype(F32) + get(("came", -1))[...].astype(F32)
    if piece == "ffn":
        rows = get("up").shape[0]
        get("down")[...] = total[: BLOCKS * rows]
        for j in range(BLOCKS):
            get("up")[:, chunk(j)] = total[(BLOCKS + j) * rows : (BLOCKS + j + 1) * rows]
    else:
        rows = get("out").shape[0]
        for j in range(3):
            get("qkv")[:, chunk(j)] = total[chunk(j, rows)]
        get("out")[...] = total[chunk(3, rows)]
        get("small")[...] = total[BLOCKS * rows : BLOCKS * rows + 8]


class RingScatter:
    def __init__(self, piece, parts, cut):
        self.piece, self.cut = piece, cut
        call = Call()
        rows = sum(own.shape[1] for own, _ in parts)
        for index, (own, other) in enumerate(parts):
            call.give(("own", index), own, VMEM)
            call.give(("other", index), to_other_core(other), VMEM)
        call.make("total", (len(RING), rows, D), BF, VMEM)
        call.make(1, (cut, D), BF, VMEM)
        call.make(-1, (rows - cut, D), BF, VMEM)
        found = call.run(partial(total_kernel, len(parts), cut), "total_" + piece, 1)
        self.total, self.rows = found["total"], rows
        self.came = {way: around(found[way], way) for way in (1, -1)}

    def give(self, call):
        call.give("total", self.total, VMEM)
        for way in (1, -1):
            call.give(("came", way), self.came[way], VMEM)

    def step(self, ahead):
        call = Call()
        self.give(call)
        for way in (1, -1):
            call.make(way, (self.rows, D), BF, VMEM)
        found = call.run(partial(merge_kernel, ahead, self.cut), "merge_" + self.piece, 1)
        self.came = {way: around(found[way], way) for way in (1, -1)}

    def finish(self, shapes):
        call = Call()
        self.give(call)
        for name, shape in shapes.items():
            call.make(name, shape, F32, VMEM)
        return call.run(partial(finish_kernel, self.piece), "finish_" + self.piece, 1)


def relay(value, steps):
    count = lax.axis_size("section")
    first, last = (max(0, -steps), min(count, count - steps))
    return lax.ppermute(
        value, "section", [(source, source + steps) for source in range(first, last)]
    )


def body(
    inputs,
    cotangent,
    lengths,
    qkv_weight,
    out_weight,
    up_weight,
    down_weight,
    biases,
    norm_gains,
    norm_shifts,
):
    shards = lax.axis_size("batch")
    ring = shards == CORES * len(RING)
    groups = len(RING) if ring else 1
    width = D // shards
    cut = BIAS // shards
    device = lax.axis_index("batch")
    section = lax.axis_index("section").astype(jnp.int32).reshape(1)
    norms = jnp.concatenate([norm_gains[0], norm_shifts[0]])
    states, weights = ({}, {}), {}
    if ring:
        order = ring_table().reshape(shards, -1)
        back = np.argsort(order, axis=1).astype(np.int32)
        table = jnp.asarray(order)[device]
        spread = lax.dynamic_update_slice(jnp.zeros((4, D), BF), norms, (0, device * width))
        attn_own, ffn_own = pack(
            qkv_weight[0], out_weight[0], up_weight[0], down_weight[0], biases, spread
        )
        attn_shards = both_cores(ring_gather(attn_own, 2 * width))
        small = jnp.stack([shard[-1][-SMALL_ROWS : 8 - SMALL_ROWS] for shard in attn_shards])
        small = small.astype(F32)
        small = jnp.concatenate(
            [
                small[:, 0, :cut][jnp.asarray(back)[device]].reshape(BIAS_ROWS, D),
                jnp.sum(small[:, 1:5], axis=0),
                jnp.zeros((4, D), F32),
            ]
        )
    else:
        table = jnp.array([0, 1], jnp.int32)
        gather = lambda value: lax.all_gather(value, "batch", axis=0, tiled=True)
        halves = lambda value: jnp.split(gather(value), CORES)
        blocks = lambda half: [half[:, chunk(j)] for j in range(half.shape[1] // D)]
        attn_shards = [
            (jnp.concatenate(blocks(qkv) + [out]),)
            for qkv, out in zip(halves(qkv_weight[0]), halves(out_weight[0]))
        ]
        ffn_shards = [
            (jnp.concatenate([down] + blocks(up)),)
            for up, down in zip(halves(up_weight[0]), halves(down_weight[0]))
        ]
        packed = gather(jnp.concatenate([biases[0], norms.reshape(-1)])[None]).astype(F32)
        norms_all = packed[:, cut:].reshape(shards, 4, width).transpose(1, 0, 2)
        small = jnp.concatenate(
            [
                packed[:, :cut].reshape(BIAS_ROWS, D),
                norms_all.reshape(4, D),
                jnp.zeros((4, D), F32),
            ]
        )
    common = (section, table, lengths[:, 0])

    def run_forward(origin, row, source, parts=("attn", "up", "down"), shards=None, earlier=()):
        return forward(
            origin, row, parts, common, small, source, states[row], weights, shards, earlier
        )

    def run_backward(origin, row, source, parts=("ffn", "attn"), earlier=()):
        return backward(
            origin, row, parts, section, small, source, states[row], weights, earlier
        )

    mark = run_forward(0, 0, inputs, ("attn",), attn_shards)[1]
    if ring:
        ffn_shards = ring_gather(ffn_own, BLOCKS * width)
        far = tuple(after(piece, mark) for piece in ffn_shards[-1])
        ffn_shards = both_cores(ffn_shards[:-1] + [far])
    run_forward(0, 0, None, ("up",), ffn_shards)
    result = run_forward(0, 0, None, ("down",), ffn_shards)[0]
    coming = relay(result, 1)
    second = relay(run_forward(0, 1, inputs)[0], 1)
    run_forward(1, 0, coming)
    run_forward(1, 1, second, earlier=(states[0]["scale2"],))
    coming = relay(run_backward(1, 1, cotangent), -1)
    second = relay(run_backward(1, 0, cotangent, earlier=(states[1]["attn_sums"],)), -1)
    run_backward(0, 1, coming)
    run_backward(0, 0, second, ("ffn",), (states[1]["attn_sums"],))
    down_parts = weight_grad("down", groups, table, states)
    up_parts = weight_grad("up", groups, table, states, down_parts[1:])
    begun = ()
    if ring:
        ffn_ring = RingScatter("ffn", (down_parts, up_parts), BLOCKS * width)
        begun = (ffn_ring.total,)
    run_backward(0, 0, None, ("attn",), begun)
    if ring:
        ffn_ring.step(3)
        begun = (ffn_ring.came[1], ffn_ring.came[-1])
    attn_parts = weight_grad("first", groups, table, states, begun)
    if ring:
        attn_ring = RingScatter("attn", (attn_parts,), 2 * width)
        ffn_ring.step(2)
        attn_ring.step(3)
        ffn_ring.step(1)
        attn_ring.step(2)
        attn_ring.step(1)
        ffn = ffn_ring.finish({"down": (BLOCKS * width, D), "up": (width, FF)})
        attn = attn_ring.finish(
            {"qkv": (width, 3 * D), "out": (width, D), "small": (8, D)}
        )
        down_sum, up_sum, qkv_sum, out_sum = ffn["down"], ffn["up"], attn["qkv"], attn["out"]
        bias_sum = attn["small"][:1, :cut]
        norm_sum = lax.dynamic_slice(attn["small"], (1, device * width), (4, width))
    else:
        scatter = lambda value: lax.psum_scatter(
            value, "batch", scatter_dimension=0, tiled=True
        ).astype(F32)
        half = D // CORES
        join = lambda parts: jnp.concatenate(
            [
                jnp.concatenate([part[0, chunk(j, half)] for part in parts])
                for j in range(BLOCKS)
            ],
            axis=1,
        )
        down_sum = scatter(jnp.concatenate([part[0] for part in down_parts]))
        up_sum, attn_sum = scatter(join(up_parts)), scatter(join(attn_parts))
        qkv_sum, out_sum = attn_sum[:, : 3 * D], attn_sum[:, 3 * D :]
        ffn_sums = states[0]["ffn_sums"] + states[1]["ffn_sums"]
        attn_sums = states[0]["attn_sums"] + states[1]["attn_sums"]
        bias_total = jnp.concatenate([attn_sums[:2], ffn_sums[4:10]]).reshape(shards, cut)
        norm_rows = ffn_sums[:4].reshape(4, shards, width).transpose(1, 0, 2)
        small_sum = scatter(
            jnp.concatenate([bias_total, norm_rows.reshape(shards, 4 * width)], axis=1)
        )
        bias_sum = small_sum[:, :cut]
        norm_sum = small_sum[:, cut:].reshape(4, width)
    return (
        jnp.stack([state["result"] for state in states])[None, :, None],
        jnp.stack([state["grad"] for state in states])[None, :, None],
        qkv_sum[None],
        out_sum[None],
        up_sum[None],
        down_sum[None],
        bias_sum,
        norm_sum[None, :2],
        norm_sum[None, 2:],
    )


def solution(mesh):
    in_specs = (
        P(None, "batch", None, None),
        P(None, "batch", None, None),
        P(None, "batch", None),
        P("section", "batch", None),
        P("section", "batch", None),
        P("section", "batch", None),
        P("section", "batch", None),
        P("section", "batch"),
        P("section", None, "batch"),
        P("section", None, "batch"),
    )
    out_specs = (
        P("section", None, "batch", None, None),
        P("section", None, "batch", None, None),
        P("section", "batch", None),
        P("section", "batch", None),
        P("section", "batch", None),
        P("section", "batch", None),
        P("section", "batch"),
        P("section", None, "batch"),
        P("section", None, "batch"),
    )
    return jax.shard_map(body, mesh=mesh, in_specs=in_specs, out_specs=out_specs, check_vma=False)
```

```python
from functools import partial

import jax
import jax.numpy as jnp
import numpy as np
from jax import lax
from jax.experimental import pallas as pl
from jax.experimental.pallas import tpu as pltpu
from jax.sharding import PartitionSpec as P

D = 768
HEADS = 12
FF = 3072
HEAD_DIM = 64
ROW = 256
PAIRS = HEADS // 2
PAIR = 2 * HEAD_DIM
FFC = FF // D
BIAS = 6144
VMEM_LIMIT = 10 * 1024 * 1024

BF = jnp.bfloat16
F32 = jnp.float32
epsilon = 1e-12
masked_value = -1e30
inv_sqrt2 = 0.7071067811865476
inv_sqrt2pi = 0.3989422804014327


def nn(a, b):
    return jnp.dot(a, b, preferred_element_type=F32)


def nt(a, b):
    return lax.dot_general(a, b, (((1,), (1,)), ((), ())), preferred_element_type=F32)


def tn(a, b):
    return lax.dot_general(a, b, (((0,), (0,)), ((), ())), preferred_element_type=F32)


def head_masks():
    lane = lax.broadcasted_iota(jnp.int32, (1, PAIR), 1)
    low = (lane < HEAD_DIM).astype(F32)
    return (low.astype(BF), (1.0 - low).astype(BF))


def segment_penalty(lengths_ref, micro):
    first = lengths_ref[micro, 0]
    second = first + lengths_ref[micro, 1]
    third = second + lengths_ref[micro, 2]

    def number(axis):
        place = lax.broadcasted_iota(jnp.int32, (ROW, ROW), axis)
        one = jnp.where(place >= first, 1, 0)
        two = jnp.where(place >= second, 1, 0)
        return one + two + jnp.where(place >= third, 1, 0)

    return jnp.where(number(0) == number(1), 0.0, masked_value)


def standardize(values):
    centred = values - jnp.mean(values, axis=-1, keepdims=True)
    spread = jnp.mean(centred * centred, axis=-1, keepdims=True)
    scale = lax.rsqrt(spread + epsilon)
    return centred * scale, scale


def norm_back(grad, unit, scale, gain):
    scaled = grad * gain
    mean_one = jnp.mean(scaled, axis=-1, keepdims=True)
    mean_two = jnp.mean(scaled * unit, axis=-1, keepdims=True)
    return scale * (scaled - mean_one - unit * mean_two)


class Copies:
    def __init__(self, sems):
        self.sems = sems
        self.used = 0

    def start(self, src, dst):
        copy = pltpu.make_async_copy(src, dst, self.sems.at[self.used])
        self.used += 1
        copy.start()
        return copy


class Reader:
    def __init__(self, refs):
        self.refs = list(refs)

    def take(self, count=None):
        if count is None:
            return self.refs.pop(0)
        taken, self.refs = self.refs[:count], self.refs[count:]
        return taken


def chunk(index, size=D):
    return slice(index * size, (index + 1) * size)


HBM = pl.BlockSpec(memory_space=pltpu.HBM)
SMEM = pl.BlockSpec(memory_space=pltpu.SMEM)
VMEM = pl.BlockSpec(memory_space=pltpu.VMEM)
LANES = 128
BLOCKS = 4
SMALL_ROWS = 16
BIAS_ROWS = BIAS // D

SHAPES = {
    "tokens": ((ROW, D), BF),
    "qkv": ((ROW, 3 * D), BF),
    "probs": ((HEADS, ROW, ROW), BF),
    "context": ((ROW, D), BF),
    "hidden": ((ROW, D), BF),
    "unit1": ((ROW, D), F32),
    "scale1": ((ROW, LANES), F32),
    "active": ((ROW, FF), BF),
    "slope": ((ROW, FF), BF),
    "unit2": ((ROW, D), F32),
    "scale2": ((ROW, LANES), F32),
    "down_side": ((ROW, D), BF),
    "attended": ((ROW, D), BF),
    "sum1": ((ROW, D), F32),
    "result": ((ROW, D), BF),
    "grad": ((ROW, D), BF),
    "ffn_sums": ((16, D), F32),
    "attn_sums": ((8, D), F32),
}
PIECES = {"first": (BLOCKS, D, D), "up": (BLOCKS, D, D), "down": (FF, D)}
PART_PIECE = {"attn": "first", "up": "up", "down": "down"}
MAKES = {
    "attn": ("tokens", "qkv", "probs", "context", "unit1", "scale1", "hidden"),
    "up": ("active", "slope"),
    "down": ("unit2", "scale2", "result"),
}
TAKES = {"attn": (), "up": ("hidden",), "down": ("unit1", "active")}
BACK_MAKES = {
    "ffn": ("down_side", "slope", "attended", "ffn_sums"),
    "attn": ("qkv", "attn_sums", "grad"),
}
BACK_PASSES = {"ffn": ("sum1",), "attn": ()}
BACK_TAKES = {
    "ffn": ("unit2", "scale2", "unit1", "scale1"),
    "attn": ("probs", "attended", "sum1"),
}
BACK_PIECES = {"ffn": ("down", "up"), "attn": ("first",)}


class Call:
    def __init__(self):
        self.operands, self.specs, self.in_names = [], [], []
        self.outs, self.out_specs, self.out_names = [], [], []
        self.scratch, self.scratch_names = [], []
        self.aliases = {}

    def give(self, name, value, spec):
        if spec is not SMEM:
            value = pltpu.with_memory_space_constraint(value, spec.memory_space)
        self.in_names.append(name)
        self.operands.append(value)
        self.specs.append(spec)

    def make(self, name, shape, kind, spec, old=None):
        if old is not None:
            self.aliases[len(self.operands)] = len(self.outs)
            self.give("old_" + name, old, spec)
        self.out_names.append(name)
        self.outs.append((pltpu.VMEM if spec is VMEM else pltpu.HBM)(shape, kind))
        self.out_specs.append(spec)

    def follow(self, values):
        for place, value in enumerate(values):
            self.give(("earlier", place), value, VMEM)

    def of_parts(self, parts, state, takes, makes, passes=None):
        inside = [key for part in parts for key in makes[part]]
        inside += [key for part in parts for key in (passes[part] if passes else ())]
        for part in parts:
            for key in takes[part]:
                if key not in inside:
                    self.give(key, state[key], VMEM)
        for part in parts:
            for key in makes[part]:
                self.make(key, *SHAPES[key], VMEM, state.get(key))
            for key in passes[part] if passes else ():
                if part == parts[-1]:
                    self.make(key, *SHAPES[key], VMEM)
                else:
                    self.hold(key, pltpu.VMEM(*SHAPES[key]))

    def hold(self, name, value):
        self.scratch_names.append(name)
        self.scratch.append(value)

    def run(self, kernel, name, time):
        names = self.in_names + self.out_names + self.scratch_names

        def named(*refs):
            kernel(dict(zip(names, refs)))

        found = pl.pallas_call(
            named,
            out_shape=self.outs,
            in_specs=self.specs,
            out_specs=self.out_specs,
            scratch_shapes=self.scratch,
            input_output_aliases=self.aliases,
            name=name,
            compiler_params=pltpu.CompilerParams(vmem_limit_bytes=VMEM_LIMIT),
            cost_estimate=pl.CostEstimate(
                flops=int(time * 1.1e9), bytes_accessed=1 << 20, transcendentals=0
            ),
        )(*self.operands)
        return dict(zip(self.out_names, found))


def rows_of(pieces, start, size):
    for piece in pieces:
        if start < piece.shape[0]:
            return piece[start : start + size]
        start -= piece.shape[0]


STREAMS = {
    "one": [("first", j) for j in range(BLOCKS)] + [("small", 0), ("down", 0)],
    "two": [("down", 1)] + [("up", j) for j in range(BLOCKS)],
}
FAR_CUT = {"one": 3, "two": 3}


def stream_sizes(stream, rows):
    size = {"first": rows, "up": rows, "small": SMALL_ROWS, "down": 2 * rows}
    return [size[name] for name, _ in STREAMS[stream]]


def place_kernel(plan, refs):
    get = refs.__getitem__
    stream, devices, own, swapped = plan
    table = get("table")
    rows = D // devices
    small = refs.get("small")
    if small is not None and "old_small" not in refs:
        small[...] = jnp.zeros(small.shape, F32)

    def put(place, pieces):
        device = table[place]
        start = 0
        for (name, block), size in zip(STREAMS[stream], stream_sizes(stream, rows)):
            part = rows_of(pieces, start, size)
            start += size
            if name == "down":
                at = pl.multiple_of(device * BLOCKS * rows + block * size, size)
                get("down")[pl.ds(at, size)] = part
            elif name != "small":
                get(name)[block, pl.ds(pl.multiple_of(device * rows, rows), rows)] = part
            elif small is not None:
                more = part.astype(F32)
                width = BIAS // devices
                per_row = D // width
                line = lax.broadcasted_iota(jnp.int32, (BIAS_ROWS, D), 0)
                lane_part = lax.broadcasted_iota(jnp.int32, (BIAS_ROWS, D), 1) // width
                mine = (line == device // per_row) & (lane_part == device % per_row)
                bias = jnp.concatenate([more[0:1, :width]] * per_row, axis=1)
                small[:BIAS_ROWS] += jnp.where(mine, bias, 0.0)
                small[BIAS_ROWS : BIAS_ROWS + 4] += more[1:5]

    for index, (place, count) in enumerate(own):
        pieces = [get(("shard", index, part)) for part in range(count)]
        put(place, pieces)
        if "packed" in refs:
            start = 0
            for piece in pieces:
                stop = start + piece.shape[0]
                get("packed")[index, start:stop] = piece[...]
                start = stop
    for index, place in enumerate(swapped):
        put(place, [get("came").at[index]])


def place_shards(
    stream, table, own, weights, came=None, swapped=(), small=False, earlier=(), pack=False
):
    call = Call()
    call.follow(earlier)
    call.give("table", table, SMEM)
    rows = sum(stream_sizes(stream, D // table.shape[0]))
    for index, (place, shard) in enumerate(own):
        for part, piece in enumerate(shard):
            call.give(("shard", index, part), piece, VMEM)
    if came is not None:
        call.give("came", came, VMEM)
    for key in ("first", "down") if stream == "one" else ("up", "down"):
        call.make(key, PIECES[key], BF, VMEM, weights.get(key))
    if small:
        call.make("small", (SMALL_ROWS, D), F32, VMEM, weights.get("small"))
    if pack:
        call.make("packed", (len(own), rows, D), BF, VMEM)
    counts = [(place, len(shard)) for place, shard in own]
    plan = (stream, table.shape[0], counts, swapped)
    found = call.run(partial(place_kernel, plan), "place_" + stream, 0.5)
    for key in ("first", "up", "down", "small"):
        if key in found:
            weights[key] = found[key]
    return found


def forward_kernel(origin, row, parts, refs):
    get = refs.__getitem__
    small = get("small")
    bias = lambda index: small[index : index + 1, :]
    gain = lambda index: bias(BIAS_ROWS + index)
    shift = lambda index: bias(BIAS_ROWS + 2 + index)
    section = get("section")[0]
    @pl.when(section == origin)
    def _():
        if "attn" in parts:
            tokens = get("source")[row, 0] if origin == 0 else get("source")[...]
            get("tokens")[...] = tokens
            qkv, probs, context, weight = get("qkv"), get("probs"), get("context"), get("first")
            penalty = segment_penalty(get("lengths"), row)
            for j in range(3):
                part = nn(tokens, weight[j])
                if j != 1:
                    part = part + bias(j // 2)
                qkv[:, chunk(j)] = part.astype(BF)
            masks = head_masks()
            for pair in range(PAIRS):
                at = pair * PAIR
                queries = qkv[:, at : at + PAIR]
                keys = qkv[:, D + at : D + at + PAIR]
                values = qkv[:, 2 * D + at : 2 * D + at + PAIR]
                total = None
                for half in range(2):
                    scores = nt(queries * masks[half], keys) * HEAD_DIM ** (-0.5) + penalty
                    raised = jnp.exp(scores - jnp.max(scores, axis=-1, keepdims=True))
                    share = raised * (1.0 / jnp.sum(raised, axis=-1, keepdims=True))
                    share = share.astype(BF)
                    probs[2 * pair + half] = share
                    term = nn(share, values * masks[half])
                    total = term if total is None else total + term
                context[:, at : at + PAIR] = total.astype(BF)
            attended = nn(context[...], weight[3]) + bias(2)
            unit, scale = standardize(tokens.astype(F32) + attended)
            get("unit1")[...] = unit
            get("scale1")[...] = jnp.broadcast_to(scale, (ROW, LANES))
            get("hidden")[...] = (unit * gain(0) + shift(0)).astype(BF)
        if "up" in parts:
            hidden, active, slope = get("hidden"), get("active"), get("slope")
            for j in range(FFC):
                inner = nn(hidden[...], get("up")[j]) + bias(3 + j)
                phi = 0.5 * (1.0 + lax.erf(inner * inv_sqrt2))
                active[:, chunk(j)] = (inner * phi).astype(BF)
                bell = jnp.exp(inner * inner * -0.5) * inv_sqrt2pi
                slope[:, chunk(j)] = (phi + inner * bell).astype(BF)
        if "down" in parts:
            normed = get("unit1")[...] * gain(0) + shift(0)
            total = normed + bias(7) + nn(get("active")[...], get("down")[...])
            unit, scale = standardize(total)
            get("result")[...] = (unit * gain(1) + shift(1)).astype(BF)
            get("unit2")[...] = unit
            get("scale2")[...] = jnp.broadcast_to(scale, (ROW, LANES))

    if "mark" in refs:
        get("mark")[...] = jnp.zeros((8, LANES), F32)


def forward(origin, row, parts, common, small, source, state, weights, marked=False, earlier=()):
    section, lengths = common
    call = Call()
    call.follow(earlier)
    call.give("section", section, SMEM)
    call.give("small", small, VMEM)
    if "attn" in parts:
        call.give("lengths", lengths, SMEM)
        call.give("source", source, VMEM)
    for part in parts:
        key = PART_PIECE[part]
        call.give(key, weights[key], VMEM)
    if marked:
        call.make("mark", (8, LANES), F32, VMEM)
    call.of_parts(parts, state, TAKES, MAKES)
    found = call.run(
        partial(forward_kernel, origin, row, parts), "forward_" + "_".join(parts), 3 * len(parts)
    )
    mark = found.pop("mark", None)
    state.update(found)
    return mark if marked else found.get("result")


def backward_kernel(origin, row, parts, refs):
    get = refs.__getitem__
    small = get("small")
    gain = lambda index: small[BIAS_ROWS + index : BIAS_ROWS + index + 1, :]

    @pl.when(get("section")[0] == origin)
    def _():
        if "ffn" in parts:
            grad = get("source")[row, 0] if origin == 1 else get("source")[...]
            sums, inner = get("ffn_sums"), get("slope")
            grad = grad.astype(F32)
            unit = get("unit2")[...]
            sums[1:2, :] = jnp.sum(grad * unit, axis=0, keepdims=True)
            sums[3:4, :] = jnp.sum(grad, axis=0, keepdims=True)
            grad = norm_back(grad, unit, get("scale2")[:, 0:1], gain(1))
            sums[9:10, :] = jnp.sum(grad, axis=0, keepdims=True)
            side = grad.astype(BF)
            get("down_side")[...] = side
            sum_v = get("sum_v")
            sum_v[...] = grad
            for j in range(FFC):
                through = nt(side, get("down")[chunk(j)])
                through = through * inner[:, chunk(j)].astype(F32)
                sums[5 + j : 6 + j, :] = jnp.sum(through, axis=0, keepdims=True)
                inner[:, chunk(j)] = through.astype(BF)
            grad = sum_v[...]
            for j in range(BLOCKS):
                grad = grad + nt(inner[:, chunk(j)], get("up")[j])
            unit = get("unit1")[...]
            sums[0:1, :] = jnp.sum(grad * unit, axis=0, keepdims=True)
            sums[2:3, :] = jnp.sum(grad, axis=0, keepdims=True)
            grad = norm_back(grad, unit, get("scale1")[:, 0:1], gain(0))
            sums[4:5, :] = jnp.sum(grad, axis=0, keepdims=True)
            sums[10:16, :] = jnp.zeros((6, D), F32)
            get("sum1")[...] = grad
            get("attended")[...] = grad.astype(BF)
        if "attn" in parts:
            weight = get("first")
            context_grad = nt(get("attended")[...], weight[3]).astype(BF)
            masks = head_masks()
            qkv, sums = get("qkv"), get("attn_sums")
            sums[2:8, :] = jnp.zeros((6, D), F32)
            for pair in range(PAIRS):
                at = pair * PAIR
                queries = qkv[:, at : at + PAIR]
                keys = qkv[:, D + at : D + at + PAIR]
                values = qkv[:, 2 * D + at : 2 * D + at + PAIR]
                pair_grad = context_grad[:, at : at + PAIR]
                totals = [None, None, None]
                for half in range(2):
                    mask = masks[half]
                    share = get("probs")[2 * pair + half]
                    own_grad = pair_grad * mask
                    prob_grad = nt(own_grad, values)
                    wide = share.astype(F32)
                    weighted = wide * prob_grad
                    inner_sum = jnp.sum(weighted, axis=-1, keepdims=True)
                    score_grad = (weighted - wide * inner_sum) * HEAD_DIM ** (-0.5)
                    score_grad = score_grad.astype(BF)
                    terms = (
                        nn(score_grad, keys * mask),
                        tn(score_grad, queries * mask),
                        tn(share, own_grad),
                    )
                    totals = [t if s is None else s + t for s, t in zip(totals, terms)]
                for which in range(3):
                    qkv[:, which * D + at : which * D + at + PAIR] = totals[which].astype(BF)
                    if which != 1:
                        line = which // 2
                        sums[line : line + 1, at : at + PAIR] = jnp.sum(
                            totals[which], axis=0, keepdims=True
                        )
            grad = get("sum1")[...]
            for j in range(3):
                grad = grad + nt(qkv[:, chunk(j)], weight[j])
            get("grad")[...] = grad.astype(BF)


def backward(origin, row, parts, section, small, source, state, weights, earlier=()):
    call = Call()
    call.follow(earlier)
    call.give("section", section, SMEM)
    call.give("small", small, VMEM)
    for part in parts:
        for key in BACK_PIECES[part]:
            call.give(key, weights[key], VMEM)
    if "ffn" in parts:
        call.give("source", source, VMEM)
        call.hold("sum_v", pltpu.VMEM((ROW, D), F32))
    call.of_parts(parts, state, BACK_TAKES, BACK_MAKES, BACK_PASSES)
    found = call.run(
        partial(backward_kernel, origin, row, parts), "backward_" + "_".join(parts), 5 * len(parts)
    )
    state.update(found)
    return found.get("grad")


WEIGHT_TAKES = {
    "down": ("active", "down_side"),
    "up": ("hidden", "slope"),
    "first": ("context", "attended", "tokens", "qkv"),
}


def weight_kernel(piece, groups, refs):
    get = refs.__getitem__
    table, held = get("table"), get("held")
    targets = (get("own"), get("other"))
    rows = D // (2 * groups)

    def both(key, j=0):
        return jnp.concatenate([get((key, row))[:, chunk(j)] for row in range(2)], axis=0)

    places = [(place // groups, place % groups) for place in range(2 * groups)]
    if piece == "down":
        right = both("down_side")
        for j in range(FFC):
            held[chunk(j)] = tn(both("active", j), right).astype(BF)
        for side, place in places:
            at = pl.multiple_of(table[side * groups + place] * BLOCKS * rows, BLOCKS * rows)
            targets[side][place] = held[pl.ds(at, BLOCKS * rows)]
        return
    names = WEIGHT_TAKES[piece]
    jobs = [(names[0], names[1], j, j) for j in range(BLOCKS)]
    if piece == "first":
        sums, row = get("sums"), get("row_sums")
        bias_rows = [get(("attn_sums", 0))[k : k + 1] + get(("attn_sums", 1))[k : k + 1] for k in range(2)]
        ffn = get(("ffn_sums", 0))[...] + get(("ffn_sums", 1))[...]
        bias_rows += [ffn[4 + k : 5 + k] for k in range(6)]
        row[...] = jnp.zeros((SMALL_ROWS, D), F32)
        row[1:5, :] = ffn[:4]
        if groups > 1:
            per_row = 2 * groups // BIAS_ROWS
            width = D // per_row
            for device in range(2 * groups):
                start = device % per_row * width
                row[0:1, :width] = bias_rows[device // per_row][:, start : start + width]
                sums[device] = row[...].astype(BF)
            for side, place in places:
                targets[side][place, BLOCKS * rows :] = sums[table[side * groups + place]]
        jobs = [("context", "attended", 0, 3)] + [("tokens", "qkv", j, j) for j in range(3)]
    for left, right, j, block in jobs:
        held[:D] = tn(both(left), both(right, j)).astype(BF)
        for side, place in places:
            at = pl.multiple_of(table[side * groups + place] * rows, rows)
            targets[side][place, chunk(block, rows)] = held[pl.ds(at, rows)]


def weight_grad(piece, groups, table, states, earlier=()):
    call = Call()
    call.follow(earlier)
    call.give("table", table, SMEM)
    for key in WEIGHT_TAKES[piece]:
        for row, state in enumerate(states):
            call.give((key, row), state[key], VMEM)
    rows = BLOCKS * D // (2 * groups)
    if piece == "first":
        rows += SMALL_ROWS
        for key in ("attn_sums", "ffn_sums"):
            for row, state in enumerate(states):
                call.give((key, row), state[key], VMEM)
        call.hold("sums", pltpu.VMEM((2 * groups, SMALL_ROWS, D), BF))
        call.hold("row_sums", pltpu.VMEM((SMALL_ROWS, D), F32))
    for name in ("own", "other"):
        call.make(name, (groups, rows, D), BF, VMEM)
    call.hold("held", pltpu.VMEM((FF if piece == "down" else D, D), BF))
    found = call.run(partial(weight_kernel, piece, groups), "weight_" + piece, 4)
    return found["own"], found["other"]


CORES = 2
RING = (0, -1, 1, -2, 2, -3, 3, 4)


def ring_device(place, core):
    place = place % len(RING)
    z, y = (place, 0) if place < 4 else (7 - place, 1)
    return (z * 2 + y) * 2 + core


def ring_places():
    return [(place, core) for place in range(len(RING)) for core in range(CORES)]


def ring_table():
    rows = {}
    for place, core in ring_places():
        rows[ring_device(place, core)] = [
            [ring_device(place + ahead, core ^ side) for ahead in RING] for side in range(CORES)
        ]
    return np.array([rows[device] for device in range(len(rows))], np.int32)


def around(value, steps):
    pairs = [(ring_device(p, c), ring_device(p + steps, c)) for p, c in ring_places()]
    return lax.ppermute(value, "batch", pairs)


def to_other_core(value):
    pairs = [(ring_device(p, c), ring_device(p, 1 - c)) for p, c in ring_places()]
    return lax.ppermute(value, "batch", pairs)


def after(value, *earlier):
    return lax.optimization_barrier((value,) + earlier)[0]


def pack_kernel(refs):
    get = refs.__getitem__
    row, out = get("row"), {"one": get("one"), "two": get("two")}
    rows = get("out").shape[0]
    copies = Copies(get("sems"))
    small = [
        copies.start(get("bias"), get("bias_v")),
        copies.start(get("gains"), get("gains_v")),
        copies.start(get("shifts"), get("shifts_v")),
    ]
    arriving = []
    small_at = 0
    for stream, parts in STREAMS.items():
        start = 0
        for (name, block), size in zip(parts, stream_sizes(stream, rows)):
            target = out[stream].at[pl.ds(start, size)]
            if name == "small":
                small_at = start
            elif name == "down":
                source = get("down").at[pl.ds(block * size, size)]
                arriving.append(copies.start(source, target))
            elif name == "first" and block == 3:
                arriving.append(copies.start(get("out"), target))
            else:
                source = get("qkv" if name == "first" else "up").at[:, chunk(block)]
                arriving.append(copies.start(source, target))
            start += size
    row[...] = jnp.zeros((SMALL_ROWS, D), F32)
    for copy in small:
        copy.wait()
    row[1:3, :rows] = get("gains_v")[...].astype(F32)
    row[3:5, :rows] = get("shifts_v")[...].astype(F32)
    row[...] = pltpu.roll(row[...], get("device")[0] * rows, 1)
    row[0:1, : get("bias").shape[1]] = get("bias_v")[...].astype(F32)
    out["one"][small_at : small_at + SMALL_ROWS] = row[...].astype(BF)
    for copy in arriving:
        copy.wait()


def pack(scalars, qkv, out, up, down, bias, gains, shifts):
    call = Call()
    for name, value in scalars.items():
        call.give(name, value, SMEM)
    values = dict(qkv=qkv, out=out, up=up, down=down, bias=bias, gains=gains, shifts=shifts)
    for name, value in values.items():
        call.give(name, value, HBM)
    for stream in STREAMS:
        call.make(stream, (sum(stream_sizes(stream, out.shape[0])), D), BF, VMEM)
    call.hold("row", pltpu.VMEM((SMALL_ROWS, D), F32))
    for name in ("bias", "gains", "shifts"):
        call.hold(name + "_v", pltpu.VMEM(values[name].shape, BF))
    call.hold("sems", pltpu.SemaphoreType.DMA((16,)))
    found = call.run(pack_kernel, "pack", 1)
    return {stream: found[stream] for stream in STREAMS}


def cut_kernel(cut, refs):
    get = refs.__getitem__
    get(1)[...] = get("forwards")[:cut]
    get(-1)[...] = get("backwards")[cut:]


def cut_two(forwards, backwards, cut):
    call = Call()
    call.give("forwards", forwards, VMEM)
    call.give("backwards", backwards, VMEM)
    call.make(1, (cut, D), BF, VMEM)
    call.make(-1, (forwards.shape[0] - cut, D), BF, VMEM)
    found = call.run(partial(cut_kernel, cut), "cut", 0.3)
    return found[1], found[-1]


def ring_gather(own, table, weights, rows):
    held = {stream: {0: (value,)} for stream, value in own.items()}

    def hop(stream, ahead):
        here = held[stream]
        here[-ahead] = (around(here[1 - ahead][0], 1),)
        here[ahead] = (around(here[ahead - 1][0], -1),)

    def put(stream, aheads):
        shards = [(RING.index(ahead), held[stream][ahead]) for ahead in aheads]
        found = place_shards(stream, table, shards, weights, small=stream == "one", pack=True)
        return found, to_other_core(found["packed"])

    def put_other(stream, aheads, came, earlier=()):
        places = [RING.index(ahead) + len(RING) for ahead in aheads]
        place_shards(stream, table, (), weights, came, places, stream == "one", earlier)

    for ahead in (1, 2, 3):
        for stream in STREAMS:
            hop(stream, ahead)
    for stream in STREAMS:
        here = held[stream]
        cut = sum(stream_sizes(stream, rows)[: FAR_CUT[stream]])
        sends = cut_two(here[-3][0], here[3][0], cut)
        here[4] = tuple(around(send, way) for send, way in zip(sends, (1, -1)))
    came = {stream: put(stream, RING)[1] for stream in STREAMS}
    put_other("one", RING, came["one"])
    return lambda mark: put_other("two", RING, came["two"], (mark,))


def both_cores(get, index, place, part=slice(None)):
    return get(("own", index))[place, part].astype(F32) + get(("other", index))[place, part].astype(F32)


def far_kernel(index, cuts, refs):
    get = refs.__getitem__
    for way, part in cuts.items():
        get(way)[...] = both_cores(get, index, RING.index(4), part).astype(BF)


def merge_kernel(ahead, cut, count, refs):
    get = refs.__getitem__
    for way in (1, -1):
        out, came = get(way), get(("came", way))
        place = RING.index(way * ahead)
        parts = [both_cores(get, index, place) for index in range(count)]
        total = jnp.concatenate(parts, axis=0) if count > 1 else parts[0]
        if ahead < 3:
            out[...] = (total + came[...].astype(F32)).astype(BF)
        else:
            near, far = (slice(0, cut), slice(cut, None))[::way]
            out[near] = (total[near] + came[...].astype(F32)).astype(BF)
            out[far] = total[far].astype(BF)


def finish_kernel(piece, count, refs):
    get = refs.__getitem__
    copies, leaving = Copies(get("sems")), []

    def leave(name):
        leaving.append(copies.start(get(name + "_v"), get(name)))

    total = [both_cores(get, index, 0) for index in range(count)]
    total = jnp.concatenate(total, axis=0) if count > 1 else total[0]
    total = total + get(("came", 1))[...].astype(F32) + get(("came", -1))[...].astype(F32)
    if piece == "ffn":
        rows = get("up").shape[0]
        get("down_v")[...] = total[: BLOCKS * rows]
        leave("down")
        for j in range(BLOCKS):
            get("up_v")[:, chunk(j)] = total[chunk(BLOCKS + j, rows)]
        leave("up")
    else:
        rows = get("out").shape[0]
        for j in range(3):
            get("qkv_v")[:, chunk(j)] = total[chunk(j, rows)]
        leave("qkv")
        get("out_v")[...] = total[chunk(3, rows)]
        leave("out")
        small = total[BLOCKS * rows : BLOCKS * rows + 8]
        get("bias_v")[...] = small[:1, : get("bias").shape[1]]
        leave("bias")
        turned = pltpu.roll(small, lax.rem(D - get("device")[0] * rows, D), 1)
        get("gains_v")[...] = turned[1:3, :rows]
        leave("gains")
        get("shifts_v")[...] = turned[3:5, :rows]
        leave("shifts")
    for copy in leaving:
        copy.wait()


class RingScatter:
    order = ()

    def __init__(self, piece, cut):
        self.piece, self.cut, self.rows = piece, cut, 0
        self.parts, self.came = [], {}

    def run(self, call, kernel, name):
        call.follow(RingScatter.order)
        found = call.run(kernel, name + "_" + self.piece, 0.5)
        sent = [way for way in (1, -1) if way in found]
        RingScatter.order = (found[sent[0]],)
        self.came.update((way, around(found[way], way)) for way in sent)

    def add(self, own, other, cuts):
        index = len(self.parts)
        self.parts.append((own, other))
        self.rows += own.shape[1]
        call = Call()
        self.give(call, index)
        for way, part in cuts.items():
            call.make(way, (len(range(*part.indices(own.shape[1]))), D), BF, VMEM)
        self.run(call, partial(far_kernel, index, cuts), "far")

    def give(self, call, only=None):
        for index, (own, other) in enumerate(self.parts):
            if only in (None, index):
                call.give(("own", index), own, VMEM)
                call.give(("other", index), other, VMEM)
        if only is None:
            for way in (1, -1):
                call.give(("came", way), self.came[way], VMEM)

    def step(self, ahead):
        call = Call()
        self.give(call)
        for way in (1, -1):
            call.make(way, (self.rows, D), BF, VMEM)
        self.run(call, partial(merge_kernel, ahead, self.cut, len(self.parts)), "merge")

    def finish(self, shapes, device):
        call = Call()
        self.give(call)
        call.give("device", device, SMEM)
        for name, shape in shapes.items():
            call.make(name, shape, F32, HBM)
            call.hold(name + "_v", pltpu.VMEM(shape, F32))
        call.hold("sems", pltpu.SemaphoreType.DMA((8,)))
        kernel = partial(finish_kernel, self.piece, len(self.parts))
        return call.run(kernel, "finish_" + self.piece, 1)


def leave_kernel(refs):
    copies = Copies(refs["sems"])
    leaving = []
    for name in ("activations", "input_grads"):
        for row in range(2):
            leaving.append(copies.start(refs[name, row], refs[name].at[row]))
    for copy in leaving:
        copy.wait()


def leave_rows(states, earlier=()):
    call = Call()
    call.follow(earlier)
    for name, key in (("activations", "result"), ("input_grads", "grad")):
        for row, state in enumerate(states):
            call.give((name, row), state[key], VMEM)
        call.make(name, (2, ROW, D), BF, HBM)
    call.hold("sems", pltpu.SemaphoreType.DMA((4,)))
    return call.run(leave_kernel, "leave_rows", 1)


def relay(value, steps):
    count = lax.axis_size("section")
    first, last = (max(0, -steps), min(count, count - steps))
    return lax.ppermute(
        value, "section", [(source, source + steps) for source in range(first, last)]
    )


def body(
    inputs,
    cotangent,
    lengths,
    qkv_weight,
    out_weight,
    up_weight,
    down_weight,
    biases,
    norm_gains,
    norm_shifts,
):
    shards = lax.axis_size("batch")
    ring = shards == CORES * len(RING)
    groups = len(RING) if ring else 1
    width = D // shards
    cut = BIAS // shards
    device = lax.axis_index("batch")
    section = lax.axis_index("section").astype(jnp.int32).reshape(1)
    states, weights = ({}, {}), {}
    mine = device.astype(jnp.int32).reshape(1)
    RingScatter.order = ()
    if ring:
        table = jnp.asarray(ring_table().reshape(shards, -1))[device]
        own = pack(
            {"device": mine, "section": section, "table": table, "lengths": lengths[:, 0]},
            qkv_weight[0],
            out_weight[0],
            up_weight[0],
            down_weight[0],
            biases,
            norm_gains[0],
            norm_shifts[0],
        )
        put_last = ring_gather(own, table, weights, width)
        small = weights["small"]
    else:
        table = jnp.array([0, 1], jnp.int32)
        gather = lambda value: lax.all_gather(value, "batch", axis=0, tiled=True)
        halves = [gather(value[0]) for value in (qkv_weight, out_weight, up_weight, down_weight)]
        blocks = lambda half: [half[:, chunk(j)] for j in range(half.shape[1] // D)]
        split = {"one": {}, "two": {}}
        for half, (qkv, out, up, down) in enumerate(
            zip(*(jnp.split(value, CORES) for value in halves))
        ):
            upper, lower = jnp.split(down, 2)
            gap = jnp.zeros((SMALL_ROWS, D), BF)
            split["one"][half] = (jnp.concatenate(blocks(qkv) + [out, gap, upper]),)
            split["two"][half] = (jnp.concatenate([lower] + blocks(up)),)
        place_shards("one", table, list(split["one"].items()), weights)
        put_last = lambda mark: place_shards("two", table, list(split["two"].items()), weights)
        norms = jnp.concatenate([norm_gains[0], norm_shifts[0]])
        packed = gather(jnp.concatenate([biases[0], norms.reshape(-1)])[None]).astype(F32)
        norms_all = packed[:, cut:].reshape(shards, 4, width).transpose(1, 0, 2)
        small = jnp.concatenate(
            [
                packed[:, :cut].reshape(BIAS_ROWS, D),
                norms_all.reshape(4, D),
                jnp.zeros((4, D), F32),
            ]
        )
    common = (section, lengths[:, 0])

    def run_forward(origin, row, source, parts=("attn", "up", "down"), marked=False, earlier=()):
        return forward(
            origin, row, parts, common, small, source, states[row], weights, marked, earlier
        )

    def run_backward(origin, row, source, parts=("ffn", "attn"), earlier=()):
        return backward(
            origin, row, parts, section, small, source, states[row], weights, earlier
        )

    mark = run_forward(0, 0, inputs, ("attn",), True)
    put_last(mark)
    run_forward(0, 0, None, ("up",))
    result = run_forward(0, 0, None, ("down",))
    coming = relay(result, 1)
    second = relay(run_forward(0, 1, inputs), 1)
    run_forward(1, 0, coming)
    run_forward(1, 1, second, earlier=(states[0]["scale2"],))
    coming = relay(run_backward(1, 1, cotangent), -1)
    second = relay(run_backward(1, 0, cotangent, earlier=(states[1]["attn_sums"],)), -1)
    run_backward(0, 1, coming)
    run_backward(0, 0, second, ("ffn",), (states[1]["attn_sums"],))
    down_parts = weight_grad("down", groups, table, states)
    up_parts = weight_grad("up", groups, table, states, down_parts[1:])
    run_backward(0, 0, None, ("attn",), up_parts[1:])
    begun = ()
    if ring:
        RingScatter.order = (states[0]["attn_sums"],)
        ffn_ring = RingScatter("ffn", BLOCKS * width)
        down_other = to_other_core(down_parts[1])
        up_other = to_other_core(after(up_parts[1], down_other))
        ffn_ring.add(down_parts[0], down_other, {1: slice(None)})
        ffn_ring.add(up_parts[0], up_other, {-1: slice(None)})
        begun = RingScatter.order
    attn_parts = weight_grad("first", groups, table, states, begun)
    if ring:
        RingScatter.order = (attn_parts[1],)
        ffn_ring.step(3)
        attn_ring = RingScatter("attn", 2 * width)
        cuts = {1: slice(0, 2 * width), -1: slice(2 * width, None)}
        attn_ring.add(attn_parts[0], to_other_core(attn_parts[1]), cuts)
        attn_ring.step(3)
        ffn_ring.step(2)
        attn_ring.step(2)
        ffn_ring.step(1)
        attn_ring.step(1)
        ffn = ffn_ring.finish({"down": (BLOCKS * width, D), "up": (width, FF)}, mine)
        down_sum, up_sum = ffn["down"], ffn["up"]
        shapes = {"qkv": (width, 3 * D), "out": (width, D), "bias": (1, cut)}
        shapes.update({"gains": (2, width), "shifts": (2, width)})
        attn = attn_ring.finish(shapes, mine)
        qkv_sum, out_sum, bias_sum = attn["qkv"], attn["out"], attn["bias"]
        gain_sum, shift_sum = attn["gains"], attn["shifts"]
    else:
        scatter = lambda value: lax.psum_scatter(
            value, "batch", scatter_dimension=0, tiled=True
        ).astype(F32)
        half = D // CORES
        join = lambda parts: jnp.concatenate(
            [
                jnp.concatenate([part[0, chunk(j, half)] for part in parts])
                for j in range(BLOCKS)
            ],
            axis=1,
        )
        down_sum = scatter(jnp.concatenate([part[0] for part in down_parts]))
        up_sum, attn_sum = scatter(join(up_parts)), scatter(join(attn_parts))
        qkv_sum, out_sum = attn_sum[:, : 3 * D], attn_sum[:, 3 * D :]
        ffn_sums = states[0]["ffn_sums"] + states[1]["ffn_sums"]
        attn_sums = states[0]["attn_sums"] + states[1]["attn_sums"]
        bias_total = jnp.concatenate([attn_sums[:2], ffn_sums[4:10]]).reshape(shards, cut)
        norm_rows = ffn_sums[:4].reshape(4, shards, width).transpose(1, 0, 2)
        small_sum = scatter(
            jnp.concatenate([bias_total, norm_rows.reshape(shards, 4 * width)], axis=1)
        )
        bias_sum = small_sum[:, :cut]
        norm_sum = small_sum[:, cut:].reshape(4, width)
        gain_sum, shift_sum = norm_sum[:2], norm_sum[2:]
    rows = leave_rows(states, RingScatter.order)
    return (
        rows["activations"][None, :, None],
        rows["input_grads"][None, :, None],
        qkv_sum[None],
        out_sum[None],
        up_sum[None],
        down_sum[None],
        bias_sum,
        gain_sum[None],
        shift_sum[None],
    )


def solution(mesh):
    in_specs = (
        P(None, "batch", None, None),
        P(None, "batch", None, None),
        P(None, "batch", None),
        P("section", "batch", None),
        P("section", "batch", None),
        P("section", "batch", None),
        P("section", "batch", None),
        P("section", "batch"),
        P("section", None, "batch"),
        P("section", None, "batch"),
    )
    out_specs = (
        P("section", None, "batch", None, None),
        P("section", None, "batch", None, None),
        P("section", "batch", None),
        P("section", "batch", None),
        P("section", "batch", None),
        P("section", "batch", None),
        P("section", "batch"),
        P("section", None, "batch"),
        P("section", None, "batch"),
    )
    return jax.shard_map(body, mesh=mesh, in_specs=in_specs, out_specs=out_specs, check_vma=False)
```

```python
from functools import partial

import jax
import jax.numpy as jnp
import numpy as np
from jax import lax
from jax.experimental import pallas as pl
from jax.experimental.pallas import tpu as pltpu
from jax.sharding import PartitionSpec as P

D = 768
HEADS = 12
FF = 3072
HEAD_DIM = 64
ROW = 256
HALF = 128
PAIRS = HEADS // 2
PAIR = 2 * HEAD_DIM
FFC = FF // D
BIAS = 6144
VMEM_LIMIT = 10 * 1024 * 1024

BF = jnp.bfloat16
F32 = jnp.float32
epsilon = 1e-12
masked_value = -1e30
inv_sqrt2 = 0.7071067811865476
inv_sqrt2pi = 0.3989422804014327


def nn(a, b):
    return jnp.dot(a, b, preferred_element_type=F32)


def nt(a, b):
    return lax.dot_general(a, b, (((1,), (1,)), ((), ())), preferred_element_type=F32)


def tn(a, b):
    return lax.dot_general(a, b, (((0,), (0,)), ((), ())), preferred_element_type=F32)


def head_masks():
    lane = lax.broadcasted_iota(jnp.int32, (1, PAIR), 1)
    low = (lane < HEAD_DIM).astype(F32)
    return (low.astype(BF), (1.0 - low).astype(BF))


def by_head(values, masks):
    return jnp.concatenate([values * masks[0], values * masks[1]], axis=0)


def own_head(values):
    lane = lax.broadcasted_iota(jnp.int32, (1, PAIR), 1)
    return jnp.where(lane < HEAD_DIM, values[:HALF], values[HALF:])


def bounds_of(lengths_ref, micro):
    first = lengths_ref[micro, 0]
    second = first + lengths_ref[micro, 1]
    return first, second, second + lengths_ref[micro, 2]


def longest_start(lengths_ref, micro):
    bounds = bounds_of(lengths_ref, micro)
    start = jnp.int32(0)
    for place, bound in enumerate(bounds):
        start = jnp.where(lengths_ref[micro, place + 1] == HALF, bound, start)
    return start


def turn(lengths_ref, micro, back=False):
    start = longest_start(lengths_ref, micro)
    here = lax.broadcasted_iota(jnp.int32, (ROW, ROW), 0)
    there = lax.broadcasted_iota(jnp.int32, (ROW, ROW), 1)
    if back:
        here, there = there, here
    return jnp.where((here + start) & (ROW - 1) == there, 1.0, 0.0).astype(BF)


def segment_penalty(lengths_ref, micro):
    bounds = bounds_of(lengths_ref, micro)
    start = longest_start(lengths_ref, micro)

    def number(axis):
        place = lax.broadcasted_iota(jnp.int32, (HALF, HALF), axis)
        place = (place + start + HALF) & (ROW - 1)
        total = jnp.zeros((HALF, HALF), jnp.int32)
        for bound in bounds:
            total = total + jnp.where(place >= bound, 1, 0)
        return total

    return jnp.where(number(0) == number(1), 0.0, masked_value)


def standardize(values):
    centred = values - jnp.mean(values, axis=-1, keepdims=True)
    spread = jnp.mean(centred * centred, axis=-1, keepdims=True)
    scale = lax.rsqrt(spread + epsilon)
    return centred * scale, scale


def norm_back(grad, unit, scale, gain):
    scaled = grad * gain
    mean_one = jnp.mean(scaled, axis=-1, keepdims=True)
    mean_two = jnp.mean(scaled * unit, axis=-1, keepdims=True)
    return scale * (scaled - mean_one - unit * mean_two)


class Copies:
    def __init__(self, sems):
        self.sems = sems
        self.used = 0

    def start(self, src, dst):
        copy = pltpu.make_async_copy(src, dst, self.sems.at[self.used])
        self.used += 1
        copy.start()
        return copy


class Reader:
    def __init__(self, refs):
        self.refs = list(refs)

    def take(self, count=None):
        if count is None:
            return self.refs.pop(0)
        taken, self.refs = self.refs[:count], self.refs[count:]
        return taken


def chunk(index, size=D):
    return slice(index * size, (index + 1) * size)


HBM = pl.BlockSpec(memory_space=pltpu.HBM)
SMEM = pl.BlockSpec(memory_space=pltpu.SMEM)
VMEM = pl.BlockSpec(memory_space=pltpu.VMEM)
LANES = 128
BLOCKS = 4
SMALL_ROWS = 16
BIAS_ROWS = BIAS // D

SHAPES = {
    "tokens": ((ROW, D), BF),
    "qkv": ((ROW, 3 * D), BF),
    "probs": ((PAIRS, 2, 2 * HALF, HALF), BF),
    "context": ((ROW, D), BF),
    "hidden": ((ROW, D), BF),
    "unit1": ((ROW, D), F32),
    "scale1": ((ROW, LANES), F32),
    "active": ((ROW, FF), BF),
    "slope": ((ROW, FF), BF),
    "unit2": ((ROW, D), F32),
    "scale2": ((ROW, LANES), F32),
    "down_side": ((ROW, D), BF),
    "attended": ((ROW, D), BF),
    "sum1": ((ROW, D), F32),
    "result": ((ROW, D), BF),
    "grad": ((ROW, D), BF),
    "ffn_sums": ((16, D), F32),
    "attn_sums": ((8, D), F32),
}
PIECES = {"first": (BLOCKS, D, D), "up": (BLOCKS, D, D), "down": (FF, D)}
PART_PIECE = {"attn": "first", "up": "up", "down": "down"}
MAKES = {
    "attn": ("tokens", "qkv", "probs", "context", "unit1", "scale1", "hidden"),
    "up": ("active", "slope"),
    "down": ("unit2", "scale2", "result"),
}
TAKES = {"attn": (), "up": ("hidden",), "down": ("unit1", "active")}
BACK_MAKES = {
    "ffn": ("down_side", "slope", "attended", "ffn_sums"),
    "attn": ("qkv", "attn_sums", "grad"),
}
BACK_PASSES = {"ffn": ("sum1",), "attn": ()}
BACK_TAKES = {
    "ffn": ("unit2", "scale2", "unit1", "scale1"),
    "attn": ("probs", "attended", "sum1"),
}
BACK_PIECES = {"ffn": ("down", "up"), "attn": ("first",)}


class Call:
    def __init__(self):
        self.operands, self.specs, self.in_names = [], [], []
        self.outs, self.out_specs, self.out_names = [], [], []
        self.scratch, self.scratch_names = [], []
        self.aliases = {}

    def give(self, name, value, spec):
        if spec is not SMEM:
            value = pltpu.with_memory_space_constraint(value, spec.memory_space)
        self.in_names.append(name)
        self.operands.append(value)
        self.specs.append(spec)

    def make(self, name, shape, kind, spec, old=None):
        if old is not None:
            self.aliases[len(self.operands)] = len(self.outs)
            self.give("old_" + name, old, spec)
        self.out_names.append(name)
        self.outs.append((pltpu.VMEM if spec is VMEM else pltpu.HBM)(shape, kind))
        self.out_specs.append(spec)

    def follow(self, values):
        for place, value in enumerate(values):
            self.give(("earlier", place), value, VMEM)

    def of_parts(self, parts, state, takes, makes, passes=None):
        inside = [key for part in parts for key in makes[part]]
        inside += [key for part in parts for key in (passes[part] if passes else ())]
        for part in parts:
            for key in takes[part]:
                if key not in inside:
                    self.give(key, state[key], VMEM)
        for part in parts:
            for key in makes[part]:
                self.make(key, *SHAPES[key], VMEM, state.get(key))
            for key in passes[part] if passes else ():
                if part == parts[-1]:
                    self.make(key, *SHAPES[key], VMEM)
                else:
                    self.hold(key, pltpu.VMEM(*SHAPES[key]))

    def hold(self, name, value):
        self.scratch_names.append(name)
        self.scratch.append(value)

    def run(self, kernel, name, time):
        names = self.in_names + self.out_names + self.scratch_names

        def named(*refs):
            kernel(dict(zip(names, refs)))

        found = pl.pallas_call(
            named,
            out_shape=self.outs,
            in_specs=self.specs,
            out_specs=self.out_specs,
            scratch_shapes=self.scratch,
            input_output_aliases=self.aliases,
            name=name,
            compiler_params=pltpu.CompilerParams(vmem_limit_bytes=VMEM_LIMIT),
            cost_estimate=pl.CostEstimate(
                flops=int(time * 1.1e9), bytes_accessed=1 << 20, transcendentals=0
            ),
        )(*self.operands)
        return dict(zip(self.out_names, found))


def rows_of(pieces, start, size):
    for piece in pieces:
        if start < piece.shape[0]:
            return piece[start : start + size]
        start -= piece.shape[0]


STREAMS = {
    "one": [("first", j) for j in range(BLOCKS)] + [("small", 0), ("down", 0)],
    "two": [("down", 1)] + [("up", j) for j in range(BLOCKS)],
}
FAR_CUT = {"one": 3, "two": 3}


def stream_sizes(stream, rows):
    size = {"first": rows, "up": rows, "small": SMALL_ROWS, "down": 2 * rows}
    return [size[name] for name, _ in STREAMS[stream]]


def place_kernel(plan, refs):
    get = refs.__getitem__
    stream, devices, own, swapped = plan
    table = get("table")
    rows = D // devices
    small = refs.get("small")
    if small is not None and "old_small" not in refs:
        small[...] = jnp.zeros(small.shape, F32)

    def put(place, pieces):
        device = table[place]
        start = 0
        for (name, block), size in zip(STREAMS[stream], stream_sizes(stream, rows)):
            part = rows_of(pieces, start, size)
            start += size
            if name == "down":
                at = pl.multiple_of(device * BLOCKS * rows + block * size, size)
                get("down")[pl.ds(at, size)] = part
            elif name != "small":
                get(name)[block, pl.ds(pl.multiple_of(device * rows, rows), rows)] = part
            elif small is not None:
                more = part.astype(F32)
                width = BIAS // devices
                per_row = D // width
                line = lax.broadcasted_iota(jnp.int32, (BIAS_ROWS, D), 0)
                lane_part = lax.broadcasted_iota(jnp.int32, (BIAS_ROWS, D), 1) // width
                mine = (line == device // per_row) & (lane_part == device % per_row)
                bias = jnp.concatenate([more[0:1, :width]] * per_row, axis=1)
                small[:BIAS_ROWS] += jnp.where(mine, bias, 0.0)
                small[BIAS_ROWS : BIAS_ROWS + 4] += more[1:5]

    for index, (place, count) in enumerate(own):
        pieces = [get(("shard", index, part)) for part in range(count)]
        put(place, pieces)
        if "packed" in refs:
            start = 0
            for piece in pieces:
                stop = start + piece.shape[0]
                get("packed")[index, start:stop] = piece[...]
                start = stop
    for index, place in enumerate(swapped):
        put(place, [get("came").at[index]])


def place_shards(
    stream, table, own, weights, came=None, swapped=(), small=False, earlier=(), pack=False
):
    call = Call()
    call.follow(earlier)
    call.give("table", table, SMEM)
    rows = sum(stream_sizes(stream, D // table.shape[0]))
    for index, (place, shard) in enumerate(own):
        for part, piece in enumerate(shard):
            call.give(("shard", index, part), piece, VMEM)
    if came is not None:
        call.give("came", came, VMEM)
    for key in ("first", "down") if stream == "one" else ("up", "down"):
        call.make(key, PIECES[key], BF, VMEM, weights.get(key))
    if small:
        call.make("small", (SMALL_ROWS, D), F32, VMEM, weights.get("small"))
    if pack:
        call.make("packed", (len(own), rows, D), BF, VMEM)
    counts = [(place, len(shard)) for place, shard in own]
    plan = (stream, table.shape[0], counts, swapped)
    found = call.run(partial(place_kernel, plan), "place_" + stream, 0.5)
    for key in ("first", "up", "down", "small"):
        if key in found:
            weights[key] = found[key]
    return found


def forward_kernel(origin, row, parts, refs):
    get = refs.__getitem__
    small = get("small")
    bias = lambda index: small[index : index + 1, :]
    gain = lambda index: bias(BIAS_ROWS + index)
    shift = lambda index: bias(BIAS_ROWS + 2 + index)
    section = get("section")[0]
    @pl.when(section == origin)
    def _():
        if "attn" in parts:
            tokens = get("source")[...]
            get("tokens")[...] = tokens
            qkv, probs, context, weight = get("qkv"), get("probs"), get("context"), get("first")
            penalty = segment_penalty(get("lengths"), row)
            for j in range(3):
                part = nn(tokens, weight[j])
                if j != 1:
                    part = part + bias(j // 2)
                qkv[:, chunk(j)] = part.astype(BF)
            masks = head_masks()
            for pair in range(PAIRS):
                at = pair * PAIR
                for half in range(2):
                    rows = chunk(half, HALF)
                    keys = by_head(qkv[rows, D + at : D + at + PAIR], masks)
                    scores = nt(keys, qkv[rows, at : at + PAIR]).reshape(2, HALF, HALF)
                    if half == 1:
                        scores = scores + penalty
                    peak = jnp.max(scores, axis=1, keepdims=True)
                    raised = jnp.exp((scores - peak) * HEAD_DIM ** (-0.5))
                    share = raised * (1.0 / jnp.sum(raised, axis=1, keepdims=True))
                    share = share.reshape(2 * HALF, HALF).astype(BF)
                    probs[pair, half] = share
                    values = by_head(qkv[rows, 2 * D + at : 2 * D + at + PAIR], masks)
                    context[rows, at : at + PAIR] = tn(share, values).astype(BF)
            attended = nn(context[...], weight[3]) + bias(2)
            unit, scale = standardize(tokens.astype(F32) + attended)
            get("unit1")[...] = unit
            get("scale1")[...] = jnp.broadcast_to(scale, (ROW, LANES))
            get("hidden")[...] = (unit * gain(0) + shift(0)).astype(BF)
        if "up" in parts:
            hidden, active, slope = get("hidden"), get("active"), get("slope")
            for j in range(FFC):
                inner = nn(hidden[...], get("up")[j]) + bias(3 + j)
                phi = 0.5 * (1.0 + lax.erf(inner * inv_sqrt2))
                active[:, chunk(j)] = (inner * phi).astype(BF)
                bell = jnp.exp(inner * inner * -0.5) * inv_sqrt2pi
                slope[:, chunk(j)] = (phi + inner * bell).astype(BF)
        if "down" in parts:
            normed = get("unit1")[...] * gain(0) + shift(0)
            total = normed + bias(7) + nn(get("active")[...], get("down")[...])
            unit, scale = standardize(total)
            get("result")[...] = (unit * gain(1) + shift(1)).astype(BF)
            get("unit2")[...] = unit
            get("scale2")[...] = jnp.broadcast_to(scale, (ROW, LANES))

    if "mark" in refs:
        get("mark")[...] = jnp.zeros((8, LANES), F32)


def forward(origin, row, parts, common, small, source, state, weights, marked=False, earlier=()):
    section, lengths = common
    call = Call()
    call.follow(earlier)
    call.give("section", section, SMEM)
    call.give("small", small, VMEM)
    if "attn" in parts:
        call.give("lengths", lengths, SMEM)
        call.give("source", source, VMEM)
    for part in parts:
        key = PART_PIECE[part]
        call.give(key, weights[key], VMEM)
    if marked:
        call.make("mark", (8, LANES), F32, VMEM)
    call.of_parts(parts, state, TAKES, MAKES)
    found = call.run(
        partial(forward_kernel, origin, row, parts),
        "forward_" + "_".join(parts),
        0.1 if marked else 3 * len(parts),
    )
    mark = found.pop("mark", None)
    state.update(found)
    return mark if marked else found.get("result")


def backward_kernel(origin, row, parts, refs):
    get = refs.__getitem__
    small = get("small")
    gain = lambda index: small[BIAS_ROWS + index : BIAS_ROWS + index + 1, :]

    @pl.when(get("section")[0] == origin)
    def _():
        if "ffn" in parts:
            grad = get("source")[...].astype(F32)
            sums, inner = get("ffn_sums"), get("slope")
            unit = get("unit2")[...]
            sums[1:2, :] = jnp.sum(grad * unit, axis=0, keepdims=True)
            sums[3:4, :] = jnp.sum(grad, axis=0, keepdims=True)
            grad = norm_back(grad, unit, get("scale2")[:, 0:1], gain(1))
            sums[9:10, :] = jnp.sum(grad, axis=0, keepdims=True)
            side = grad.astype(BF)
            get("down_side")[...] = side
            sum_v = get("sum_v")
            sum_v[...] = grad
            for j in range(FFC):
                through = nt(side, get("down")[chunk(j)])
                through = through * inner[:, chunk(j)].astype(F32)
                sums[5 + j : 6 + j, :] = jnp.sum(through, axis=0, keepdims=True)
                inner[:, chunk(j)] = through.astype(BF)
            grad = sum_v[...]
            for j in range(BLOCKS):
                grad = grad + nt(inner[:, chunk(j)], get("up")[j])
            unit = get("unit1")[...]
            sums[0:1, :] = jnp.sum(grad * unit, axis=0, keepdims=True)
            sums[2:3, :] = jnp.sum(grad, axis=0, keepdims=True)
            grad = norm_back(grad, unit, get("scale1")[:, 0:1], gain(0))
            sums[4:5, :] = jnp.sum(grad, axis=0, keepdims=True)
            sums[10:16, :] = jnp.zeros((6, D), F32)
            get("sum1")[...] = grad
            get("attended")[...] = grad.astype(BF)
        if "attn" in parts:
            weight = get("first")
            context_grad = nt(get("attended")[...], weight[3]).astype(BF)
            masks = head_masks()
            qkv, sums = get("qkv"), get("attn_sums")
            sums[2:8, :] = jnp.zeros((6, D), F32)
            for pair in range(PAIRS):
                at = pair * PAIR
                spans = [slice(which * D + at, which * D + at + PAIR) for which in range(3)]
                biases = [0.0, 0.0]
                for half in range(2):
                    rows = chunk(half, HALF)
                    queries = qkv[rows, spans[0]]
                    keys = by_head(qkv[rows, spans[1]], masks)
                    values = by_head(qkv[rows, spans[2]], masks)
                    pair_grad = context_grad[rows, at : at + PAIR]
                    share = get("probs")[pair, half]
                    wide = share.astype(F32)
                    weighted = wide * nt(values, pair_grad)
                    inner_sum = jnp.sum(weighted.reshape(2, HALF, HALF), axis=1, keepdims=True)
                    score_grad = weighted.reshape(2, HALF, HALF)
                    score_grad = score_grad - wide.reshape(2, HALF, HALF) * inner_sum
                    score_grad = (score_grad * HEAD_DIM ** (-0.5)).reshape(2 * HALF, HALF)
                    score_grad = score_grad.astype(BF)
                    grads = (
                        tn(score_grad, keys),
                        own_head(nn(score_grad, queries)),
                        own_head(nn(share, pair_grad)),
                    )
                    for span, value in zip(spans, grads):
                        qkv[rows, span] = value.astype(BF)
                    for line in range(2):
                        biases[line] = biases[line] + jnp.sum(
                            grads[2 * line], axis=0, keepdims=True
                        )
                for line in range(2):
                    sums[line : line + 1, at : at + PAIR] = biases[line]
            grad = get("sum1")[...]
            for j in range(3):
                grad = grad + nt(qkv[:, chunk(j)], weight[j])
            get("grad")[...] = grad.astype(BF)


def backward(origin, row, parts, common, small, source, state, weights, earlier=()):
    call = Call()
    call.follow(earlier)
    call.give("section", common[0], SMEM)
    call.give("small", small, VMEM)
    for part in parts:
        for key in BACK_PIECES[part]:
            call.give(key, weights[key], VMEM)
    if "ffn" in parts:
        call.give("source", source, VMEM)
        call.hold("sum_v", pltpu.VMEM((ROW, D), F32))
    call.of_parts(parts, state, BACK_TAKES, BACK_MAKES, BACK_PASSES)
    found = call.run(
        partial(backward_kernel, origin, row, parts), "backward_" + "_".join(parts), 5 * len(parts)
    )
    state.update(found)
    return found.get("grad")


def other_groups(groups):
    if groups == 1:
        return [("other0", (0,))]
    return [("other0", (7,)), ("other1", tuple(range(7)))]


def other_at(groups, place):
    for name, places in other_groups(groups):
        if place in places:
            return name, places.index(place)


WEIGHT_TAKES = {
    "down": ("active", "down_side"),
    "up": ("hidden", "slope"),
    "first": ("context", "attended", "tokens", "qkv"),
}


def weight_kernel(piece, groups, refs):
    get = refs.__getitem__
    table, held = get("table"), get("held")
    rows = D // (2 * groups)

    def store(side, place, span, value):
        if side == 0:
            get("own")[place, span] = value
        else:
            name, index = other_at(groups, place)
            get(name)[index, span] = value

    def both(key, j=0):
        return jnp.concatenate([get((key, row))[:, chunk(j)] for row in range(2)], axis=0)

    places = [(place // groups, place % groups) for place in range(2 * groups)]
    if piece == "down":
        right = both("down_side")
        for j in range(FFC):
            held[chunk(j)] = tn(both("active", j), right).astype(BF)
        for side, place in places:
            at = pl.multiple_of(table[side * groups + place] * BLOCKS * rows, BLOCKS * rows)
            store(side, place, slice(None), held[pl.ds(at, BLOCKS * rows)])
        return
    names = WEIGHT_TAKES[piece]
    jobs = [(names[0], names[1], j, j) for j in range(BLOCKS)]
    if piece == "first":
        sums, row = get("sums"), get("row_sums")
        bias_rows = [get(("attn_sums", 0))[k : k + 1] + get(("attn_sums", 1))[k : k + 1] for k in range(2)]
        ffn = get(("ffn_sums", 0))[...] + get(("ffn_sums", 1))[...]
        bias_rows += [ffn[4 + k : 5 + k] for k in range(6)]
        row[...] = jnp.zeros((SMALL_ROWS, D), F32)
        row[1:5, :] = ffn[:4]
        if groups > 1:
            per_row = 2 * groups // BIAS_ROWS
            width = D // per_row
            for device in range(2 * groups):
                start = device % per_row * width
                row[0:1, :width] = bias_rows[device // per_row][:, start : start + width]
                sums[device] = row[...].astype(BF)
            for side, place in places:
                device = table[side * groups + place]
                store(side, place, slice(BLOCKS * rows, None), sums[device])
        jobs = [("context", "attended", 0, 3)] + [("tokens", "qkv", j, j) for j in range(3)]
    for left, right, j, block in jobs:
        held[:D] = tn(both(left), both(right, j)).astype(BF)
        for side, place in places:
            at = pl.multiple_of(table[side * groups + place] * rows, rows)
            store(side, place, chunk(block, rows), held[pl.ds(at, rows)])


def weight_grad(piece, groups, table, states, earlier=()):
    call = Call()
    call.follow(earlier)
    call.give("table", table, SMEM)
    for key in WEIGHT_TAKES[piece]:
        for row, state in enumerate(states):
            call.give((key, row), state[key], VMEM)
    rows = BLOCKS * D // (2 * groups)
    if piece == "first":
        rows += SMALL_ROWS
        for key in ("attn_sums", "ffn_sums"):
            for row, state in enumerate(states):
                call.give((key, row), state[key], VMEM)
        call.hold("sums", pltpu.VMEM((2 * groups, SMALL_ROWS, D), BF))
        call.hold("row_sums", pltpu.VMEM((SMALL_ROWS, D), F32))
    call.make("own", (groups, rows, D), BF, VMEM)
    for name, places in other_groups(groups):
        call.make(name, (len(places), rows, D), BF, VMEM)
    call.hold("held", pltpu.VMEM((FF if piece == "down" else D, D), BF))
    found = call.run(partial(weight_kernel, piece, groups), "weight_" + piece, 4)
    return found["own"], [found[name] for name, _ in other_groups(groups)]


CORES = 2
RING = (0, -1, 1, -2, 2, -3, 3, 4)


def ring_device(place, core):
    place = place % len(RING)
    z, y = (place, 0) if place < 4 else (7 - place, 1)
    return (z * 2 + y) * 2 + core


def ring_places():
    return [(place, core) for place in range(len(RING)) for core in range(CORES)]


def ring_table():
    rows = {}
    for place, core in ring_places():
        rows[ring_device(place, core)] = [
            [ring_device(place + ahead, core ^ side) for ahead in RING] for side in range(CORES)
        ]
    return np.array([rows[device] for device in range(len(rows))], np.int32)


def around(value, steps):
    pairs = [(ring_device(p, c), ring_device(p + steps, c)) for p, c in ring_places()]
    return lax.ppermute(value, "batch", pairs)


def to_other_core(value):
    pairs = [(ring_device(p, c), ring_device(p, 1 - c)) for p, c in ring_places()]
    return lax.ppermute(value, "batch", pairs)


def after(value, *earlier):
    return lax.optimization_barrier((value,) + earlier)[0]


def pack_kernel(refs):
    get = refs.__getitem__
    row, out = get("row"), {"one": get("one"), "two": get("two")}
    rows = get("out").shape[0]
    copies = Copies(get("sems"))
    small = [
        copies.start(get("bias"), get("bias_v")),
        copies.start(get("gains"), get("gains_v")),
        copies.start(get("shifts"), get("shifts_v")),
    ]
    arriving = []
    small_at = 0
    for stream, parts in STREAMS.items():
        start = 0
        for (name, block), size in zip(parts, stream_sizes(stream, rows)):
            target = out[stream].at[pl.ds(start, size)]
            if name == "small":
                small_at = start
            elif name == "down":
                source = get("down").at[pl.ds(block * size, size)]
                arriving.append(copies.start(source, target))
            elif name == "first" and block == 3:
                arriving.append(copies.start(get("out"), target))
            else:
                source = get("qkv" if name == "first" else "up").at[:, chunk(block)]
                arriving.append(copies.start(source, target))
            start += size
    row[...] = jnp.zeros((SMALL_ROWS, D), F32)
    for copy in small:
        copy.wait()
    row[1:3, :rows] = get("gains_v")[...].astype(F32)
    row[3:5, :rows] = get("shifts_v")[...].astype(F32)
    row[...] = pltpu.roll(row[...], get("device")[0] * rows, 1)
    row[0:1, : get("bias").shape[1]] = get("bias_v")[...].astype(F32)
    out["one"][small_at : small_at + SMALL_ROWS] = row[...].astype(BF)
    for copy in arriving:
        copy.wait()


def pack(scalars, qkv, out, up, down, bias, gains, shifts):
    call = Call()
    for name, value in scalars.items():
        call.give(name, value, SMEM)
    values = dict(qkv=qkv, out=out, up=up, down=down, bias=bias, gains=gains, shifts=shifts)
    for name, value in values.items():
        call.give(name, value, HBM)
    for stream in STREAMS:
        call.make(stream, (sum(stream_sizes(stream, out.shape[0])), D), BF, VMEM)
    call.hold("row", pltpu.VMEM((SMALL_ROWS, D), F32))
    for name in ("bias", "gains", "shifts"):
        call.hold(name + "_v", pltpu.VMEM(values[name].shape, BF))
    call.hold("sems", pltpu.SemaphoreType.DMA((16,)))
    found = call.run(pack_kernel, "pack", 1)
    return {stream: found[stream] for stream in STREAMS}


def cut_kernel(cut, refs):
    get = refs.__getitem__
    get(1)[...] = get("forwards")[:cut]
    get(-1)[...] = get("backwards")[cut:]


def cut_two(forwards, backwards, cut, earlier):
    call = Call()
    call.follow(earlier)
    call.give("forwards", forwards, VMEM)
    call.give("backwards", backwards, VMEM)
    call.make(1, (cut, D), BF, VMEM)
    call.make(-1, (forwards.shape[0] - cut, D), BF, VMEM)
    found = call.run(partial(cut_kernel, cut), "cut", 0.3)
    return found[1], found[-1]


def ring_gather(own, table, weights, rows, earlier):
    held = {stream: {0: (value,)} for stream, value in own.items()}

    def hop(stream, ahead):
        here = held[stream]
        here[-ahead] = (around(here[1 - ahead][0], 1),)
        here[ahead] = (around(here[ahead - 1][0], -1),)

    def put(stream, aheads):
        shards = [(RING.index(ahead), held[stream][ahead]) for ahead in aheads]
        found = place_shards(stream, table, shards, weights, small=stream == "one", pack=True)
        return found, to_other_core(found["packed"])

    def put_other(stream, aheads, came, earlier=()):
        places = [RING.index(ahead) + len(RING) for ahead in aheads]
        place_shards(stream, table, (), weights, came, places, stream == "one", earlier)

    for ahead in (1, 2, 3):
        for stream in STREAMS:
            hop(stream, ahead)
    for stream in STREAMS:
        here = held[stream]
        cut = sum(stream_sizes(stream, rows)[: FAR_CUT[stream]])
        sends = cut_two(here[-3][0], here[3][0], cut, earlier)
        here[4] = tuple(around(send, way) for send, way in zip(sends, (1, -1)))
    came = {stream: put(stream, RING)[1] for stream in STREAMS}
    put_other("one", RING, came["one"])
    return lambda mark: put_other("two", RING, came["two"], (mark,))


def both_cores(get, index, place, part=slice(None)):
    name, at = other_at(len(RING), place)
    other = get((name, index))[at, part].astype(F32)
    return get(("own", index))[place, part].astype(F32) + other


def far_kernel(index, cuts, refs):
    get = refs.__getitem__
    for way, part in cuts.items():
        get(way)[...] = both_cores(get, index, RING.index(4), part).astype(BF)


def merge_kernel(ahead, cut, count, refs):
    get = refs.__getitem__
    for way in (1, -1):
        out, came = get(way), get(("came", way))
        place = RING.index(way * ahead)
        parts = [both_cores(get, index, place) for index in range(count)]
        total = jnp.concatenate(parts, axis=0) if count > 1 else parts[0]
        if ahead < 3:
            out[...] = (total + came[...].astype(F32)).astype(BF)
        else:
            near, far = (slice(0, cut), slice(cut, None))[::way]
            out[near] = (total[near] + came[...].astype(F32)).astype(BF)
            out[far] = total[far].astype(BF)


def finish_kernel(piece, count, refs):
    get = refs.__getitem__
    copies, leaving = Copies(get("sems")), []

    def leave(name):
        leaving.append(copies.start(get(name + "_v"), get(name)))

    total = [both_cores(get, index, 0) for index in range(count)]
    total = jnp.concatenate(total, axis=0) if count > 1 else total[0]
    total = total + get(("came", 1))[...].astype(F32) + get(("came", -1))[...].astype(F32)
    if piece == "ffn":
        rows = get("up").shape[0]
        get("down_v")[...] = total[: BLOCKS * rows]
        leave("down")
        for j in range(BLOCKS):
            get("up_v")[:, chunk(j)] = total[chunk(BLOCKS + j, rows)]
        leave("up")
    else:
        rows = get("out").shape[0]
        for j in range(3):
            get("qkv_v")[:, chunk(j)] = total[chunk(j, rows)]
        leave("qkv")
        get("out_v")[...] = total[chunk(3, rows)]
        leave("out")
        small = total[BLOCKS * rows : BLOCKS * rows + 8]
        get("bias_v")[...] = small[:1, : get("bias").shape[1]]
        leave("bias")
        turned = pltpu.roll(small, lax.rem(D - get("device")[0] * rows, D), 1)
        get("gains_v")[...] = turned[1:3, :rows]
        leave("gains")
        get("shifts_v")[...] = turned[3:5, :rows]
        leave("shifts")
    for copy in leaving:
        copy.wait()


class RingScatter:
    order = ()

    def __init__(self, piece, cut):
        self.piece, self.cut, self.rows = piece, cut, 0
        self.parts, self.came = [], {}

    def run(self, call, kernel, name):
        call.follow(RingScatter.order)
        found = call.run(kernel, name + "_" + self.piece, 0.5)
        sent = [way for way in (1, -1) if way in found]
        RingScatter.order = (found[sent[0]],)
        self.came.update((way, around(found[way], way)) for way in sent)

    def add(self, own, others, cuts, late=()):
        index = len(self.parts)
        held = {"other0": to_other_core(others[0])}
        self.parts.append((own, held))
        self.rows += own.shape[1]
        call = Call()
        self.give(call, ("other0",), index)
        for way, part in cuts.items():
            call.make(way, (len(range(*part.indices(own.shape[1]))), D), BF, VMEM)
        self.run(call, partial(far_kernel, index, cuts), "far")
        earlier = late + tuple(self.came.values()) if late else (held["other0"],)
        held["other1"] = to_other_core(after(others[1], *earlier))

    def give(self, call, names, only=None):
        for index, (own, others) in enumerate(self.parts):
            if only in (None, index):
                call.give(("own", index), own, VMEM)
                for name in names:
                    call.give((name, index), others[name], VMEM)
        if only is None:
            for way in (1, -1):
                call.give(("came", way), self.came[way], VMEM)

    def step(self, ahead):
        call = Call()
        self.give(call, ("other1",))
        for way in (1, -1):
            call.make(way, (self.rows, D), BF, VMEM)
        self.run(call, partial(merge_kernel, ahead, self.cut, len(self.parts)), "merge")

    def finish(self, shapes, device):
        call = Call()
        self.give(call, ("other1",))
        call.give("device", device, SMEM)
        for name, shape in shapes.items():
            call.make(name, shape, F32, HBM)
            call.hold(name + "_v", pltpu.VMEM(shape, F32))
        call.hold("sems", pltpu.SemaphoreType.DMA((8,)))
        kernel = partial(finish_kernel, self.piece, len(self.parts))
        return call.run(kernel, "finish_" + self.piece, 1)


def turn_kernel(refs):
    for row in range(2):
        matrix = turn(refs["lengths"], row)
        for name in ("inputs", "cotangent"):
            refs[name, row][...] = nn(matrix, refs[name][row, 0]).astype(BF)


def turn_rows(lengths, inputs, cotangent):
    call = Call()
    call.give("lengths", lengths, SMEM)
    call.give("inputs", inputs, VMEM)
    call.give("cotangent", cotangent, VMEM)
    for name in ("inputs", "cotangent"):
        for row in range(2):
            call.make((name, row), (ROW, D), BF, VMEM)
    found = call.run(turn_kernel, "turn_rows", 1)
    return [[found[name, row] for row in range(2)] for name in ("inputs", "cotangent")]


def leave_kernel(refs):
    copies = Copies(refs["sems"])
    leaving = []
    for row in range(2):
        back = turn(refs["lengths"], row, True)
        for place, name in enumerate(("activations", "input_grads")):
            held = refs["held"].at[2 * row + place]
            held[...] = nn(back, refs[name, row][...]).astype(BF)
            leaving.append(copies.start(held, refs[name].at[row]))
    for copy in leaving:
        copy.wait()


def leave_rows(states, lengths, earlier=()):
    call = Call()
    call.follow(earlier)
    call.give("lengths", lengths, SMEM)
    for name, key in (("activations", "result"), ("input_grads", "grad")):
        for row, state in enumerate(states):
            call.give((name, row), state[key], VMEM)
        call.make(name, (2, ROW, D), BF, HBM)
    call.hold("held", pltpu.VMEM((4, ROW, D), BF))
    call.hold("sems", pltpu.SemaphoreType.DMA((4,)))
    return call.run(leave_kernel, "leave_rows", 1)


def relay(value, steps):
    count = lax.axis_size("section")
    first, last = (max(0, -steps), min(count, count - steps))
    return lax.ppermute(
        value, "section", [(source, source + steps) for source in range(first, last)]
    )


def body(
    inputs,
    cotangent,
    lengths,
    qkv_weight,
    out_weight,
    up_weight,
    down_weight,
    biases,
    norm_gains,
    norm_shifts,
):
    shards = lax.axis_size("batch")
    ring = shards == CORES * len(RING)
    groups = len(RING) if ring else 1
    width = D // shards
    cut = BIAS // shards
    device = lax.axis_index("batch")
    section = lax.axis_index("section").astype(jnp.int32).reshape(1)
    states, weights = ({}, {}), {}
    mine = device.astype(jnp.int32).reshape(1)
    RingScatter.order = ()
    if ring:
        table = jnp.asarray(ring_table().reshape(shards, -1))[device]
        own = pack(
            {"device": mine, "section": section, "table": table, "lengths": lengths[:, 0]},
            qkv_weight[0],
            out_weight[0],
            up_weight[0],
            down_weight[0],
            biases,
            norm_gains[0],
            norm_shifts[0],
        )
        inputs, cotangent = turn_rows(lengths[:, 0], inputs, cotangent)
        put_last = ring_gather(own, table, weights, width, inputs)
        small = weights["small"]
    else:
        table = jnp.array([0, 1], jnp.int32)
        gather = lambda value: lax.all_gather(value, "batch", axis=0, tiled=True)
        halves = [gather(value[0]) for value in (qkv_weight, out_weight, up_weight, down_weight)]
        blocks = lambda half: [half[:, chunk(j)] for j in range(half.shape[1] // D)]
        split = {"one": {}, "two": {}}
        for half, (qkv, out, up, down) in enumerate(
            zip(*(jnp.split(value, CORES) for value in halves))
        ):
            upper, lower = jnp.split(down, 2)
            gap = jnp.zeros((SMALL_ROWS, D), BF)
            split["one"][half] = (jnp.concatenate(blocks(qkv) + [out, gap, upper]),)
            split["two"][half] = (jnp.concatenate([lower] + blocks(up)),)
        place_shards("one", table, list(split["one"].items()), weights)
        put_last = lambda mark: place_shards("two", table, list(split["two"].items()), weights)
        norms = jnp.concatenate([norm_gains[0], norm_shifts[0]])
        packed = gather(jnp.concatenate([biases[0], norms.reshape(-1)])[None]).astype(F32)
        norms_all = packed[:, cut:].reshape(shards, 4, width).transpose(1, 0, 2)
        small = jnp.concatenate(
            [
                packed[:, :cut].reshape(BIAS_ROWS, D),
                norms_all.reshape(4, D),
                jnp.zeros((4, D), F32),
            ]
        )
    common = (section, lengths[:, 0])
    if not ring:
        inputs, cotangent = turn_rows(lengths[:, 0], inputs, cotangent)

    def run_forward(origin, row, source, parts=("attn", "up", "down"), marked=False, earlier=()):
        return forward(
            origin, row, parts, common, small, source, states[row], weights, marked, earlier
        )

    def run_backward(origin, row, source, parts=("ffn", "attn"), earlier=()):
        return backward(
            origin, row, parts, common, small, source, states[row], weights, earlier
        )

    mark = run_forward(0, 0, inputs[0], ("attn",), True)
    put_last(mark)
    run_forward(0, 0, None, ("up",))
    result = run_forward(0, 0, None, ("down",))
    coming = relay(result, 1)
    second = relay(run_forward(0, 1, inputs[1]), 1)
    run_forward(1, 0, coming)
    run_forward(1, 1, second, earlier=(states[0]["scale2"],))
    coming = relay(run_backward(1, 1, cotangent[1]), -1)
    second = relay(run_backward(1, 0, cotangent[0], earlier=(states[1]["attn_sums"],)), -1)
    run_backward(0, 1, coming)
    run_backward(0, 0, second, ("ffn",), (states[1]["attn_sums"],))
    down_own, down_others = weight_grad("down", groups, table, states)
    up_own, up_others = weight_grad("up", groups, table, states, (down_own,))
    RingScatter.order = (up_own,)
    if ring:
        ffn_ring = RingScatter("ffn", BLOCKS * width)
        ffn_ring.add(down_own, down_others, {1: slice(None)})
        ffn_ring.add(up_own, up_others, {-1: slice(None)})
    run_backward(0, 0, None, ("attn",), RingScatter.order)
    attn_own, attn_others = weight_grad("first", groups, table, states)
    if ring:
        RingScatter.order = (attn_own,)
        ffn_ring.step(3)
        attn_ring = RingScatter("attn", 2 * width)
        cuts = {1: slice(0, 2 * width), -1: slice(2 * width, None)}
        attn_ring.add(attn_own, attn_others, cuts, tuple(ffn_ring.came.values()))
        ffn_ring.step(2)
        attn_ring.step(3)
        ffn_ring.step(1)
        attn_ring.step(2)
        attn_ring.step(1)
        ffn = ffn_ring.finish({"down": (BLOCKS * width, D), "up": (width, FF)}, mine)
        down_sum, up_sum = ffn["down"], ffn["up"]
        shapes = {"qkv": (width, 3 * D), "out": (width, D), "bias": (1, cut)}
        shapes.update({"gains": (2, width), "shifts": (2, width)})
        attn = attn_ring.finish(shapes, mine)
        qkv_sum, out_sum, bias_sum = attn["qkv"], attn["out"], attn["bias"]
        gain_sum, shift_sum = attn["gains"], attn["shifts"]
    else:
        scatter = lambda value: lax.psum_scatter(
            value, "batch", scatter_dimension=0, tiled=True
        ).astype(F32)
        half = D // CORES
        join = lambda parts: jnp.concatenate(
            [
                jnp.concatenate([part[0, chunk(j, half)] for part in parts])
                for j in range(BLOCKS)
            ],
            axis=1,
        )
        down_sum = scatter(jnp.concatenate([down_own[0], down_others[0][0]]))
        up_sum = scatter(join((up_own, up_others[0])))
        attn_sum = scatter(join((attn_own, attn_others[0])))
        qkv_sum, out_sum = attn_sum[:, : 3 * D], attn_sum[:, 3 * D :]
        ffn_sums = states[0]["ffn_sums"] + states[1]["ffn_sums"]
        attn_sums = states[0]["attn_sums"] + states[1]["attn_sums"]
        bias_total = jnp.concatenate([attn_sums[:2], ffn_sums[4:10]]).reshape(shards, cut)
        norm_rows = ffn_sums[:4].reshape(4, shards, width).transpose(1, 0, 2)
        small_sum = scatter(
            jnp.concatenate([bias_total, norm_rows.reshape(shards, 4 * width)], axis=1)
        )
        bias_sum = small_sum[:, :cut]
        norm_sum = small_sum[:, cut:].reshape(4, width)
        gain_sum, shift_sum = norm_sum[:2], norm_sum[2:]
    rows = leave_rows(states, lengths[:, 0], RingScatter.order if ring else ())
    return (
        rows["activations"][None, :, None],
        rows["input_grads"][None, :, None],
        qkv_sum[None],
        out_sum[None],
        up_sum[None],
        down_sum[None],
        bias_sum,
        gain_sum[None],
        shift_sum[None],
    )


def solution(mesh):
    in_specs = (
        P(None, "batch", None, None),
        P(None, "batch", None, None),
        P(None, "batch", None),
        P("section", "batch", None),
        P("section", "batch", None),
        P("section", "batch", None),
        P("section", "batch", None),
        P("section", "batch"),
        P("section", None, "batch"),
        P("section", None, "batch"),
    )
    out_specs = (
        P("section", None, "batch", None, None),
        P("section", None, "batch", None, None),
        P("section", "batch", None),
        P("section", "batch", None),
        P("section", "batch", None),
        P("section", "batch", None),
        P("section", "batch"),
        P("section", None, "batch"),
        P("section", None, "batch"),
    )
    return jax.shard_map(body, mesh=mesh, in_specs=in_specs, out_specs=out_specs, check_vma=False)
```

```python
from functools import partial

import jax
import jax.numpy as jnp
import numpy as np
from jax import lax
from jax.experimental import pallas as pl
from jax.experimental.pallas import tpu as pltpu
from jax.sharding import PartitionSpec as P

D = 768
HEADS = 12
FF = 3072
HEAD_DIM = 64
ROW = 256
HALF = 128
PAIRS = HEADS // 2
PAIR = 2 * HEAD_DIM
FFC = FF // D
BIAS = 6144
VMEM_LIMIT = 10 * 1024 * 1024

BF = jnp.bfloat16
F32 = jnp.float32
epsilon = 1e-12
masked_value = -1e30
inv_sqrt2 = 0.7071067811865476
inv_sqrt2pi = 0.3989422804014327


def nn(a, b):
    return jnp.dot(a, b, preferred_element_type=F32)


def nt(a, b):
    return lax.dot_general(a, b, (((1,), (1,)), ((), ())), preferred_element_type=F32)


def tn(a, b):
    return lax.dot_general(a, b, (((0,), (0,)), ((), ())), preferred_element_type=F32)


def head_masks():
    lane = lax.broadcasted_iota(jnp.int32, (1, PAIR), 1)
    low = (lane < HEAD_DIM).astype(F32)
    return (low.astype(BF), (1.0 - low).astype(BF))


def by_head(values, masks):
    return jnp.concatenate([values * masks[0], values * masks[1]], axis=0)


def own_head(values):
    lane = lax.broadcasted_iota(jnp.int32, (1, PAIR), 1)
    return jnp.where(lane < HEAD_DIM, values[:HALF], values[HALF:])


def bounds_of(lengths_ref, micro):
    first = lengths_ref[micro, 0]
    second = first + lengths_ref[micro, 1]
    return first, second, second + lengths_ref[micro, 2]


def longest_start(lengths_ref, micro):
    bounds = bounds_of(lengths_ref, micro)
    start = jnp.int32(0)
    for place, bound in enumerate(bounds):
        start = jnp.where(lengths_ref[micro, place + 1] == HALF, bound, start)
    return start


def turn(lengths_ref, micro, back=False):
    start = longest_start(lengths_ref, micro)
    here = lax.broadcasted_iota(jnp.int32, (ROW, ROW), 0)
    there = lax.broadcasted_iota(jnp.int32, (ROW, ROW), 1)
    if back:
        here, there = there, here
    return jnp.where((here + start) & (ROW - 1) == there, 1.0, 0.0).astype(BF)


def segment_penalty(lengths_ref, micro):
    bounds = bounds_of(lengths_ref, micro)
    start = longest_start(lengths_ref, micro)

    def number(axis):
        place = lax.broadcasted_iota(jnp.int32, (HALF, HALF), axis)
        place = (place + start + HALF) & (ROW - 1)
        total = jnp.zeros((HALF, HALF), jnp.int32)
        for bound in bounds:
            total = total + jnp.where(place >= bound, 1, 0)
        return total

    return jnp.where(number(0) == number(1), 0.0, masked_value)


def standardize(values):
    centred = values - jnp.mean(values, axis=-1, keepdims=True)
    spread = jnp.mean(centred * centred, axis=-1, keepdims=True)
    scale = lax.rsqrt(spread + epsilon)
    return centred * scale, scale


def norm_back(grad, unit, scale, gain):
    scaled = grad * gain
    mean_one = jnp.mean(scaled, axis=-1, keepdims=True)
    mean_two = jnp.mean(scaled * unit, axis=-1, keepdims=True)
    return scale * (scaled - mean_one - unit * mean_two)


class Copies:
    def __init__(self, sems):
        self.sems = sems
        self.used = 0

    def start(self, src, dst):
        copy = pltpu.make_async_copy(src, dst, self.sems.at[self.used])
        self.used += 1
        copy.start()
        return copy


class Reader:
    def __init__(self, refs):
        self.refs = list(refs)

    def take(self, count=None):
        if count is None:
            return self.refs.pop(0)
        taken, self.refs = self.refs[:count], self.refs[count:]
        return taken


def chunk(index, size=D):
    return slice(index * size, (index + 1) * size)


HBM = pl.BlockSpec(memory_space=pltpu.HBM)
SMEM = pl.BlockSpec(memory_space=pltpu.SMEM)
VMEM = pl.BlockSpec(memory_space=pltpu.VMEM)
LANES = 128
BLOCKS = 4
SMALL_ROWS = 16
BIAS_ROWS = BIAS // D

SHAPES = {
    "tokens": ((ROW, D), BF),
    "qkv": ((ROW, 3 * D), BF),
    "probs": ((PAIRS, 2, 2 * HALF, HALF), BF),
    "context": ((ROW, D), BF),
    "hidden": ((ROW, D), BF),
    "unit1": ((ROW, D), F32),
    "scale1": ((ROW, LANES), F32),
    "active": ((ROW, FF), BF),
    "slope": ((ROW, FF), BF),
    "unit2": ((ROW, D), F32),
    "scale2": ((ROW, LANES), F32),
    "down_side": ((ROW, D), BF),
    "attended": ((ROW, D), BF),
    "sum1": ((ROW, D), F32),
    "result": ((ROW, D), BF),
    "grad": ((ROW, D), BF),
    "ffn_sums": ((16, D), F32),
    "attn_sums": ((8, D), F32),
}
PIECES = {"first": (BLOCKS, D, D), "up": (BLOCKS, D, D), "down": (FF, D)}
PART_PIECE = {"attn": "first", "up": "up", "down": "down"}
MAKES = {
    "attn": ("tokens", "qkv", "probs", "context", "unit1", "scale1", "hidden"),
    "up": ("active", "slope"),
    "down": ("unit2", "scale2", "result"),
}
TAKES = {"attn": (), "up": ("hidden",), "down": ("unit1", "active")}
BACK_MAKES = {
    "ffn": ("down_side", "slope", "attended", "ffn_sums"),
    "attn": ("qkv", "attn_sums", "grad"),
}
BACK_PASSES = {"ffn": ("sum1",), "attn": ()}
BACK_TAKES = {
    "ffn": ("unit2", "scale2", "unit1", "scale1"),
    "attn": ("probs", "attended", "sum1"),
}
BACK_PIECES = {"ffn": ("down", "up"), "attn": ("first",)}


class Call:
    def __init__(self):
        self.operands, self.specs, self.in_names = [], [], []
        self.outs, self.out_specs, self.out_names = [], [], []
        self.scratch, self.scratch_names = [], []
        self.aliases = {}

    def give(self, name, value, spec):
        if spec is not SMEM:
            value = pltpu.with_memory_space_constraint(value, spec.memory_space)
        self.in_names.append(name)
        self.operands.append(value)
        self.specs.append(spec)

    def make(self, name, shape, kind, spec, old=None):
        if old is not None:
            self.aliases[len(self.operands)] = len(self.outs)
            self.give("old_" + name, old, spec)
        self.out_names.append(name)
        self.outs.append((pltpu.VMEM if spec is VMEM else pltpu.HBM)(shape, kind))
        self.out_specs.append(spec)

    def follow(self, values):
        for place, value in enumerate(values):
            self.give(("earlier", place), value, VMEM)

    def of_parts(self, parts, state, takes, makes, passes=None):
        inside = [key for part in parts for key in makes[part]]
        inside += [key for part in parts for key in (passes[part] if passes else ())]
        for part in parts:
            for key in takes[part]:
                if key not in inside:
                    self.give(key, state[key], VMEM)
        for part in parts:
            for key in makes[part]:
                self.make(key, *SHAPES[key], VMEM, state.get(key))
            for key in passes[part] if passes else ():
                if part == parts[-1]:
                    self.make(key, *SHAPES[key], VMEM)
                else:
                    self.hold(key, pltpu.VMEM(*SHAPES[key]))

    def hold(self, name, value):
        self.scratch_names.append(name)
        self.scratch.append(value)

    def run(self, kernel, name, time):
        names = self.in_names + self.out_names + self.scratch_names

        def named(*refs):
            kernel(dict(zip(names, refs)))

        found = pl.pallas_call(
            named,
            out_shape=self.outs,
            in_specs=self.specs,
            out_specs=self.out_specs,
            scratch_shapes=self.scratch,
            input_output_aliases=self.aliases,
            name=name,
            compiler_params=pltpu.CompilerParams(vmem_limit_bytes=VMEM_LIMIT),
            cost_estimate=pl.CostEstimate(
                flops=int(time * 1.1e9), bytes_accessed=1 << 20, transcendentals=0
            ),
        )(*self.operands)
        return dict(zip(self.out_names, found))


def rows_of(pieces, start, size):
    for piece in pieces:
        if start < piece.shape[0]:
            return piece[start : start + size]
        start -= piece.shape[0]


STREAMS = {
    "one": [("first", j) for j in range(BLOCKS)] + [("small", 0), ("down", 0)],
    "two": [("down", 1)] + [("up", j) for j in range(BLOCKS)],
}
FAR_CUT = {"one": 3, "two": 3}


def stream_sizes(stream, rows):
    size = {"first": rows, "up": rows, "small": SMALL_ROWS, "down": 2 * rows}
    return [size[name] for name, _ in STREAMS[stream]]


def place_kernel(plan, refs):
    get = refs.__getitem__
    stream, devices, own, swapped = plan
    table = get("table")
    rows = D // devices
    small = refs.get("small")
    if small is not None and "old_small" not in refs:
        small[...] = jnp.zeros(small.shape, F32)

    def put(place, pieces):
        device = table[place]
        start = 0
        for (name, block), size in zip(STREAMS[stream], stream_sizes(stream, rows)):
            part = rows_of(pieces, start, size)
            start += size
            if name == "down":
                at = pl.multiple_of(device * BLOCKS * rows + block * size, size)
                get("down")[pl.ds(at, size)] = part
            elif name != "small":
                get(name)[block, pl.ds(pl.multiple_of(device * rows, rows), rows)] = part
            elif small is not None:
                more = part.astype(F32)
                width = BIAS // devices
                per_row = D // width
                line = lax.broadcasted_iota(jnp.int32, (BIAS_ROWS, D), 0)
                lane_part = lax.broadcasted_iota(jnp.int32, (BIAS_ROWS, D), 1) // width
                mine = (line == device // per_row) & (lane_part == device % per_row)
                bias = jnp.concatenate([more[0:1, :width]] * per_row, axis=1)
                small[:BIAS_ROWS] += jnp.where(mine, bias, 0.0)
                small[BIAS_ROWS : BIAS_ROWS + 4] += more[1:5]

    for index, (place, count) in enumerate(own):
        pieces = [get(("shard", index, part)) for part in range(count)]
        put(place, pieces)
        if "packed" in refs:
            start = 0
            for piece in pieces:
                stop = start + piece.shape[0]
                get("packed")[index, start:stop] = piece[...]
                start = stop
    for index, place in enumerate(swapped):
        put(place, [get("came").at[index]])


def place_shards(
    stream, table, own, weights, came=None, swapped=(), small=False, earlier=(), pack=False
):
    call = Call()
    call.follow(earlier)
    call.give("table", table, SMEM)
    rows = sum(stream_sizes(stream, D // table.shape[0]))
    for index, (place, shard) in enumerate(own):
        for part, piece in enumerate(shard):
            call.give(("shard", index, part), piece, VMEM)
    if came is not None:
        call.give("came", came, VMEM)
    for key in ("first", "down") if stream == "one" else ("up", "down"):
        call.make(key, PIECES[key], BF, VMEM, weights.get(key))
    if small:
        call.make("small", (SMALL_ROWS, D), F32, VMEM, weights.get("small"))
    if pack:
        call.make("packed", (len(own), rows, D), BF, VMEM)
    counts = [(place, len(shard)) for place, shard in own]
    plan = (stream, table.shape[0], counts, swapped)
    found = call.run(partial(place_kernel, plan), "place_" + stream, 0.5)
    for key in ("first", "up", "down", "small"):
        if key in found:
            weights[key] = found[key]
    return found


def forward_kernel(origin, row, parts, refs):
    get = refs.__getitem__
    small = get("small")
    bias = lambda index: small[index : index + 1, :]
    gain = lambda index: bias(BIAS_ROWS + index)
    shift = lambda index: bias(BIAS_ROWS + 2 + index)
    section = get("section")[0]
    @pl.when(section == origin)
    def _():
        if "attn" in parts:
            tokens = get("source")[...]
            get("tokens")[...] = tokens
            qkv, probs, context, weight = get("qkv"), get("probs"), get("context"), get("first")
            penalty = segment_penalty(get("lengths"), row)
            for j in range(3):
                part = nn(tokens, weight[j])
                if j != 1:
                    part = part + bias(j // 2)
                qkv[:, chunk(j)] = part.astype(BF)
            masks = head_masks()
            for pair in range(PAIRS):
                at = pair * PAIR
                for half in range(2):
                    rows = chunk(half, HALF)
                    keys = by_head(qkv[rows, D + at : D + at + PAIR], masks)
                    scores = nt(keys, qkv[rows, at : at + PAIR]).reshape(2, HALF, HALF)
                    if half == 1:
                        scores = scores + penalty
                    peak = jnp.max(scores, axis=1, keepdims=True)
                    raised = jnp.exp((scores - peak) * HEAD_DIM ** (-0.5))
                    share = raised * (1.0 / jnp.sum(raised, axis=1, keepdims=True))
                    share = share.reshape(2 * HALF, HALF).astype(BF)
                    probs[pair, half] = share
                    values = by_head(qkv[rows, 2 * D + at : 2 * D + at + PAIR], masks)
                    context[rows, at : at + PAIR] = tn(share, values).astype(BF)
            attended = nn(context[...], weight[3]) + bias(2)
            unit, scale = standardize(tokens.astype(F32) + attended)
            get("unit1")[...] = unit
            get("scale1")[...] = jnp.broadcast_to(scale, (ROW, LANES))
            get("hidden")[...] = (unit * gain(0) + shift(0)).astype(BF)
        if "up" in parts:
            hidden, active, slope = get("hidden"), get("active"), get("slope")
            for j in range(FFC):
                inner = nn(hidden[...], get("up")[j]) + bias(3 + j)
                phi = 0.5 * (1.0 + lax.erf(inner * inv_sqrt2))
                active[:, chunk(j)] = (inner * phi).astype(BF)
                bell = jnp.exp(inner * inner * -0.5) * inv_sqrt2pi
                slope[:, chunk(j)] = (phi + inner * bell).astype(BF)
        if "down" in parts:
            normed = get("unit1")[...] * gain(0) + shift(0)
            total = normed + bias(7) + nn(get("active")[...], get("down")[...])
            unit, scale = standardize(total)
            get("result")[...] = (unit * gain(1) + shift(1)).astype(BF)
            get("unit2")[...] = unit
            get("scale2")[...] = jnp.broadcast_to(scale, (ROW, LANES))

    if "mark" in refs:
        get("mark")[...] = jnp.zeros((8, LANES), F32)


def forward(origin, row, parts, common, small, source, state, weights, marked=False, earlier=()):
    section, lengths = common
    call = Call()
    call.follow(earlier)
    call.give("section", section, SMEM)
    call.give("small", small, VMEM)
    if "attn" in parts:
        call.give("lengths", lengths, SMEM)
        call.give("source", source, VMEM)
    for part in parts:
        key = PART_PIECE[part]
        call.give(key, weights[key], VMEM)
    if marked:
        call.make("mark", (8, LANES), F32, VMEM)
    call.of_parts(parts, state, TAKES, MAKES)
    found = call.run(
        partial(forward_kernel, origin, row, parts),
        "forward_" + "_".join(parts),
        0.1 if marked else 3 * len(parts),
    )
    mark = found.pop("mark", None)
    state.update(found)
    return mark if marked else found.get("result")


def backward_kernel(origin, row, parts, refs):
    get = refs.__getitem__
    small = get("small")
    gain = lambda index: small[BIAS_ROWS + index : BIAS_ROWS + index + 1, :]

    @pl.when(get("section")[0] == origin)
    def _():
        if "ffn" in parts:
            grad = get("source")[...].astype(F32)
            sums, inner = get("ffn_sums"), get("slope")
            unit = get("unit2")[...]
            sums[1:2, :] = jnp.sum(grad * unit, axis=0, keepdims=True)
            sums[3:4, :] = jnp.sum(grad, axis=0, keepdims=True)
            grad = norm_back(grad, unit, get("scale2")[:, 0:1], gain(1))
            sums[9:10, :] = jnp.sum(grad, axis=0, keepdims=True)
            side = grad.astype(BF)
            get("down_side")[...] = side
            sum_v = get("sum_v")
            sum_v[...] = grad
            for j in range(FFC):
                through = nt(side, get("down")[chunk(j)])
                through = through * inner[:, chunk(j)].astype(F32)
                sums[5 + j : 6 + j, :] = jnp.sum(through, axis=0, keepdims=True)
                inner[:, chunk(j)] = through.astype(BF)
            grad = sum_v[...]
            for j in range(BLOCKS):
                grad = grad + nt(inner[:, chunk(j)], get("up")[j])
            unit = get("unit1")[...]
            sums[0:1, :] = jnp.sum(grad * unit, axis=0, keepdims=True)
            sums[2:3, :] = jnp.sum(grad, axis=0, keepdims=True)
            grad = norm_back(grad, unit, get("scale1")[:, 0:1], gain(0))
            sums[4:5, :] = jnp.sum(grad, axis=0, keepdims=True)
            sums[10:16, :] = jnp.zeros((6, D), F32)
            get("sum1")[...] = grad
            get("attended")[...] = grad.astype(BF)
        if "attn" in parts:
            weight = get("first")
            context_grad = nt(get("attended")[...], weight[3]).astype(BF)
            masks = head_masks()
            qkv, sums = get("qkv"), get("attn_sums")
            sums[2:8, :] = jnp.zeros((6, D), F32)
            for pair in range(PAIRS):
                at = pair * PAIR
                spans = [slice(which * D + at, which * D + at + PAIR) for which in range(3)]
                biases = [0.0, 0.0]
                for half in range(2):
                    rows = chunk(half, HALF)
                    queries = qkv[rows, spans[0]]
                    keys = by_head(qkv[rows, spans[1]], masks)
                    values = by_head(qkv[rows, spans[2]], masks)
                    pair_grad = context_grad[rows, at : at + PAIR]
                    share = get("probs")[pair, half]
                    wide = share.astype(F32)
                    weighted = wide * nt(values, pair_grad)
                    inner_sum = jnp.sum(weighted.reshape(2, HALF, HALF), axis=1, keepdims=True)
                    score_grad = weighted.reshape(2, HALF, HALF)
                    score_grad = score_grad - wide.reshape(2, HALF, HALF) * inner_sum
                    score_grad = (score_grad * HEAD_DIM ** (-0.5)).reshape(2 * HALF, HALF)
                    score_grad = score_grad.astype(BF)
                    grads = (
                        tn(score_grad, keys),
                        own_head(nn(score_grad, queries)),
                        own_head(nn(share, pair_grad)),
                    )
                    for span, value in zip(spans, grads):
                        qkv[rows, span] = value.astype(BF)
                    for line in range(2):
                        biases[line] = biases[line] + jnp.sum(
                            grads[2 * line], axis=0, keepdims=True
                        )
                for line in range(2):
                    sums[line : line + 1, at : at + PAIR] = biases[line]
            grad = get("sum1")[...]
            for j in range(3):
                grad = grad + nt(qkv[:, chunk(j)], weight[j])
            get("grad")[...] = grad.astype(BF)


def backward(origin, row, parts, common, small, source, state, weights, earlier=()):
    call = Call()
    call.follow(earlier)
    call.give("section", common[0], SMEM)
    call.give("small", small, VMEM)
    for part in parts:
        for key in BACK_PIECES[part]:
            call.give(key, weights[key], VMEM)
    if "ffn" in parts:
        call.give("source", source, VMEM)
        call.hold("sum_v", pltpu.VMEM((ROW, D), F32))
    call.of_parts(parts, state, BACK_TAKES, BACK_MAKES, BACK_PASSES)
    found = call.run(
        partial(backward_kernel, origin, row, parts), "backward_" + "_".join(parts), 5 * len(parts)
    )
    state.update(found)
    return found.get("grad")


def other_groups(groups):
    if groups == 1:
        return [("other0", (0,))]
    return [("other0", (7,)), ("other1", tuple(range(7)))]


def other_at(groups, place):
    for name, places in other_groups(groups):
        if place in places:
            return name, places.index(place)


WEIGHT_TAKES = {
    "down": ("active", "down_side"),
    "up": ("hidden", "slope"),
    "first": ("context", "attended", "tokens", "qkv"),
}


def product_of(piece, block, get):
    if piece == "down":
        return tn(get("active")[:, chunk(block)], get("down_side")[...])
    if piece == "up":
        return tn(get("hidden")[...], get("slope")[:, chunk(block)])
    if block == 3:
        return tn(get("context")[...], get("attended")[...])
    return tn(get("tokens")[...], get("qkv")[:, chunk(block)])


def first_row_kernel(piece, refs):
    for block in range(BLOCKS):
        product = product_of(piece, block, refs.__getitem__)
        refs["product"][block] = product.astype(BF)


def first_row_grad(piece, state, earlier):
    call = Call()
    call.follow(earlier)
    for key in WEIGHT_TAKES[piece]:
        call.give(key, state[key], VMEM)
    call.make("product", (BLOCKS, D, D), BF, VMEM)
    return call.run(partial(first_row_kernel, piece), "row_" + piece, 2)["product"]


def weight_kernel(piece, groups, refs):
    get = refs.__getitem__
    table, held = get("table"), get("held")
    rows = D // (2 * groups)

    def store(side, place, span, value):
        if side == 0:
            get("own")[place, span] = value
        else:
            name, index = other_at(groups, place)
            get(name)[index, span] = value

    def block_of(block):
        before = get("before")[block].astype(F32)
        return (before + product_of(piece, block, get)).astype(BF)

    places = [(place // groups, place % groups) for place in range(2 * groups)]
    if piece == "down":
        for block in range(BLOCKS):
            held[chunk(block)] = block_of(block)
        for side, place in places:
            at = pl.multiple_of(table[side * groups + place] * BLOCKS * rows, BLOCKS * rows)
            store(side, place, slice(None), held[pl.ds(at, BLOCKS * rows)])
        return
    if piece == "first" and groups > 1:
        sums, row = get("sums"), get("row_sums")
        bias_rows = [get(("attn_sums", 0))[k : k + 1] + get(("attn_sums", 1))[k : k + 1] for k in range(2)]
        ffn = get(("ffn_sums", 0))[...] + get(("ffn_sums", 1))[...]
        bias_rows += [ffn[4 + k : 5 + k] for k in range(6)]
        row[...] = jnp.zeros((SMALL_ROWS, D), F32)
        row[1:5, :] = ffn[:4]
        per_row = 2 * groups // BIAS_ROWS
        width = D // per_row
        for device in range(2 * groups):
            start = device % per_row * width
            row[0:1, :width] = bias_rows[device // per_row][:, start : start + width]
            sums[device] = row[...].astype(BF)
        for side, place in places:
            device = table[side * groups + place]
            store(side, place, slice(BLOCKS * rows, None), sums[device])
    for block in (3, 0, 1, 2):
        held[...] = block_of(block)
        for side, place in places:
            at = pl.multiple_of(table[side * groups + place] * rows, rows)
            store(side, place, chunk(block, rows), held[pl.ds(at, rows)])


def weight_grad(piece, groups, table, states, before, earlier=()):
    call = Call()
    call.follow(earlier)
    call.give("table", table, SMEM)
    call.give("before", before, VMEM)
    for key in WEIGHT_TAKES[piece]:
        call.give(key, states[1][key], VMEM)
    rows = BLOCKS * D // (2 * groups)
    if piece == "first":
        rows += SMALL_ROWS
        for key in ("attn_sums", "ffn_sums"):
            for row, state in enumerate(states):
                call.give((key, row), state[key], VMEM)
        call.hold("sums", pltpu.VMEM((2 * groups, SMALL_ROWS, D), BF))
        call.hold("row_sums", pltpu.VMEM((SMALL_ROWS, D), F32))
    call.make("own", (groups, rows, D), BF, VMEM)
    for name, places in other_groups(groups):
        call.make(name, (len(places), rows, D), BF, VMEM)
    call.hold("held", pltpu.VMEM((FF if piece == "down" else D, D), BF))
    found = call.run(partial(weight_kernel, piece, groups), "weight_" + piece, 3)
    return [found["own"]] + [found[name] for name, _ in other_groups(groups)]


CORES = 2
RING = (0, -1, 1, -2, 2, -3, 3, 4)


def ring_device(place, core):
    place = place % len(RING)
    z, y = (place, 0) if place < 4 else (7 - place, 1)
    return (z * 2 + y) * 2 + core


def ring_places():
    return [(place, core) for place in range(len(RING)) for core in range(CORES)]


def ring_table():
    rows = {}
    for place, core in ring_places():
        rows[ring_device(place, core)] = [
            [ring_device(place + ahead, core ^ side) for ahead in RING] for side in range(CORES)
        ]
    return np.array([rows[device] for device in range(len(rows))], np.int32)


def around(value, steps):
    pairs = [(ring_device(p, c), ring_device(p + steps, c)) for p, c in ring_places()]
    return lax.ppermute(value, "batch", pairs)


def to_other_core(value):
    pairs = [(ring_device(p, c), ring_device(p, 1 - c)) for p, c in ring_places()]
    return lax.ppermute(value, "batch", pairs)


def after(value, *earlier):
    return lax.optimization_barrier((value,) + earlier)[0]


def pack_kernel(refs):
    get = refs.__getitem__
    row, out = get("row"), {"one": get("one"), "two": get("two")}
    rows = get("out").shape[0]
    copies = Copies(get("sems"))
    small = [
        copies.start(get("bias"), get("bias_v")),
        copies.start(get("gains"), get("gains_v")),
        copies.start(get("shifts"), get("shifts_v")),
    ]
    arriving = []
    small_at = 0
    for stream, parts in STREAMS.items():
        start = 0
        for (name, block), size in zip(parts, stream_sizes(stream, rows)):
            target = out[stream].at[pl.ds(start, size)]
            if name == "small":
                small_at = start
            elif name == "down":
                source = get("down").at[pl.ds(block * size, size)]
                arriving.append(copies.start(source, target))
            elif name == "first" and block == 3:
                arriving.append(copies.start(get("out"), target))
            else:
                source = get("qkv" if name == "first" else "up").at[:, chunk(block)]
                arriving.append(copies.start(source, target))
            start += size
    row[...] = jnp.zeros((SMALL_ROWS, D), F32)
    for copy in small:
        copy.wait()
    row[1:3, :rows] = get("gains_v")[...].astype(F32)
    row[3:5, :rows] = get("shifts_v")[...].astype(F32)
    row[...] = pltpu.roll(row[...], get("device")[0] * rows, 1)
    row[0:1, : get("bias").shape[1]] = get("bias_v")[...].astype(F32)
    out["one"][small_at : small_at + SMALL_ROWS] = row[...].astype(BF)
    for copy in arriving:
        copy.wait()


def pack(scalars, qkv, out, up, down, bias, gains, shifts):
    call = Call()
    for name, value in scalars.items():
        call.give(name, value, SMEM)
    values = dict(qkv=qkv, out=out, up=up, down=down, bias=bias, gains=gains, shifts=shifts)
    for name, value in values.items():
        call.give(name, value, HBM)
    for stream in STREAMS:
        call.make(stream, (sum(stream_sizes(stream, out.shape[0])), D), BF, VMEM)
    call.hold("row", pltpu.VMEM((SMALL_ROWS, D), F32))
    for name in ("bias", "gains", "shifts"):
        call.hold(name + "_v", pltpu.VMEM(values[name].shape, BF))
    call.hold("sems", pltpu.SemaphoreType.DMA((16,)))
    found = call.run(pack_kernel, "pack", 1)
    return {stream: found[stream] for stream in STREAMS}


def cut_kernel(cut, refs):
    get = refs.__getitem__
    get(1)[...] = get("forwards")[:cut]
    get(-1)[...] = get("backwards")[cut:]


def cut_two(forwards, backwards, cut, earlier):
    call = Call()
    call.follow(earlier)
    call.give("forwards", forwards, VMEM)
    call.give("backwards", backwards, VMEM)
    call.make(1, (cut, D), BF, VMEM)
    call.make(-1, (forwards.shape[0] - cut, D), BF, VMEM)
    found = call.run(partial(cut_kernel, cut), "cut", 0.3)
    return found[1], found[-1]


def ring_gather(own, table, weights, rows, earlier):
    held = {stream: {0: (value,)} for stream, value in own.items()}

    def hop(stream, ahead):
        here = held[stream]
        here[-ahead] = (around(here[1 - ahead][0], 1),)
        here[ahead] = (around(here[ahead - 1][0], -1),)

    def put(stream, aheads):
        shards = [(RING.index(ahead), held[stream][ahead]) for ahead in aheads]
        found = place_shards(stream, table, shards, weights, small=stream == "one", pack=True)
        return found, to_other_core(found["packed"])

    def put_other(stream, aheads, came, earlier=()):
        places = [RING.index(ahead) + len(RING) for ahead in aheads]
        place_shards(stream, table, (), weights, came, places, stream == "one", earlier)

    for ahead in (1, 2, 3):
        for stream in STREAMS:
            hop(stream, ahead)
    for stream in STREAMS:
        here = held[stream]
        cut = sum(stream_sizes(stream, rows)[: FAR_CUT[stream]])
        sends = cut_two(here[-3][0], here[3][0], cut, earlier)
        here[4] = tuple(around(send, way) for send, way in zip(sends, (1, -1)))
    came = {stream: put(stream, RING)[1] for stream in STREAMS}
    put_other("one", RING, came["one"])
    return lambda mark: put_other("two", RING, came["two"], (mark,))


def both_cores(get, index, place, part=slice(None)):
    name, at = other_at(len(RING), place)
    other = get((name, index))[at, part].astype(F32)
    return get(("own", index))[place, part].astype(F32) + other


def far_kernel(index, cuts, refs):
    get = refs.__getitem__
    for way, part in cuts.items():
        get(way)[...] = both_cores(get, index, RING.index(4), part).astype(BF)


def merge_kernel(ahead, cut, count, refs):
    get = refs.__getitem__
    for way in (1, -1):
        out, came = get(way), get(("came", way))
        place = RING.index(way * ahead)
        parts = [both_cores(get, index, place) for index in range(count)]
        total = jnp.concatenate(parts, axis=0) if count > 1 else parts[0]
        if ahead < 3:
            out[...] = (total + came[...].astype(F32)).astype(BF)
        else:
            near, far = (slice(0, cut), slice(cut, None))[::way]
            out[near] = (total[near] + came[...].astype(F32)).astype(BF)
            out[far] = total[far].astype(BF)


def finish_kernel(piece, count, refs):
    get = refs.__getitem__
    copies, leaving = Copies(get("sems")), []

    def leave(name):
        leaving.append(copies.start(get(name + "_v"), get(name)))

    total = [both_cores(get, index, 0) for index in range(count)]
    total = jnp.concatenate(total, axis=0) if count > 1 else total[0]
    total = total + get(("came", 1))[...].astype(F32) + get(("came", -1))[...].astype(F32)
    if piece == "ffn":
        rows = get("up").shape[0]
        get("down_v")[...] = total[: BLOCKS * rows]
        leave("down")
        for j in range(BLOCKS):
            get("up_v")[:, chunk(j)] = total[chunk(BLOCKS + j, rows)]
        leave("up")
    else:
        rows = get("out").shape[0]
        for j in range(3):
            get("qkv_v")[:, chunk(j)] = total[chunk(j, rows)]
        leave("qkv")
        get("out_v")[...] = total[chunk(3, rows)]
        leave("out")
        small = total[BLOCKS * rows : BLOCKS * rows + 8]
        get("bias_v")[...] = small[:1, : get("bias").shape[1]]
        leave("bias")
        turned = pltpu.roll(small, lax.rem(D - get("device")[0] * rows, D), 1)
        get("gains_v")[...] = turned[1:3, :rows]
        leave("gains")
        get("shifts_v")[...] = turned[3:5, :rows]
        leave("shifts")
    for copy in leaving:
        copy.wait()


class RingScatter:
    order = ()

    def __init__(self, piece, cut):
        self.piece, self.cut, self.rows = piece, cut, 0
        self.parts, self.came = [], {}

    def run(self, call, kernel, name):
        call.follow(RingScatter.order)
        found = call.run(kernel, name + "_" + self.piece, 0.5)
        sent = [way for way in (1, -1) if way in found]
        RingScatter.order = (found[sent[0]],)
        self.came.update((way, around(found[way], way)) for way in sent)

    def add(self, own, others, cuts, late=()):
        index = len(self.parts)
        held = {"other0": to_other_core(others[0])}
        self.parts.append((own, held))
        self.rows += own.shape[1]
        call = Call()
        self.give(call, ("other0",), index)
        for way, part in cuts.items():
            call.make(way, (len(range(*part.indices(own.shape[1]))), D), BF, VMEM)
        self.run(call, partial(far_kernel, index, cuts), "far")
        earlier = late + tuple(self.came.values()) if late else (held["other0"],)
        held["other1"] = to_other_core(after(others[1], *earlier))

    def give(self, call, names, only=None):
        for index, (own, others) in enumerate(self.parts):
            if only in (None, index):
                call.give(("own", index), own, VMEM)
                for name in names:
                    call.give((name, index), others[name], VMEM)
        if only is None:
            for way in (1, -1):
                call.give(("came", way), self.came[way], VMEM)

    def step(self, ahead):
        call = Call()
        self.give(call, ("other1",))
        for way in (1, -1):
            call.make(way, (self.rows, D), BF, VMEM)
        self.run(call, partial(merge_kernel, ahead, self.cut, len(self.parts)), "merge")

    def finish(self, shapes, device):
        call = Call()
        self.give(call, ("other1",))
        call.give("device", device, SMEM)
        for name, shape in shapes.items():
            call.make(name, shape, F32, HBM)
            call.hold(name + "_v", pltpu.VMEM(shape, F32))
        call.hold("sems", pltpu.SemaphoreType.DMA((8,)))
        kernel = partial(finish_kernel, self.piece, len(self.parts))
        return call.run(kernel, "finish_" + self.piece, 1)


def turn_kernel(refs):
    for row in range(2):
        matrix = turn(refs["lengths"], row)
        for name in ("inputs", "cotangent"):
            refs[name, row][...] = nn(matrix, refs[name][row, 0]).astype(BF)


def turn_rows(lengths, inputs, cotangent):
    call = Call()
    call.give("lengths", lengths, SMEM)
    call.give("inputs", inputs, VMEM)
    call.give("cotangent", cotangent, VMEM)
    for name in ("inputs", "cotangent"):
        for row in range(2):
            call.make((name, row), (ROW, D), BF, VMEM)
    found = call.run(turn_kernel, "turn_rows", 1)
    return [[found[name, row] for row in range(2)] for name in ("inputs", "cotangent")]


def leave_kernel(refs):
    copies = Copies(refs["sems"])
    leaving = []
    for row in range(2):
        back = turn(refs["lengths"], row, True)
        for place, name in enumerate(("activations", "input_grads")):
            held = refs["held"].at[2 * row + place]
            held[...] = nn(back, refs[name, row][...]).astype(BF)
            leaving.append(copies.start(held, refs[name].at[row]))
    for copy in leaving:
        copy.wait()


def leave_rows(states, lengths, earlier=()):
    call = Call()
    call.follow(earlier)
    call.give("lengths", lengths, SMEM)
    for name, key in (("activations", "result"), ("input_grads", "grad")):
        for row, state in enumerate(states):
            call.give((name, row), state[key], VMEM)
        call.make(name, (2, ROW, D), BF, HBM)
    call.hold("held", pltpu.VMEM((4, ROW, D), BF))
    call.hold("sems", pltpu.SemaphoreType.DMA((4,)))
    return call.run(leave_kernel, "leave_rows", 1)


def relay(value, steps):
    count = lax.axis_size("section")
    first, last = (max(0, -steps), min(count, count - steps))
    return lax.ppermute(
        value, "section", [(source, source + steps) for source in range(first, last)]
    )


def body(
    inputs,
    cotangent,
    lengths,
    qkv_weight,
    out_weight,
    up_weight,
    down_weight,
    biases,
    norm_gains,
    norm_shifts,
):
    shards = lax.axis_size("batch")
    ring = shards == CORES * len(RING)
    groups = len(RING) if ring else 1
    width = D // shards
    cut = BIAS // shards
    device = lax.axis_index("batch")
    section = lax.axis_index("section").astype(jnp.int32).reshape(1)
    states, weights = ({}, {}), {}
    mine = device.astype(jnp.int32).reshape(1)
    RingScatter.order = ()
    if ring:
        table = jnp.asarray(ring_table().reshape(shards, -1))[device]
        own = pack(
            {"device": mine, "section": section, "table": table, "lengths": lengths[:, 0]},
            qkv_weight[0],
            out_weight[0],
            up_weight[0],
            down_weight[0],
            biases,
            norm_gains[0],
            norm_shifts[0],
        )
        inputs, cotangent = turn_rows(lengths[:, 0], inputs, cotangent)
        put_last = ring_gather(own, table, weights, width, inputs)
        small = weights["small"]
    else:
        table = jnp.array([0, 1], jnp.int32)
        gather = lambda value: lax.all_gather(value, "batch", axis=0, tiled=True)
        halves = [gather(value[0]) for value in (qkv_weight, out_weight, up_weight, down_weight)]
        blocks = lambda half: [half[:, chunk(j)] for j in range(half.shape[1] // D)]
        split = {"one": {}, "two": {}}
        for half, (qkv, out, up, down) in enumerate(
            zip(*(jnp.split(value, CORES) for value in halves))
        ):
            upper, lower = jnp.split(down, 2)
            gap = jnp.zeros((SMALL_ROWS, D), BF)
            split["one"][half] = (jnp.concatenate(blocks(qkv) + [out, gap, upper]),)
            split["two"][half] = (jnp.concatenate([lower] + blocks(up)),)
        place_shards("one", table, list(split["one"].items()), weights)
        put_last = lambda mark: place_shards("two", table, list(split["two"].items()), weights)
        norms = jnp.concatenate([norm_gains[0], norm_shifts[0]])
        packed = gather(jnp.concatenate([biases[0], norms.reshape(-1)])[None]).astype(F32)
        norms_all = packed[:, cut:].reshape(shards, 4, width).transpose(1, 0, 2)
        small = jnp.concatenate(
            [
                packed[:, :cut].reshape(BIAS_ROWS, D),
                norms_all.reshape(4, D),
                jnp.zeros((4, D), F32),
            ]
        )
    common = (section, lengths[:, 0])
    if not ring:
        inputs, cotangent = turn_rows(lengths[:, 0], inputs, cotangent)

    def run_forward(origin, row, source, parts=("attn", "up", "down"), marked=False, earlier=()):
        return forward(
            origin, row, parts, common, small, source, states[row], weights, marked, earlier
        )

    def run_backward(origin, row, source, parts=("ffn", "attn"), earlier=()):
        return backward(
            origin, row, parts, common, small, source, states[row], weights, earlier
        )

    mark = run_forward(0, 0, inputs[0], ("attn",), True)
    put_last(mark)
    run_forward(0, 0, None, ("up",))
    result = run_forward(0, 0, None, ("down",))
    coming = relay(result, 1)
    second = relay(run_forward(0, 1, inputs[1]), 1)
    run_forward(1, 0, coming)
    coming = relay(run_backward(1, 0, cotangent[0]), -1)
    run_forward(1, 1, second, earlier=(states[0]["attn_sums"],))
    second = relay(run_backward(1, 1, cotangent[1]), -1)
    run_backward(0, 0, coming)
    halves = {}
    earlier = ()
    for piece in ("down", "up", "first"):
        halves[piece] = first_row_grad(piece, states[0], earlier)
        earlier = (halves[piece],)
    run_backward(0, 1, second, ("ffn",), earlier)
    down_own, *down_others = weight_grad("down", groups, table, states, halves["down"])
    up_own, *up_others = weight_grad(
        "up", groups, table, states, halves["up"], (down_own,)
    )
    RingScatter.order = (up_own,)
    if ring:
        ffn_ring = RingScatter("ffn", BLOCKS * width)
        ffn_ring.add(down_own, down_others, {1: slice(None)})
        ffn_ring.add(up_own, up_others, {-1: slice(None)})
    run_backward(0, 1, None, ("attn",), RingScatter.order)
    attn_own, *attn_others = weight_grad(
        "first", groups, table, states, halves["first"]
    )
    if ring:
        RingScatter.order = (attn_own,)
        ffn_ring.step(3)
        attn_ring = RingScatter("attn", 2 * width)
        cuts = {1: slice(0, 2 * width), -1: slice(2 * width, None)}
        attn_ring.add(attn_own, attn_others, cuts, tuple(ffn_ring.came.values()))
        ffn_ring.step(2)
        attn_ring.step(3)
        ffn_ring.step(1)
        attn_ring.step(2)
        attn_ring.step(1)
        ffn = ffn_ring.finish({"down": (BLOCKS * width, D), "up": (width, FF)}, mine)
        down_sum, up_sum = ffn["down"], ffn["up"]
        shapes = {"qkv": (width, 3 * D), "out": (width, D), "bias": (1, cut)}
        shapes.update({"gains": (2, width), "shifts": (2, width)})
        attn = attn_ring.finish(shapes, mine)
        qkv_sum, out_sum, bias_sum = attn["qkv"], attn["out"], attn["bias"]
        gain_sum, shift_sum = attn["gains"], attn["shifts"]
    else:
        scatter = lambda value: lax.psum_scatter(
            value, "batch", scatter_dimension=0, tiled=True
        ).astype(F32)
        half = D // CORES
        join = lambda parts: jnp.concatenate(
            [
                jnp.concatenate([part[0, chunk(j, half)] for part in parts])
                for j in range(BLOCKS)
            ],
            axis=1,
        )
        down_sum = scatter(jnp.concatenate([down_own[0], down_others[0][0]]))
        up_sum = scatter(join((up_own, up_others[0])))
        attn_sum = scatter(join((attn_own, attn_others[0])))
        qkv_sum, out_sum = attn_sum[:, : 3 * D], attn_sum[:, 3 * D :]
        ffn_sums = states[0]["ffn_sums"] + states[1]["ffn_sums"]
        attn_sums = states[0]["attn_sums"] + states[1]["attn_sums"]
        bias_total = jnp.concatenate([attn_sums[:2], ffn_sums[4:10]]).reshape(shards, cut)
        norm_rows = ffn_sums[:4].reshape(4, shards, width).transpose(1, 0, 2)
        small_sum = scatter(
            jnp.concatenate([bias_total, norm_rows.reshape(shards, 4 * width)], axis=1)
        )
        bias_sum = small_sum[:, :cut]
        norm_sum = small_sum[:, cut:].reshape(4, width)
        gain_sum, shift_sum = norm_sum[:2], norm_sum[2:]
    rows = leave_rows(states, lengths[:, 0], RingScatter.order if ring else ())
    return (
        rows["activations"][None, :, None],
        rows["input_grads"][None, :, None],
        qkv_sum[None],
        out_sum[None],
        up_sum[None],
        down_sum[None],
        bias_sum,
        gain_sum[None],
        shift_sum[None],
    )


def solution(mesh):
    in_specs = (
        P(None, "batch", None, None),
        P(None, "batch", None, None),
        P(None, "batch", None),
        P("section", "batch", None),
        P("section", "batch", None),
        P("section", "batch", None),
        P("section", "batch", None),
        P("section", "batch"),
        P("section", None, "batch"),
        P("section", None, "batch"),
    )
    out_specs = (
        P("section", None, "batch", None, None),
        P("section", None, "batch", None, None),
        P("section", "batch", None),
        P("section", "batch", None),
        P("section", "batch", None),
        P("section", "batch", None),
        P("section", "batch"),
        P("section", None, "batch"),
        P("section", None, "batch"),
    )
    return jax.shard_map(body, mesh=mesh, in_specs=in_specs, out_specs=out_specs, check_vma=False)
```

```python
from functools import partial

import jax
import jax.numpy as jnp
import numpy as np
from jax import lax
from jax.experimental import pallas as pl
from jax.experimental.pallas import tpu as pltpu
from jax.sharding import PartitionSpec as P

D = 768
HEADS = 12
FF = 3072
HEAD_DIM = 64
ROW = 256
HALF = 128
PAIRS = HEADS // 2
PAIR = 2 * HEAD_DIM
FFC = FF // D
BIAS = 6144
VMEM_LIMIT = 10 * 1024 * 1024

BF = jnp.bfloat16
F32 = jnp.float32
epsilon = 1e-12
masked_value = -1e30
inv_sqrt2 = 0.7071067811865476
inv_sqrt2pi = 0.3989422804014327


def nn(a, b):
    return jnp.dot(a, b, preferred_element_type=F32)


def nt(a, b):
    return lax.dot_general(a, b, (((1,), (1,)), ((), ())), preferred_element_type=F32)


def tn(a, b):
    return lax.dot_general(a, b, (((0,), (0,)), ((), ())), preferred_element_type=F32)


def head_masks():
    lane = lax.broadcasted_iota(jnp.int32, (1, PAIR), 1)
    low = (lane < HEAD_DIM).astype(F32)
    return (low.astype(BF), (1.0 - low).astype(BF))


def by_head(values, masks):
    return jnp.concatenate([values * masks[0], values * masks[1]], axis=0)


def own_head(values):
    lane = lax.broadcasted_iota(jnp.int32, (1, PAIR), 1)
    return jnp.where(lane < HEAD_DIM, values[:HALF], values[HALF:])


def bounds_of(lengths_ref, micro):
    first = lengths_ref[micro, 0]
    second = first + lengths_ref[micro, 1]
    return first, second, second + lengths_ref[micro, 2]


def longest_start(lengths_ref, micro):
    bounds = bounds_of(lengths_ref, micro)
    start = jnp.int32(0)
    for place, bound in enumerate(bounds):
        start = jnp.where(lengths_ref[micro, place + 1] == HALF, bound, start)
    return start


def turn(lengths_ref, micro, back=False):
    start = longest_start(lengths_ref, micro)
    here = lax.broadcasted_iota(jnp.int32, (ROW, ROW), 0)
    there = lax.broadcasted_iota(jnp.int32, (ROW, ROW), 1)
    if back:
        here, there = there, here
    return jnp.where((here + start) & (ROW - 1) == there, 1.0, 0.0).astype(BF)


def segment_penalty(lengths_ref, micro):
    bounds = bounds_of(lengths_ref, micro)
    start = longest_start(lengths_ref, micro)

    def number(axis):
        place = lax.broadcasted_iota(jnp.int32, (HALF, HALF), axis)
        place = (place + start + HALF) & (ROW - 1)
        total = jnp.zeros((HALF, HALF), jnp.int32)
        for bound in bounds:
            total = total + jnp.where(place >= bound, 1, 0)
        return total

    return jnp.where(number(0) == number(1), 0.0, masked_value)


def standardize(values):
    centred = values - jnp.mean(values, axis=-1, keepdims=True)
    spread = jnp.mean(centred * centred, axis=-1, keepdims=True)
    scale = lax.rsqrt(spread + epsilon)
    return centred * scale, scale


def norm_back(grad, unit, scale, gain):
    scaled = grad * gain
    mean_one = jnp.mean(scaled, axis=-1, keepdims=True)
    mean_two = jnp.mean(scaled * unit, axis=-1, keepdims=True)
    return scale * (scaled - mean_one - unit * mean_two)


class Copies:
    def __init__(self, sems):
        self.sems = sems
        self.used = 0

    def start(self, src, dst):
        copy = pltpu.make_async_copy(src, dst, self.sems.at[self.used])
        self.used += 1
        copy.start()
        return copy


class Reader:
    def __init__(self, refs):
        self.refs = list(refs)

    def take(self, count=None):
        if count is None:
            return self.refs.pop(0)
        taken, self.refs = self.refs[:count], self.refs[count:]
        return taken


def chunk(index, size=D):
    return slice(index * size, (index + 1) * size)


HBM = pl.BlockSpec(memory_space=pltpu.HBM)
SMEM = pl.BlockSpec(memory_space=pltpu.SMEM)
VMEM = pl.BlockSpec(memory_space=pltpu.VMEM)
LANES = 128
BLOCKS = 4
SMALL_ROWS = 16
BIAS_ROWS = BIAS // D

SHAPES = {
    "tokens": ((ROW, D), BF),
    "qkv": ((ROW, 3 * D), BF),
    "probs": ((PAIRS, 2, 2 * HALF, HALF), BF),
    "context": ((ROW, D), BF),
    "hidden": ((ROW, D), BF),
    "unit1": ((ROW, D), F32),
    "scale1": ((ROW, LANES), F32),
    "active": ((ROW, FF), BF),
    "slope": ((ROW, FF), BF),
    "unit2": ((ROW, D), F32),
    "scale2": ((ROW, LANES), F32),
    "down_side": ((ROW, D), BF),
    "attended": ((ROW, D), BF),
    "sum1": ((ROW, D), F32),
    "result": ((ROW, D), BF),
    "grad": ((ROW, D), BF),
    "ffn_sums": ((16, D), F32),
    "attn_sums": ((8, D), F32),
}
PIECES = {"first": (BLOCKS, D, D), "up": (BLOCKS, D, D), "down": (FF, D)}
PART_PIECE = {"attn": "first", "up": "up", "down": "down"}
MAKES = {
    "attn": ("tokens", "qkv", "probs", "context", "unit1", "scale1", "hidden"),
    "up": ("active", "slope"),
    "down": ("unit2", "scale2", "result"),
}
TAKES = {"attn": (), "up": ("hidden",), "down": ("unit1", "active")}
BACK_MAKES = {
    "ffn": ("down_side", "slope", "attended", "ffn_sums"),
    "attn": ("qkv", "attn_sums", "grad"),
}
BACK_PASSES = {"ffn": ("sum1",), "attn": ()}
BACK_TAKES = {
    "ffn": ("unit2", "scale2", "unit1", "scale1"),
    "attn": ("probs", "attended", "sum1"),
}
BACK_PIECES = {"ffn": ("down", "up"), "attn": ("first",)}


class Call:
    def __init__(self):
        self.operands, self.specs, self.in_names = [], [], []
        self.outs, self.out_specs, self.out_names = [], [], []
        self.scratch, self.scratch_names = [], []
        self.aliases = {}

    def give(self, name, value, spec):
        if spec is not SMEM:
            value = pltpu.with_memory_space_constraint(value, spec.memory_space)
        self.in_names.append(name)
        self.operands.append(value)
        self.specs.append(spec)

    def make(self, name, shape, kind, spec, old=None):
        if old is not None:
            self.aliases[len(self.operands)] = len(self.outs)
            self.give("old_" + name, old, spec)
        self.out_names.append(name)
        self.outs.append((pltpu.VMEM if spec is VMEM else pltpu.HBM)(shape, kind))
        self.out_specs.append(spec)

    def follow(self, values):
        for place, value in enumerate(values):
            self.give(("earlier", place), value, VMEM)

    def of_parts(self, parts, state, takes, makes, passes=None):
        inside = [key for part in parts for key in makes[part]]
        inside += [key for part in parts for key in (passes[part] if passes else ())]
        for part in parts:
            for key in takes[part]:
                if key not in inside:
                    self.give(key, state[key], VMEM)
        for part in parts:
            for key in makes[part]:
                self.make(key, *SHAPES[key], VMEM, state.get(key))
            for key in passes[part] if passes else ():
                if part == parts[-1]:
                    self.make(key, *SHAPES[key], VMEM)
                else:
                    self.hold(key, pltpu.VMEM(*SHAPES[key]))

    def hold(self, name, value):
        self.scratch_names.append(name)
        self.scratch.append(value)

    def run(self, kernel, name, time):
        names = self.in_names + self.out_names + self.scratch_names

        def named(*refs):
            kernel(dict(zip(names, refs)))

        found = pl.pallas_call(
            named,
            out_shape=self.outs,
            in_specs=self.specs,
            out_specs=self.out_specs,
            scratch_shapes=self.scratch,
            input_output_aliases=self.aliases,
            name=name,
            compiler_params=pltpu.CompilerParams(vmem_limit_bytes=VMEM_LIMIT),
            cost_estimate=pl.CostEstimate(
                flops=int(time * 1.1e9), bytes_accessed=1 << 20, transcendentals=0
            ),
        )(*self.operands)
        return dict(zip(self.out_names, found))


def rows_of(pieces, start, size):
    for piece in pieces:
        if start < piece.shape[0]:
            return piece[start : start + size]
        start -= piece.shape[0]


STREAMS = {
    "one": [("first", j) for j in range(BLOCKS)] + [("small", 0), ("down", 0)],
    "two": [("up", j) for j in range(BLOCKS)] + [("down", 1)],
}
EARLY = {"one": BLOCKS + 1, "two": BLOCKS}
FAR_CUT = {"one": 3, "two": 3}


def stream_sizes(stream, rows):
    size = {"first": rows, "up": rows, "small": SMALL_ROWS, "down": 2 * rows}
    return [size[name] for name, _ in STREAMS[stream]]


def place_kernel(plan, refs):
    get = refs.__getitem__
    devices, stream, own, came = plan
    table = get("table")
    rows = D // devices
    small = refs.get("small")
    if small is not None and "old_small" not in refs:
        small[...] = jnp.zeros(small.shape, F32)

    def put(stream, entries, place, pieces):
        device = table[place]
        start = 0
        sizes = stream_sizes(stream, rows)[entries]
        for (name, block), size in zip(STREAMS[stream][entries], sizes):
            part = rows_of(pieces, start, size)
            start += size
            if name == "down":
                at = pl.multiple_of(device * BLOCKS * rows + block * size, size)
                get("down")[pl.ds(at, size)] = part
            elif name != "small":
                get(name)[block, pl.ds(pl.multiple_of(device * rows, rows), rows)] = part
            elif small is not None:
                more = part.astype(F32)
                width = BIAS // devices
                per_row = D // width
                line = lax.broadcasted_iota(jnp.int32, (BIAS_ROWS, D), 0)
                lane_part = lax.broadcasted_iota(jnp.int32, (BIAS_ROWS, D), 1) // width
                mine = (line == device // per_row) & (lane_part == device % per_row)
                bias = jnp.concatenate([more[0:1, :width]] * per_row, axis=1)
                small[:BIAS_ROWS] += jnp.where(mine, bias, 0.0)
                small[BIAS_ROWS : BIAS_ROWS + 4] += more[1:5]

    for index, (place, count) in enumerate(own):
        pieces = [get(("shard", index, part)) for part in range(count)]
        put(stream, slice(None), place, pieces)
        if ("packed", 0) in refs:
            edge = sum(stream_sizes(stream, rows)[: EARLY[stream]])
            start = 0
            for piece in pieces:
                stop = start + piece.shape[0]
                middle = min(max(edge, start), stop)
                if middle > start:
                    get(("packed", 0))[index, start:middle] = piece[: middle - start]
                if middle < stop:
                    get(("packed", 1))[index, middle - edge : stop - edge] = piece[middle - start :]
                start = stop
    for number, (stream, entries) in enumerate(came):
        for index in range(len(RING)):
            put(stream, entries, index + len(RING), [get(("came", number)).at[index]])


def place_shards(stream, table, own, weights, made, came=(), earlier=(), pack=False):
    call = Call()
    call.follow(earlier)
    call.give("table", table, SMEM)
    for index, (place, shard) in enumerate(own):
        for part, piece in enumerate(shard):
            call.give(("shard", index, part), piece, VMEM)
    for number, (value, _, _) in enumerate(came):
        call.give(("came", number), value, VMEM)
    for key in made:
        if key == "small":
            call.make(key, (SMALL_ROWS, D), F32, VMEM, weights.get(key))
        else:
            call.make(key, PIECES[key], BF, VMEM, weights.get(key))
    if pack:
        sizes = stream_sizes(stream, D // table.shape[0])
        for number, part in enumerate((sizes[: EARLY[stream]], sizes[EARLY[stream] :])):
            call.make(("packed", number), (len(own), sum(part), D), BF, VMEM)
    counts = [(place, len(shard)) for place, shard in own]
    plan = (table.shape[0], stream, counts, [spec[1:] for spec in came])
    found = call.run(partial(place_kernel, plan), "place_" + "_".join(made), 0.5)
    weights.update((key, found[key]) for key in made)
    return [found[key] for key in found if key not in made]


def forward_kernel(origin, row, parts, refs):
    get = refs.__getitem__
    small = get("small")
    bias = lambda index: small[index : index + 1, :]
    gain = lambda index: bias(BIAS_ROWS + index)
    shift = lambda index: bias(BIAS_ROWS + 2 + index)
    section = get("section")[0]
    @pl.when(section == origin)
    def _():
        if "attn" in parts:
            tokens = get("source")[...]
            get("tokens")[...] = tokens
            qkv, probs, context, weight = get("qkv"), get("probs"), get("context"), get("first")
            penalty = segment_penalty(get("lengths"), row)
            for j in range(3):
                part = nn(tokens, weight[j])
                if j != 1:
                    part = part + bias(j // 2)
                qkv[:, chunk(j)] = part.astype(BF)
            masks = head_masks()
            for pair in range(PAIRS):
                at = pair * PAIR
                for half in range(2):
                    rows = chunk(half, HALF)
                    keys = by_head(qkv[rows, D + at : D + at + PAIR], masks)
                    scores = nt(keys, qkv[rows, at : at + PAIR]).reshape(2, HALF, HALF)
                    if half == 1:
                        scores = scores + penalty
                    peak = jnp.max(scores, axis=1, keepdims=True)
                    raised = jnp.exp((scores - peak) * HEAD_DIM ** (-0.5))
                    share = raised * (1.0 / jnp.sum(raised, axis=1, keepdims=True))
                    share = share.reshape(2 * HALF, HALF).astype(BF)
                    probs[pair, half] = share
                    values = by_head(qkv[rows, 2 * D + at : 2 * D + at + PAIR], masks)
                    context[rows, at : at + PAIR] = tn(share, values).astype(BF)
            attended = nn(context[...], weight[3]) + bias(2)
            unit, scale = standardize(tokens.astype(F32) + attended)
            get("unit1")[...] = unit
            get("scale1")[...] = jnp.broadcast_to(scale, (ROW, LANES))
            get("hidden")[...] = (unit * gain(0) + shift(0)).astype(BF)
        if "up" in parts:
            hidden, active, slope = get("hidden"), get("active"), get("slope")
            for j in range(FFC):
                inner = nn(hidden[...], get("up")[j]) + bias(3 + j)
                phi = 0.5 * (1.0 + lax.erf(inner * inv_sqrt2))
                active[:, chunk(j)] = (inner * phi).astype(BF)
                bell = jnp.exp(inner * inner * -0.5) * inv_sqrt2pi
                slope[:, chunk(j)] = (phi + inner * bell).astype(BF)
        if "down" in parts:
            normed = get("unit1")[...] * gain(0) + shift(0)
            total = normed + bias(7) + nn(get("active")[...], get("down")[...])
            unit, scale = standardize(total)
            get("result")[...] = (unit * gain(1) + shift(1)).astype(BF)
            get("unit2")[...] = unit
            get("scale2")[...] = jnp.broadcast_to(scale, (ROW, LANES))

    if "mark" in refs:
        get("mark")[...] = jnp.zeros((8, LANES), F32)


def forward(origin, row, parts, common, small, source, state, weights, marked=False, earlier=()):
    section, lengths = common
    call = Call()
    call.follow(earlier)
    call.give("section", section, SMEM)
    call.give("small", small, VMEM)
    if "attn" in parts:
        call.give("lengths", lengths, SMEM)
        call.give("source", source, VMEM)
    for part in parts:
        key = PART_PIECE[part]
        call.give(key, weights[key], VMEM)
    if marked:
        call.make("mark", (8, LANES), F32, VMEM)
    call.of_parts(parts, state, TAKES, MAKES)
    found = call.run(
        partial(forward_kernel, origin, row, parts),
        "forward_" + "_".join(parts),
        0.1 if marked else 3 * len(parts),
    )
    mark = found.pop("mark", None)
    state.update(found)
    return mark if marked else found.get("result")


def backward_kernel(origin, row, parts, refs):
    get = refs.__getitem__
    small = get("small")
    gain = lambda index: small[BIAS_ROWS + index : BIAS_ROWS + index + 1, :]

    @pl.when(get("section")[0] == origin)
    def _():
        if "ffn" in parts:
            grad = get("source")[...].astype(F32)
            sums, inner = get("ffn_sums"), get("slope")
            unit = get("unit2")[...]
            sums[1:2, :] = jnp.sum(grad * unit, axis=0, keepdims=True)
            sums[3:4, :] = jnp.sum(grad, axis=0, keepdims=True)
            grad = norm_back(grad, unit, get("scale2")[:, 0:1], gain(1))
            sums[9:10, :] = jnp.sum(grad, axis=0, keepdims=True)
            side = grad.astype(BF)
            get("down_side")[...] = side
            sum_v = get("sum_v")
            sum_v[...] = grad
            for j in range(FFC):
                through = nt(side, get("down")[chunk(j)])
                through = through * inner[:, chunk(j)].astype(F32)
                sums[5 + j : 6 + j, :] = jnp.sum(through, axis=0, keepdims=True)
                inner[:, chunk(j)] = through.astype(BF)
            grad = sum_v[...]
            for j in range(BLOCKS):
                grad = grad + nt(inner[:, chunk(j)], get("up")[j])
            unit = get("unit1")[...]
            sums[0:1, :] = jnp.sum(grad * unit, axis=0, keepdims=True)
            sums[2:3, :] = jnp.sum(grad, axis=0, keepdims=True)
            grad = norm_back(grad, unit, get("scale1")[:, 0:1], gain(0))
            sums[4:5, :] = jnp.sum(grad, axis=0, keepdims=True)
            sums[10:16, :] = jnp.zeros((6, D), F32)
            get("sum1")[...] = grad
            get("attended")[...] = grad.astype(BF)
        if "attn" in parts:
            weight = get("first")
            context_grad = nt(get("attended")[...], weight[3]).astype(BF)
            masks = head_masks()
            qkv, sums = get("qkv"), get("attn_sums")
            sums[2:8, :] = jnp.zeros((6, D), F32)
            for pair in range(PAIRS):
                at = pair * PAIR
                spans = [slice(which * D + at, which * D + at + PAIR) for which in range(3)]
                biases = [0.0, 0.0]
                for half in range(2):
                    rows = chunk(half, HALF)
                    queries = qkv[rows, spans[0]]
                    keys = by_head(qkv[rows, spans[1]], masks)
                    values = by_head(qkv[rows, spans[2]], masks)
                    pair_grad = context_grad[rows, at : at + PAIR]
                    share = get("probs")[pair, half]
                    wide = share.astype(F32)
                    weighted = wide * nt(values, pair_grad)
                    inner_sum = jnp.sum(weighted.reshape(2, HALF, HALF), axis=1, keepdims=True)
                    score_grad = weighted.reshape(2, HALF, HALF)
                    score_grad = score_grad - wide.reshape(2, HALF, HALF) * inner_sum
                    score_grad = (score_grad * HEAD_DIM ** (-0.5)).reshape(2 * HALF, HALF)
                    score_grad = score_grad.astype(BF)
                    grads = (
                        tn(score_grad, keys),
                        own_head(nn(score_grad, queries)),
                        own_head(nn(share, pair_grad)),
                    )
                    for span, value in zip(spans, grads):
                        qkv[rows, span] = value.astype(BF)
                    for line in range(2):
                        biases[line] = biases[line] + jnp.sum(
                            grads[2 * line], axis=0, keepdims=True
                        )
                for line in range(2):
                    sums[line : line + 1, at : at + PAIR] = biases[line]
            grad = get("sum1")[...]
            for j in range(3):
                grad = grad + nt(qkv[:, chunk(j)], weight[j])
            get("grad")[...] = grad.astype(BF)


def backward(origin, row, parts, common, small, source, state, weights, earlier=()):
    call = Call()
    call.follow(earlier)
    call.give("section", common[0], SMEM)
    call.give("small", small, VMEM)
    for part in parts:
        for key in BACK_PIECES[part]:
            call.give(key, weights[key], VMEM)
    if "ffn" in parts:
        call.give("source", source, VMEM)
        call.hold("sum_v", pltpu.VMEM((ROW, D), F32))
    call.of_parts(parts, state, BACK_TAKES, BACK_MAKES, BACK_PASSES)
    found = call.run(
        partial(backward_kernel, origin, row, parts), "backward_" + "_".join(parts), 5 * len(parts)
    )
    state.update(found)
    return found.get("grad")


def other_groups(groups):
    if groups == 1:
        return [("other0", (0,))]
    return [("other0", (7,)), ("other1", tuple(range(7)))]


def other_at(groups, place):
    for name, places in other_groups(groups):
        if place in places:
            return name, places.index(place)


WEIGHT_TAKES = {
    "down": ("active", "down_side"),
    "up": ("hidden", "slope"),
    "first": ("context", "attended", "tokens", "qkv"),
}


def product_of(piece, block, get):
    if piece == "down":
        return tn(get("active")[:, chunk(block)], get("down_side")[...])
    if piece == "up":
        return tn(get("hidden")[...], get("slope")[:, chunk(block)])
    if block == 3:
        return tn(get("context")[...], get("attended")[...])
    return tn(get("tokens")[...], get("qkv")[:, chunk(block)])


def first_row_kernel(piece, refs):
    for block in range(BLOCKS):
        product = product_of(piece, block, refs.__getitem__)
        refs["product"][block] = product.astype(BF)


def first_row_grad(piece, state, earlier):
    call = Call()
    call.follow(earlier)
    for key in WEIGHT_TAKES[piece]:
        call.give(key, state[key], VMEM)
    call.make("product", (BLOCKS, D, D), BF, VMEM)
    return call.run(partial(first_row_kernel, piece), "row_" + piece, 2)["product"]


def weight_kernel(piece, groups, refs):
    get = refs.__getitem__
    table, held = get("table"), get("held")
    rows = D // (2 * groups)

    def store(side, place, span, value):
        if side == 0:
            get("own")[place, span] = value
        else:
            name, index = other_at(groups, place)
            get(name)[index, span] = value

    def block_of(block):
        before = get("before")[block].astype(F32)
        return (before + product_of(piece, block, get)).astype(BF)

    places = [(place // groups, place % groups) for place in range(2 * groups)]
    if piece == "down":
        for block in range(BLOCKS):
            held[chunk(block)] = block_of(block)
        for side, place in places:
            at = pl.multiple_of(table[side * groups + place] * BLOCKS * rows, BLOCKS * rows)
            store(side, place, slice(None), held[pl.ds(at, BLOCKS * rows)])
        return
    if piece == "first" and groups > 1:
        sums, row = get("sums"), get("row_sums")
        bias_rows = [get(("attn_sums", 0))[k : k + 1] + get(("attn_sums", 1))[k : k + 1] for k in range(2)]
        ffn = get(("ffn_sums", 0))[...] + get(("ffn_sums", 1))[...]
        bias_rows += [ffn[4 + k : 5 + k] for k in range(6)]
        row[...] = jnp.zeros((SMALL_ROWS, D), F32)
        row[1:5, :] = ffn[:4]
        per_row = 2 * groups // BIAS_ROWS
        width = D // per_row
        for device in range(2 * groups):
            start = device % per_row * width
            row[0:1, :width] = bias_rows[device // per_row][:, start : start + width]
            sums[device] = row[...].astype(BF)
        for side, place in places:
            device = table[side * groups + place]
            store(side, place, slice(BLOCKS * rows, None), sums[device])
    for block in (3, 0, 1, 2):
        held[...] = block_of(block)
        for side, place in places:
            at = pl.multiple_of(table[side * groups + place] * rows, rows)
            store(side, place, chunk(block, rows), held[pl.ds(at, rows)])


def weight_grad(piece, groups, table, states, before, earlier=()):
    call = Call()
    call.follow(earlier)
    call.give("table", table, SMEM)
    call.give("before", before, VMEM)
    for key in WEIGHT_TAKES[piece]:
        call.give(key, states[1][key], VMEM)
    rows = BLOCKS * D // (2 * groups)
    if piece == "first":
        rows += SMALL_ROWS
        for key in ("attn_sums", "ffn_sums"):
            for row, state in enumerate(states):
                call.give((key, row), state[key], VMEM)
        call.hold("sums", pltpu.VMEM((2 * groups, SMALL_ROWS, D), BF))
        call.hold("row_sums", pltpu.VMEM((SMALL_ROWS, D), F32))
    call.make("own", (groups, rows, D), BF, VMEM)
    for name, places in other_groups(groups):
        call.make(name, (len(places), rows, D), BF, VMEM)
    call.hold("held", pltpu.VMEM((FF if piece == "down" else D, D), BF))
    found = call.run(partial(weight_kernel, piece, groups), "weight_" + piece, 3)
    return [found["own"]] + [found[name] for name, _ in other_groups(groups)]


CORES = 2
RING = (0, -1, 1, -2, 2, -3, 3, 4)


def ring_device(place, core):
    place = place % len(RING)
    z, y = (place, 0) if place < 4 else (7 - place, 1)
    return (z * 2 + y) * 2 + core


def ring_places():
    return [(place, core) for place in range(len(RING)) for core in range(CORES)]


def ring_table():
    rows = {}
    for place, core in ring_places():
        rows[ring_device(place, core)] = [
            [ring_device(place + ahead, core ^ side) for ahead in RING] for side in range(CORES)
        ]
    return np.array([rows[device] for device in range(len(rows))], np.int32)


def around(value, steps):
    pairs = [(ring_device(p, c), ring_device(p + steps, c)) for p, c in ring_places()]
    return lax.ppermute(value, "batch", pairs)


def to_other_core(value):
    pairs = [(ring_device(p, c), ring_device(p, 1 - c)) for p, c in ring_places()]
    return lax.ppermute(value, "batch", pairs)


def after(value, *earlier):
    return lax.optimization_barrier((value,) + earlier)[0]


def pack_kernel(refs):
    get = refs.__getitem__
    row, out = get("row"), {"one": get("one"), "two": get("two")}
    rows = get("out").shape[0]
    copies = Copies(get("sems"))
    small = [
        copies.start(get("bias"), get("bias_v")),
        copies.start(get("gains"), get("gains_v")),
        copies.start(get("shifts"), get("shifts_v")),
    ]
    arriving = []
    small_at = 0
    for stream, parts in STREAMS.items():
        start = 0
        for (name, block), size in zip(parts, stream_sizes(stream, rows)):
            target = out[stream].at[pl.ds(start, size)]
            if name == "small":
                small_at = start
            elif name == "down":
                source = get("down").at[pl.ds(block * size, size)]
                arriving.append(copies.start(source, target))
            elif name == "first" and block == 3:
                arriving.append(copies.start(get("out"), target))
            else:
                source = get("qkv" if name == "first" else "up").at[:, chunk(block)]
                arriving.append(copies.start(source, target))
            start += size
    row[...] = jnp.zeros((SMALL_ROWS, D), F32)
    for copy in small:
        copy.wait()
    row[1:3, :rows] = get("gains_v")[...].astype(F32)
    row[3:5, :rows] = get("shifts_v")[...].astype(F32)
    row[...] = pltpu.roll(row[...], get("device")[0] * rows, 1)
    row[0:1, : get("bias").shape[1]] = get("bias_v")[...].astype(F32)
    out["one"][small_at : small_at + SMALL_ROWS] = row[...].astype(BF)
    for copy in arriving:
        copy.wait()


def pack(scalars, qkv, out, up, down, bias, gains, shifts):
    call = Call()
    for name, value in scalars.items():
        call.give(name, value, SMEM)
    values = dict(qkv=qkv, out=out, up=up, down=down, bias=bias, gains=gains, shifts=shifts)
    for name, value in values.items():
        call.give(name, value, HBM)
    for stream in STREAMS:
        call.make(stream, (sum(stream_sizes(stream, out.shape[0])), D), BF, VMEM)
    call.hold("row", pltpu.VMEM((SMALL_ROWS, D), F32))
    for name in ("bias", "gains", "shifts"):
        call.hold(name + "_v", pltpu.VMEM(values[name].shape, BF))
    call.hold("sems", pltpu.SemaphoreType.DMA((16,)))
    found = call.run(pack_kernel, "pack", 1)
    return {stream: found[stream] for stream in STREAMS}


def cut_kernel(cut, refs):
    get = refs.__getitem__
    get(1)[...] = get("forwards")[:cut]
    get(-1)[...] = get("backwards")[cut:]


def cut_two(forwards, backwards, cut, earlier):
    call = Call()
    call.follow(earlier)
    call.give("forwards", forwards, VMEM)
    call.give("backwards", backwards, VMEM)
    call.make(1, (cut, D), BF, VMEM)
    call.make(-1, (forwards.shape[0] - cut, D), BF, VMEM)
    found = call.run(partial(cut_kernel, cut), "cut", 0.3)
    return found[1], found[-1]


def ring_gather(own, table, weights, rows, earlier):
    held = {stream: {0: (value,)} for stream, value in own.items()}

    def hop(stream, ahead):
        here = held[stream]
        here[-ahead] = (around(here[1 - ahead][0], 1),)
        here[ahead] = (around(here[ahead - 1][0], -1),)

    for ahead in (1, 2, 3):
        for stream in STREAMS:
            hop(stream, ahead)
    for stream in STREAMS:
        here = held[stream]
        cut = sum(stream_sizes(stream, rows)[: FAR_CUT[stream]])
        sends = cut_two(here[-3][0], here[3][0], cut, earlier)
        here[4] = tuple(around(send, way) for send, way in zip(sends, (1, -1)))
    came = {}
    for stream, made in (("one", ("first", "down", "small")), ("two", ("up", "down"))):
        shards = [(RING.index(ahead), held[stream][ahead]) for ahead in RING]
        packed = place_shards(stream, table, shards, weights, made, pack=True)
        came[stream] = [to_other_core(value) for value in packed]

    def put_other(made, streams, early, earlier=()):
        number = 0 if early else 1
        entries = {s: slice(0, EARLY[s]) if early else slice(EARLY[s], None) for s in streams}
        values = [(came[s][number], s, entries[s]) for s in streams]
        place_shards(None, table, (), weights, made, values, earlier)

    put_other(("first", "small"), ("one",), True)
    return (
        lambda mark: put_other(("up",), ("two",), True, (mark,)),
        lambda mark: put_other(("down",), ("one", "two"), False, (mark,)),
    )


def both_cores(get, index, place, part=slice(None)):
    name, at = other_at(len(RING), place)
    other = get((name, index))[at, part].astype(F32)
    return get(("own", index))[place, part].astype(F32) + other


def far_kernel(index, cuts, refs):
    get = refs.__getitem__
    for way, part in cuts.items():
        get(way)[...] = both_cores(get, index, RING.index(4), part).astype(BF)


def merge_kernel(ahead, cut, count, refs):
    get = refs.__getitem__
    for way in (1, -1):
        out, came = get(way), get(("came", way))
        place = RING.index(way * ahead)
        parts = [both_cores(get, index, place) for index in range(count)]
        total = jnp.concatenate(parts, axis=0) if count > 1 else parts[0]
        if ahead < 3:
            out[...] = (total + came[...].astype(F32)).astype(BF)
        else:
            near, far = (slice(0, cut), slice(cut, None))[::way]
            out[near] = (total[near] + came[...].astype(F32)).astype(BF)
            out[far] = total[far].astype(BF)


def merge_part_kernel(index, rows, refs):
    get = refs.__getitem__
    for way in (1, -1):
        total = both_cores(get, index, RING.index(way)) + get(("came", way))[rows].astype(F32)
        get(way)[...] = total.astype(BF)


def finish_kernel(piece, count, refs):
    get = refs.__getitem__
    copies, leaving = Copies(get("sems")), []

    def leave(name):
        leaving.append(copies.start(get(name + "_v"), get(name)))

    total = []
    for index in range(count):
        part = both_cores(get, index, 0)
        for way in (1, -1):
            came = get(("last", index, way) if count > 1 else ("came", way))
            part = part + came[...].astype(F32)
        total.append(part)
    total = jnp.concatenate(total, axis=0) if count > 1 else total[0]
    if piece == "ffn":
        rows = get("up").shape[0]
        get("down_v")[...] = total[: BLOCKS * rows]
        leave("down")
        for j in range(BLOCKS):
            get("up_v")[:, chunk(j)] = total[chunk(BLOCKS + j, rows)]
        leave("up")
    else:
        rows = get("out").shape[0]
        for j in range(3):
            get("qkv_v")[:, chunk(j)] = total[chunk(j, rows)]
        leave("qkv")
        get("out_v")[...] = total[chunk(3, rows)]
        leave("out")
        small = total[BLOCKS * rows : BLOCKS * rows + 8]
        get("bias_v")[...] = small[:1, : get("bias").shape[1]]
        leave("bias")
        turned = pltpu.roll(small, lax.rem(D - get("device")[0] * rows, D), 1)
        get("gains_v")[...] = turned[1:3, :rows]
        leave("gains")
        get("shifts_v")[...] = turned[3:5, :rows]
        leave("shifts")
    for copy in leaving:
        copy.wait()


class RingScatter:
    order = ()

    def __init__(self, piece, cut):
        self.piece, self.cut, self.rows = piece, cut, 0
        self.parts, self.came, self.last = [], {}, []

    def run(self, call, kernel, name):
        call.follow(RingScatter.order)
        found = call.run(kernel, name + "_" + self.piece, 0.5)
        sent = [way for way in (1, -1) if way in found]
        RingScatter.order = (found[sent[0]],)
        self.came.update((way, around(found[way], way)) for way in sent)

    def add(self, own, others, cuts, late=()):
        index = len(self.parts)
        held = {"other0": to_other_core(others[0])}
        self.parts.append((own, held))
        self.rows += own.shape[1]
        call = Call()
        self.give(call, ("other0",), index)
        for way, part in cuts.items():
            call.make(way, (len(range(*part.indices(own.shape[1]))), D), BF, VMEM)
        self.run(call, partial(far_kernel, index, cuts), "far")
        earlier = late + tuple(self.came.values()) if late else (held["other0"],)
        held["other1"] = to_other_core(after(others[1], *earlier))

    def give(self, call, names, only=None):
        for index, (own, others) in enumerate(self.parts):
            if only in (None, index):
                call.give(("own", index), own, VMEM)
                for name in names:
                    call.give((name, index), others[name], VMEM)
        if only is None:
            for way, value in self.came.items():
                call.give(("came", way), value, VMEM)

    def step(self, ahead):
        call = Call()
        self.give(call, ("other1",))
        for way in (1, -1):
            call.make(way, (self.rows, D), BF, VMEM)
        self.run(call, partial(merge_kernel, ahead, self.cut, len(self.parts)), "merge")

    def last_step(self, index):
        call = Call()
        before = tuple(self.last[index - 1].values()) if index else ()
        call.follow(RingScatter.order + before)
        own, others = self.parts[index]
        call.give(("own", index), own, VMEM)
        call.give(("other1", index), others["other1"], VMEM)
        for way in (1, -1):
            call.give(("came", way), self.came[way], VMEM)
            call.make(way, own.shape[1:], BF, VMEM)
        start = sum(part.shape[1] for part, _ in self.parts[:index])
        kernel = partial(merge_part_kernel, index, slice(start, start + own.shape[1]))
        found = call.run(kernel, "merge_part_" + self.piece, 0.5)
        RingScatter.order = (found[1],)
        self.last.append({way: around(found[way], way) for way in (1, -1)})

    def finish(self, shapes, device):
        call = Call()
        if self.last:
            self.came = {}
            for index, came in enumerate(self.last):
                for way, value in came.items():
                    call.give(("last", index, way), value, VMEM)
        self.give(call, ("other1",))
        call.give("device", device, SMEM)
        for name, shape in shapes.items():
            call.make(name, shape, F32, HBM)
            call.hold(name + "_v", pltpu.VMEM(shape, F32))
        call.hold("sems", pltpu.SemaphoreType.DMA((8,)))
        kernel = partial(finish_kernel, self.piece, len(self.parts))
        return call.run(kernel, "finish_" + self.piece, 1)


def turn_kernel(refs):
    for row in range(2):
        matrix = turn(refs["lengths"], row)
        for name in ("inputs", "cotangent"):
            refs[name, row][...] = nn(matrix, refs[name][row, 0]).astype(BF)


def turn_rows(lengths, inputs, cotangent):
    call = Call()
    call.give("lengths", lengths, SMEM)
    call.give("inputs", inputs, VMEM)
    call.give("cotangent", cotangent, VMEM)
    for name in ("inputs", "cotangent"):
        for row in range(2):
            call.make((name, row), (ROW, D), BF, VMEM)
    found = call.run(turn_kernel, "turn_rows", 1)
    return [[found[name, row] for row in range(2)] for name in ("inputs", "cotangent")]


def leave_kernel(refs):
    copies = Copies(refs["sems"])
    leaving = []
    for row in range(2):
        back = turn(refs["lengths"], row, True)
        for place, name in enumerate(("activations", "input_grads")):
            held = refs["held"].at[2 * row + place]
            held[...] = nn(back, refs[name, row][...]).astype(BF)
            leaving.append(copies.start(held, refs[name].at[row]))
    for copy in leaving:
        copy.wait()


def leave_rows(states, lengths, earlier=()):
    call = Call()
    call.follow(earlier)
    call.give("lengths", lengths, SMEM)
    for name, key in (("activations", "result"), ("input_grads", "grad")):
        for row, state in enumerate(states):
            call.give((name, row), state[key], VMEM)
        call.make(name, (2, ROW, D), BF, HBM)
    call.hold("held", pltpu.VMEM((4, ROW, D), BF))
    call.hold("sems", pltpu.SemaphoreType.DMA((4,)))
    return call.run(leave_kernel, "leave_rows", 1)


def relay(value, steps):
    count = lax.axis_size("section")
    first, last = (max(0, -steps), min(count, count - steps))
    return lax.ppermute(
        value, "section", [(source, source + steps) for source in range(first, last)]
    )


def body(
    inputs,
    cotangent,
    lengths,
    qkv_weight,
    out_weight,
    up_weight,
    down_weight,
    biases,
    norm_gains,
    norm_shifts,
):
    shards = lax.axis_size("batch")
    ring = shards == CORES * len(RING)
    groups = len(RING) if ring else 1
    width = D // shards
    cut = BIAS // shards
    device = lax.axis_index("batch")
    section = lax.axis_index("section").astype(jnp.int32).reshape(1)
    states, weights = ({}, {}), {}
    mine = device.astype(jnp.int32).reshape(1)
    RingScatter.order = ()
    if ring:
        table = jnp.asarray(ring_table().reshape(shards, -1))[device]
        own = pack(
            {"device": mine, "section": section, "table": table, "lengths": lengths[:, 0]},
            qkv_weight[0],
            out_weight[0],
            up_weight[0],
            down_weight[0],
            biases,
            norm_gains[0],
            norm_shifts[0],
        )
        inputs, cotangent = turn_rows(lengths[:, 0], inputs, cotangent)
        put_up, put_down = ring_gather(own, table, weights, width, inputs)
        small = weights["small"]
    else:
        table = jnp.array([0, 1], jnp.int32)
        gather = lambda value: lax.all_gather(value, "batch", axis=0, tiled=True)
        halves = [gather(value[0]) for value in (qkv_weight, out_weight, up_weight, down_weight)]
        blocks = lambda half: [half[:, chunk(j)] for j in range(half.shape[1] // D)]
        split = {"one": {}, "two": {}}
        for half, (qkv, out, up, down) in enumerate(
            zip(*(jnp.split(value, CORES) for value in halves))
        ):
            upper, lower = jnp.split(down, 2)
            gap = jnp.zeros((SMALL_ROWS, D), BF)
            split["one"][half] = (jnp.concatenate(blocks(qkv) + [out, gap, upper]),)
            split["two"][half] = (jnp.concatenate(blocks(up) + [lower]),)
        place_shards("one", table, list(split["one"].items()), weights, ("first", "down"))
        place_shards("two", table, list(split["two"].items()), weights, ("up", "down"))
        put_up = put_down = lambda mark: None
        norms = jnp.concatenate([norm_gains[0], norm_shifts[0]])
        packed = gather(jnp.concatenate([biases[0], norms.reshape(-1)])[None]).astype(F32)
        norms_all = packed[:, cut:].reshape(shards, 4, width).transpose(1, 0, 2)
        small = jnp.concatenate(
            [
                packed[:, :cut].reshape(BIAS_ROWS, D),
                norms_all.reshape(4, D),
                jnp.zeros((4, D), F32),
            ]
        )
    common = (section, lengths[:, 0])
    if not ring:
        inputs, cotangent = turn_rows(lengths[:, 0], inputs, cotangent)

    def run_forward(origin, row, source, parts=("attn", "up", "down"), marked=False, earlier=()):
        return forward(
            origin, row, parts, common, small, source, states[row], weights, marked, earlier
        )

    def run_backward(origin, row, source, parts=("ffn", "attn"), earlier=()):
        return backward(
            origin, row, parts, common, small, source, states[row], weights, earlier
        )

    mark = run_forward(0, 0, inputs[0], ("attn",), True)
    put_up(mark)
    run_forward(0, 0, None, ("up",))
    put_down(states[0]["slope"])
    result = run_forward(0, 0, None, ("down",))
    coming = relay(result, 1)
    second = relay(run_forward(0, 1, inputs[1]), 1)
    run_forward(1, 0, coming)
    coming = relay(run_backward(1, 0, cotangent[0]), -1)
    run_forward(1, 1, second, earlier=(states[0]["attn_sums"],))
    second = relay(run_backward(1, 1, cotangent[1]), -1)
    run_backward(0, 0, coming)
    halves = {}
    earlier = ()
    for piece in ("down", "up", "first"):
        halves[piece] = first_row_grad(piece, states[0], earlier)
        earlier = (halves[piece],)
    run_backward(0, 1, second, ("ffn",), earlier)
    down_own, *down_others = weight_grad("down", groups, table, states, halves["down"])
    up_own, *up_others = weight_grad(
        "up", groups, table, states, halves["up"], (down_own,)
    )
    RingScatter.order = (up_own,)
    if ring:
        ffn_ring = RingScatter("ffn", BLOCKS * width)
        ffn_ring.add(down_own, down_others, {1: slice(None)})
        ffn_ring.add(up_own, up_others, {-1: slice(None)})
    run_backward(0, 1, None, ("attn",), RingScatter.order)
    attn_own, *attn_others = weight_grad(
        "first", groups, table, states, halves["first"]
    )
    if ring:
        RingScatter.order = (attn_own,)
        ffn_ring.step(3)
        attn_ring = RingScatter("attn", 2 * width)
        cuts = {1: slice(0, 2 * width), -1: slice(2 * width, None)}
        attn_ring.add(attn_own, attn_others, cuts, tuple(ffn_ring.came.values()))
        ffn_ring.step(2)
        attn_ring.step(3)
        ffn_ring.last_step(0)
        attn_ring.step(2)
        ffn_ring.last_step(1)
        attn_ring.step(1)
        ffn = ffn_ring.finish({"down": (BLOCKS * width, D), "up": (width, FF)}, mine)
        down_sum, up_sum = ffn["down"], ffn["up"]
        shapes = {"qkv": (width, 3 * D), "out": (width, D), "bias": (1, cut)}
        shapes.update({"gains": (2, width), "shifts": (2, width)})
        attn = attn_ring.finish(shapes, mine)
        qkv_sum, out_sum, bias_sum = attn["qkv"], attn["out"], attn["bias"]
        gain_sum, shift_sum = attn["gains"], attn["shifts"]
    else:
        scatter = lambda value: lax.psum_scatter(
            value, "batch", scatter_dimension=0, tiled=True
        ).astype(F32)
        half = D // CORES
        join = lambda parts: jnp.concatenate(
            [
                jnp.concatenate([part[0, chunk(j, half)] for part in parts])
                for j in range(BLOCKS)
            ],
            axis=1,
        )
        down_sum = scatter(jnp.concatenate([down_own[0], down_others[0][0]]))
        up_sum = scatter(join((up_own, up_others[0])))
        attn_sum = scatter(join((attn_own, attn_others[0])))
        qkv_sum, out_sum = attn_sum[:, : 3 * D], attn_sum[:, 3 * D :]
        ffn_sums = states[0]["ffn_sums"] + states[1]["ffn_sums"]
        attn_sums = states[0]["attn_sums"] + states[1]["attn_sums"]
        bias_total = jnp.concatenate([attn_sums[:2], ffn_sums[4:10]]).reshape(shards, cut)
        norm_rows = ffn_sums[:4].reshape(4, shards, width).transpose(1, 0, 2)
        small_sum = scatter(
            jnp.concatenate([bias_total, norm_rows.reshape(shards, 4 * width)], axis=1)
        )
        bias_sum = small_sum[:, :cut]
        norm_sum = small_sum[:, cut:].reshape(4, width)
        gain_sum, shift_sum = norm_sum[:2], norm_sum[2:]
    rows = leave_rows(states, lengths[:, 0], RingScatter.order if ring else ())
    return (
        rows["activations"][None, :, None],
        rows["input_grads"][None, :, None],
        qkv_sum[None],
        out_sum[None],
        up_sum[None],
        down_sum[None],
        bias_sum,
        gain_sum[None],
        shift_sum[None],
    )


def solution(mesh):
    in_specs = (
        P(None, "batch", None, None),
        P(None, "batch", None, None),
        P(None, "batch", None),
        P("section", "batch", None),
        P("section", "batch", None),
        P("section", "batch", None),
        P("section", "batch", None),
        P("section", "batch"),
        P("section", None, "batch"),
        P("section", None, "batch"),
    )
    out_specs = (
        P("section", None, "batch", None, None),
        P("section", None, "batch", None, None),
        P("section", "batch", None),
        P("section", "batch", None),
        P("section", "batch", None),
        P("section", "batch", None),
        P("section", "batch"),
        P("section", None, "batch"),
        P("section", None, "batch"),
    )
    return jax.shard_map(body, mesh=mesh, in_specs=in_specs, out_specs=out_specs, check_vma=False)
```

```python
from functools import partial

import jax
import jax.numpy as jnp
from jax import lax
from jax.experimental import pallas as pl
from jax.experimental.pallas import tpu as pltpu
from jax.sharding import PartitionSpec as P

D = 768
HEADS = 12
FF = 3072
HEAD_DIM = 64
ROW = 256
HALF = 128
PAIRS = HEADS // 2
PAIR = 2 * HEAD_DIM
FFC = FF // D
BIAS = 6144
VMEM_LIMIT = 10 * 1024 * 1024

BF = jnp.bfloat16
F32 = jnp.float32
epsilon = 1e-12
masked_value = -1e30
inv_sqrt2 = 0.7071067811865476
inv_sqrt2pi = 0.3989422804014327


def nn(a, b):
    return jnp.dot(a, b, preferred_element_type=F32)


def nt(a, b):
    return lax.dot_general(a, b, (((1,), (1,)), ((), ())), preferred_element_type=F32)


def tn(a, b):
    return lax.dot_general(a, b, (((0,), (0,)), ((), ())), preferred_element_type=F32)


def head_masks():
    lane = lax.broadcasted_iota(jnp.int32, (1, PAIR), 1)
    low = (lane < HEAD_DIM).astype(F32)
    return (low.astype(BF), (1.0 - low).astype(BF))


def by_head(values, masks):
    return jnp.concatenate([values * masks[0], values * masks[1]], axis=0)


def own_head(values):
    lane = lax.broadcasted_iota(jnp.int32, (1, PAIR), 1)
    return jnp.where(lane < HEAD_DIM, values[:HALF], values[HALF:])


def bounds_of(lengths_ref, micro):
    first = lengths_ref[micro, 0]
    second = first + lengths_ref[micro, 1]
    return first, second, second + lengths_ref[micro, 2]


def longest_start(lengths_ref, micro):
    bounds = bounds_of(lengths_ref, micro)
    start = jnp.int32(0)
    for place, bound in enumerate(bounds):
        start = jnp.where(lengths_ref[micro, place + 1] == HALF, bound, start)
    return start


def turn(lengths_ref, micro, back=False):
    start = longest_start(lengths_ref, micro)
    here = lax.broadcasted_iota(jnp.int32, (ROW, ROW), 0)
    there = lax.broadcasted_iota(jnp.int32, (ROW, ROW), 1)
    if back:
        here, there = there, here
    return jnp.where((here + start) & (ROW - 1) == there, 1.0, 0.0).astype(BF)


def segment_penalty(lengths_ref, micro):
    bounds = bounds_of(lengths_ref, micro)
    start = longest_start(lengths_ref, micro)

    def number(axis):
        place = lax.broadcasted_iota(jnp.int32, (HALF, HALF), axis)
        place = (place + start + HALF) & (ROW - 1)
        total = jnp.zeros((HALF, HALF), jnp.int32)
        for bound in bounds:
            total = total + jnp.where(place >= bound, 1, 0)
        return total

    return jnp.where(number(0) == number(1), 0.0, masked_value)


def standardize(values):
    centred = values - jnp.mean(values, axis=-1, keepdims=True)
    spread = jnp.mean(centred * centred, axis=-1, keepdims=True)
    scale = lax.rsqrt(spread + epsilon)
    return centred * scale, scale


def norm_back(grad, unit, scale, gain):
    scaled = grad * gain
    mean_one = jnp.mean(scaled, axis=-1, keepdims=True)
    mean_two = jnp.mean(scaled * unit, axis=-1, keepdims=True)
    return scale * (scaled - mean_one - unit * mean_two)


class Copies:
    def __init__(self, sems):
        self.sems = sems
        self.used = 0

    def start(self, src, dst):
        copy = pltpu.make_async_copy(src, dst, self.sems.at[self.used])
        self.used += 1
        copy.start()
        return copy


class Reader:
    def __init__(self, refs):
        self.refs = list(refs)

    def take(self, count=None):
        if count is None:
            return self.refs.pop(0)
        taken, self.refs = self.refs[:count], self.refs[count:]
        return taken


def chunk(index, size=D):
    return slice(index * size, (index + 1) * size)


HBM = pl.BlockSpec(memory_space=pltpu.HBM)
SMEM = pl.BlockSpec(memory_space=pltpu.SMEM)
VMEM = pl.BlockSpec(memory_space=pltpu.VMEM)
LANES = 128
BLOCKS = 4
SMALL_ROWS = 16
BIAS_ROWS = BIAS // D

SHAPES = {
    "tokens": ((ROW, D), BF),
    "qkv": ((ROW, 3 * D), BF),
    "probs": ((PAIRS, 2, 2 * HALF, HALF), BF),
    "context": ((ROW, D), BF),
    "hidden": ((ROW, D), BF),
    "unit1": ((ROW, D), F32),
    "scale1": ((ROW, LANES), F32),
    "active": ((ROW, FF), BF),
    "slope": ((ROW, FF), BF),
    "unit2": ((ROW, D), F32),
    "scale2": ((ROW, LANES), F32),
    "down_side": ((ROW, D), BF),
    "attended": ((ROW, D), BF),
    "sum1": ((ROW, D), F32),
    "result": ((ROW, D), BF),
    "grad": ((ROW, D), BF),
    "ffn_sums": ((16, D), F32),
    "attn_sums": ((8, D), F32),
}
PIECES = {"first": (BLOCKS, D, D), "up": (BLOCKS, D, D), "down": (FF, D)}
PART_PIECE = {"attn": "first", "up": "up", "down": "down"}
MAKES = {
    "attn": ("tokens", "qkv", "probs", "context", "unit1", "scale1", "hidden"),
    "up": ("active", "slope"),
    "down": ("unit2", "scale2", "result"),
}
TAKES = {"attn": (), "up": ("hidden",), "down": ("unit1", "active")}
BACK_MAKES = {
    "ffn": ("down_side", "slope", "attended", "ffn_sums"),
    "attn": ("qkv", "attn_sums", "grad"),
}
BACK_PASSES = {"ffn": ("sum1",), "attn": ()}
BACK_TAKES = {
    "ffn": ("unit2", "scale2", "unit1", "scale1"),
    "attn": ("probs", "attended", "sum1"),
}
BACK_PIECES = {"ffn": ("down", "up"), "attn": ("first",)}


class Call:
    def __init__(self):
        self.operands, self.specs, self.in_names = [], [], []
        self.outs, self.out_specs, self.out_names = [], [], []
        self.scratch, self.scratch_names = [], []
        self.aliases = {}

    def give(self, name, value, spec):
        if spec is not SMEM:
            value = pltpu.with_memory_space_constraint(value, spec.memory_space)
        self.in_names.append(name)
        self.operands.append(value)
        self.specs.append(spec)

    def make(self, name, shape, kind, spec, old=None):
        if old is not None:
            self.aliases[len(self.operands)] = len(self.outs)
            self.give("old_" + name, old, spec)
        self.out_names.append(name)
        self.outs.append((pltpu.VMEM if spec is VMEM else pltpu.HBM)(shape, kind))
        self.out_specs.append(spec)

    def follow(self, values):
        for place, value in enumerate(values):
            self.give(("earlier", place), value, VMEM)

    def of_parts(self, parts, state, takes, makes, passes=None):
        inside = [key for part in parts for key in makes[part]]
        inside += [key for part in parts for key in (passes[part] if passes else ())]
        for part in parts:
            for key in takes[part]:
                if key not in inside:
                    self.give(key, state[key], VMEM)
        for part in parts:
            for key in makes[part]:
                self.make(key, *SHAPES[key], VMEM, state.get(key))
            for key in passes[part] if passes else ():
                if part == parts[-1]:
                    self.make(key, *SHAPES[key], VMEM)
                else:
                    self.hold(key, pltpu.VMEM(*SHAPES[key]))

    def hold(self, name, value):
        self.scratch_names.append(name)
        self.scratch.append(value)

    def run(self, kernel, name, time):
        names = self.in_names + self.out_names + self.scratch_names

        def named(*refs):
            kernel(dict(zip(names, refs)))

        found = pl.pallas_call(
            named,
            out_shape=self.outs,
            in_specs=self.specs,
            out_specs=self.out_specs,
            scratch_shapes=self.scratch,
            input_output_aliases=self.aliases,
            name=name,
            compiler_params=pltpu.CompilerParams(vmem_limit_bytes=VMEM_LIMIT),
            cost_estimate=pl.CostEstimate(
                flops=int(time * 1.1e9), bytes_accessed=1 << 20, transcendentals=0
            ),
        )(*self.operands)
        return dict(zip(self.out_names, found))


def rows_of(pieces, start, size):
    for piece in pieces:
        if start < piece.shape[0]:
            return piece[start : start + size]
        start -= piece.shape[0]


STREAMS = {
    "one": [("first", j) for j in range(BLOCKS)] + [("small", 0), ("down", 0)],
    "two": [("up", j) for j in range(BLOCKS)] + [("down", 1)],
}
EARLY = {"one": BLOCKS + 1, "two": BLOCKS}
FAR_CUT = {"one": 3, "two": 3}


def stream_sizes(stream, rows):
    size = {"first": rows, "up": rows, "small": SMALL_ROWS, "down": 2 * rows}
    return [size[name] for name, _ in STREAMS[stream]]


def device_at(get, place, devices):
    if devices == CORES:
        return place
    side, index = divmod(place, len(RING))
    own = get("device")[0]
    z, y, core = own // 4, (own // 2) & 1, own & 1
    spot = (jnp.where(y == 0, z, 7 - z) + RING[index]) & 7
    z, y = jnp.where(spot < 4, spot, 7 - spot), jnp.where(spot < 4, 0, 1)
    return (z * 2 + y) * 2 + (core if side == 0 else 1 - core)


def place_kernel(plan, refs):
    get = refs.__getitem__
    devices, stream, own, came = plan
    rows = D // devices
    small = refs.get("small")
    if small is not None and "old_small" not in refs:
        small[...] = jnp.zeros(small.shape, F32)

    def put(stream, entries, place, pieces):
        device = device_at(get, place, devices)
        start = 0
        sizes = stream_sizes(stream, rows)[entries]
        for (name, block), size in zip(STREAMS[stream][entries], sizes):
            part = rows_of(pieces, start, size)
            start += size
            if name == "down":
                at = pl.multiple_of(device * BLOCKS * rows + block * size, size)
                get("down")[pl.ds(at, size)] = part
            elif name != "small":
                get(name)[block, pl.ds(pl.multiple_of(device * rows, rows), rows)] = part
            elif small is not None:
                more = part.astype(F32)
                width = BIAS // devices
                per_row = D // width
                line = lax.broadcasted_iota(jnp.int32, (BIAS_ROWS, D), 0)
                lane_part = lax.broadcasted_iota(jnp.int32, (BIAS_ROWS, D), 1) // width
                mine = (line == device // per_row) & (lane_part == device % per_row)
                bias = jnp.concatenate([more[0:1, :width]] * per_row, axis=1)
                small[:BIAS_ROWS] += jnp.where(mine, bias, 0.0)
                small[BIAS_ROWS : BIAS_ROWS + 4] += more[1:5]

    for index, (place, count) in enumerate(own):
        pieces = [get(("shard", index, part)) for part in range(count)]
        put(stream, slice(None), place, pieces)
        if ("packed", 0) in refs:
            edge = sum(stream_sizes(stream, rows)[: EARLY[stream]])
            start = 0
            for piece in pieces:
                stop = start + piece.shape[0]
                middle = min(max(edge, start), stop)
                if middle > start:
                    get(("packed", 0))[index, start:middle] = piece[: middle - start]
                if middle < stop:
                    get(("packed", 1))[index, middle - edge : stop - edge] = piece[middle - start :]
                start = stop
    for number, (stream, entries) in enumerate(came):
        for index in range(len(RING)):
            put(stream, entries, index + len(RING), [get(("came", number)).at[index]])


def place_shards(stream, device, devices, own, weights, made, came=(), earlier=(), pack=False):
    call = Call()
    call.follow(earlier)
    call.give("device", device, SMEM)
    for index, (place, shard) in enumerate(own):
        for part, piece in enumerate(shard):
            call.give(("shard", index, part), piece, VMEM)
    for number, (value, _, _) in enumerate(came):
        call.give(("came", number), value, VMEM)
    for key in made:
        if key == "small":
            call.make(key, (SMALL_ROWS, D), F32, VMEM, weights.get(key))
        else:
            call.make(key, PIECES[key], BF, VMEM, weights.get(key))
    if pack:
        sizes = stream_sizes(stream, D // devices)
        for number, part in enumerate((sizes[: EARLY[stream]], sizes[EARLY[stream] :])):
            call.make(("packed", number), (len(own), sum(part), D), BF, VMEM)
    counts = [(place, len(shard)) for place, shard in own]
    plan = (devices, stream, counts, [spec[1:] for spec in came])
    found = call.run(partial(place_kernel, plan), "place_" + "_".join(made), 0.5)
    weights.update((key, found[key]) for key in made)
    return [found[key] for key in found if key not in made]


def forward_kernel(origin, row, parts, refs):
    get = refs.__getitem__
    small = get("small")
    bias = lambda index: small[index : index + 1, :]
    gain = lambda index: bias(BIAS_ROWS + index)
    shift = lambda index: bias(BIAS_ROWS + 2 + index)
    section = get("section")[0]
    @pl.when(section == origin)
    def _():
        if "attn" in parts:
            tokens = get("source")[...]
            get("tokens")[...] = tokens
            qkv, probs, context, weight = get("qkv"), get("probs"), get("context"), get("first")
            penalty = segment_penalty(get("lengths"), row)
            for j in range(3):
                part = nn(tokens, weight[j])
                if j != 1:
                    part = part + bias(j // 2)
                qkv[:, chunk(j)] = part.astype(BF)
            masks = head_masks()
            for pair in range(PAIRS):
                at = pair * PAIR
                for half in range(2):
                    rows = chunk(half, HALF)
                    keys = by_head(qkv[rows, D + at : D + at + PAIR], masks)
                    scores = nt(keys, qkv[rows, at : at + PAIR]).reshape(2, HALF, HALF)
                    if half == 1:
                        scores = scores + penalty
                    peak = jnp.max(scores, axis=1, keepdims=True)
                    raised = jnp.exp((scores - peak) * HEAD_DIM ** (-0.5))
                    share = raised * (1.0 / jnp.sum(raised, axis=1, keepdims=True))
                    share = share.reshape(2 * HALF, HALF).astype(BF)
                    probs[pair, half] = share
                    values = by_head(qkv[rows, 2 * D + at : 2 * D + at + PAIR], masks)
                    context[rows, at : at + PAIR] = tn(share, values).astype(BF)
            attended = nn(context[...], weight[3]) + bias(2)
            unit, scale = standardize(tokens.astype(F32) + attended)
            get("unit1")[...] = unit
            get("scale1")[...] = jnp.broadcast_to(scale, (ROW, LANES))
            get("hidden")[...] = (unit * gain(0) + shift(0)).astype(BF)
        if "up" in parts:
            hidden, active, slope = get("hidden"), get("active"), get("slope")
            for j in range(FFC):
                inner = nn(hidden[...], get("up")[j]) + bias(3 + j)
                phi = 0.5 * (1.0 + lax.erf(inner * inv_sqrt2))
                active[:, chunk(j)] = (inner * phi).astype(BF)
                bell = jnp.exp(inner * inner * -0.5) * inv_sqrt2pi
                slope[:, chunk(j)] = (phi + inner * bell).astype(BF)
        if "down" in parts:
            normed = get("unit1")[...] * gain(0) + shift(0)
            total = normed + bias(7) + nn(get("active")[...], get("down")[...])
            unit, scale = standardize(total)
            get("result")[...] = (unit * gain(1) + shift(1)).astype(BF)
            get("unit2")[...] = unit
            get("scale2")[...] = jnp.broadcast_to(scale, (ROW, LANES))

    if "mark" in refs:
        get("mark")[...] = jnp.zeros((8, LANES), F32)


def forward(origin, row, parts, common, small, source, state, weights, marked=False, earlier=()):
    section, lengths = common
    call = Call()
    call.follow(earlier)
    call.give("section", section, SMEM)
    call.give("small", small, VMEM)
    if "attn" in parts:
        call.give("lengths", lengths, SMEM)
        call.give("source", source, VMEM)
    for part in parts:
        key = PART_PIECE[part]
        call.give(key, weights[key], VMEM)
    if marked:
        call.make("mark", (8, LANES), F32, VMEM)
    call.of_parts(parts, state, TAKES, MAKES)
    found = call.run(
        partial(forward_kernel, origin, row, parts),
        "forward_" + "_".join(parts),
        0.1 if marked else 3 * len(parts),
    )
    mark = found.pop("mark", None)
    state.update(found)
    return mark if marked else found.get("result")


def backward_kernel(origin, row, parts, refs):
    get = refs.__getitem__
    small = get("small")
    gain = lambda index: small[BIAS_ROWS + index : BIAS_ROWS + index + 1, :]

    @pl.when(get("section")[0] == origin)
    def _():
        if "ffn" in parts:
            grad = get("source")[...].astype(F32)
            sums, inner = get("ffn_sums"), get("slope")
            unit = get("unit2")[...]
            sums[1:2, :] = jnp.sum(grad * unit, axis=0, keepdims=True)
            sums[3:4, :] = jnp.sum(grad, axis=0, keepdims=True)
            grad = norm_back(grad, unit, get("scale2")[:, 0:1], gain(1))
            sums[9:10, :] = jnp.sum(grad, axis=0, keepdims=True)
            side = grad.astype(BF)
            get("down_side")[...] = side
            sum_v = get("sum_v")
            sum_v[...] = grad
            for j in range(FFC):
                through = nt(side, get("down")[chunk(j)])
                through = through * inner[:, chunk(j)].astype(F32)
                sums[5 + j : 6 + j, :] = jnp.sum(through, axis=0, keepdims=True)
                inner[:, chunk(j)] = through.astype(BF)
            grad = sum_v[...]
            for j in range(BLOCKS):
                grad = grad + nt(inner[:, chunk(j)], get("up")[j])
            unit = get("unit1")[...]
            sums[0:1, :] = jnp.sum(grad * unit, axis=0, keepdims=True)
            sums[2:3, :] = jnp.sum(grad, axis=0, keepdims=True)
            grad = norm_back(grad, unit, get("scale1")[:, 0:1], gain(0))
            sums[4:5, :] = jnp.sum(grad, axis=0, keepdims=True)
            sums[10:16, :] = jnp.zeros((6, D), F32)
            get("sum1")[...] = grad
            get("attended")[...] = grad.astype(BF)
        if "attn" in parts:
            weight = get("first")
            context_grad = nt(get("attended")[...], weight[3]).astype(BF)
            masks = head_masks()
            qkv, sums = get("qkv"), get("attn_sums")
            sums[2:8, :] = jnp.zeros((6, D), F32)
            for pair in range(PAIRS):
                at = pair * PAIR
                spans = [slice(which * D + at, which * D + at + PAIR) for which in range(3)]
                biases = [0.0, 0.0]
                for half in range(2):
                    rows = chunk(half, HALF)
                    queries = qkv[rows, spans[0]]
                    keys = by_head(qkv[rows, spans[1]], masks)
                    values = by_head(qkv[rows, spans[2]], masks)
                    pair_grad = context_grad[rows, at : at + PAIR]
                    share = get("probs")[pair, half]
                    wide = share.astype(F32)
                    weighted = wide * nt(values, pair_grad)
                    inner_sum = jnp.sum(weighted.reshape(2, HALF, HALF), axis=1, keepdims=True)
                    score_grad = weighted.reshape(2, HALF, HALF)
                    score_grad = score_grad - wide.reshape(2, HALF, HALF) * inner_sum
                    score_grad = (score_grad * HEAD_DIM ** (-0.5)).reshape(2 * HALF, HALF)
                    score_grad = score_grad.astype(BF)
                    grads = (
                        tn(score_grad, keys),
                        own_head(nn(score_grad, queries)),
                        own_head(nn(share, pair_grad)),
                    )
                    for span, value in zip(spans, grads):
                        qkv[rows, span] = value.astype(BF)
                    for line in range(2):
                        biases[line] = biases[line] + jnp.sum(
                            grads[2 * line], axis=0, keepdims=True
                        )
                for line in range(2):
                    sums[line : line + 1, at : at + PAIR] = biases[line]
            grad = get("sum1")[...]
            for j in range(3):
                grad = grad + nt(qkv[:, chunk(j)], weight[j])
            get("grad")[...] = grad.astype(BF)


def backward(origin, row, parts, common, small, source, state, weights, earlier=()):
    call = Call()
    call.follow(earlier)
    call.give("section", common[0], SMEM)
    call.give("small", small, VMEM)
    for part in parts:
        for key in BACK_PIECES[part]:
            call.give(key, weights[key], VMEM)
    if "ffn" in parts:
        call.give("source", source, VMEM)
        call.hold("sum_v", pltpu.VMEM((ROW, D), F32))
    call.of_parts(parts, state, BACK_TAKES, BACK_MAKES, BACK_PASSES)
    found = call.run(
        partial(backward_kernel, origin, row, parts), "backward_" + "_".join(parts), 5 * len(parts)
    )
    state.update(found)
    return found.get("grad")


def other_groups(groups):
    if groups == 1:
        return [("other0", (0,))]
    return [("other0", (7,)), ("other1", tuple(range(7)))]


def other_at(groups, place):
    for name, places in other_groups(groups):
        if place in places:
            return name, places.index(place)


WEIGHT_TAKES = {
    "down": ("active", "down_side"),
    "up": ("hidden", "slope"),
    "first": ("context", "attended", "tokens", "qkv"),
}


def product_of(piece, block, get):
    if piece == "down":
        return tn(get("active")[:, chunk(block)], get("down_side")[...])
    if piece == "up":
        return tn(get("hidden")[...], get("slope")[:, chunk(block)])
    if block == 3:
        return tn(get("context")[...], get("attended")[...])
    return tn(get("tokens")[...], get("qkv")[:, chunk(block)])


def first_row_kernel(piece, refs):
    for block in range(BLOCKS):
        product = product_of(piece, block, refs.__getitem__)
        refs["product"][block] = product.astype(BF)


def first_row_grad(piece, state, earlier):
    call = Call()
    call.follow(earlier)
    for key in WEIGHT_TAKES[piece]:
        call.give(key, state[key], VMEM)
    call.make("product", (BLOCKS, D, D), BF, VMEM)
    return call.run(partial(first_row_kernel, piece), "row_" + piece, 2)["product"]


def weight_kernel(piece, groups, refs):
    get = refs.__getitem__
    held = get("held")
    rows = D // (2 * groups)
    goes = [device_at(get, place, 2 * groups) for place in range(2 * groups)]

    def store(side, place, span, value):
        if side == 0:
            get("own")[place, span] = value
        else:
            name, index = other_at(groups, place)
            get(name)[index, span] = value

    def block_of(block):
        before = get("before")[block].astype(F32)
        return (before + product_of(piece, block, get)).astype(BF)

    places = [(place // groups, place % groups) for place in range(2 * groups)]
    if piece == "down":
        for block in range(BLOCKS):
            held[chunk(block)] = block_of(block)
        for side, place in places:
            at = pl.multiple_of(goes[side * groups + place] * BLOCKS * rows, BLOCKS * rows)
            store(side, place, slice(None), held[pl.ds(at, BLOCKS * rows)])
        return
    if piece == "first" and groups > 1:
        sums, row = get("sums"), get("row_sums")
        bias_rows = [get(("attn_sums", 0))[k : k + 1] + get(("attn_sums", 1))[k : k + 1] for k in range(2)]
        ffn = get(("ffn_sums", 0))[...] + get(("ffn_sums", 1))[...]
        bias_rows += [ffn[4 + k : 5 + k] for k in range(6)]
        row[...] = jnp.zeros((SMALL_ROWS, D), F32)
        row[1:5, :] = ffn[:4]
        per_row = 2 * groups // BIAS_ROWS
        width = D // per_row
        for device in range(2 * groups):
            start = device % per_row * width
            row[0:1, :width] = bias_rows[device // per_row][:, start : start + width]
            sums[device] = row[...].astype(BF)
        for side, place in places:
            device = goes[side * groups + place]
            store(side, place, slice(BLOCKS * rows, None), sums[device])
    for block in (3, 0, 1, 2):
        held[...] = block_of(block)
        for side, place in places:
            at = pl.multiple_of(goes[side * groups + place] * rows, rows)
            store(side, place, chunk(block, rows), held[pl.ds(at, rows)])


def weight_grad(piece, groups, device, states, before, earlier=()):
    call = Call()
    call.follow(earlier)
    call.give("device", device, SMEM)
    call.give("before", before, VMEM)
    for key in WEIGHT_TAKES[piece]:
        call.give(key, states[1][key], VMEM)
    rows = BLOCKS * D // (2 * groups)
    if piece == "first":
        rows += SMALL_ROWS
        for key in ("attn_sums", "ffn_sums"):
            for row, state in enumerate(states):
                call.give((key, row), state[key], VMEM)
        call.hold("sums", pltpu.VMEM((2 * groups, SMALL_ROWS, D), BF))
        call.hold("row_sums", pltpu.VMEM((SMALL_ROWS, D), F32))
    call.make("own", (groups, rows, D), BF, VMEM)
    for name, places in other_groups(groups):
        call.make(name, (len(places), rows, D), BF, VMEM)
    call.hold("held", pltpu.VMEM((FF if piece == "down" else D, D), BF))
    found = call.run(partial(weight_kernel, piece, groups), "weight_" + piece, 3)
    return [found["own"]] + [found[name] for name, _ in other_groups(groups)]


CORES = 2
RING = (0, -1, 1, -2, 2, -3, 3, 4)


def ring_device(place, core):
    place = place % len(RING)
    z, y = (place, 0) if place < 4 else (7 - place, 1)
    return (z * 2 + y) * 2 + core


def ring_places():
    return [(place, core) for place in range(len(RING)) for core in range(CORES)]


def around(value, steps):
    pairs = [(ring_device(p, c), ring_device(p + steps, c)) for p, c in ring_places()]
    return lax.ppermute(value, "batch", pairs)


def to_other_core(value):
    pairs = [(ring_device(p, c), ring_device(p, 1 - c)) for p, c in ring_places()]
    return lax.ppermute(value, "batch", pairs)


def after(value, *earlier):
    return lax.optimization_barrier((value,) + earlier)[0]


def pack_kernel(refs):
    get = refs.__getitem__
    row, out = get("row"), {"one": get("one"), "two": get("two")}
    rows = get("out").shape[0]
    copies = Copies(get("sems"))
    small = [
        copies.start(get("bias"), get("bias_v")),
        copies.start(get("gains"), get("gains_v")),
        copies.start(get("shifts"), get("shifts_v")),
    ]
    arriving = []
    small_at = 0
    for stream, parts in STREAMS.items():
        start = 0
        for (name, block), size in zip(parts, stream_sizes(stream, rows)):
            target = out[stream].at[pl.ds(start, size)]
            if name == "small":
                small_at = start
            elif name == "down":
                source = get("down").at[pl.ds(block * size, size)]
                arriving.append(copies.start(source, target))
            elif name == "first" and block == 3:
                arriving.append(copies.start(get("out"), target))
            else:
                source = get("qkv" if name == "first" else "up").at[:, chunk(block)]
                arriving.append(copies.start(source, target))
            start += size
    row[...] = jnp.zeros((SMALL_ROWS, D), F32)
    for copy in small:
        copy.wait()
    row[1:3, :rows] = get("gains_v")[...].astype(F32)
    row[3:5, :rows] = get("shifts_v")[...].astype(F32)
    row[...] = pltpu.roll(row[...], get("device")[0] * rows, 1)
    row[0:1, : get("bias").shape[1]] = get("bias_v")[...].astype(F32)
    out["one"][small_at : small_at + SMALL_ROWS] = row[...].astype(BF)
    for copy in arriving:
        copy.wait()


def pack(scalars, qkv, out, up, down, bias, gains, shifts):
    call = Call()
    for name, value in scalars.items():
        call.give(name, value, SMEM)
    values = dict(qkv=qkv, out=out, up=up, down=down, bias=bias, gains=gains, shifts=shifts)
    for name, value in values.items():
        call.give(name, value, HBM)
    for stream in STREAMS:
        call.make(stream, (sum(stream_sizes(stream, out.shape[0])), D), BF, VMEM)
    call.hold("row", pltpu.VMEM((SMALL_ROWS, D), F32))
    for name in ("bias", "gains", "shifts"):
        call.hold(name + "_v", pltpu.VMEM(values[name].shape, BF))
    call.hold("sems", pltpu.SemaphoreType.DMA((16,)))
    found = call.run(pack_kernel, "pack", 1)
    return {stream: found[stream] for stream in STREAMS}


def cut_kernel(cut, refs):
    get = refs.__getitem__
    get(1)[...] = get("forwards")[:cut]
    get(-1)[...] = get("backwards")[cut:]


def cut_two(forwards, backwards, cut, earlier):
    call = Call()
    call.follow(earlier)
    call.give("forwards", forwards, VMEM)
    call.give("backwards", backwards, VMEM)
    call.make(1, (cut, D), BF, VMEM)
    call.make(-1, (forwards.shape[0] - cut, D), BF, VMEM)
    found = call.run(partial(cut_kernel, cut), "cut", 0.3)
    return found[1], found[-1]


def ring_gather(own, device, weights, rows, earlier):
    held = {stream: {0: (value,)} for stream, value in own.items()}

    def hop(stream, ahead):
        here = held[stream]
        here[-ahead] = (around(here[1 - ahead][0], 1),)
        here[ahead] = (around(here[ahead - 1][0], -1),)

    for ahead in (1, 2, 3):
        for stream in STREAMS:
            hop(stream, ahead)
    for stream in STREAMS:
        here = held[stream]
        cut = sum(stream_sizes(stream, rows)[: FAR_CUT[stream]])
        sends = cut_two(here[-3][0], here[3][0], cut, earlier)
        here[4] = tuple(around(send, way) for send, way in zip(sends, (1, -1)))
    came = {}
    for stream, made in (("one", ("first", "down", "small")), ("two", ("up", "down"))):
        shards = [(RING.index(ahead), held[stream][ahead]) for ahead in RING]
        packed = place_shards(stream, device, D // rows, shards, weights, made, pack=True)
        came[stream] = [to_other_core(value) for value in packed]

    def put_other(made, streams, early, earlier=()):
        number = 0 if early else 1
        entries = {s: slice(0, EARLY[s]) if early else slice(EARLY[s], None) for s in streams}
        values = [(came[s][number], s, entries[s]) for s in streams]
        place_shards(None, device, D // rows, (), weights, made, values, earlier)

    put_other(("first", "small"), ("one",), True)
    return (
        lambda mark: put_other(("up",), ("two",), True, (mark,)),
        lambda mark: put_other(("down",), ("one", "two"), False, (mark,)),
    )


def both_cores(get, index, place, part=slice(None)):
    name, at = other_at(len(RING), place)
    other = get((name, index))[at, part].astype(F32)
    return get(("own", index))[place, part].astype(F32) + other


def far_kernel(index, cuts, refs):
    get = refs.__getitem__
    for way, part in cuts.items():
        get(way)[...] = both_cores(get, index, RING.index(4), part).astype(BF)


def merge_kernel(ahead, cut, count, refs):
    get = refs.__getitem__
    for way in (1, -1):
        out, came = get(way), get(("came", way))
        place = RING.index(way * ahead)
        parts = [both_cores(get, index, place) for index in range(count)]
        total = jnp.concatenate(parts, axis=0) if count > 1 else parts[0]
        if ahead < 3:
            out[...] = (total + came[...].astype(F32)).astype(BF)
        else:
            near, far = (slice(0, cut), slice(cut, None))[::way]
            out[near] = (total[near] + came[...].astype(F32)).astype(BF)
            out[far] = total[far].astype(BF)


def merge_part_kernel(index, rows, refs):
    get = refs.__getitem__
    for way in (1, -1):
        total = both_cores(get, index, RING.index(way)) + get(("came", way))[rows].astype(F32)
        get(way)[...] = total.astype(BF)


def finish_kernel(piece, count, refs):
    get = refs.__getitem__
    copies, leaving = Copies(get("sems")), []

    def leave(name):
        leaving.append(copies.start(get(name + "_v"), get(name)))

    total = []
    for index in range(count):
        part = both_cores(get, index, 0)
        for way in (1, -1):
            came = get(("last", index, way) if count > 1 else ("came", way))
            part = part + came[...].astype(F32)
        total.append(part)
    total = jnp.concatenate(total, axis=0) if count > 1 else total[0]
    if piece == "ffn":
        rows = get("up").shape[0]
        get("down_v")[...] = total[: BLOCKS * rows]
        leave("down")
        for j in range(BLOCKS):
            get("up_v")[:, chunk(j)] = total[chunk(BLOCKS + j, rows)]
        leave("up")
    else:
        rows = get("out").shape[0]
        for j in range(3):
            get("qkv_v")[:, chunk(j)] = total[chunk(j, rows)]
        leave("qkv")
        get("out_v")[...] = total[chunk(3, rows)]
        leave("out")
        small = total[BLOCKS * rows : BLOCKS * rows + 8]
        get("bias_v")[...] = small[:1, : get("bias").shape[1]]
        leave("bias")
        turned = pltpu.roll(small, lax.rem(D - get("device")[0] * rows, D), 1)
        get("gains_v")[...] = turned[1:3, :rows]
        leave("gains")
        get("shifts_v")[...] = turned[3:5, :rows]
        leave("shifts")
    for copy in leaving:
        copy.wait()


class RingScatter:
    order = ()

    def __init__(self, piece, cut):
        self.piece, self.cut, self.rows = piece, cut, 0
        self.parts, self.came, self.last = [], {}, []

    def run(self, call, kernel, name):
        call.follow(RingScatter.order)
        found = call.run(kernel, name + "_" + self.piece, 0.5)
        sent = [way for way in (1, -1) if way in found]
        RingScatter.order = (found[sent[0]],)
        self.came.update((way, around(found[way], way)) for way in sent)

    def add(self, own, others, cuts, late=()):
        index = len(self.parts)
        held = {"other0": to_other_core(others[0])}
        self.parts.append((own, held))
        self.rows += own.shape[1]
        call = Call()
        self.give(call, ("other0",), index)
        for way, part in cuts.items():
            call.make(way, (len(range(*part.indices(own.shape[1]))), D), BF, VMEM)
        self.run(call, partial(far_kernel, index, cuts), "far")
        earlier = late + tuple(self.came.values()) if late else (held["other0"],)
        held["other1"] = to_other_core(after(others[1], *earlier))

    def give(self, call, names, only=None):
        for index, (own, others) in enumerate(self.parts):
            if only in (None, index):
                call.give(("own", index), own, VMEM)
                for name in names:
                    call.give((name, index), others[name], VMEM)
        if only is None:
            for way, value in self.came.items():
                call.give(("came", way), value, VMEM)

    def step(self, ahead):
        call = Call()
        self.give(call, ("other1",))
        for way in (1, -1):
            call.make(way, (self.rows, D), BF, VMEM)
        self.run(call, partial(merge_kernel, ahead, self.cut, len(self.parts)), "merge")

    def last_step(self, index):
        call = Call()
        before = tuple(self.last[index - 1].values()) if index else ()
        call.follow(RingScatter.order + before)
        own, others = self.parts[index]
        call.give(("own", index), own, VMEM)
        call.give(("other1", index), others["other1"], VMEM)
        for way in (1, -1):
            call.give(("came", way), self.came[way], VMEM)
            call.make(way, own.shape[1:], BF, VMEM)
        start = sum(part.shape[1] for part, _ in self.parts[:index])
        kernel = partial(merge_part_kernel, index, slice(start, start + own.shape[1]))
        found = call.run(kernel, "merge_part_" + self.piece, 0.5)
        RingScatter.order = (found[1],)
        self.last.append({way: around(found[way], way) for way in (1, -1)})

    def finish(self, shapes, device):
        call = Call()
        if self.last:
            self.came = {}
            for index, came in enumerate(self.last):
                for way, value in came.items():
                    call.give(("last", index, way), value, VMEM)
        self.give(call, ("other1",))
        call.give("device", device, SMEM)
        for name, shape in shapes.items():
            call.make(name, shape, F32, HBM)
            call.hold(name + "_v", pltpu.VMEM(shape, F32))
        call.hold("sems", pltpu.SemaphoreType.DMA((8,)))
        kernel = partial(finish_kernel, self.piece, len(self.parts))
        return call.run(kernel, "finish_" + self.piece, 1)


def turn_kernel(refs):
    for row in range(2):
        matrix = turn(refs["lengths"], row)
        for name in ("inputs", "cotangent"):
            refs[name, row][...] = nn(matrix, refs[name][row, 0]).astype(BF)


def turn_rows(lengths, inputs, cotangent):
    call = Call()
    call.give("lengths", lengths, SMEM)
    call.give("inputs", inputs, VMEM)
    call.give("cotangent", cotangent, VMEM)
    for name in ("inputs", "cotangent"):
        for row in range(2):
            call.make((name, row), (ROW, D), BF, VMEM)
    found = call.run(turn_kernel, "turn_rows", 1)
    return [[found[name, row] for row in range(2)] for name in ("inputs", "cotangent")]


def leave_kernel(refs):
    copies = Copies(refs["sems"])
    leaving = []
    for row in range(2):
        back = turn(refs["lengths"], row, True)
        for place, name in enumerate(("activations", "input_grads")):
            held = refs["held"].at[2 * row + place]
            held[...] = nn(back, refs[name, row][...]).astype(BF)
            leaving.append(copies.start(held, refs[name].at[row]))
    for copy in leaving:
        copy.wait()


def leave_rows(states, lengths, earlier=()):
    call = Call()
    call.follow(earlier)
    call.give("lengths", lengths, SMEM)
    for name, key in (("activations", "result"), ("input_grads", "grad")):
        for row, state in enumerate(states):
            call.give((name, row), state[key], VMEM)
        call.make(name, (2, ROW, D), BF, HBM)
    call.hold("held", pltpu.VMEM((4, ROW, D), BF))
    call.hold("sems", pltpu.SemaphoreType.DMA((4,)))
    return call.run(leave_kernel, "leave_rows", 1)


def relay(value, steps):
    count = lax.axis_size("section")
    first, last = (max(0, -steps), min(count, count - steps))
    return lax.ppermute(
        value, "section", [(source, source + steps) for source in range(first, last)]
    )


def body(
    inputs,
    cotangent,
    lengths,
    qkv_weight,
    out_weight,
    up_weight,
    down_weight,
    biases,
    norm_gains,
    norm_shifts,
):
    shards = lax.axis_size("batch")
    ring = shards == CORES * len(RING)
    groups = len(RING) if ring else 1
    width = D // shards
    cut = BIAS // shards
    device = lax.axis_index("batch")
    section = lax.axis_index("section").astype(jnp.int32).reshape(1)
    states, weights = ({}, {}), {}
    mine = device.astype(jnp.int32).reshape(1)
    RingScatter.order = ()
    if ring:
        own = pack(
            {"device": mine, "section": section},
            qkv_weight[0],
            out_weight[0],
            up_weight[0],
            down_weight[0],
            biases,
            norm_gains[0],
            norm_shifts[0],
        )
        inputs, cotangent = turn_rows(lengths[:, 0], inputs, cotangent)
        put_up, put_down = ring_gather(own, mine, weights, width, inputs)
        small = weights["small"]
    else:
        gather = lambda value: lax.all_gather(value, "batch", axis=0, tiled=True)
        halves = [gather(value[0]) for value in (qkv_weight, out_weight, up_weight, down_weight)]
        blocks = lambda half: [half[:, chunk(j)] for j in range(half.shape[1] // D)]
        split = {"one": {}, "two": {}}
        for half, (qkv, out, up, down) in enumerate(
            zip(*(jnp.split(value, CORES) for value in halves))
        ):
            upper, lower = jnp.split(down, 2)
            gap = jnp.zeros((SMALL_ROWS, D), BF)
            split["one"][half] = (jnp.concatenate(blocks(qkv) + [out, gap, upper]),)
            split["two"][half] = (jnp.concatenate(blocks(up) + [lower]),)
        place_shards("one", mine, CORES, list(split["one"].items()), weights, ("first", "down"))
        place_shards("two", mine, CORES, list(split["two"].items()), weights, ("up", "down"))
        put_up = put_down = lambda mark: None
        norms = jnp.concatenate([norm_gains[0], norm_shifts[0]])
        packed = gather(jnp.concatenate([biases[0], norms.reshape(-1)])[None]).astype(F32)
        norms_all = packed[:, cut:].reshape(shards, 4, width).transpose(1, 0, 2)
        small = jnp.concatenate(
            [
                packed[:, :cut].reshape(BIAS_ROWS, D),
                norms_all.reshape(4, D),
                jnp.zeros((4, D), F32),
            ]
        )
    common = (section, lengths[:, 0])
    if not ring:
        inputs, cotangent = turn_rows(lengths[:, 0], inputs, cotangent)

    def run_forward(origin, row, source, parts=("attn", "up", "down"), marked=False, earlier=()):
        return forward(
            origin, row, parts, common, small, source, states[row], weights, marked, earlier
        )

    def run_backward(origin, row, source, parts=("ffn", "attn"), earlier=()):
        return backward(
            origin, row, parts, common, small, source, states[row], weights, earlier
        )

    mark = run_forward(0, 0, inputs[0], ("attn",), True)
    put_up(mark)
    run_forward(0, 0, None, ("up",))
    put_down(states[0]["slope"])
    result = run_forward(0, 0, None, ("down",))
    coming = relay(result, 1)
    second = relay(run_forward(0, 1, inputs[1]), 1)
    run_forward(1, 0, coming)
    coming = relay(run_backward(1, 0, cotangent[0]), -1)
    run_forward(1, 1, second, earlier=(states[0]["attn_sums"],))
    second = relay(run_backward(1, 1, cotangent[1]), -1)
    run_backward(0, 0, coming)
    halves = {}
    earlier = ()
    for piece in ("down", "up", "first"):
        halves[piece] = first_row_grad(piece, states[0], earlier)
        earlier = (halves[piece],)
    run_backward(0, 1, second, ("ffn",), earlier)
    down_own, *down_others = weight_grad("down", groups, mine, states, halves["down"])
    up_own, *up_others = weight_grad(
        "up", groups, mine, states, halves["up"], (down_own,)
    )
    RingScatter.order = (up_own,)
    if ring:
        ffn_ring = RingScatter("ffn", BLOCKS * width)
        ffn_ring.add(down_own, down_others, {1: slice(None)})
        ffn_ring.add(up_own, up_others, {-1: slice(None)})
    run_backward(0, 1, None, ("attn",), RingScatter.order)
    attn_own, *attn_others = weight_grad(
        "first", groups, mine, states, halves["first"]
    )
    if ring:
        RingScatter.order = (attn_own,)
        ffn_ring.step(3)
        attn_ring = RingScatter("attn", 2 * width)
        cuts = {1: slice(0, 2 * width), -1: slice(2 * width, None)}
        attn_ring.add(attn_own, attn_others, cuts, tuple(ffn_ring.came.values()))
        ffn_ring.step(2)
        attn_ring.step(3)
        ffn_ring.last_step(0)
        attn_ring.step(2)
        ffn_ring.last_step(1)
        attn_ring.step(1)
        ffn = ffn_ring.finish({"down": (BLOCKS * width, D), "up": (width, FF)}, mine)
        down_sum, up_sum = ffn["down"], ffn["up"]
        shapes = {"qkv": (width, 3 * D), "out": (width, D), "bias": (1, cut)}
        shapes.update({"gains": (2, width), "shifts": (2, width)})
        attn = attn_ring.finish(shapes, mine)
        qkv_sum, out_sum, bias_sum = attn["qkv"], attn["out"], attn["bias"]
        gain_sum, shift_sum = attn["gains"], attn["shifts"]
    else:
        scatter = lambda value: lax.psum_scatter(
            value, "batch", scatter_dimension=0, tiled=True
        ).astype(F32)
        half = D // CORES
        join = lambda parts: jnp.concatenate(
            [
                jnp.concatenate([part[0, chunk(j, half)] for part in parts])
                for j in range(BLOCKS)
            ],
            axis=1,
        )
        down_sum = scatter(jnp.concatenate([down_own[0], down_others[0][0]]))
        up_sum = scatter(join((up_own, up_others[0])))
        attn_sum = scatter(join((attn_own, attn_others[0])))
        qkv_sum, out_sum = attn_sum[:, : 3 * D], attn_sum[:, 3 * D :]
        ffn_sums = states[0]["ffn_sums"] + states[1]["ffn_sums"]
        attn_sums = states[0]["attn_sums"] + states[1]["attn_sums"]
        bias_total = jnp.concatenate([attn_sums[:2], ffn_sums[4:10]]).reshape(shards, cut)
        norm_rows = ffn_sums[:4].reshape(4, shards, width).transpose(1, 0, 2)
        small_sum = scatter(
            jnp.concatenate([bias_total, norm_rows.reshape(shards, 4 * width)], axis=1)
        )
        bias_sum = small_sum[:, :cut]
        norm_sum = small_sum[:, cut:].reshape(4, width)
        gain_sum, shift_sum = norm_sum[:2], norm_sum[2:]
    rows = leave_rows(states, lengths[:, 0], RingScatter.order if ring else ())
    return (
        rows["activations"][None, :, None],
        rows["input_grads"][None, :, None],
        qkv_sum[None],
        out_sum[None],
        up_sum[None],
        down_sum[None],
        bias_sum,
        gain_sum[None],
        shift_sum[None],
    )


def solution(mesh):
    in_specs = (
        P(None, "batch", None, None),
        P(None, "batch", None, None),
        P(None, "batch", None),
        P("section", "batch", None),
        P("section", "batch", None),
        P("section", "batch", None),
        P("section", "batch", None),
        P("section", "batch"),
        P("section", None, "batch"),
        P("section", None, "batch"),
    )
    out_specs = (
        P("section", None, "batch", None, None),
        P("section", None, "batch", None, None),
        P("section", "batch", None),
        P("section", "batch", None),
        P("section", "batch", None),
        P("section", "batch", None),
        P("section", "batch"),
        P("section", None, "batch"),
        P("section", None, "batch"),
    )
    return jax.shard_map(body, mesh=mesh, in_specs=in_specs, out_specs=out_specs, check_vma=False)
```

```python
from functools import partial

import jax
import jax.numpy as jnp
from jax import lax
from jax.experimental import pallas as pl
from jax.experimental.pallas import tpu as pltpu
from jax.sharding import PartitionSpec as P

D = 768
HEADS = 12
FF = 3072
HEAD_DIM = 64
ROW = 256
HALF = 128
PAIRS = HEADS // 2
PAIR = 2 * HEAD_DIM
FFC = FF // D
BIAS = 6144
VMEM_LIMIT = 10 * 1024 * 1024

BF = jnp.bfloat16
F32 = jnp.float32
epsilon = 1e-12
masked_value = -1e30
inv_sqrt2 = 0.7071067811865476
inv_sqrt2pi = 0.3989422804014327


def nn(a, b):
    return jnp.dot(a, b, preferred_element_type=F32)


def nt(a, b):
    return lax.dot_general(a, b, (((1,), (1,)), ((), ())), preferred_element_type=F32)


def tn(a, b):
    return lax.dot_general(a, b, (((0,), (0,)), ((), ())), preferred_element_type=F32)


def head_masks():
    lane = lax.broadcasted_iota(jnp.int32, (1, PAIR), 1)
    low = (lane < HEAD_DIM).astype(F32)
    return (low.astype(BF), (1.0 - low).astype(BF))


def by_head(values, masks):
    return jnp.concatenate([values * masks[0], values * masks[1]], axis=0)


def own_head(values):
    lane = lax.broadcasted_iota(jnp.int32, (1, PAIR), 1)
    return jnp.where(lane < HEAD_DIM, values[:HALF], values[HALF:])


def bounds_of(lengths_ref, micro):
    first = lengths_ref[micro, 0]
    second = first + lengths_ref[micro, 1]
    return first, second, second + lengths_ref[micro, 2]


def longest_start(lengths_ref, micro):
    bounds = bounds_of(lengths_ref, micro)
    start = jnp.int32(0)
    for place, bound in enumerate(bounds):
        start = jnp.where(lengths_ref[micro, place + 1] == HALF, bound, start)
    return start


def turn(lengths_ref, micro, back=False):
    start = longest_start(lengths_ref, micro)
    here = lax.broadcasted_iota(jnp.int32, (ROW, ROW), 0)
    there = lax.broadcasted_iota(jnp.int32, (ROW, ROW), 1)
    if back:
        here, there = there, here
    return jnp.where((here + start) & (ROW - 1) == there, 1.0, 0.0).astype(BF)


def segment_penalty(lengths_ref, micro):
    bounds = bounds_of(lengths_ref, micro)
    start = longest_start(lengths_ref, micro)

    def number(axis):
        place = lax.broadcasted_iota(jnp.int32, (HALF, HALF), axis)
        place = (place + start + HALF) & (ROW - 1)
        total = jnp.zeros((HALF, HALF), jnp.int32)
        for bound in bounds:
            total = total + jnp.where(place >= bound, 1, 0)
        return total

    return jnp.where(number(0) == number(1), 0.0, masked_value)


def standardize(values):
    centred = values - jnp.mean(values, axis=-1, keepdims=True)
    spread = jnp.mean(centred * centred, axis=-1, keepdims=True)
    scale = lax.rsqrt(spread + epsilon)
    return centred * scale, scale


def norm_back(grad, unit, scale, gain):
    scaled = grad * gain
    mean_one = jnp.mean(scaled, axis=-1, keepdims=True)
    mean_two = jnp.mean(scaled * unit, axis=-1, keepdims=True)
    return scale * (scaled - mean_one - unit * mean_two)


class Copies:
    def __init__(self, sems):
        self.sems = sems
        self.used = 0

    def start(self, src, dst):
        copy = pltpu.make_async_copy(src, dst, self.sems.at[self.used])
        self.used += 1
        copy.start()
        return copy


class Reader:
    def __init__(self, refs):
        self.refs = list(refs)

    def take(self, count=None):
        if count is None:
            return self.refs.pop(0)
        taken, self.refs = self.refs[:count], self.refs[count:]
        return taken


def chunk(index, size=D):
    return slice(index * size, (index + 1) * size)


HBM = pl.BlockSpec(memory_space=pltpu.HBM)
SMEM = pl.BlockSpec(memory_space=pltpu.SMEM)
VMEM = pl.BlockSpec(memory_space=pltpu.VMEM)
LANES = 128
BLOCKS = 4
SMALL_ROWS = 16
BIAS_ROWS = BIAS // D

SHAPES = {
    "tokens": ((ROW, D), BF),
    "qkv": ((ROW, 3 * D), BF),
    "probs": ((PAIRS, 2, 2 * HALF, HALF), BF),
    "context": ((ROW, D), BF),
    "hidden": ((ROW, D), BF),
    "unit1": ((ROW, D), F32),
    "scale1": ((ROW, LANES), F32),
    "active": ((ROW, FF), BF),
    "slope": ((ROW, FF), BF),
    "unit2": ((ROW, D), F32),
    "scale2": ((ROW, LANES), F32),
    "down_side": ((ROW, D), BF),
    "attended": ((ROW, D), BF),
    "sum1": ((ROW, D), F32),
    "result": ((ROW, D), BF),
    "grad": ((ROW, D), BF),
    "ffn_sums": ((16, D), F32),
    "attn_sums": ((8, D), F32),
}
PIECES = {"first": (BLOCKS, D, D), "up": (BLOCKS, D, D), "down": (FF, D)}
PART_PIECE = {"attn": "first", "up": "up", "down": "down"}
MAKES = {
    "attn": ("tokens", "qkv", "probs", "context", "unit1", "scale1", "hidden"),
    "up": ("active", "slope"),
    "down": ("unit2", "scale2", "result"),
}
TAKES = {"attn": (), "up": ("hidden",), "down": ("unit1", "active")}
BACK_MAKES = {
    "ffn": ("down_side", "slope", "attended", "ffn_sums"),
    "attn": ("qkv", "attn_sums", "grad"),
}
BACK_PASSES = {"ffn": ("sum1",), "attn": ()}
BACK_TAKES = {
    "ffn": ("unit2", "scale2", "unit1", "scale1"),
    "attn": ("probs", "attended", "sum1"),
}
BACK_PIECES = {"ffn": ("down", "up"), "attn": ("first",)}


class Call:
    def __init__(self):
        self.operands, self.specs, self.in_names = [], [], []
        self.outs, self.out_specs, self.out_names = [], [], []
        self.scratch, self.scratch_names = [], []
        self.aliases = {}

    def give(self, name, value, spec):
        if spec is not SMEM:
            value = pltpu.with_memory_space_constraint(value, spec.memory_space)
        self.in_names.append(name)
        self.operands.append(value)
        self.specs.append(spec)

    def make(self, name, shape, kind, spec, old=None):
        if old is not None:
            self.aliases[len(self.operands)] = len(self.outs)
            self.give("old_" + name, old, spec)
        self.out_names.append(name)
        self.outs.append((pltpu.VMEM if spec is VMEM else pltpu.HBM)(shape, kind))
        self.out_specs.append(spec)

    def follow(self, values):
        for place, value in enumerate(values):
            self.give(("earlier", place), value, VMEM)

    def of_parts(self, parts, state, takes, makes, passes=None):
        inside = [key for part in parts for key in makes[part]]
        inside += [key for part in parts for key in (passes[part] if passes else ())]
        for part in parts:
            for key in takes[part]:
                if key not in inside:
                    self.give(key, state[key], VMEM)
        for part in parts:
            for key in makes[part]:
                self.make(key, *SHAPES[key], VMEM, state.get(key))
            for key in passes[part] if passes else ():
                if part == parts[-1]:
                    self.make(key, *SHAPES[key], VMEM)
                else:
                    self.hold(key, pltpu.VMEM(*SHAPES[key]))

    def hold(self, name, value):
        self.scratch_names.append(name)
        self.scratch.append(value)

    def run(self, kernel, name, time):
        names = self.in_names + self.out_names + self.scratch_names

        def named(*refs):
            kernel(dict(zip(names, refs)))

        found = pl.pallas_call(
            named,
            out_shape=self.outs,
            in_specs=self.specs,
            out_specs=self.out_specs,
            scratch_shapes=self.scratch,
            input_output_aliases=self.aliases,
            name=name,
            compiler_params=pltpu.CompilerParams(vmem_limit_bytes=VMEM_LIMIT),
            cost_estimate=pl.CostEstimate(
                flops=int(time * 1.1e9), bytes_accessed=1 << 20, transcendentals=0
            ),
        )(*self.operands)
        return dict(zip(self.out_names, found))


def rows_of(pieces, start, size):
    for piece in pieces:
        if start < piece.shape[0]:
            return piece[start : start + size]
        start -= piece.shape[0]


STREAMS = {
    "one": [("first", j) for j in range(BLOCKS)] + [("small", 0), ("down", 0)],
    "two": [("up", j) for j in range(BLOCKS)] + [("down", 1)],
}
EARLY = {"one": BLOCKS + 1, "two": BLOCKS}
FAR_CUT = {"one": 3, "two": 3}


def stream_sizes(stream, rows):
    size = {"first": rows, "up": rows, "small": SMALL_ROWS, "down": 2 * rows}
    return [size[name] for name, _ in STREAMS[stream]]


def device_at(get, place, devices):
    if devices == CORES:
        return place
    side, index = divmod(place, len(RING))
    own = get("device")[0]
    z, y, core = own // 4, (own // 2) & 1, own & 1
    spot = (jnp.where(y == 0, z, 7 - z) + RING[index]) & 7
    z, y = jnp.where(spot < 4, spot, 7 - spot), jnp.where(spot < 4, 0, 1)
    return (z * 2 + y) * 2 + (core if side == 0 else 1 - core)


def place_kernel(plan, refs):
    get = refs.__getitem__
    devices, stream, own, came = plan
    rows = D // devices
    small = refs.get("small")
    if small is not None and "old_small" not in refs:
        small[...] = jnp.zeros(small.shape, F32)

    def put(stream, entries, place, pieces):
        device = device_at(get, place, devices)
        start = 0
        sizes = stream_sizes(stream, rows)[entries]
        for (name, block), size in zip(STREAMS[stream][entries], sizes):
            part = rows_of(pieces, start, size)
            start += size
            if name == "down":
                at = pl.multiple_of(device * BLOCKS * rows + block * size, size)
                get("down")[pl.ds(at, size)] = part
            elif name != "small":
                get(name)[block, pl.ds(pl.multiple_of(device * rows, rows), rows)] = part
            elif small is not None:
                more = part.astype(F32)
                width = BIAS // devices
                per_row = D // width
                line = lax.broadcasted_iota(jnp.int32, (BIAS_ROWS, D), 0)
                lane_part = lax.broadcasted_iota(jnp.int32, (BIAS_ROWS, D), 1) // width
                mine = (line == device // per_row) & (lane_part == device % per_row)
                bias = jnp.concatenate([more[0:1, :width]] * per_row, axis=1)
                small[:BIAS_ROWS] += jnp.where(mine, bias, 0.0)
                small[BIAS_ROWS : BIAS_ROWS + 4] += more[1:5]

    for index, (place, count) in enumerate(own):
        pieces = [get(("shard", index, part)) for part in range(count)]
        put(stream, slice(None), place, pieces)
        if ("packed", 0) in refs:
            edge = sum(stream_sizes(stream, rows)[: EARLY[stream]])
            start = 0
            for piece in pieces:
                stop = start + piece.shape[0]
                middle = min(max(edge, start), stop)
                if middle > start:
                    get(("packed", 0))[index, start:middle] = piece[: middle - start]
                if middle < stop:
                    get(("packed", 1))[index, middle - edge : stop - edge] = piece[middle - start :]
                start = stop
    for number, (stream, entries) in enumerate(came):
        for index in range(len(RING)):
            put(stream, entries, index + len(RING), [get(("came", number)).at[index]])


def place_shards(stream, device, devices, own, weights, made, came=(), earlier=(), pack=False):
    call = Call()
    call.follow(earlier)
    call.give("device", device, SMEM)
    for index, (place, shard) in enumerate(own):
        for part, piece in enumerate(shard):
            call.give(("shard", index, part), piece, VMEM)
    for number, (value, _, _) in enumerate(came):
        call.give(("came", number), value, VMEM)
    for key in made:
        if key == "small":
            call.make(key, (SMALL_ROWS, D), F32, VMEM, weights.get(key))
        else:
            call.make(key, PIECES[key], BF, VMEM, weights.get(key))
    if pack:
        sizes = stream_sizes(stream, D // devices)
        for number, part in enumerate((sizes[: EARLY[stream]], sizes[EARLY[stream] :])):
            call.make(("packed", number), (len(own), sum(part), D), BF, VMEM)
    counts = [(place, len(shard)) for place, shard in own]
    plan = (devices, stream, counts, [spec[1:] for spec in came])
    found = call.run(partial(place_kernel, plan), "place_" + "_".join(made), 0.5)
    weights.update((key, found[key]) for key in made)
    return [found[key] for key in found if key not in made]


def forward_kernel(origin, row, parts, refs):
    get = refs.__getitem__
    small = get("small")
    bias = lambda index: small[index : index + 1, :]
    gain = lambda index: bias(BIAS_ROWS + index)
    shift = lambda index: bias(BIAS_ROWS + 2 + index)
    section = get("section")[0]
    @pl.when(section == origin)
    def _():
        if "attn" in parts:
            tokens = get("source")[...]
            get("tokens")[...] = tokens
            qkv, probs, context, weight = get("qkv"), get("probs"), get("context"), get("first")
            penalty = segment_penalty(get("lengths"), row)
            for j in range(3):
                part = nn(tokens, weight[j])
                if j != 1:
                    part = part + bias(j // 2)
                qkv[:, chunk(j)] = part.astype(BF)
            masks = head_masks()
            for pair in range(PAIRS):
                at = pair * PAIR
                for half in range(2):
                    rows = chunk(half, HALF)
                    keys = by_head(qkv[rows, D + at : D + at + PAIR], masks)
                    scores = nt(keys, qkv[rows, at : at + PAIR]).reshape(2, HALF, HALF)
                    if half == 1:
                        scores = scores + penalty
                    peak = jnp.max(scores, axis=1, keepdims=True)
                    raised = jnp.exp((scores - peak) * HEAD_DIM ** (-0.5))
                    share = raised * (1.0 / jnp.sum(raised, axis=1, keepdims=True))
                    share = share.reshape(2 * HALF, HALF).astype(BF)
                    probs[pair, half] = share
                    values = by_head(qkv[rows, 2 * D + at : 2 * D + at + PAIR], masks)
                    context[rows, at : at + PAIR] = tn(share, values).astype(BF)
            attended = nn(context[...], weight[3]) + bias(2)
            unit, scale = standardize(tokens.astype(F32) + attended)
            get("unit1")[...] = unit
            get("scale1")[...] = jnp.broadcast_to(scale, (ROW, LANES))
            get("hidden")[...] = (unit * gain(0) + shift(0)).astype(BF)
        if "down" in parts:
            total = get("unit1")[...] * gain(0) + shift(0) + bias(7)
        if "up" in parts:
            hidden, active, slope = get("hidden"), get("active"), get("slope")
            for j in range(FFC):
                inner = nn(hidden[...], get("up")[j]) + bias(3 + j)
                phi = 0.5 * (1.0 + lax.erf(inner * inv_sqrt2))
                active[:, chunk(j)] = (inner * phi).astype(BF)
                bell = jnp.exp(inner * inner * -0.5) * inv_sqrt2pi
                slope[:, chunk(j)] = (phi + inner * bell).astype(BF)
                if "down" in parts:
                    total = total + nn(active[:, chunk(j)], get("down")[chunk(j)])
        if "down" in parts:
            if "up" not in parts:
                total = total + nn(get("active")[...], get("down")[...])
            unit, scale = standardize(total)
            get("result")[...] = (unit * gain(1) + shift(1)).astype(BF)
            get("unit2")[...] = unit
            get("scale2")[...] = jnp.broadcast_to(scale, (ROW, LANES))

    if "mark" in refs:
        get("mark")[...] = jnp.zeros((8, LANES), F32)


def forward(origin, row, parts, common, small, source, state, weights, marked=False, earlier=()):
    section, lengths = common
    call = Call()
    call.follow(earlier)
    call.give("section", section, SMEM)
    call.give("small", small, VMEM)
    if "attn" in parts:
        call.give("lengths", lengths, SMEM)
        call.give("source", source, VMEM)
    for part in parts:
        key = PART_PIECE[part]
        call.give(key, weights[key], VMEM)
    if marked:
        call.make("mark", (8, LANES), F32, VMEM)
    call.of_parts(parts, state, TAKES, MAKES)
    found = call.run(
        partial(forward_kernel, origin, row, parts),
        "forward_" + "_".join(parts),
        0.1 if marked else 3 * len(parts),
    )
    mark = found.pop("mark", None)
    state.update(found)
    return mark if marked else found.get("result")


def backward_kernel(origin, row, parts, refs):
    get = refs.__getitem__
    small = get("small")
    gain = lambda index: small[BIAS_ROWS + index : BIAS_ROWS + index + 1, :]

    @pl.when(get("section")[0] == origin)
    def _():
        if "ffn" in parts:
            grad = get("source")[...].astype(F32)
            sums, inner = get("ffn_sums"), get("slope")
            unit = get("unit2")[...]
            sums[1:2, :] = jnp.sum(grad * unit, axis=0, keepdims=True)
            sums[3:4, :] = jnp.sum(grad, axis=0, keepdims=True)
            grad = norm_back(grad, unit, get("scale2")[:, 0:1], gain(1))
            sums[9:10, :] = jnp.sum(grad, axis=0, keepdims=True)
            side = grad.astype(BF)
            get("down_side")[...] = side
            sum_v = get("sum_v")
            sum_v[...] = grad
            for j in range(FFC):
                through = nt(side, get("down")[chunk(j)])
                through = through * inner[:, chunk(j)].astype(F32)
                sums[5 + j : 6 + j, :] = jnp.sum(through, axis=0, keepdims=True)
                inner[:, chunk(j)] = through.astype(BF)
            grad = sum_v[...]
            for j in range(BLOCKS):
                grad = grad + nt(inner[:, chunk(j)], get("up")[j])
            unit = get("unit1")[...]
            sums[0:1, :] = jnp.sum(grad * unit, axis=0, keepdims=True)
            sums[2:3, :] = jnp.sum(grad, axis=0, keepdims=True)
            grad = norm_back(grad, unit, get("scale1")[:, 0:1], gain(0))
            sums[4:5, :] = jnp.sum(grad, axis=0, keepdims=True)
            sums[10:16, :] = jnp.zeros((6, D), F32)
            get("sum1")[...] = grad
            get("attended")[...] = grad.astype(BF)
        if "attn" in parts:
            weight = get("first")
            context_grad = nt(get("attended")[...], weight[3]).astype(BF)
            masks = head_masks()
            qkv, sums = get("qkv"), get("attn_sums")
            sums[2:8, :] = jnp.zeros((6, D), F32)
            for pair in range(PAIRS):
                at = pair * PAIR
                spans = [slice(which * D + at, which * D + at + PAIR) for which in range(3)]
                biases = [0.0, 0.0]
                for half in range(2):
                    rows = chunk(half, HALF)
                    queries = qkv[rows, spans[0]]
                    keys = by_head(qkv[rows, spans[1]], masks)
                    values = by_head(qkv[rows, spans[2]], masks)
                    pair_grad = context_grad[rows, at : at + PAIR]
                    share = get("probs")[pair, half]
                    wide = share.astype(F32)
                    weighted = wide * nt(values, pair_grad)
                    inner_sum = jnp.sum(weighted.reshape(2, HALF, HALF), axis=1, keepdims=True)
                    score_grad = weighted.reshape(2, HALF, HALF)
                    score_grad = score_grad - wide.reshape(2, HALF, HALF) * inner_sum
                    score_grad = (score_grad * HEAD_DIM ** (-0.5)).reshape(2 * HALF, HALF)
                    score_grad = score_grad.astype(BF)
                    grads = (
                        tn(score_grad, keys),
                        own_head(nn(score_grad, queries)),
                        own_head(nn(share, pair_grad)),
                    )
                    for span, value in zip(spans, grads):
                        qkv[rows, span] = value.astype(BF)
                    for line in range(2):
                        biases[line] = biases[line] + jnp.sum(
                            grads[2 * line], axis=0, keepdims=True
                        )
                for line in range(2):
                    sums[line : line + 1, at : at + PAIR] = biases[line]
            grad = get("sum1")[...]
            for j in range(3):
                grad = grad + nt(qkv[:, chunk(j)], weight[j])
            get("grad")[...] = grad.astype(BF)


def backward(origin, row, parts, common, small, source, state, weights, earlier=()):
    call = Call()
    call.follow(earlier)
    call.give("section", common[0], SMEM)
    call.give("small", small, VMEM)
    for part in parts:
        for key in BACK_PIECES[part]:
            call.give(key, weights[key], VMEM)
    if "ffn" in parts:
        call.give("source", source, VMEM)
        call.hold("sum_v", pltpu.VMEM((ROW, D), F32))
    call.of_parts(parts, state, BACK_TAKES, BACK_MAKES, BACK_PASSES)
    found = call.run(
        partial(backward_kernel, origin, row, parts), "backward_" + "_".join(parts), 5 * len(parts)
    )
    state.update(found)
    return found.get("grad")


def other_groups(groups):
    if groups == 1:
        return [("other0", (0,))]
    return [("other0", (7,)), ("other1", tuple(range(7)))]


def other_at(groups, place):
    for name, places in other_groups(groups):
        if place in places:
            return name, places.index(place)


WEIGHT_TAKES = {
    "down": ("active", "down_side"),
    "up": ("hidden", "slope"),
    "first": ("context", "attended", "tokens", "qkv"),
}


def product_of(piece, block, get):
    if piece == "down":
        return tn(get("active")[:, chunk(block)], get("down_side")[...])
    if piece == "up":
        return tn(get("hidden")[...], get("slope")[:, chunk(block)])
    if block == 3:
        return tn(get("context")[...], get("attended")[...])
    return tn(get("tokens")[...], get("qkv")[:, chunk(block)])


def first_row_kernel(piece, refs):
    for block in range(BLOCKS):
        product = product_of(piece, block, refs.__getitem__)
        refs["product"][block] = product.astype(BF)


def first_row_grad(piece, state, earlier):
    call = Call()
    call.follow(earlier)
    for key in WEIGHT_TAKES[piece]:
        call.give(key, state[key], VMEM)
    call.make("product", (BLOCKS, D, D), BF, VMEM)
    return call.run(partial(first_row_kernel, piece), "row_" + piece, 2)["product"]


def weight_kernel(piece, groups, refs):
    get = refs.__getitem__
    held = get("held")
    rows = D // (2 * groups)
    goes = [device_at(get, place, 2 * groups) for place in range(2 * groups)]

    def store(side, place, span, value):
        if side == 0:
            get("own")[place, span] = value
        else:
            name, index = other_at(groups, place)
            get(name)[index, span] = value

    def block_of(block):
        before = get("before")[block].astype(F32)
        return (before + product_of(piece, block, get)).astype(BF)

    places = [(place // groups, place % groups) for place in range(2 * groups)]
    if piece == "down":
        for block in range(BLOCKS):
            held[chunk(block)] = block_of(block)
        for side, place in places:
            at = pl.multiple_of(goes[side * groups + place] * BLOCKS * rows, BLOCKS * rows)
            store(side, place, slice(None), held[pl.ds(at, BLOCKS * rows)])
        return
    if piece == "first" and groups > 1:
        sums, row = get("sums"), get("row_sums")
        bias_rows = [get(("attn_sums", 0))[k : k + 1] + get(("attn_sums", 1))[k : k + 1] for k in range(2)]
        ffn = get(("ffn_sums", 0))[...] + get(("ffn_sums", 1))[...]
        bias_rows += [ffn[4 + k : 5 + k] for k in range(6)]
        row[...] = jnp.zeros((SMALL_ROWS, D), F32)
        row[1:5, :] = ffn[:4]
        per_row = 2 * groups // BIAS_ROWS
        width = D // per_row
        for device in range(2 * groups):
            start = device % per_row * width
            row[0:1, :width] = bias_rows[device // per_row][:, start : start + width]
            sums[device] = row[...].astype(BF)
        for side, place in places:
            device = goes[side * groups + place]
            store(side, place, slice(BLOCKS * rows, None), sums[device])
    for block in (3, 0, 1, 2):
        held[...] = block_of(block)
        for side, place in places:
            at = pl.multiple_of(goes[side * groups + place] * rows, rows)
            store(side, place, chunk(block, rows), held[pl.ds(at, rows)])


def weight_grad(piece, groups, device, states, before, earlier=()):
    call = Call()
    call.follow(earlier)
    call.give("device", device, SMEM)
    call.give("before", before, VMEM)
    for key in WEIGHT_TAKES[piece]:
        call.give(key, states[1][key], VMEM)
    rows = BLOCKS * D // (2 * groups)
    if piece == "first":
        rows += SMALL_ROWS
        for key in ("attn_sums", "ffn_sums"):
            for row, state in enumerate(states):
                call.give((key, row), state[key], VMEM)
        call.hold("sums", pltpu.VMEM((2 * groups, SMALL_ROWS, D), BF))
        call.hold("row_sums", pltpu.VMEM((SMALL_ROWS, D), F32))
    call.make("own", (groups, rows, D), BF, VMEM)
    for name, places in other_groups(groups):
        call.make(name, (len(places), rows, D), BF, VMEM)
    call.hold("held", pltpu.VMEM((FF if piece == "down" else D, D), BF))
    found = call.run(partial(weight_kernel, piece, groups), "weight_" + piece, 3)
    return [found["own"]] + [found[name] for name, _ in other_groups(groups)]


CORES = 2
RING = (0, -1, 1, -2, 2, -3, 3, 4)


def ring_device(place, core):
    place = place % len(RING)
    z, y = (place, 0) if place < 4 else (7 - place, 1)
    return (z * 2 + y) * 2 + core


def ring_places():
    return [(place, core) for place in range(len(RING)) for core in range(CORES)]


def around(value, steps):
    pairs = [(ring_device(p, c), ring_device(p + steps, c)) for p, c in ring_places()]
    return lax.ppermute(value, "batch", pairs)


def to_other_core(value):
    pairs = [(ring_device(p, c), ring_device(p, 1 - c)) for p, c in ring_places()]
    return lax.ppermute(value, "batch", pairs)


def after(value, *earlier):
    return lax.optimization_barrier((value,) + earlier)[0]


def pack_kernel(refs):
    get = refs.__getitem__
    row, out = get("row"), {"one": get("one"), "two": get("two")}
    rows = get("out").shape[0]
    copies = Copies(get("sems"))
    small = [
        copies.start(get("bias"), get("bias_v")),
        copies.start(get("gains"), get("gains_v")),
        copies.start(get("shifts"), get("shifts_v")),
    ]
    arriving = []
    small_at = 0
    for stream, parts in STREAMS.items():
        start = 0
        for (name, block), size in zip(parts, stream_sizes(stream, rows)):
            target = out[stream].at[pl.ds(start, size)]
            if name == "small":
                small_at = start
            elif name == "down":
                source = get("down").at[pl.ds(block * size, size)]
                arriving.append(copies.start(source, target))
            elif name == "first" and block == 3:
                arriving.append(copies.start(get("out"), target))
            else:
                source = get("qkv" if name == "first" else "up").at[:, chunk(block)]
                arriving.append(copies.start(source, target))
            start += size
    row[...] = jnp.zeros((SMALL_ROWS, D), F32)
    for copy in small:
        copy.wait()
    row[1:3, :rows] = get("gains_v")[...].astype(F32)
    row[3:5, :rows] = get("shifts_v")[...].astype(F32)
    row[...] = pltpu.roll(row[...], get("device")[0] * rows, 1)
    row[0:1, : get("bias").shape[1]] = get("bias_v")[...].astype(F32)
    out["one"][small_at : small_at + SMALL_ROWS] = row[...].astype(BF)
    for copy in arriving:
        copy.wait()


def pack(scalars, qkv, out, up, down, bias, gains, shifts):
    call = Call()
    for name, value in scalars.items():
        call.give(name, value, SMEM)
    values = dict(qkv=qkv, out=out, up=up, down=down, bias=bias, gains=gains, shifts=shifts)
    for name, value in values.items():
        call.give(name, value, HBM)
    for stream in STREAMS:
        call.make(stream, (sum(stream_sizes(stream, out.shape[0])), D), BF, VMEM)
    call.hold("row", pltpu.VMEM((SMALL_ROWS, D), F32))
    for name in ("bias", "gains", "shifts"):
        call.hold(name + "_v", pltpu.VMEM(values[name].shape, BF))
    call.hold("sems", pltpu.SemaphoreType.DMA((16,)))
    found = call.run(pack_kernel, "pack", 1)
    return {stream: found[stream] for stream in STREAMS}


def cut_kernel(cut, refs):
    get = refs.__getitem__
    get(1)[...] = get("forwards")[:cut]
    get(-1)[...] = get("backwards")[cut:]


def cut_two(forwards, backwards, cut, earlier):
    call = Call()
    call.follow(earlier)
    call.give("forwards", forwards, VMEM)
    call.give("backwards", backwards, VMEM)
    call.make(1, (cut, D), BF, VMEM)
    call.make(-1, (forwards.shape[0] - cut, D), BF, VMEM)
    found = call.run(partial(cut_kernel, cut), "cut", 0.3)
    return found[1], found[-1]


def ring_gather(own, device, weights, rows, earlier):
    held = {stream: {0: (value,)} for stream, value in own.items()}

    def hop(stream, ahead):
        here = held[stream]
        here[-ahead] = (around(here[1 - ahead][0], 1),)
        here[ahead] = (around(here[ahead - 1][0], -1),)

    for ahead in (1, 2, 3):
        for stream in STREAMS:
            hop(stream, ahead)
    for stream in STREAMS:
        here = held[stream]
        cut = sum(stream_sizes(stream, rows)[: FAR_CUT[stream]])
        sends = cut_two(here[-3][0], here[3][0], cut, earlier)
        here[4] = tuple(around(send, way) for send, way in zip(sends, (1, -1)))
    came = {}
    for stream, made in (("one", ("first", "down", "small")), ("two", ("up", "down"))):
        shards = [(RING.index(ahead), held[stream][ahead]) for ahead in RING]
        packed = place_shards(stream, device, D // rows, shards, weights, made, pack=True)
        came[stream] = [to_other_core(value) for value in packed]

    def put_other(made, streams, early, earlier=()):
        number = 0 if early else 1
        entries = {s: slice(0, EARLY[s]) if early else slice(EARLY[s], None) for s in streams}
        values = [(came[s][number], s, entries[s]) for s in streams]
        place_shards(None, device, D // rows, (), weights, made, values, earlier)

    put_other(("first", "small"), ("one",), True)
    return (
        lambda mark: put_other(("up",), ("two",), True, (mark,)),
        lambda mark: put_other(("down",), ("one", "two"), False, (mark,)),
    )


def both_cores(get, index, place, part=slice(None)):
    name, at = other_at(len(RING), place)
    other = get((name, index))[at, part].astype(F32)
    return get(("own", index))[place, part].astype(F32) + other


def far_kernel(index, cuts, refs):
    get = refs.__getitem__
    for way, part in cuts.items():
        get(way)[...] = both_cores(get, index, RING.index(4), part).astype(BF)


def merge_kernel(ahead, cut, count, way, refs):
    get = refs.__getitem__
    out, came = get(way), get(("came", way))
    place = RING.index(way * ahead)
    parts = [both_cores(get, index, place) for index in range(count)]
    total = jnp.concatenate(parts, axis=0) if count > 1 else parts[0]
    if ahead < 3:
        out[...] = (total + came[...].astype(F32)).astype(BF)
    else:
        near, far = (slice(0, cut), slice(cut, None))[::way]
        out[near] = (total[near] + came[...].astype(F32)).astype(BF)
        out[far] = total[far].astype(BF)


def merge_part_kernel(index, rows, way, refs):
    get = refs.__getitem__
    total = both_cores(get, index, RING.index(way)) + get(("came", way))[rows].astype(F32)
    get(way)[...] = total.astype(BF)


def finish_kernel(piece, count, refs):
    get = refs.__getitem__
    copies, leaving = Copies(get("sems")), []

    def leave(name):
        leaving.append(copies.start(get(name + "_v"), get(name)))

    total = []
    for index in range(count):
        part = both_cores(get, index, 0)
        for way in (1, -1):
            came = get(("last", index, way) if count > 1 else ("came", way))
            part = part + came[...].astype(F32)
        total.append(part)
    total = jnp.concatenate(total, axis=0) if count > 1 else total[0]
    if piece == "ffn":
        rows = get("up").shape[0]
        get("down_v")[...] = total[: BLOCKS * rows]
        leave("down")
        for j in range(BLOCKS):
            get("up_v")[:, chunk(j)] = total[chunk(BLOCKS + j, rows)]
        leave("up")
    else:
        rows = get("out").shape[0]
        for j in range(3):
            get("qkv_v")[:, chunk(j)] = total[chunk(j, rows)]
        leave("qkv")
        get("out_v")[...] = total[chunk(3, rows)]
        leave("out")
        small = total[BLOCKS * rows : BLOCKS * rows + 8]
        get("bias_v")[...] = small[:1, : get("bias").shape[1]]
        leave("bias")
        turned = pltpu.roll(small, lax.rem(D - get("device")[0] * rows, D), 1)
        get("gains_v")[...] = turned[1:3, :rows]
        leave("gains")
        get("shifts_v")[...] = turned[3:5, :rows]
        leave("shifts")
    for copy in leaving:
        copy.wait()


class RingScatter:
    order = ()

    def __init__(self, piece, cut):
        self.piece, self.cut, self.rows = piece, cut, 0
        self.parts, self.came, self.last = [], {}, []

    def run(self, call, kernel, name):
        call.follow(RingScatter.order)
        found = call.run(kernel, name + "_" + self.piece, 0.5)
        sent = [way for way in (1, -1) if way in found]
        RingScatter.order = (found[sent[0]],)
        self.came.update((way, around(found[way], way)) for way in sent)

    def add(self, own, others, cuts, late=()):
        index = len(self.parts)
        held = {"other0": to_other_core(others[0])}
        self.parts.append((own, held))
        self.rows += own.shape[1]
        call = Call()
        self.give(call, ("other0",), index)
        for way, part in cuts.items():
            call.make(way, (len(range(*part.indices(own.shape[1]))), D), BF, VMEM)
        self.run(call, partial(far_kernel, index, cuts), "far")
        earlier = late + tuple(self.came.values()) if late else (held["other0"],)
        held["other1"] = to_other_core(after(others[1], *earlier))

    def give(self, call, names, only=None, ways=None):
        for index, (own, others) in enumerate(self.parts):
            if only in (None, index):
                call.give(("own", index), own, VMEM)
                for name in names:
                    call.give((name, index), others[name], VMEM)
        if only is None:
            for way, value in self.came.items():
                if ways is None or way in ways:
                    call.give(("came", way), value, VMEM)

    def step(self, ahead):
        for way in (1, -1):
            call = Call()
            self.give(call, ("other1",), ways=(way,))
            call.make(way, (self.rows, D), BF, VMEM)
            kernel = partial(merge_kernel, ahead, self.cut, len(self.parts), way)
            self.run(call, kernel, "merge")

    def last_step(self, index):
        own, others = self.parts[index]
        start = sum(part.shape[1] for part, _ in self.parts[:index])
        rows = slice(start, start + own.shape[1])
        sent = {}
        for way in (1, -1):
            call = Call()
            before = (self.last[index - 1][way],) if index else ()
            call.follow(RingScatter.order + before)
            call.give(("own", index), own, VMEM)
            call.give(("other1", index), others["other1"], VMEM)
            call.give(("came", way), self.came[way], VMEM)
            call.make(way, own.shape[1:], BF, VMEM)
            kernel = partial(merge_part_kernel, index, rows, way)
            found = call.run(kernel, "merge_part_" + self.piece, 0.5)
            RingScatter.order = (found[way],)
            sent[way] = around(found[way], way)
        self.last.append(sent)

    def finish(self, shapes, device):
        call = Call()
        if self.last:
            self.came = {}
            for index, came in enumerate(self.last):
                for way, value in came.items():
                    call.give(("last", index, way), value, VMEM)
        self.give(call, ("other1",))
        call.give("device", device, SMEM)
        for name, shape in shapes.items():
            call.make(name, shape, F32, HBM)
            call.hold(name + "_v", pltpu.VMEM(shape, F32))
        call.hold("sems", pltpu.SemaphoreType.DMA((8,)))
        kernel = partial(finish_kernel, self.piece, len(self.parts))
        return call.run(kernel, "finish_" + self.piece, 1)


def turn_kernel(refs):
    for row in range(2):
        matrix = turn(refs["lengths"], row)
        for name in ("inputs", "cotangent"):
            refs[name, row][...] = nn(matrix, refs[name][row, 0]).astype(BF)


def turn_rows(lengths, inputs, cotangent):
    call = Call()
    call.give("lengths", lengths, SMEM)
    call.give("inputs", inputs, VMEM)
    call.give("cotangent", cotangent, VMEM)
    for name in ("inputs", "cotangent"):
        for row in range(2):
            call.make((name, row), (ROW, D), BF, VMEM)
    found = call.run(turn_kernel, "turn_rows", 1)
    return [[found[name, row] for row in range(2)] for name in ("inputs", "cotangent")]


def leave_kernel(refs):
    copies = Copies(refs["sems"])
    leaving = []
    for row in range(2):
        back = turn(refs["lengths"], row, True)
        for place, name in enumerate(("activations", "input_grads")):
            held = refs["held"].at[2 * row + place]
            held[...] = nn(back, refs[name, row][...]).astype(BF)
            leaving.append(copies.start(held, refs[name].at[row]))
    for copy in leaving:
        copy.wait()


def leave_rows(states, lengths, earlier=()):
    call = Call()
    call.follow(earlier)
    call.give("lengths", lengths, SMEM)
    for name, key in (("activations", "result"), ("input_grads", "grad")):
        for row, state in enumerate(states):
            call.give((name, row), state[key], VMEM)
        call.make(name, (2, ROW, D), BF, HBM)
    call.hold("held", pltpu.VMEM((4, ROW, D), BF))
    call.hold("sems", pltpu.SemaphoreType.DMA((4,)))
    return call.run(leave_kernel, "leave_rows", 1)


def relay(value, steps):
    count = lax.axis_size("section")
    first, last = (max(0, -steps), min(count, count - steps))
    return lax.ppermute(
        value, "section", [(source, source + steps) for source in range(first, last)]
    )


def body(
    inputs,
    cotangent,
    lengths,
    qkv_weight,
    out_weight,
    up_weight,
    down_weight,
    biases,
    norm_gains,
    norm_shifts,
):
    shards = lax.axis_size("batch")
    ring = shards == CORES * len(RING)
    groups = len(RING) if ring else 1
    width = D // shards
    cut = BIAS // shards
    device = lax.axis_index("batch")
    section = lax.axis_index("section").astype(jnp.int32).reshape(1)
    states, weights = ({}, {}), {}
    mine = device.astype(jnp.int32).reshape(1)
    RingScatter.order = ()
    if ring:
        own = pack(
            {"device": mine, "section": section},
            qkv_weight[0],
            out_weight[0],
            up_weight[0],
            down_weight[0],
            biases,
            norm_gains[0],
            norm_shifts[0],
        )
        inputs, cotangent = turn_rows(lengths[:, 0], inputs, cotangent)
        put_up, put_down = ring_gather(own, mine, weights, width, inputs)
        small = weights["small"]
    else:
        gather = lambda value: lax.all_gather(value, "batch", axis=0, tiled=True)
        halves = [gather(value[0]) for value in (qkv_weight, out_weight, up_weight, down_weight)]
        blocks = lambda half: [half[:, chunk(j)] for j in range(half.shape[1] // D)]
        split = {"one": {}, "two": {}}
        for half, (qkv, out, up, down) in enumerate(
            zip(*(jnp.split(value, CORES) for value in halves))
        ):
            upper, lower = jnp.split(down, 2)
            gap = jnp.zeros((SMALL_ROWS, D), BF)
            split["one"][half] = (jnp.concatenate(blocks(qkv) + [out, gap, upper]),)
            split["two"][half] = (jnp.concatenate(blocks(up) + [lower]),)
        place_shards("one", mine, CORES, list(split["one"].items()), weights, ("first", "down"))
        place_shards("two", mine, CORES, list(split["two"].items()), weights, ("up", "down"))
        put_up = put_down = lambda mark: None
        norms = jnp.concatenate([norm_gains[0], norm_shifts[0]])
        packed = gather(jnp.concatenate([biases[0], norms.reshape(-1)])[None]).astype(F32)
        norms_all = packed[:, cut:].reshape(shards, 4, width).transpose(1, 0, 2)
        small = jnp.concatenate(
            [
                packed[:, :cut].reshape(BIAS_ROWS, D),
                norms_all.reshape(4, D),
                jnp.zeros((4, D), F32),
            ]
        )
    common = (section, lengths[:, 0])
    if not ring:
        inputs, cotangent = turn_rows(lengths[:, 0], inputs, cotangent)

    def run_forward(origin, row, source, parts=("attn", "up", "down"), marked=False, earlier=()):
        return forward(
            origin, row, parts, common, small, source, states[row], weights, marked, earlier
        )

    def run_backward(origin, row, source, parts=("ffn", "attn"), earlier=()):
        return backward(
            origin, row, parts, common, small, source, states[row], weights, earlier
        )

    mark = run_forward(0, 0, inputs[0], ("attn",), True)
    put_up(mark)
    run_forward(0, 0, None, ("up",))
    put_down(states[0]["slope"])
    result = run_forward(0, 0, None, ("down",))
    coming = relay(result, 1)
    second = relay(run_forward(0, 1, inputs[1]), 1)
    run_forward(1, 0, coming)
    coming = relay(run_backward(1, 0, cotangent[0]), -1)
    run_forward(1, 1, second, earlier=(states[0]["attn_sums"],))
    second = relay(run_backward(1, 1, cotangent[1]), -1)
    run_backward(0, 0, coming)
    halves = {}
    earlier = ()
    for piece in ("down", "up", "first"):
        halves[piece] = first_row_grad(piece, states[0], earlier)
        earlier = (halves[piece],)
    run_backward(0, 1, second, ("ffn",), earlier)
    down_own, *down_others = weight_grad("down", groups, mine, states, halves["down"])
    up_own, *up_others = weight_grad(
        "up", groups, mine, states, halves["up"], (down_own,)
    )
    RingScatter.order = (up_own,)
    if ring:
        ffn_ring = RingScatter("ffn", BLOCKS * width)
        ffn_ring.add(down_own, down_others, {1: slice(None)})
        ffn_ring.add(up_own, up_others, {-1: slice(None)})
    run_backward(0, 1, None, ("attn",), RingScatter.order)
    attn_own, *attn_others = weight_grad(
        "first", groups, mine, states, halves["first"]
    )
    if ring:
        RingScatter.order = (attn_own,)
        ffn_ring.step(3)
        attn_ring = RingScatter("attn", 2 * width)
        cuts = {1: slice(0, 2 * width), -1: slice(2 * width, None)}
        attn_ring.add(attn_own, attn_others, cuts, tuple(ffn_ring.came.values()))
        ffn_ring.step(2)
        attn_ring.step(3)
        ffn_ring.last_step(0)
        attn_ring.step(2)
        ffn_ring.last_step(1)
        attn_ring.step(1)
        ffn = ffn_ring.finish({"down": (BLOCKS * width, D), "up": (width, FF)}, mine)
        down_sum, up_sum = ffn["down"], ffn["up"]
        shapes = {"qkv": (width, 3 * D), "out": (width, D), "bias": (1, cut)}
        shapes.update({"gains": (2, width), "shifts": (2, width)})
        attn = attn_ring.finish(shapes, mine)
        qkv_sum, out_sum, bias_sum = attn["qkv"], attn["out"], attn["bias"]
        gain_sum, shift_sum = attn["gains"], attn["shifts"]
    else:
        scatter = lambda value: lax.psum_scatter(
            value, "batch", scatter_dimension=0, tiled=True
        ).astype(F32)
        half = D // CORES
        join = lambda parts: jnp.concatenate(
            [
                jnp.concatenate([part[0, chunk(j, half)] for part in parts])
                for j in range(BLOCKS)
            ],
            axis=1,
        )
        down_sum = scatter(jnp.concatenate([down_own[0], down_others[0][0]]))
        up_sum = scatter(join((up_own, up_others[0])))
        attn_sum = scatter(join((attn_own, attn_others[0])))
        qkv_sum, out_sum = attn_sum[:, : 3 * D], attn_sum[:, 3 * D :]
        ffn_sums = states[0]["ffn_sums"] + states[1]["ffn_sums"]
        attn_sums = states[0]["attn_sums"] + states[1]["attn_sums"]
        bias_total = jnp.concatenate([attn_sums[:2], ffn_sums[4:10]]).reshape(shards, cut)
        norm_rows = ffn_sums[:4].reshape(4, shards, width).transpose(1, 0, 2)
        small_sum = scatter(
            jnp.concatenate([bias_total, norm_rows.reshape(shards, 4 * width)], axis=1)
        )
        bias_sum = small_sum[:, :cut]
        norm_sum = small_sum[:, cut:].reshape(4, width)
        gain_sum, shift_sum = norm_sum[:2], norm_sum[2:]
    rows = leave_rows(states, lengths[:, 0], RingScatter.order if ring else ())
    return (
        rows["activations"][None, :, None],
        rows["input_grads"][None, :, None],
        qkv_sum[None],
        out_sum[None],
        up_sum[None],
        down_sum[None],
        bias_sum,
        gain_sum[None],
        shift_sum[None],
    )


def solution(mesh):
    in_specs = (
        P(None, "batch", None, None),
        P(None, "batch", None, None),
        P(None, "batch", None),
        P("section", "batch", None),
        P("section", "batch", None),
        P("section", "batch", None),
        P("section", "batch", None),
        P("section", "batch"),
        P("section", None, "batch"),
        P("section", None, "batch"),
    )
    out_specs = (
        P("section", None, "batch", None, None),
        P("section", None, "batch", None, None),
        P("section", "batch", None),
        P("section", "batch", None),
        P("section", "batch", None),
        P("section", "batch", None),
        P("section", "batch"),
        P("section", None, "batch"),
        P("section", None, "batch"),
    )
    return jax.shard_map(body, mesh=mesh, in_specs=in_specs, out_specs=out_specs, check_vma=False)
```

```python
from functools import partial

import jax
import jax.numpy as jnp
from jax import lax
from jax.experimental import pallas as pl
from jax.experimental.pallas import tpu as pltpu
from jax.sharding import PartitionSpec as P

D = 768
HEADS = 12
FF = 3072
HEAD_DIM = 64
ROW = 256
HALF = 128
PAIRS = HEADS // 2
PAIR = 2 * HEAD_DIM
FFC = FF // D
BIAS = 6144
VMEM_LIMIT = 10 * 1024 * 1024

BF = jnp.bfloat16
F32 = jnp.float32
epsilon = 1e-12
masked_value = -1e30
inv_sqrt2 = 0.7071067811865476
inv_sqrt2pi = 0.3989422804014327


def nn(a, b):
    return jnp.dot(a, b, preferred_element_type=F32)


def nt(a, b):
    return lax.dot_general(a, b, (((1,), (1,)), ((), ())), preferred_element_type=F32)


def tn(a, b):
    return lax.dot_general(a, b, (((0,), (0,)), ((), ())), preferred_element_type=F32)


def head_masks():
    lane = lax.broadcasted_iota(jnp.int32, (1, PAIR), 1)
    low = (lane < HEAD_DIM).astype(F32)
    return (low.astype(BF), (1.0 - low).astype(BF))


def by_head(values, masks):
    return jnp.concatenate([values * masks[0], values * masks[1]], axis=0)


def own_head(values):
    lane = lax.broadcasted_iota(jnp.int32, (1, PAIR), 1)
    return jnp.where(lane < HEAD_DIM, values[:HALF], values[HALF:])


def bounds_of(lengths_ref, micro):
    first = lengths_ref[micro, 0]
    second = first + lengths_ref[micro, 1]
    return first, second, second + lengths_ref[micro, 2]


def longest_start(lengths_ref, micro):
    bounds = bounds_of(lengths_ref, micro)
    start = jnp.int32(0)
    for place, bound in enumerate(bounds):
        start = jnp.where(lengths_ref[micro, place + 1] == HALF, bound, start)
    return start


def turn(lengths_ref, micro, back=False):
    start = longest_start(lengths_ref, micro)
    here = lax.broadcasted_iota(jnp.int32, (ROW, ROW), 0)
    there = lax.broadcasted_iota(jnp.int32, (ROW, ROW), 1)
    if back:
        here, there = there, here
    return jnp.where((here + start) & (ROW - 1) == there, 1.0, 0.0).astype(BF)


def segment_penalty(lengths_ref, micro):
    bounds = bounds_of(lengths_ref, micro)
    start = longest_start(lengths_ref, micro)

    def number(axis):
        place = lax.broadcasted_iota(jnp.int32, (HALF, HALF), axis)
        place = (place + start + HALF) & (ROW - 1)
        total = jnp.zeros((HALF, HALF), jnp.int32)
        for bound in bounds:
            total = total + jnp.where(place >= bound, 1, 0)
        return total

    return jnp.where(number(0) == number(1), 0.0, masked_value)


def standardize(values):
    centred = values - jnp.mean(values, axis=-1, keepdims=True)
    spread = jnp.mean(centred * centred, axis=-1, keepdims=True)
    scale = lax.rsqrt(spread + epsilon)
    return centred * scale, scale


def norm_back(grad, unit, scale, gain):
    scaled = grad * gain
    mean_one = jnp.mean(scaled, axis=-1, keepdims=True)
    mean_two = jnp.mean(scaled * unit, axis=-1, keepdims=True)
    return scale * (scaled - mean_one - unit * mean_two)


class Copies:
    def __init__(self, sems):
        self.sems = sems
        self.used = 0

    def start(self, src, dst):
        copy = pltpu.make_async_copy(src, dst, self.sems.at[self.used])
        self.used += 1
        copy.start()
        return copy


class Reader:
    def __init__(self, refs):
        self.refs = list(refs)

    def take(self, count=None):
        if count is None:
            return self.refs.pop(0)
        taken, self.refs = self.refs[:count], self.refs[count:]
        return taken


def chunk(index, size=D):
    return slice(index * size, (index + 1) * size)


HBM = pl.BlockSpec(memory_space=pltpu.HBM)
SMEM = pl.BlockSpec(memory_space=pltpu.SMEM)
VMEM = pl.BlockSpec(memory_space=pltpu.VMEM)
LANES = 128
BLOCKS = 4
SMALL_ROWS = 16
BIAS_ROWS = BIAS // D

SHAPES = {
    "tokens": ((ROW, D), BF),
    "qkv": ((ROW, 3 * D), BF),
    "probs": ((PAIRS, 2, 2 * HALF, HALF), BF),
    "context": ((ROW, D), BF),
    "hidden": ((ROW, D), BF),
    "unit1": ((ROW, D), F32),
    "scale1": ((ROW, LANES), F32),
    "active": ((ROW, FF), BF),
    "slope": ((ROW, FF), BF),
    "unit2": ((ROW, D), F32),
    "scale2": ((ROW, LANES), F32),
    "down_side": ((ROW, D), BF),
    "attended": ((ROW, D), BF),
    "sum1": ((ROW, D), F32),
    "result": ((ROW, D), BF),
    "grad": ((ROW, D), BF),
    "ffn_sums": ((16, D), F32),
    "attn_sums": ((8, D), F32),
}
PIECES = {"first": (BLOCKS, D, D), "up": (BLOCKS, D, D), "down": (FF, D)}
PART_PIECE = {"attn": "first", "up": "up", "down": "down"}
MAKES = {
    "attn": ("tokens", "qkv", "probs", "context", "unit1", "scale1", "hidden"),
    "up": ("active", "slope"),
    "down": ("unit2", "scale2", "result"),
}
TAKES = {"attn": (), "up": ("hidden",), "down": ("unit1", "active")}
BACK_MAKES = {
    "ffn": ("down_side", "slope", "attended", "ffn_sums"),
    "attn": ("qkv", "attn_sums", "grad"),
}
BACK_PASSES = {"ffn": ("sum1",), "attn": ()}
BACK_TAKES = {
    "ffn": ("unit2", "scale2", "unit1", "scale1"),
    "attn": ("probs", "attended", "sum1"),
}
BACK_PIECES = {"ffn": ("down", "up"), "attn": ("first",)}


class Call:
    def __init__(self):
        self.operands, self.specs, self.in_names = [], [], []
        self.outs, self.out_specs, self.out_names = [], [], []
        self.scratch, self.scratch_names = [], []
        self.aliases = {}

    def give(self, name, value, spec):
        if spec is not SMEM:
            value = pltpu.with_memory_space_constraint(value, spec.memory_space)
        self.in_names.append(name)
        self.operands.append(value)
        self.specs.append(spec)

    def make(self, name, shape, kind, spec, old=None):
        if old is not None:
            self.aliases[len(self.operands)] = len(self.outs)
            self.give("old_" + name, old, spec)
        self.out_names.append(name)
        self.outs.append((pltpu.VMEM if spec is VMEM else pltpu.HBM)(shape, kind))
        self.out_specs.append(spec)

    def follow(self, values):
        for place, value in enumerate(values):
            self.give(("earlier", place), value, VMEM)

    def of_parts(self, parts, state, takes, makes, passes=None):
        inside = [key for part in parts for key in makes[part]]
        inside += [key for part in parts for key in (passes[part] if passes else ())]
        for part in parts:
            for key in takes[part]:
                if key not in inside:
                    self.give(key, state[key], VMEM)
        for part in parts:
            for key in makes[part]:
                self.make(key, *SHAPES[key], VMEM, state.get(key))
            for key in passes[part] if passes else ():
                if part == parts[-1]:
                    self.make(key, *SHAPES[key], VMEM)
                else:
                    self.hold(key, pltpu.VMEM(*SHAPES[key]))

    def hold(self, name, value):
        self.scratch_names.append(name)
        self.scratch.append(value)

    def run(self, kernel, name, time):
        names = self.in_names + self.out_names + self.scratch_names

        def named(*refs):
            kernel(dict(zip(names, refs)))

        found = pl.pallas_call(
            named,
            out_shape=self.outs,
            in_specs=self.specs,
            out_specs=self.out_specs,
            scratch_shapes=self.scratch,
            input_output_aliases=self.aliases,
            name=name,
            compiler_params=pltpu.CompilerParams(vmem_limit_bytes=VMEM_LIMIT),
            cost_estimate=pl.CostEstimate(
                flops=int(time * 1.1e9), bytes_accessed=1 << 20, transcendentals=0
            ),
        )(*self.operands)
        return dict(zip(self.out_names, found))


def rows_of(pieces, start, size):
    for piece in pieces:
        if start < piece.shape[0]:
            return piece[start : start + size]
        start -= piece.shape[0]


STREAMS = {
    "one": [("first", j) for j in range(BLOCKS)] + [("small", 0), ("down", 0)],
    "two": [("up", j) for j in range(BLOCKS)] + [("down", 1)],
}
EARLY = {"one": BLOCKS + 1, "two": BLOCKS}
FAR_CUT = {"one": 3, "two": 3}


def stream_sizes(stream, rows):
    size = {"first": rows, "up": rows, "small": SMALL_ROWS, "down": 2 * rows}
    return [size[name] for name, _ in STREAMS[stream]]


def device_at(get, place, devices):
    if devices == CORES:
        return place
    side, index = divmod(place, len(RING))
    own = get("device")[0]
    z, y, core = own // 4, (own // 2) & 1, own & 1
    spot = (jnp.where(y == 0, z, 7 - z) + RING[index]) & 7
    z, y = jnp.where(spot < 4, spot, 7 - spot), jnp.where(spot < 4, 0, 1)
    return (z * 2 + y) * 2 + (core if side == 0 else 1 - core)


def place_kernel(plan, refs):
    get = refs.__getitem__
    devices, stream, own, came = plan
    rows = D // devices
    small = refs.get("small")
    if small is not None and "old_small" not in refs:
        small[...] = jnp.zeros(small.shape, F32)

    def put(stream, entries, place, pieces):
        device = device_at(get, place, devices)
        start = 0
        sizes = stream_sizes(stream, rows)[entries]
        for (name, block), size in zip(STREAMS[stream][entries], sizes):
            part = rows_of(pieces, start, size)
            start += size
            if name == "down":
                at = pl.multiple_of(device * BLOCKS * rows + block * size, size)
                get("down")[pl.ds(at, size)] = part
            elif name != "small":
                get(name)[block, pl.ds(pl.multiple_of(device * rows, rows), rows)] = part
            elif small is not None:
                more = part.astype(F32)
                width = BIAS // devices
                per_row = D // width
                line = lax.broadcasted_iota(jnp.int32, (BIAS_ROWS, D), 0)
                lane_part = lax.broadcasted_iota(jnp.int32, (BIAS_ROWS, D), 1) // width
                mine = (line == device // per_row) & (lane_part == device % per_row)
                bias = jnp.concatenate([more[0:1, :width]] * per_row, axis=1)
                small[:BIAS_ROWS] += jnp.where(mine, bias, 0.0)
                small[BIAS_ROWS : BIAS_ROWS + 4] += more[1:5]

    for index, (place, count) in enumerate(own):
        pieces = [get(("shard", index, part)) for part in range(count)]
        put(stream, slice(None), place, pieces)
        if ("packed", 0) in refs:
            edge = sum(stream_sizes(stream, rows)[: EARLY[stream]])
            start = 0
            for piece in pieces:
                stop = start + piece.shape[0]
                middle = min(max(edge, start), stop)
                if middle > start:
                    get(("packed", 0))[index, start:middle] = piece[: middle - start]
                if middle < stop:
                    get(("packed", 1))[index, middle - edge : stop - edge] = piece[middle - start :]
                start = stop
    for number, (stream, entries) in enumerate(came):
        for index in range(len(RING)):
            put(stream, entries, index + len(RING), [get(("came", number)).at[index]])


def place_shards(stream, device, devices, own, weights, made, came=(), earlier=(), pack=False):
    call = Call()
    call.follow(earlier)
    call.give("device", device, SMEM)
    for index, (place, shard) in enumerate(own):
        for part, piece in enumerate(shard):
            call.give(("shard", index, part), piece, VMEM)
    for number, (value, _, _) in enumerate(came):
        call.give(("came", number), value, VMEM)
    for key in made:
        if key == "small":
            call.make(key, (SMALL_ROWS, D), F32, VMEM, weights.get(key))
        else:
            call.make(key, PIECES[key], BF, VMEM, weights.get(key))
    if pack:
        sizes = stream_sizes(stream, D // devices)
        for number, part in enumerate((sizes[: EARLY[stream]], sizes[EARLY[stream] :])):
            call.make(("packed", number), (len(own), sum(part), D), BF, VMEM)
    counts = [(place, len(shard)) for place, shard in own]
    plan = (devices, stream, counts, [spec[1:] for spec in came])
    found = call.run(partial(place_kernel, plan), "place_" + "_".join(made), 0.5)
    weights.update((key, found[key]) for key in made)
    return [found[key] for key in found if key not in made]


def forward_kernel(origin, row, parts, refs):
    get = refs.__getitem__
    small = get("small")
    bias = lambda index: small[index : index + 1, :]
    gain = lambda index: bias(BIAS_ROWS + index)
    shift = lambda index: bias(BIAS_ROWS + 2 + index)
    section = get("section")[0]
    @pl.when(section == origin)
    def _():
        if "attn" in parts:
            tokens = get("source")[...]
            get("tokens")[...] = tokens
            qkv, probs, context, weight = get("qkv"), get("probs"), get("context"), get("first")
            penalty = segment_penalty(get("lengths"), row)
            for j in range(3):
                part = nn(tokens, weight[j])
                if j != 1:
                    part = part + bias(j // 2)
                qkv[:, chunk(j)] = part.astype(BF)
            masks = head_masks()
            for pair in range(PAIRS):
                at = pair * PAIR
                for half in range(2):
                    rows = chunk(half, HALF)
                    keys = by_head(qkv[rows, D + at : D + at + PAIR], masks)
                    scores = nt(keys, qkv[rows, at : at + PAIR]).reshape(2, HALF, HALF)
                    if half == 1:
                        scores = scores + penalty
                    peak = jnp.max(scores, axis=1, keepdims=True)
                    raised = jnp.exp((scores - peak) * HEAD_DIM ** (-0.5))
                    share = raised * (1.0 / jnp.sum(raised, axis=1, keepdims=True))
                    share = share.reshape(2 * HALF, HALF).astype(BF)
                    probs[pair, half] = share
                    values = by_head(qkv[rows, 2 * D + at : 2 * D + at + PAIR], masks)
                    context[rows, at : at + PAIR] = tn(share, values).astype(BF)
            attended = nn(context[...], weight[3]) + bias(2)
            unit, scale = standardize(tokens.astype(F32) + attended)
            get("unit1")[...] = unit
            get("scale1")[...] = jnp.broadcast_to(scale, (ROW, LANES))
            get("hidden")[...] = (unit * gain(0) + shift(0)).astype(BF)
        if "down" in parts:
            total = get("unit1")[...] * gain(0) + shift(0) + bias(7)
        if "up" in parts:
            hidden, active, slope = get("hidden"), get("active"), get("slope")
            for j in range(FFC):
                inner = nn(hidden[...], get("up")[j]) + bias(3 + j)
                phi = 0.5 * (1.0 + lax.erf(inner * inv_sqrt2))
                active[:, chunk(j)] = (inner * phi).astype(BF)
                bell = jnp.exp(inner * inner * -0.5) * inv_sqrt2pi
                slope[:, chunk(j)] = (phi + inner * bell).astype(BF)
                if "down" in parts:
                    total = total + nn(active[:, chunk(j)], get("down")[chunk(j)])
        if "down" in parts:
            if "up" not in parts:
                total = total + nn(get("active")[...], get("down")[...])
            unit, scale = standardize(total)
            get("result")[...] = (unit * gain(1) + shift(1)).astype(BF)
            get("unit2")[...] = unit
            get("scale2")[...] = jnp.broadcast_to(scale, (ROW, LANES))

    if "mark" in refs:
        get("mark")[...] = jnp.zeros((8, LANES), F32)


def forward(origin, row, parts, common, small, source, state, weights, marked=False, earlier=()):
    section, lengths = common
    call = Call()
    call.follow(earlier)
    call.give("section", section, SMEM)
    call.give("small", small, VMEM)
    if "attn" in parts:
        call.give("lengths", lengths, SMEM)
        call.give("source", source, VMEM)
    for part in parts:
        key = PART_PIECE[part]
        call.give(key, weights[key], VMEM)
    if marked:
        call.make("mark", (8, LANES), F32, VMEM)
    call.of_parts(parts, state, TAKES, MAKES)
    found = call.run(
        partial(forward_kernel, origin, row, parts),
        "forward_" + "_".join(parts),
        0.1 if marked else 3 * len(parts),
    )
    mark = found.pop("mark", None)
    state.update(found)
    return mark if marked else found.get("result")


def backward_kernel(origin, row, parts, refs):
    get = refs.__getitem__
    small = get("small")
    gain = lambda index: small[BIAS_ROWS + index : BIAS_ROWS + index + 1, :]

    @pl.when(get("section")[0] == origin)
    def _():
        if "ffn" in parts:
            grad = get("source")[...].astype(F32)
            sums, inner = get("ffn_sums"), get("slope")
            unit = get("unit2")[...]
            sums[1:2, :] = jnp.sum(grad * unit, axis=0, keepdims=True)
            sums[3:4, :] = jnp.sum(grad, axis=0, keepdims=True)
            grad = norm_back(grad, unit, get("scale2")[:, 0:1], gain(1))
            sums[9:10, :] = jnp.sum(grad, axis=0, keepdims=True)
            side = grad.astype(BF)
            get("down_side")[...] = side
            sum_v = get("sum_v")
            sum_v[...] = grad
            for j in range(FFC):
                through = nt(side, get("down")[chunk(j)])
                through = through * inner[:, chunk(j)].astype(F32)
                sums[5 + j : 6 + j, :] = jnp.sum(through, axis=0, keepdims=True)
                inner[:, chunk(j)] = through.astype(BF)
            grad = sum_v[...]
            for j in range(BLOCKS):
                grad = grad + nt(inner[:, chunk(j)], get("up")[j])
            unit = get("unit1")[...]
            sums[0:1, :] = jnp.sum(grad * unit, axis=0, keepdims=True)
            sums[2:3, :] = jnp.sum(grad, axis=0, keepdims=True)
            grad = norm_back(grad, unit, get("scale1")[:, 0:1], gain(0))
            sums[4:5, :] = jnp.sum(grad, axis=0, keepdims=True)
            sums[10:16, :] = jnp.zeros((6, D), F32)
            get("sum1")[...] = grad
            get("attended")[...] = grad.astype(BF)
        if "attn" in parts:
            weight = get("first")
            context_grad = nt(get("attended")[...], weight[3]).astype(BF)
            masks = head_masks()
            qkv, sums = get("qkv"), get("attn_sums")
            sums[2:8, :] = jnp.zeros((6, D), F32)
            for pair in range(PAIRS):
                at = pair * PAIR
                spans = [slice(which * D + at, which * D + at + PAIR) for which in range(3)]
                biases = [0.0, 0.0]
                for half in range(2):
                    rows = chunk(half, HALF)
                    queries = qkv[rows, spans[0]]
                    keys = by_head(qkv[rows, spans[1]], masks)
                    values = by_head(qkv[rows, spans[2]], masks)
                    pair_grad = context_grad[rows, at : at + PAIR]
                    share = get("probs")[pair, half]
                    wide = share.astype(F32)
                    weighted = wide * nt(values, pair_grad)
                    inner_sum = jnp.sum(weighted.reshape(2, HALF, HALF), axis=1, keepdims=True)
                    score_grad = weighted.reshape(2, HALF, HALF)
                    score_grad = score_grad - wide.reshape(2, HALF, HALF) * inner_sum
                    score_grad = (score_grad * HEAD_DIM ** (-0.5)).reshape(2 * HALF, HALF)
                    score_grad = score_grad.astype(BF)
                    grads = (
                        tn(score_grad, keys),
                        own_head(nn(score_grad, queries)),
                        own_head(nn(share, pair_grad)),
                    )
                    for span, value in zip(spans, grads):
                        qkv[rows, span] = value.astype(BF)
                    for line in range(2):
                        biases[line] = biases[line] + jnp.sum(
                            grads[2 * line], axis=0, keepdims=True
                        )
                for line in range(2):
                    sums[line : line + 1, at : at + PAIR] = biases[line]
            grad = get("sum1")[...]
            for j in range(3):
                grad = grad + nt(qkv[:, chunk(j)], weight[j])
            get("grad")[...] = grad.astype(BF)


def backward(origin, row, parts, common, small, source, state, weights, earlier=()):
    call = Call()
    call.follow(earlier)
    call.give("section", common[0], SMEM)
    call.give("small", small, VMEM)
    for part in parts:
        for key in BACK_PIECES[part]:
            call.give(key, weights[key], VMEM)
    if "ffn" in parts:
        call.give("source", source, VMEM)
        call.hold("sum_v", pltpu.VMEM((ROW, D), F32))
    call.of_parts(parts, state, BACK_TAKES, BACK_MAKES, BACK_PASSES)
    found = call.run(
        partial(backward_kernel, origin, row, parts), "backward_" + "_".join(parts), 5 * len(parts)
    )
    state.update(found)
    return found.get("grad")


def other_groups(groups):
    if groups == 1:
        return [("other0", (0,))]
    return [("other0", (7,)), ("other1", tuple(range(7)))]


def other_at(groups, place):
    for name, places in other_groups(groups):
        if place in places:
            return name, places.index(place)


WEIGHT_TAKES = {
    "down": ("active", "down_side"),
    "up": ("hidden", "slope"),
    "first": ("context", "attended", "tokens", "qkv"),
}


def product_of(piece, block, get):
    if piece == "down":
        return tn(get("active")[:, chunk(block)], get("down_side")[...])
    if piece == "up":
        return tn(get("hidden")[...], get("slope")[:, chunk(block)])
    if block == 3:
        return tn(get("context")[...], get("attended")[...])
    return tn(get("tokens")[...], get("qkv")[:, chunk(block)])


def first_row_kernel(piece, refs):
    for block in range(BLOCKS):
        product = product_of(piece, block, refs.__getitem__)
        refs["product"][block] = product.astype(BF)


def first_row_grad(piece, state, earlier):
    call = Call()
    call.follow(earlier)
    for key in WEIGHT_TAKES[piece]:
        call.give(key, state[key], VMEM)
    call.make("product", (BLOCKS, D, D), BF, VMEM)
    return call.run(partial(first_row_kernel, piece), "row_" + piece, 2)["product"]


def weight_kernel(piece, groups, refs):
    get = refs.__getitem__
    held = get("held")
    rows = D // (2 * groups)
    goes = [device_at(get, place, 2 * groups) for place in range(2 * groups)]

    def store(side, place, span, value):
        if side == 0:
            get("own")[place, span] = value
        else:
            name, index = other_at(groups, place)
            get(name)[index, span] = value

    def block_of(block):
        before = get("before")[block].astype(F32)
        return (before + product_of(piece, block, get)).astype(BF)

    places = [(place // groups, place % groups) for place in range(2 * groups)]
    if piece == "down":
        for block in range(BLOCKS):
            held[chunk(block)] = block_of(block)
        for side, place in places:
            at = pl.multiple_of(goes[side * groups + place] * BLOCKS * rows, BLOCKS * rows)
            store(side, place, slice(None), held[pl.ds(at, BLOCKS * rows)])
        return
    if piece == "first" and groups > 1:
        sums, row = get("sums"), get("row_sums")
        bias_rows = [get(("attn_sums", 0))[k : k + 1] + get(("attn_sums", 1))[k : k + 1] for k in range(2)]
        ffn = get(("ffn_sums", 0))[...] + get(("ffn_sums", 1))[...]
        bias_rows += [ffn[4 + k : 5 + k] for k in range(6)]
        row[...] = jnp.zeros((SMALL_ROWS, D), F32)
        row[1:5, :] = ffn[:4]
        per_row = 2 * groups // BIAS_ROWS
        width = D // per_row
        for device in range(2 * groups):
            start = device % per_row * width
            row[0:1, :width] = bias_rows[device // per_row][:, start : start + width]
            sums[device] = row[...].astype(BF)
        for side, place in places:
            device = goes[side * groups + place]
            store(side, place, slice(BLOCKS * rows, None), sums[device])
    for block in (3, 0, 1, 2):
        held[...] = block_of(block)
        for side, place in places:
            at = pl.multiple_of(goes[side * groups + place] * rows, rows)
            store(side, place, chunk(block, rows), held[pl.ds(at, rows)])


def weight_grad(piece, groups, device, states, before, earlier=()):
    call = Call()
    call.follow(earlier)
    call.give("device", device, SMEM)
    call.give("before", before, VMEM)
    for key in WEIGHT_TAKES[piece]:
        call.give(key, states[1][key], VMEM)
    rows = BLOCKS * D // (2 * groups)
    if piece == "first":
        rows += SMALL_ROWS
        for key in ("attn_sums", "ffn_sums"):
            for row, state in enumerate(states):
                call.give((key, row), state[key], VMEM)
        call.hold("sums", pltpu.VMEM((2 * groups, SMALL_ROWS, D), BF))
        call.hold("row_sums", pltpu.VMEM((SMALL_ROWS, D), F32))
    call.make("own", (groups, rows, D), BF, VMEM)
    for name, places in other_groups(groups):
        call.make(name, (len(places), rows, D), BF, VMEM)
    call.hold("held", pltpu.VMEM((FF if piece == "down" else D, D), BF))
    found = call.run(partial(weight_kernel, piece, groups), "weight_" + piece, 3)
    return [found["own"]] + [found[name] for name, _ in other_groups(groups)]


CORES = 2
RING = (0, -1, 1, -2, 2, -3, 3, 4)


def ring_device(place, core):
    place = place % len(RING)
    z, y = (place, 0) if place < 4 else (7 - place, 1)
    return (z * 2 + y) * 2 + core


def ring_places():
    return [(place, core) for place in range(len(RING)) for core in range(CORES)]


def around(value, steps):
    pairs = [(ring_device(p, c), ring_device(p + steps, c)) for p, c in ring_places()]
    return lax.ppermute(value, "batch", pairs)


def to_other_core(value):
    pairs = [(ring_device(p, c), ring_device(p, 1 - c)) for p, c in ring_places()]
    return lax.ppermute(value, "batch", pairs)


def after(value, *earlier):
    return lax.optimization_barrier((value,) + earlier)[0]


def pack_kernel(stream, refs):
    get = refs.__getitem__
    rows = get("down").shape[0] // BLOCKS
    copies = Copies(get("sems"))
    small = []
    if stream == "one":
        small = [copies.start(get(k), get(k + "_v")) for k in ("bias", "gains", "shifts")]
    arriving = []
    small_at = 0
    start = 0
    for (name, block), size in zip(STREAMS[stream], stream_sizes(stream, rows)):
        target = get(stream).at[pl.ds(start, size)]
        if name == "small":
            small_at = start
        elif name == "down":
            source = get("down").at[pl.ds(block * size, size)]
            arriving.append(copies.start(source, target))
        elif name == "first" and block == 3:
            arriving.append(copies.start(get("out"), target))
        else:
            source = get("qkv" if name == "first" else "up").at[:, chunk(block)]
            arriving.append(copies.start(source, target))
        start += size
    if small:
        pack_small(get, small, get(stream).at[pl.ds(small_at, SMALL_ROWS)], rows)
    for copy in arriving:
        copy.wait()


def pack_small(get, arriving, target, rows):
    row = get("row")
    row[...] = jnp.zeros((SMALL_ROWS, D), F32)
    for copy in arriving:
        copy.wait()
    row[1:3, :rows] = get("gains_v")[...].astype(F32)
    row[3:5, :rows] = get("shifts_v")[...].astype(F32)
    row[...] = pltpu.roll(row[...], get("device")[0] * rows, 1)
    row[0:1, : get("bias").shape[1]] = get("bias_v")[...].astype(F32)
    target[...] = row[...].astype(BF)


def pack(stream, scalars, **values):
    call = Call()
    for name, value in scalars.items():
        call.give(name, value, SMEM)
    for name, value in values.items():
        call.give(name, value, HBM)
    rows = values["down"].shape[0] // BLOCKS
    call.make(stream, (sum(stream_sizes(stream, rows)), D), BF, VMEM)
    if stream == "one":
        call.hold("row", pltpu.VMEM((SMALL_ROWS, D), F32))
        for name in ("bias", "gains", "shifts"):
            call.hold(name + "_v", pltpu.VMEM(values[name].shape, BF))
    call.hold("sems", pltpu.SemaphoreType.DMA((12,)))
    return call.run(partial(pack_kernel, stream), "pack_" + stream, 1)[stream]


def cut_kernel(cut, refs):
    get = refs.__getitem__
    get(1)[...] = get("forwards")[:cut]
    get(-1)[...] = get("backwards")[cut:]


def cut_two(forwards, backwards, cut, earlier):
    call = Call()
    call.follow(earlier)
    call.give("forwards", forwards, VMEM)
    call.give("backwards", backwards, VMEM)
    call.make(1, (cut, D), BF, VMEM)
    call.make(-1, (forwards.shape[0] - cut, D), BF, VMEM)
    found = call.run(partial(cut_kernel, cut), "cut", 0.3)
    return found[1], found[-1]


def ring_gather(own, device, weights, rows, earlier):
    held = {stream: {0: (value,)} for stream, value in own.items()}

    def hop(stream, ahead):
        here = held[stream]
        here[-ahead] = (around(here[1 - ahead][0], 1),)
        here[ahead] = (around(here[ahead - 1][0], -1),)

    for ahead in (1, 2, 3):
        for stream in STREAMS:
            hop(stream, ahead)
    for stream in STREAMS:
        here = held[stream]
        cut = sum(stream_sizes(stream, rows)[: FAR_CUT[stream]])
        sends = cut_two(here[-3][0], here[3][0], cut, earlier)
        here[4] = tuple(around(send, way) for send, way in zip(sends, (1, -1)))
    came = {}
    for stream, made in (("one", ("first", "down", "small")), ("two", ("up", "down"))):
        shards = [(RING.index(ahead), held[stream][ahead]) for ahead in RING]
        packed = place_shards(stream, device, D // rows, shards, weights, made, pack=True)
        came[stream] = [to_other_core(value) for value in packed]

    def put_other(made, streams, early, earlier=()):
        number = 0 if early else 1
        entries = {s: slice(0, EARLY[s]) if early else slice(EARLY[s], None) for s in streams}
        values = [(came[s][number], s, entries[s]) for s in streams]
        place_shards(None, device, D // rows, (), weights, made, values, earlier)

    put_other(("first", "small"), ("one",), True)
    return (
        lambda mark: put_other(("up",), ("two",), True, (mark,)),
        lambda mark: put_other(("down",), ("one", "two"), False, (mark,)),
    )


def both_cores(get, index, place, part=slice(None)):
    name, at = other_at(len(RING), place)
    other = get((name, index))[at, part].astype(F32)
    return get(("own", index))[place, part].astype(F32) + other


def far_kernel(index, cuts, refs):
    get = refs.__getitem__
    for way, part in cuts.items():
        get(way)[...] = both_cores(get, index, RING.index(4), part).astype(BF)


def merge_kernel(ahead, cut, count, way, refs):
    get = refs.__getitem__
    out, came = get(way), get(("came", way))
    place = RING.index(way * ahead)
    parts = [both_cores(get, index, place) for index in range(count)]
    total = jnp.concatenate(parts, axis=0) if count > 1 else parts[0]
    if ahead < 3:
        out[...] = (total + came[...].astype(F32)).astype(BF)
    else:
        near, far = (slice(0, cut), slice(cut, None))[::way]
        out[near] = (total[near] + came[...].astype(F32)).astype(BF)
        out[far] = total[far].astype(BF)


def merge_part_kernel(index, rows, way, refs):
    get = refs.__getitem__
    total = both_cores(get, index, RING.index(way)) + get(("came", way))[rows].astype(F32)
    get(way)[...] = total.astype(BF)


def finish_kernel(piece, count, refs):
    get = refs.__getitem__
    copies, leaving = Copies(get("sems")), []

    def leave(name):
        leaving.append(copies.start(get(name + "_v"), get(name)))

    total = []
    for index in range(count):
        part = both_cores(get, index, 0)
        for way in (1, -1):
            came = get(("last", index, way) if count > 1 else ("came", way))
            part = part + came[...].astype(F32)
        total.append(part)
    total = jnp.concatenate(total, axis=0) if count > 1 else total[0]
    if piece == "ffn":
        rows = get("up").shape[0]
        get("down_v")[...] = total[: BLOCKS * rows]
        leave("down")
        for j in range(BLOCKS):
            get("up_v")[:, chunk(j)] = total[chunk(BLOCKS + j, rows)]
        leave("up")
    else:
        rows = get("out").shape[0]
        for j in range(3):
            get("qkv_v")[:, chunk(j)] = total[chunk(j, rows)]
        leave("qkv")
        get("out_v")[...] = total[chunk(3, rows)]
        leave("out")
        small = total[BLOCKS * rows : BLOCKS * rows + 8]
        get("bias_v")[...] = small[:1, : get("bias").shape[1]]
        leave("bias")
        turned = pltpu.roll(small, lax.rem(D - get("device")[0] * rows, D), 1)
        get("gains_v")[...] = turned[1:3, :rows]
        leave("gains")
        get("shifts_v")[...] = turned[3:5, :rows]
        leave("shifts")
    for copy in leaving:
        copy.wait()


class RingScatter:
    order = ()

    def __init__(self, piece, cut):
        self.piece, self.cut, self.rows = piece, cut, 0
        self.parts, self.came, self.last = [], {}, []

    def run(self, call, kernel, name):
        call.follow(RingScatter.order)
        found = call.run(kernel, name + "_" + self.piece, 0.5)
        sent = [way for way in (1, -1) if way in found]
        RingScatter.order = (found[sent[0]],)
        self.came.update((way, around(found[way], way)) for way in sent)

    def add(self, own, others, cuts, late=()):
        index = len(self.parts)
        held = {"other0": to_other_core(others[0])}
        self.parts.append((own, held))
        self.rows += own.shape[1]
        call = Call()
        self.give(call, ("other0",), index)
        for way, part in cuts.items():
            call.make(way, (len(range(*part.indices(own.shape[1]))), D), BF, VMEM)
        self.run(call, partial(far_kernel, index, cuts), "far")
        earlier = late + tuple(self.came.values()) if late else (held["other0"],)
        held["other1"] = to_other_core(after(others[1], *earlier))

    def give(self, call, names, only=None, ways=None):
        for index, (own, others) in enumerate(self.parts):
            if only in (None, index):
                call.give(("own", index), own, VMEM)
                for name in names:
                    call.give((name, index), others[name], VMEM)
        if only is None:
            for way, value in self.came.items():
                if ways is None or way in ways:
                    call.give(("came", way), value, VMEM)

    def step(self, ahead):
        for way in (1, -1):
            call = Call()
            self.give(call, ("other1",), ways=(way,))
            call.make(way, (self.rows, D), BF, VMEM)
            kernel = partial(merge_kernel, ahead, self.cut, len(self.parts), way)
            self.run(call, kernel, "merge")

    def last_step(self, index):
        own, others = self.parts[index]
        start = sum(part.shape[1] for part, _ in self.parts[:index])
        rows = slice(start, start + own.shape[1])
        sent = {}
        for way in (1, -1):
            call = Call()
            before = (self.last[index - 1][way],) if index else ()
            call.follow(RingScatter.order + before)
            call.give(("own", index), own, VMEM)
            call.give(("other1", index), others["other1"], VMEM)
            call.give(("came", way), self.came[way], VMEM)
            call.make(way, own.shape[1:], BF, VMEM)
            kernel = partial(merge_part_kernel, index, rows, way)
            found = call.run(kernel, "merge_part_" + self.piece, 0.5)
            RingScatter.order = (found[way],)
            sent[way] = around(found[way], way)
        self.last.append(sent)

    def finish(self, shapes, device):
        call = Call()
        if self.last:
            self.came = {}
            for index, came in enumerate(self.last):
                for way, value in came.items():
                    call.give(("last", index, way), value, VMEM)
        self.give(call, ("other1",))
        call.give("device", device, SMEM)
        for name, shape in shapes.items():
            call.make(name, shape, F32, HBM)
            call.hold(name + "_v", pltpu.VMEM(shape, F32))
        call.hold("sems", pltpu.SemaphoreType.DMA((8,)))
        kernel = partial(finish_kernel, self.piece, len(self.parts))
        return call.run(kernel, "finish_" + self.piece, 1)


def turn_kernel(refs):
    for row in range(2):
        matrix = turn(refs["lengths"], row)
        for name in ("inputs", "cotangent"):
            refs[name, row][...] = nn(matrix, refs[name][row, 0]).astype(BF)


def turn_rows(lengths, inputs, cotangent):
    call = Call()
    call.give("lengths", lengths, SMEM)
    call.give("inputs", inputs, VMEM)
    call.give("cotangent", cotangent, VMEM)
    for name in ("inputs", "cotangent"):
        for row in range(2):
            call.make((name, row), (ROW, D), BF, VMEM)
    found = call.run(turn_kernel, "turn_rows", 1)
    return [[found[name, row] for row in range(2)] for name in ("inputs", "cotangent")]


def leave_kernel(refs):
    copies = Copies(refs["sems"])
    leaving = []
    for row in range(2):
        back = turn(refs["lengths"], row, True)
        for place, name in enumerate(("activations", "input_grads")):
            held = refs["held"].at[2 * row + place]
            held[...] = nn(back, refs[name, row][...]).astype(BF)
            leaving.append(copies.start(held, refs[name].at[row]))
    for copy in leaving:
        copy.wait()


def leave_rows(states, lengths, earlier=()):
    call = Call()
    call.follow(earlier)
    call.give("lengths", lengths, SMEM)
    for name, key in (("activations", "result"), ("input_grads", "grad")):
        for row, state in enumerate(states):
            call.give((name, row), state[key], VMEM)
        call.make(name, (2, ROW, D), BF, HBM)
    call.hold("held", pltpu.VMEM((4, ROW, D), BF))
    call.hold("sems", pltpu.SemaphoreType.DMA((4,)))
    return call.run(leave_kernel, "leave_rows", 1)


def relay(value, steps):
    count = lax.axis_size("section")
    first, last = (max(0, -steps), min(count, count - steps))
    return lax.ppermute(
        value, "section", [(source, source + steps) for source in range(first, last)]
    )


def body(
    inputs,
    cotangent,
    lengths,
    qkv_weight,
    out_weight,
    up_weight,
    down_weight,
    biases,
    norm_gains,
    norm_shifts,
):
    shards = lax.axis_size("batch")
    ring = shards == CORES * len(RING)
    groups = len(RING) if ring else 1
    width = D // shards
    cut = BIAS // shards
    device = lax.axis_index("batch")
    section = lax.axis_index("section").astype(jnp.int32).reshape(1)
    states, weights = ({}, {}), {}
    mine = device.astype(jnp.int32).reshape(1)
    RingScatter.order = ()
    if ring:
        scalars = {"device": mine, "section": section}
        small = {"bias": biases, "gains": norm_gains[0], "shifts": norm_shifts[0]}
        down = down_weight[0]
        own = {
            "one": pack("one", scalars, qkv=qkv_weight[0], out=out_weight[0], down=down, **small),
            "two": pack("two", scalars, up=up_weight[0], down=down),
        }
        inputs, cotangent = turn_rows(lengths[:, 0], inputs, cotangent)
        put_up, put_down = ring_gather(own, mine, weights, width, inputs)
        small = weights["small"]
    else:
        gather = lambda value: lax.all_gather(value, "batch", axis=0, tiled=True)
        halves = [gather(value[0]) for value in (qkv_weight, out_weight, up_weight, down_weight)]
        blocks = lambda half: [half[:, chunk(j)] for j in range(half.shape[1] // D)]
        split = {"one": {}, "two": {}}
        for half, (qkv, out, up, down) in enumerate(
            zip(*(jnp.split(value, CORES) for value in halves))
        ):
            upper, lower = jnp.split(down, 2)
            gap = jnp.zeros((SMALL_ROWS, D), BF)
            split["one"][half] = (jnp.concatenate(blocks(qkv) + [out, gap, upper]),)
            split["two"][half] = (jnp.concatenate(blocks(up) + [lower]),)
        place_shards("one", mine, CORES, list(split["one"].items()), weights, ("first", "down"))
        place_shards("two", mine, CORES, list(split["two"].items()), weights, ("up", "down"))
        put_up = put_down = lambda mark: None
        norms = jnp.concatenate([norm_gains[0], norm_shifts[0]])
        packed = gather(jnp.concatenate([biases[0], norms.reshape(-1)])[None]).astype(F32)
        norms_all = packed[:, cut:].reshape(shards, 4, width).transpose(1, 0, 2)
        small = jnp.concatenate(
            [
                packed[:, :cut].reshape(BIAS_ROWS, D),
                norms_all.reshape(4, D),
                jnp.zeros((4, D), F32),
            ]
        )
    common = (section, lengths[:, 0])
    if not ring:
        inputs, cotangent = turn_rows(lengths[:, 0], inputs, cotangent)

    def run_forward(origin, row, source, parts=("attn", "up", "down"), marked=False, earlier=()):
        return forward(
            origin, row, parts, common, small, source, states[row], weights, marked, earlier
        )

    def run_backward(origin, row, source, parts=("ffn", "attn"), earlier=()):
        return backward(
            origin, row, parts, common, small, source, states[row], weights, earlier
        )

    mark = run_forward(0, 0, inputs[0], ("attn",), True)
    put_up(mark)
    run_forward(0, 0, None, ("up",))
    put_down(states[0]["slope"])
    result = run_forward(0, 0, None, ("down",))
    coming = relay(result, 1)
    second = relay(run_forward(0, 1, inputs[1]), 1)
    run_forward(1, 0, coming)
    coming = relay(run_backward(1, 0, cotangent[0]), -1)
    run_forward(1, 1, second, earlier=(states[0]["attn_sums"],))
    second = relay(run_backward(1, 1, cotangent[1]), -1)
    run_backward(0, 0, coming)
    halves = {}
    earlier = ()
    for piece in ("down", "up", "first"):
        halves[piece] = first_row_grad(piece, states[0], earlier)
        earlier = (halves[piece],)
    run_backward(0, 1, second, ("ffn",), earlier)
    down_own, *down_others = weight_grad("down", groups, mine, states, halves["down"])
    up_own, *up_others = weight_grad(
        "up", groups, mine, states, halves["up"], (down_own,)
    )
    RingScatter.order = (up_own,)
    if ring:
        ffn_ring = RingScatter("ffn", BLOCKS * width)
        ffn_ring.add(down_own, down_others, {1: slice(None)})
        ffn_ring.add(up_own, up_others, {-1: slice(None)})
    run_backward(0, 1, None, ("attn",), RingScatter.order)
    attn_own, *attn_others = weight_grad(
        "first", groups, mine, states, halves["first"]
    )
    if ring:
        RingScatter.order = (attn_own,)
        ffn_ring.step(3)
        attn_ring = RingScatter("attn", 2 * width)
        cuts = {1: slice(0, 2 * width), -1: slice(2 * width, None)}
        attn_ring.add(attn_own, attn_others, cuts, tuple(ffn_ring.came.values()))
        ffn_ring.step(2)
        attn_ring.step(3)
        ffn_ring.last_step(0)
        attn_ring.step(2)
        ffn_ring.last_step(1)
        attn_ring.step(1)
        ffn = ffn_ring.finish({"down": (BLOCKS * width, D), "up": (width, FF)}, mine)
        down_sum, up_sum = ffn["down"], ffn["up"]
        shapes = {"qkv": (width, 3 * D), "out": (width, D), "bias": (1, cut)}
        shapes.update({"gains": (2, width), "shifts": (2, width)})
        attn = attn_ring.finish(shapes, mine)
        qkv_sum, out_sum, bias_sum = attn["qkv"], attn["out"], attn["bias"]
        gain_sum, shift_sum = attn["gains"], attn["shifts"]
    else:
        scatter = lambda value: lax.psum_scatter(
            value, "batch", scatter_dimension=0, tiled=True
        ).astype(F32)
        half = D // CORES
        join = lambda parts: jnp.concatenate(
            [
                jnp.concatenate([part[0, chunk(j, half)] for part in parts])
                for j in range(BLOCKS)
            ],
            axis=1,
        )
        down_sum = scatter(jnp.concatenate([down_own[0], down_others[0][0]]))
        up_sum = scatter(join((up_own, up_others[0])))
        attn_sum = scatter(join((attn_own, attn_others[0])))
        qkv_sum, out_sum = attn_sum[:, : 3 * D], attn_sum[:, 3 * D :]
        ffn_sums = states[0]["ffn_sums"] + states[1]["ffn_sums"]
        attn_sums = states[0]["attn_sums"] + states[1]["attn_sums"]
        bias_total = jnp.concatenate([attn_sums[:2], ffn_sums[4:10]]).reshape(shards, cut)
        norm_rows = ffn_sums[:4].reshape(4, shards, width).transpose(1, 0, 2)
        small_sum = scatter(
            jnp.concatenate([bias_total, norm_rows.reshape(shards, 4 * width)], axis=1)
        )
        bias_sum = small_sum[:, :cut]
        norm_sum = small_sum[:, cut:].reshape(4, width)
        gain_sum, shift_sum = norm_sum[:2], norm_sum[2:]
    rows = leave_rows(states, lengths[:, 0], RingScatter.order if ring else ())
    return (
        rows["activations"][None, :, None],
        rows["input_grads"][None, :, None],
        qkv_sum[None],
        out_sum[None],
        up_sum[None],
        down_sum[None],
        bias_sum,
        gain_sum[None],
        shift_sum[None],
    )


def solution(mesh):
    in_specs = (
        P(None, "batch", None, None),
        P(None, "batch", None, None),
        P(None, "batch", None),
        P("section", "batch", None),
        P("section", "batch", None),
        P("section", "batch", None),
        P("section", "batch", None),
        P("section", "batch"),
        P("section", None, "batch"),
        P("section", None, "batch"),
    )
    out_specs = (
        P("section", None, "batch", None, None),
        P("section", None, "batch", None, None),
        P("section", "batch", None),
        P("section", "batch", None),
        P("section", "batch", None),
        P("section", "batch", None),
        P("section", "batch"),
        P("section", None, "batch"),
        P("section", None, "batch"),
    )
    return jax.shard_map(body, mesh=mesh, in_specs=in_specs, out_specs=out_specs, check_vma=False)
```
